32 devices in a mesh: ctx: 8 (over y, x, core), head: 4 (over z).
Axes of the slice: x: 2, y: 2, z: 4, core: 2. Of those that a mesh axis runs over, the one named last changes fastest.
Arguments:
- query_rows: bfloat16 [4096, 2048], P('ctx', 'head'), may hold values from -12 to 12
- key_rows: bfloat16 [4096, 2048], P('ctx', 'head'), may hold values from -12 to 12
- value_rows: bfloat16 [4096, 2048], P('ctx', 'head'), may hold values from -6 to 6
- grad_out: bfloat16 [4096, 2048], P('ctx', 'head'), may hold values from -6 to 6
- house_dirs: float32 [32, 2048], P('ctx', 'head'), may hold values from -6 to 6
- owners: int32 [32, 2], P('ctx'), may hold values from 0 to 7, all different within a row; in each aligned block of 4 rows (0 to 3, 4 to 7, ...) at most 2 rows name the same one
- offsets: int32 [32, 2], P('ctx'), may hold values from 0 to 3
- w_query: bfloat16 [4096, 2048], P(None, 'head'), may hold values from -0.09375 to 0.09375
- w_key: bfloat16 [4096, 2048], P(None, 'head'), may hold values from -0.09375 to 0.09375
- w_value: bfloat16 [4096, 2048], P(None, 'head'), may hold values from -0.09375 to 0.09375
Outputs:
- input_grad: bfloat16 [4096, 4096], P('ctx', 'head')
- house_grad: float32 [32, 2048], P('ctx', 'head')
The draws below stay inside these ranges and needn't reach their ends.
Inputs may be any that keep to these rules, and one draw needn't show every extreme that they name: `owners`: each query block names 2 different ctx indices; the query blocks of one ctx index name any one ctx index at most 2 times, and exactly 2 times for some.
All inputs are finite; a program needn't handle non-finite values.
Results may differ from the reference program's by a relative error of at most 0.025.
Values may be sent and summed in bfloat16 or wider, within the bound.
No kernel may reach another device: no remote copies, remote signals or barrier semaphores. Data moves between devices by JAX's collectives and lax.ppermute only.
A program may use at most 128 MiB of HBM per device.

```python
import math
import jax
import jax.numpy as jnp
import numpy as np
from jax import lax

D = 4096
HEADS = 16
DH = 128
BLK = 128
MAXL = 2
CAP = 2
BLK_DEV = 4
NB = 32
TOKENS = 4096
HGRP = 4
N_CTX = 8
N_HEAD = 4


def paired_rows(key, which):
    fresh_rows = jax.random.normal(jax.random.fold_in(key, 31 + which), (TOKENS, HEADS * DH), jnp.float32)
    fresh_rows = jnp.clip(fresh_rows, -6.0, 6.0)
    return fresh_rows


def draw_query_rows(key, part):
    return paired_rows(key, 0).astype(jnp.bfloat16)


def draw_key_rows(key, part):
    return paired_rows(key, 1).astype(jnp.bfloat16)


def place_ends(array, rng, least, high):
    longest = array.shape.index(max(array.shape))
    spots = []
    for shift in (0, 1):
        where = [jax.random.randint(jax.random.fold_in(rng, axis), (), 0, length) for axis, length in enumerate(array.shape)]
        where[longest] = (where[longest] + shift) % array.shape[longest]
        spots.append(tuple(where))
    return array.at[spots[0]].set(least).at[spots[1]].set(high)


def steps_of(stream_key, dims, cuts, smallest, largest):
    gain = 1.0
    for dim, parts in cuts:
        steps = jax.random.uniform(jax.random.fold_in(jax.random.fold_in(stream_key, 6), dim), (parts,), jnp.float32, smallest / len(cuts), largest / len(cuts))
        gain = gain * jnp.repeat(jnp.exp(steps), dims[dim] // parts).reshape((-1,) + (1,) * (len(dims) - 1 - dim))
    return gain


def shared_out(key, own, number, rows, amount, top, limit, skew):
    order = jax.random.permutation(key, amount)
    heavy_load, ordinary = portions_of(amount, rows * top, limit, skew, True), portions_of(amount, rows * top, limit, skew, False)
    places = jnp.arange(amount)

    def named(sizes, rotation):
        used = int((sizes > 0).sum())
        fixed = max(1, used // 4)
        moved = fixed + (places - fixed + rotation * (used - fixed)) % max(1, amount - fixed)
        return jnp.zeros((amount,), jnp.int32).at[order[jnp.where(places < fixed, places, moved)]].set(jnp.asarray(sizes, jnp.int32))

    sizes = jnp.where(number % 4 == 0, named(heavy_load, number // 4), named(ordinary, number - number // 4 - 1))
    mixed = jax.random.permutation(jax.random.fold_in(own, 3), amount)
    source_of, taker = mixed[0:amount // 2 * 2:2], mixed[1:amount // 2 * 2:2]
    margin = jnp.minimum(sizes[source_of] - 1, limit - sizes[taker]) // 2
    margin = jnp.where((source_of == order[0]) | (taker == order[0]) | (sizes[taker] == 0), 0, jnp.maximum(margin, 0))
    moved = jax.random.randint(jax.random.fold_in(own, 4), (amount // 2,), 0, 1 << 20) % (margin + 1)
    sizes = sizes.at[source_of].add(-moved).at[taker].add(moved)
    labels = jnp.searchsorted(jnp.cumsum(sizes), jnp.arange(rows * top), side="right").astype(jnp.int32)
    listing = labels.reshape(top, rows).T
    listing = listing[jax.random.permutation(jax.random.fold_in(own, 1), rows)]
    rotation = jax.random.randint(jax.random.fold_in(own, 2), (rows, 1), 0, top)
    return jnp.take_along_axis(listing, (jnp.arange(top)[None, :] + rotation) % top, axis=1)


def portions_of(count, total, bound, skew, full):
    portions = [(1 << 20) // math.isqrt(standing ** skew) + 1 for standing in range(1, count + 1)]
    largest = bound if full else min(bound, max(-(-total // count), total * portions[0] // sum(portions)))
    least = 1 if total - largest >= count - 1 else 0
    counts, rest = [largest] + [least] * (count - 1), total - largest - least * (count - 1)
    while rest > 0:
        movable = [i for i in range(1, count) if counts[i] < largest] or [i for i in range(1, count) if counts[i] < bound]
        whole, remaining = sum([portions[i] for i in movable]), rest
        for i in movable:
            addition = min(bound - counts[i], max(1, remaining * portions[i] // whole), rest)
            counts[i] = counts[i] + addition
            rest = rest - addition
    return np.array(counts)


def centred(rng, shape, width, limit, shards=(), kind=jnp.bfloat16):
    result = width * jax.random.normal(rng, shape, jnp.float32)
    if shards:
        result = result * steps_of(rng, shape, shards, -0.22, 0.18)
    return jnp.clip(result, -limit, limit).astype(kind)


def setup_inputs(seed: int = 0) -> dict:
    key_of = jax.random.split(jax.random.key(seed), 11)
    query_rows = draw_query_rows(jax.random.fold_in(key_of[10], 71), 0)
    key_rows = draw_key_rows(jax.random.fold_in(key_of[10], 71), 0)
    value_rows = centred(key_of[2], (TOKENS, HEADS * DH), 1.0, 6.0, ((0, 8), (1, 4)))
    grad_out = centred(key_of[3], (TOKENS, HEADS * DH), 1.0, 6.0, ((0, 8), (1, 4)))
    house_dirs = centred(key_of[4], (NB, HEADS * DH), 1.0, 6.0, ((0, 8), (1, 4)), jnp.float32)
    owners_keys = jax.random.split(jax.random.fold_in(key_of[5], 1), NB // BLK_DEV)
    owners_turns = jax.random.permutation(jax.random.fold_in(key_of[5], 3), NB // BLK_DEV)
    owners = jax.vmap(lambda own, number: shared_out(jax.random.fold_in(key_of[5], 2), own, number, BLK_DEV, N_CTX, MAXL, CAP, 2))(owners_keys, owners_turns).reshape((NB, MAXL))
    offsets = place_ends(jax.random.randint(key_of[6], (NB, MAXL), 0, BLK_DEV), jax.random.fold_in(key_of[6], 1), 0, BLK_DEV - 1).astype(jnp.int32)
    w_query = centred(key_of[7], (D, HEADS * DH), D ** -0.5, 0.09375, ((1, 4),))
    w_key = centred(key_of[8], (D, HEADS * DH), D ** -0.5, 0.09375, ((1, 4),))
    w_value = centred(key_of[9], (D, HEADS * DH), D ** -0.5, 0.09375, ((1, 4),))
    return dict(query_rows=query_rows, key_rows=key_rows, value_rows=value_rows, grad_out=grad_out, house_dirs=house_dirs, owners=owners, offsets=offsets, w_query=w_query, w_key=w_key, w_value=w_value)


HIGH = lax.Precision.HIGHEST

def narrowed(values_in):
    return lax.optimization_barrier(values_in.astype(jnp.bfloat16)).astype(jnp.float32)

def reflect_apply(unit_dirs, matrices):
    projected = jnp.einsum('hn,hnk->hk', unit_dirs, matrices, precision=HIGH)
    return matrices - 2.0 * unit_dirs[:, :, None] * projected[:, None, :]

def attend(query_blk, key_blk, value_blk, grad_blk, remote_keys, remote_values, scaling):
    block_count, block_rows, head_count, head_size = query_blk.shape
    tok_rows = block_count * block_rows
    query_tok = query_blk.reshape(tok_rows, head_count, head_size)
    key_tok = key_blk.reshape(tok_rows, head_count, head_size)
    value_tok = value_blk.reshape(tok_rows, head_count, head_size)
    grad_tok = grad_blk.reshape(tok_rows, head_count, head_size)
    position = jnp.arange(tok_rows)
    local_scores = jnp.einsum('thd,uhd->htu', query_tok, key_tok) * scaling
    local_scores = jnp.where(position[:, None] >= position[None, :], local_scores, -jnp.inf)
    remote_scores = jnp.einsum('bthd,bkhd->bhtk', query_blk, remote_keys) * scaling

    def to_heads(per_block):
        return per_block.transpose(1, 0, 2).reshape(head_count, tok_rows)

    def to_blocks(per_head):
        return per_head.reshape(head_count, block_count, block_rows).transpose(1, 0, 2)[..., None]
    top_score = jnp.maximum(lax.optimization_barrier(jnp.max(local_scores, axis=2)), to_heads(lax.optimization_barrier(jnp.max(remote_scores, axis=3))))
    exp_total = lax.optimization_barrier(jnp.sum(jnp.exp(local_scores - top_score[:, :, None]), axis=2))
    exp_total = exp_total + to_heads(lax.optimization_barrier(jnp.sum(jnp.exp(remote_scores - to_blocks(top_score)), axis=3)))
    log_total = top_score + jnp.log(exp_total)
    local_probs = jnp.exp(local_scores - log_total[:, :, None])
    remote_probs = jnp.exp(remote_scores - to_blocks(log_total))
    local_pb = narrowed(local_probs)
    remote_pb = narrowed(remote_probs)
    attended = jnp.einsum('htu,uhd->thd', local_pb, value_tok)
    attended = attended + jnp.einsum('bhtk,bkhd->bthd', remote_pb, remote_values).reshape(tok_rows, head_count, head_size)
    delta = lax.optimization_barrier(jnp.sum(grad_tok * attended, axis=2)).T
    local_ds = narrowed(local_probs * (jnp.einsum('thd,uhd->htu', grad_tok, value_tok) - delta[:, :, None]))
    remote_ds = narrowed(remote_probs * (jnp.einsum('bthd,bkhd->bhtk', grad_blk, remote_values) - to_blocks(delta)))
    dq_rot = jnp.einsum('htu,uhd->thd', local_ds, key_tok)
    dq_rot = scaling * (dq_rot + jnp.einsum('bhtk,bkhd->bthd', remote_ds, remote_keys).reshape(tok_rows, head_count, head_size))
    dk_local = scaling * jnp.einsum('htu,thd->uhd', local_ds, query_tok)
    dv_local = jnp.einsum('htu,thd->uhd', local_pb, grad_tok)
    part_key = (scaling * jnp.einsum('bhtk,bthd->bkhd', remote_ds, query_blk)).astype(jnp.bfloat16)
    part_value = jnp.einsum('bhtk,bthd->bkhd', remote_pb, grad_blk).astype(jnp.bfloat16)
    return (dq_rot, dk_local, dv_local, part_key, part_value)

def reference(query_rows, key_rows, value_rows, grad_out, house_dirs, owners, offsets, w_query, w_key, w_value):
    all_blocks = BLK_DEV * N_CTX
    house_heads = house_dirs.reshape(all_blocks, HEADS, DH)
    lengths = jnp.sqrt(lax.optimization_barrier(jnp.sum(house_heads * house_heads, axis=-1, keepdims=True)) + 1e-06)
    unit_dirs = house_heads / lengths
    identity = jnp.broadcast_to(jnp.eye(DH, dtype=jnp.float32), (HEADS, DH, DH))

    def forward(carry, unit_now):
        updated = reflect_apply(unit_now, carry)
        return (updated, updated)
    _, cumulative = lax.scan(forward, identity, unit_dirs)
    query_f32 = query_rows.astype(jnp.float32).reshape(all_blocks, BLK, HEADS, DH)
    key_f32 = key_rows.astype(jnp.float32).reshape(all_blocks, BLK, HEADS, DH)
    query_rot = narrowed(jnp.einsum('bthn,bhnm->bthm', query_f32, cumulative, precision=HIGH))
    key_rot = narrowed(jnp.einsum('bthn,bhnm->bthm', key_f32, cumulative, precision=HIGH))
    value_f32 = value_rows.astype(jnp.float32).reshape(all_blocks, BLK, HEADS, DH)
    grad_f32 = grad_out.astype(jnp.float32).reshape(all_blocks, BLK, HEADS, DH)
    block_ids = (owners * BLK_DEV + offsets).astype(jnp.int32)
    segment_ids = block_ids.reshape(N_CTX, BLK_DEV * MAXL)
    scaling = DH ** (-0.5)

    def by_segment(array_in):
        return array_in.reshape(N_CTX, BLK_DEV, BLK, HEADS, DH)

    def one_segment(inputs):
        query_seg, key_seg, value_seg, grad_seg, listed = inputs
        remote_keys = key_rot[listed].reshape(BLK_DEV, MAXL * BLK, HEADS, DH)
        remote_values = value_f32[listed].reshape(BLK_DEV, MAXL * BLK, HEADS, DH)
        return attend(query_seg, key_seg, value_seg, grad_seg, remote_keys, remote_values, scaling)
    dq_rot, dk_local, dv_local, part_key, part_value = lax.map(one_segment, (by_segment(query_rot), by_segment(key_rot), by_segment(value_f32), by_segment(grad_f32), segment_ids))
    flat_ids = block_ids.reshape(all_blocks * MAXL)
    part_key = lax.optimization_barrier(part_key).astype(jnp.float32).reshape(all_blocks * MAXL, BLK, HEADS, DH)
    part_value = lax.optimization_barrier(part_value).astype(jnp.float32).reshape(all_blocks * MAXL, BLK, HEADS, DH)
    dq_rot = dq_rot.reshape(all_blocks, BLK, HEADS, DH)
    dk_rot = dk_local.reshape(all_blocks, BLK, HEADS, DH) + jax.ops.segment_sum(part_key, flat_ids, num_segments=all_blocks)
    dv_all = dv_local.reshape(all_blocks, BLK, HEADS, DH) + jax.ops.segment_sum(part_value, flat_ids, num_segments=all_blocks)
    dq_out = jnp.einsum('bthm,bhnm->bthn', dq_rot, cumulative, precision=HIGH).astype(jnp.bfloat16).reshape(TOKENS, HEADS * DH)
    dk_out = jnp.einsum('bthm,bhnm->bthn', dk_rot, cumulative, precision=HIGH).astype(jnp.bfloat16).reshape(TOKENS, HEADS * DH)
    dv_out = dv_all.astype(jnp.bfloat16).reshape(TOKENS, HEADS * DH)
    dcum = jnp.einsum('bthn,bthm->bhnm', query_f32, dq_rot, precision=HIGH)
    dcum = dcum + jnp.einsum('bthn,bthm->bhnm', key_f32, dk_rot, precision=HIGH)
    previous = jnp.concatenate([identity[None], cumulative[:-1]], axis=0)

    def backward(carry, inputs):
        dcum_now, unit_now, before = inputs
        adjoint = dcum_now + carry
        dreflect = jnp.einsum('hmn,hkn->hmk', adjoint, before, precision=HIGH)
        return (reflect_apply(unit_now, adjoint), dreflect)
    _, dreflect = lax.scan(backward, jnp.zeros((HEADS, DH, DH), jnp.float32), (dcum, unit_dirs, previous), reverse=True)
    dunit = jnp.einsum('bhmn,bhn->bhm', dreflect, unit_dirs, precision=HIGH)
    dunit = -2.0 * (dunit + jnp.einsum('bhnm,bhn->bhm', dreflect, unit_dirs, precision=HIGH))
    house_grad = (dunit - unit_dirs * lax.optimization_barrier(jnp.sum(unit_dirs * dunit, axis=-1, keepdims=True))) / lengths
    house_grad = house_grad.reshape(all_blocks, HEADS * DH)
    group_width = HGRP * DH
    summed = jnp.zeros((TOKENS, D), jnp.float32)
    for group in range(N_HEAD):
        first = group * group_width
        term = jnp.dot(dq_out[:, first:first + group_width], w_query[:, first:first + group_width].T, preferred_element_type=jnp.float32)
        term = term + jnp.dot(dk_out[:, first:first + group_width], w_key[:, first:first + group_width].T, preferred_element_type=jnp.float32)
        term = term + jnp.dot(dv_out[:, first:first + group_width], w_value[:, first:first + group_width].T, preferred_element_type=jnp.float32)
        summed = summed + narrowed(term)
    return (summed.astype(jnp.bfloat16), house_grad)
```

```python
import functools

import jax
import jax.numpy as jnp
from jax import lax
from jax.experimental import pallas as pl
from jax.experimental.pallas import tpu as pltpu
from jax.sharding import PartitionSpec as P

DH = 128
BLK = 128
MAXL = 2
HIGH = lax.Precision.HIGHEST
F32 = jnp.float32
BF16 = jnp.bfloat16
VMEM_BYTES = 52 * 1024 * 1024


def nn(a, b):
    return lax.dot_general(a, b, (((1,), (0,)), ((), ())), preferred_element_type=F32)


def nt(a, b):
    return lax.dot_general(a, b, (((1,), (1,)), ((), ())), preferred_element_type=F32)


def tn(a, b):
    return lax.dot_general(a, b, (((0,), (0,)), ((), ())), preferred_element_type=F32)


def nn_high(a, b):
    return lax.dot_general(
        a, b, (((1,), (0,)), ((), ())), precision=HIGH, preferred_element_type=F32
    )


def nt_high(a, b):
    return lax.dot_general(
        a, b, (((1,), (1,)), ((), ())), precision=HIGH, preferred_element_type=F32
    )


def split(value):
    top = value.astype(BF16)
    return top, (value - top.astype(F32)).astype(BF16)


def iota(shape, dim):
    return lax.broadcasted_iota(jnp.int32, shape, dim)


def head(h):
    return slice(h * DH, (h + 1) * DH)


def compiler_params():
    return pltpu.CompilerParams(vmem_limit_bytes=VMEM_BYTES)


def in_vmem(count):
    return [pl.BlockSpec(memory_space=pltpu.VMEM)] * count


def chain_kernel(
    heads,
    blocks,
    base_ref,
    owners_ref,
    offsets_ref,
    house_ref,
    query_ref,
    key_ref,
    unit_ref,
    rows_ref,
    inv_ref,
    qrot_ref,
    krot_ref,
    local_ref,
    list_hi_ref,
    list_lo_ref,
    unit_t,
    unit_h,
):
    count = house_ref.shape[0]
    eye = (iota((count, count), 0) == iota((count, count), 1)).astype(F32)
    for h in range(heads):
        house = house_ref[:, head(h)]
        lengths = jnp.sqrt(jnp.sum(house * house, axis=1, keepdims=True) + 1e-06)
        unit_ref[:, head(h)] = house / lengths
        unit_h[h] = house / lengths
        inv_ref[h] = eye

    def eliminate(step, carry):
        below = iota((count, 1), 0) > step
        for h in range(heads):
            pivot = unit_h[h, pl.ds(step, 1), :]
            overlap = jnp.sum(unit_h[h] * pivot, axis=1, keepdims=True)
            factor = jnp.where(below, 2.0 * overlap, 0.0)
            inv_ref[h] = inv_ref[h] - factor * inv_ref[h, pl.ds(step, 1), :]
        return carry

    lax.fori_loop(0, count, eliminate, 0)
    eye_wide = (iota((DH, DH), 0) == iota((DH, DH), 1)).astype(F32)
    for h in range(heads):
        units = unit_ref[:, head(h)]
        rows_ref[:, head(h)] = nn_high(inv_ref[h], units)
        unit_t[h] = nt_high(eye_wide, units)

    def cumulative(h, block):
        kept = jnp.where(iota((DH, count), 1) <= block, unit_t[h], 0.0)
        return split(eye_wide - 2.0 * nn_high(kept, rows_ref[:, head(h)]))

    base = base_ref[0] * blocks

    def local_block(b, carry):
        here = pl.ds(pl.multiple_of(b * BLK, BLK), BLK)
        for h in range(heads):
            hi, lo = cumulative(h, base + b)
            local_ref[b, h] = hi
            query, key = query_ref[here, head(h)], key_ref[here, head(h)]
            qrot_ref[here, head(h)] = (nn(query, hi) + nn(query, lo)).astype(BF16)
            krot_ref[here, head(h)] = (nn(key, hi) + nn(key, lo)).astype(BF16)
        return carry

    lax.fori_loop(0, blocks, local_block, 0)

    def listed_block(e, carry):
        a, l = e // MAXL, e % MAXL
        block = owners_ref[a, l] * blocks + offsets_ref[a, l]
        for h in range(heads):
            hi, lo = cumulative(h, block)
            list_hi_ref[e, h] = hi
            list_lo_ref[e, h] = lo
        return carry

    lax.fori_loop(0, blocks * MAXL, listed_block, 0)


def run_chain(me, owners, offsets, house_all, query_rows, key_rows, heads, blocks):
    count = house_all.shape[0]
    rows, width = query_rows.shape
    entries = blocks * MAXL
    smem = [pl.BlockSpec(memory_space=pltpu.SMEM)] * 3
    return pl.pallas_call(
        functools.partial(chain_kernel, heads, blocks),
        out_shape=[
            jax.ShapeDtypeStruct((count, width), F32),
            jax.ShapeDtypeStruct((count, width), F32),
            jax.ShapeDtypeStruct((heads, count, count), F32),
            jax.ShapeDtypeStruct((rows, width), BF16),
            jax.ShapeDtypeStruct((rows, width), BF16),
            jax.ShapeDtypeStruct((blocks, heads, DH, DH), BF16),
            jax.ShapeDtypeStruct((entries, heads, DH, DH), BF16),
            jax.ShapeDtypeStruct((entries, heads, DH, DH), BF16),
        ],
        in_specs=smem + in_vmem(3),
        out_specs=in_vmem(8),
        scratch_shapes=[
            pltpu.VMEM((heads, DH, count), F32),
            pltpu.VMEM((heads, count, DH), F32),
        ],
        compiler_params=compiler_params(),
        name="house_chain",
    )(me, owners, offsets, house_all, query_rows, key_rows)


def attend_kernel(heads, blocks, sources, pieces, *refs):
    me_ref, owners_ref, offsets_ref = refs[:3]
    key_srcs = refs[3 : 3 + sources]
    value_srcs = refs[3 + sources : 3 + 2 * sources]
    refs = refs[3 + 2 * sources :]
    (query_ref, qrot_ref, krot_ref, value_ref, grad_ref, local_ref, hi_ref, lo_ref) = refs[:8]
    dq_ref, dcum_ref, dk_ref, dv_ref = refs[8:12]
    outs = refs[12 : 12 + max(pieces, 1)]
    refs = refs[12 + max(pieces, 1) :]
    far_keys, far_values, sems = refs[:3]
    width = heads * DH
    entries = blocks * MAXL
    scaling = DH ** (-0.5)

    def start(e, src, kind, slot, where):
        pltpu.make_async_copy(src.at[where], slot.at[e], sems.at[kind, e]).start()

    for e in range(entries):
        owner, offset = owners_ref[e // MAXL, e % MAXL], offsets_ref[e // MAXL, e % MAXL]
        here = pl.ds(pl.multiple_of(offset * BLK, BLK), BLK)
        if sources == 1:
            start(e, key_srcs[0], 0, far_keys, (owner, here))
            start(e, value_srcs[0], 1, far_values, (owner, here))
        else:
            distance = owner ^ me_ref[0]
            for r in range(sources):

                @pl.when(distance == r)
                def _():
                    start(e, key_srcs[r], 0, far_keys, here)
                    start(e, value_srcs[r], 1, far_values, here)

    if pieces:
        payload, out_sems = refs[3:5]
        payload[...] = jnp.zeros_like(payload)
    else:
        payload = None
    for kind, slots in ((0, far_keys), (1, far_values)):
        for e in range(entries):
            pltpu.make_async_copy(slots.at[e], slots.at[e], sems.at[kind, e]).wait()

    for h in range(heads):
        lanes = head(h)
        v_lanes = slice(width + h * DH, width + (h + 1) * DH)
        for a in range(blocks):
            near = (a + 1) * BLK
            here = slice(a * BLK, near)
            keys, values = [krot_ref[:near, lanes]], [value_ref[:near, lanes]]
            for l in range(MAXL):
                e = a * MAXL + l
                raw = far_keys[e, :, lanes]
                keys.append((nn(raw, hi_ref[e, h]) + nn(raw, lo_ref[e, h])).astype(BF16))
                values.append(far_values[e, :, lanes])
            keys, values = jnp.concatenate(keys, axis=0), jnp.concatenate(values, axis=0)
            qrot, grad = qrot_ref[here, lanes], grad_ref[here, lanes]
            scores = nt(keys, qrot) * scaling
            shape = scores.shape
            row, col = iota(shape, 0), iota(shape, 1)
            hidden = (row < near) & (row - a * BLK > col)
            scores = jnp.where(hidden, -jnp.inf, scores)
            top = jnp.max(scores, axis=0, keepdims=True)
            weight = jnp.exp(scores - top)
            probs = weight * (1.0 / jnp.sum(weight, axis=0, keepdims=True))
            probs_b = probs.astype(BF16)
            dprobs = nt(values, grad)
            delta = jnp.sum(probs_b.astype(F32) * dprobs, axis=0, keepdims=True)
            dscores = (probs * (dprobs - delta)).astype(BF16)
            dq_rot = tn(dscores, keys) * scaling
            dq_top, dq_low = split(dq_rot)
            dq_ref[here, lanes] = nt(dq_top, local_ref[a, h]).astype(BF16)
            query = query_ref[here, lanes]
            dcum_ref[a, h] = tn(query, dq_top) + tn(query, dq_low)
            dkeys = nn(dscores, qrot) * scaling
            dvalues = nn(probs_b, grad)
            if a > 0:
                dk_ref[: near - BLK, lanes] += dkeys[: near - BLK]
                dv_ref[: near - BLK, lanes] += dvalues[: near - BLK]
            dk_ref[here, lanes] = dkeys[near - BLK : near]
            dv_ref[here, lanes] = dvalues[near - BLK : near]
            for l in range(MAXL):
                e = a * MAXL + l
                part = slice(near + l * BLK, near + (l + 1) * BLK)
                part_k, part_v = dkeys[part].astype(BF16), dvalues[part].astype(BF16)
                if pieces:
                    distance = owners_ref[a, l] ^ me_ref[0]
                    spot = (distance & 1) * blocks + offsets_ref[a, l]
                    chip = distance >> 1
                    payload[spot, chip, :, lanes] += part_k
                    payload[spot, chip, :, v_lanes] += part_v
                else:
                    outs[0][e, :, lanes] = part_k
                    outs[0][e, :, v_lanes] = part_v
    if pieces:
        copies = [
            pltpu.make_async_copy(payload.at[i], outs[i], out_sems.at[i]) for i in range(pieces)
        ]
        for copy in copies:
            copy.start()
        for copy in copies:
            copy.wait()


def run_attend(me, owners, offsets, key_srcs, value_srcs, arrays, heads, blocks, pieces):
    rows, width = arrays[0].shape
    entries = blocks * MAXL
    sources = len(key_srcs)
    any_spec = pl.BlockSpec(memory_space=pl.ANY)
    smem = [pl.BlockSpec(memory_space=pltpu.SMEM)] * 3
    scratch = [
        pltpu.VMEM((entries, BLK, width), BF16),
        pltpu.VMEM((entries, BLK, width), BF16),
        pltpu.SemaphoreType.DMA((2, entries)),
    ]
    if pieces:
        chips = sources // 2
        out_parts = [jax.ShapeDtypeStruct((chips, BLK, 2 * width), BF16)] * pieces
        part_specs = [any_spec] * pieces
        scratch += [
            pltpu.VMEM((pieces, chips, BLK, 2 * width), BF16),
            pltpu.SemaphoreType.DMA((pieces,)),
        ]
    else:
        out_parts = [jax.ShapeDtypeStruct((entries, BLK, 2 * width), BF16)]
        part_specs = in_vmem(1)
    return pl.pallas_call(
        functools.partial(attend_kernel, heads, blocks, sources, pieces),
        out_shape=[
            jax.ShapeDtypeStruct((rows, width), BF16),
            jax.ShapeDtypeStruct((blocks, heads, DH, DH), F32),
            jax.ShapeDtypeStruct((rows, width), F32),
            jax.ShapeDtypeStruct((rows, width), F32),
        ]
        + out_parts,
        in_specs=smem + [any_spec] * (2 * sources) + in_vmem(8),
        out_specs=in_vmem(4) + part_specs,
        scratch_shapes=scratch,
        compiler_params=compiler_params(),
        name="attend",
    )(me, owners, offsets, *key_srcs, *value_srcs, *arrays)


def project_kernel(heads, parts, *refs):
    part_refs = refs[:parts]
    dk_loc, dv_loc, dq_ref, key_ref, dcum_in, cum_ref, wq, wk, wv = refs[parts : parts + 9]
    out_ref, dcum_out, dk_ref, dv_ref = refs[parts + 9 :]
    width = heads * DH

    @pl.when(pl.program_id(0) == 0)
    def _():
        total = part_refs[0][...].astype(F32)
        for ref in part_refs[1:]:
            total = total + ref[...].astype(F32)
        dv_ref[...] = (dv_loc[...] + total[:, width:]).astype(BF16)
        for h in range(heads):
            dk_rot = dk_loc[:, head(h)] + total[:, head(h)]
            dk_top, dk_low = split(dk_rot)
            dk_ref[:, head(h)] = nt(dk_top, cum_ref[0, h]).astype(BF16)
            key = key_ref[:, head(h)]
            dcum_out[h] = dcum_in[0, h] + tn(key, dk_top) + tn(key, dk_low)

    term = nt(dq_ref[...], wq[...]) + nt(dk_ref[...], wk[...]) + nt(dv_ref[...], wv[...])
    out_ref[0] = term.astype(BF16)


def run_project(block, parts, dk_loc, dv_loc, dq, key_rows, dcum, cum, weights, heads, groups):
    width = heads * DH
    model = weights[0].shape[0]
    chunk = model // groups
    tile = min(512, chunk)
    per = chunk // tile
    rows_spec = pl.BlockSpec((BLK, width), lambda t: (block, 0))
    part_spec = pl.BlockSpec((BLK, 2 * width), lambda t: (0, 0))
    head_spec = pl.BlockSpec((1, heads, DH, DH), lambda t: (block, 0, 0, 0))
    weight_spec = pl.BlockSpec((tile, width), lambda t: (t, 0))
    return pl.pallas_call(
        functools.partial(project_kernel, heads, len(parts)),
        grid=(model // tile,),
        out_shape=[
            jax.ShapeDtypeStruct((groups, BLK, chunk), BF16),
            jax.ShapeDtypeStruct((heads, DH, DH), F32),
        ],
        in_specs=[part_spec] * len(parts)
        + [rows_spec] * 4
        + [head_spec] * 2
        + [weight_spec] * 3,
        out_specs=[
            pl.BlockSpec((1, BLK, tile), lambda t: (t // per, 0, t % per)),
            pl.BlockSpec((heads, DH, DH), lambda t: (0, 0, 0)),
        ],
        scratch_shapes=[pltpu.VMEM((BLK, width), BF16), pltpu.VMEM((BLK, width), BF16)],
        compiler_params=compiler_params(),
        cost_estimate=pl.CostEstimate(
            flops=6 * BLK * model * width, bytes_accessed=6 * model * width, transcendentals=0
        ),
        name="project",
    )(*parts, dk_loc, dv_loc, dq, key_rows, dcum, cum, *weights)


def adjoint_kernel(heads, blocks, base_ref, *refs):
    dcums = refs[:blocks]
    unit_ref, rows_ref, inv_ref, out_ref = refs[blocks:]
    count, width = unit_ref.shape
    square = (count, count)
    eye = (iota(square, 0) == iota(square, 1)).astype(F32)
    row, col = iota(square, 0), iota(square, 1)
    for h in range(heads):
        units, rows, inverse = unit_ref[:, head(h)], rows_ref[:, head(h)], inv_ref[h]
        inverse_t = nt_high(eye, inverse)
        x_total = jnp.zeros((count, DH), F32)
        y_total = jnp.zeros((count, DH), F32)
        for j in range(blocks):
            mine = base_ref[0] * blocks + j
            dcum = dcums[j][h]
            live = iota((count, 1), 0) <= mine
            moved = nt_high(rows, dcum)
            overlap = jnp.where(col <= mine, nt_high(moved, units), 0.0)
            gamma = nn_high(overlap, inverse)
            gamma = jnp.where((row < col) & (col <= mine), gamma, 0.0)
            x_total += jnp.where(live, moved - 2.0 * nn_high(gamma, units), 0.0)
            beta = jnp.where(col <= mine, eye - inverse_t, 0.0)
            turned = jnp.where(live, units - nn_high(beta, units), 0.0)
            y_total += nn_high(turned, dcum)
        out_ref[:, head(h)] = x_total
        out_ref[:, slice(width + h * DH, width + (h + 1) * DH)] = y_total


def run_adjoint(me, dcums, unit, rows, inverse, heads, blocks):
    count, width = unit.shape
    return pl.pallas_call(
        functools.partial(adjoint_kernel, heads, blocks),
        out_shape=jax.ShapeDtypeStruct((count, 2 * width), F32),
        in_specs=[pl.BlockSpec(memory_space=pltpu.SMEM)] + in_vmem(blocks + 3),
        out_specs=pl.BlockSpec(memory_space=pltpu.VMEM),
        compiler_params=compiler_params(),
        name="adjoint",
    )(me, *dcums, unit, rows, inverse)


def house_kernel(heads, blocks, base_ref, got_ref, unit_ref, rows_ref, house_ref, out_ref):
    count, width = unit_ref.shape
    total = jnp.sum(got_ref[...], axis=0)
    for h in range(heads):
        x_part = total[:, head(h)]
        y_part = total[:, slice(width + h * DH, width + (h + 1) * DH)]
        along = nt_high(y_part, rows_ref[:, head(h)])
        spot = iota((blocks, count), 0) + base_ref[0] * blocks
        along = jnp.where(iota((blocks, count), 1) < spot, along, 0.0)
        turned = y_part - 2.0 * nn_high(along, unit_ref[:, head(h)])
        dunit = -2.0 * (x_part + turned)
        house = house_ref[:, head(h)]
        lengths = jnp.sqrt(jnp.sum(house * house, axis=1, keepdims=True) + 1e-06)
        unit = house / lengths
        inner = jnp.sum(unit * dunit, axis=1, keepdims=True)
        out_ref[:, head(h)] = (dunit - unit * inner) / lengths


def run_house(me, got, unit, rows, house_dirs, heads, blocks):
    return pl.pallas_call(
        functools.partial(house_kernel, heads, blocks),
        out_shape=jax.ShapeDtypeStruct(house_dirs.shape, F32),
        in_specs=[pl.BlockSpec(memory_space=pltpu.SMEM)] + in_vmem(4),
        out_specs=pl.BlockSpec(memory_space=pltpu.VMEM),
        compiler_params=compiler_params(),
        name="house_grad",
    )(me, got, unit, rows, house_dirs)


def hop(value, distance, count):
    return lax.ppermute(value, "ctx", [(i, i ^ distance) for i in range(count)])


def shards(
    query_rows, key_rows, value_rows, grad_out, house_dirs, owners, offsets, w_query, w_key, w_value
):
    tok_rows, width = query_rows.shape
    heads, blocks = width // DH, tok_rows // BLK
    ctx_count, groups = lax.axis_size("ctx"), lax.axis_size("head")
    my_index = lax.axis_index("ctx")
    me = my_index.astype(jnp.int32).reshape(1)
    by_hand = ctx_count == 8
    core, across, along = 1, 2, 4

    if by_hand:
        pieces_house = [house_dirs] + [hop(house_dirs, r, 8) for r in range(1, 8)]
        order = jnp.arange(8) ^ my_index
        house_all = jnp.stack(pieces_house)[order].reshape(8 * blocks, width)
        key_y, value_x = hop(key_rows, along, 8), hop(value_rows, across, 8)
        key_x, value_y = hop(key_rows, across, 8), hop(value_rows, along, 8)
        key_d, value_d = hop(key_y, across, 8), hop(value_x, along, 8)
        keys = [key_rows, key_x, key_y, key_d]
        values = [value_rows, value_x, value_y, value_d]
        key_srcs = [part for key in keys for part in (key, hop(key, core, 8))]
        value_srcs = [part for value in values for part in (value, hop(value, core, 8))]
    else:
        house_all = lax.all_gather(house_dirs, "ctx", axis=0, tiled=True)
        key_srcs = [lax.all_gather(key_rows, "ctx")]
        value_srcs = [lax.all_gather(value_rows, "ctx")]

    unit, rows, inverse, qrot, krot, local, list_hi, list_lo = run_chain(
        me, owners, offsets, house_all, query_rows, key_rows, heads, blocks
    )
    pieces = 2 * blocks if by_hand else 0
    dq, dcum, dk_loc, dv_loc, *outs = run_attend(
        me,
        owners,
        offsets,
        key_srcs,
        value_srcs,
        (query_rows, qrot, krot, value_rows, grad_out, local, list_hi, list_lo),
        heads,
        blocks,
        pieces,
    )
    if not by_hand:
        spots = (owners * blocks + offsets).reshape(-1)
        empty = jnp.zeros((ctx_count * blocks, BLK, 2 * width), BF16)
        filled = empty.at[spots].add(outs[0])
        back = lax.psum_scatter(filled, "ctx", scatter_dimension=0, tiled=True)

    weights = (w_query, w_key, w_value)
    shares, dcums = [], []
    for j in range(blocks):
        if by_hand:
            near = outs[j] + hop(outs[blocks + j], core, 8)
            far_k = hop(near[3, :, :width], across, 8)
            far_v = hop(near[3, :, width:], along, 8)
            to_x = jnp.concatenate([near[1, :, :width], near[1, :, width:] + far_v], axis=1)
            to_y = jnp.concatenate([near[2, :, :width] + far_k, near[2, :, width:]], axis=1)
            parts = [near[0], hop(to_x, across, 8), hop(to_y, along, 8)]
        else:
            parts = [back[j]]
        term, dcum_j = run_project(
            j, parts, dk_loc, dv_loc, dq, key_rows, dcum, local, weights, heads, groups
        )
        dcums.append(dcum_j)
        shares.append(lax.psum_scatter(term, "head", scatter_dimension=0, tiled=False))

    sums = run_adjoint(me, dcums, unit, rows, inverse, heads, blocks)
    sums = sums.reshape(ctx_count, blocks, 2 * width)
    got = lax.all_to_all(sums, "ctx", split_axis=0, concat_axis=0, tiled=True)
    house_grad = run_house(me, got, unit, rows, house_dirs, heads, blocks)
    return (jnp.concatenate(shares, axis=0), house_grad)


def solution(mesh):
    placed = (
        P("ctx", "head"),
        P("ctx", "head"),
        P("ctx", "head"),
        P("ctx", "head"),
        P("ctx", "head"),
        P("ctx", None),
        P("ctx", None),
        P(None, "head"),
        P(None, "head"),
        P(None, "head"),
    )
    return jax.shard_map(
        shards,
        mesh=mesh,
        in_specs=placed,
        out_specs=(P("ctx", "head"), P("ctx", "head")),
        check_vma=False,
    )
```

```python
import functools
import math

import jax
import jax.numpy as jnp
from jax import lax
from jax.experimental import pallas as pl
from jax.experimental.pallas import tpu as pltpu
from jax.sharding import PartitionSpec as P

DH = 128
BLK = 128
MAXL = 2
HIGH = lax.Precision.HIGHEST
F32 = jnp.float32
BF16 = jnp.bfloat16
VMEM_BYTES = 60 * 1024 * 1024


def nn(a, b):
    return lax.dot_general(a, b, (((1,), (0,)), ((), ())), preferred_element_type=F32)


def nt(a, b):
    return lax.dot_general(a, b, (((1,), (1,)), ((), ())), preferred_element_type=F32)


def tn(a, b):
    return lax.dot_general(a, b, (((0,), (0,)), ((), ())), preferred_element_type=F32)


def nn_high(a, b):
    return lax.dot_general(
        a, b, (((1,), (0,)), ((), ())), precision=HIGH, preferred_element_type=F32
    )


def nt_high(a, b):
    return lax.dot_general(
        a, b, (((1,), (1,)), ((), ())), precision=HIGH, preferred_element_type=F32
    )


def split(value):
    top = value.astype(BF16)
    return top, (value - top.astype(F32)).astype(BF16)


def iota(shape, dim):
    return lax.broadcasted_iota(jnp.int32, shape, dim)


def head(h):
    return slice(h * DH, (h + 1) * DH)


def listed(ints_ref, entry, entries):
    return ints_ref[1 + entry], ints_ref[1 + entries + entry]


def compiler_params():
    return pltpu.CompilerParams(vmem_limit_bytes=VMEM_BYTES)


def cost(microseconds):
    return pl.CostEstimate(
        flops=int(microseconds * 1.15e9), bytes_accessed=1 << 20, transcendentals=0
    )


def in_smem(count):
    return [pl.BlockSpec(memory_space=pltpu.SMEM)] * count


def in_vmem(count):
    return [pl.BlockSpec(memory_space=pltpu.VMEM)] * count


def chain_kernel(heads, house_ref, unit_ref, rows_ref, inv_ref, unit_t_ref, unit_h):
    count = house_ref.shape[0]
    eye = (iota((count, count), 0) == iota((count, count), 1)).astype(F32)
    for h in range(heads):
        house = house_ref[:, head(h)]
        lengths = jnp.sqrt(jnp.sum(house * house, axis=1, keepdims=True) + 1e-06)
        unit_ref[:, head(h)] = house / lengths
        unit_h[h] = house / lengths
        inv_ref[h] = eye

    def eliminate(step, carry):
        below = iota((count, 1), 0) > step
        for h in range(heads):
            pivot = unit_h[h, pl.ds(step, 1), :]
            overlap = jnp.sum(unit_h[h] * pivot, axis=1, keepdims=True)
            factor = jnp.where(below, 2.0 * overlap, 0.0)
            inv_ref[h] = inv_ref[h] - factor * inv_ref[h, pl.ds(step, 1), :]
        return carry

    lax.fori_loop(0, count, eliminate, 0)
    eye_wide = (iota((DH, DH), 0) == iota((DH, DH), 1)).astype(F32)
    for h in range(heads):
        units = unit_ref[:, head(h)]
        rows_ref[:, head(h)] = nn_high(inv_ref[h], units)
        unit_t_ref[h] = nt_high(eye_wide, units)


def run_chain(house_all, heads):
    count, width = house_all.shape
    return pl.pallas_call(
        functools.partial(chain_kernel, heads),
        out_shape=[
            jax.ShapeDtypeStruct((count, width), F32),
            jax.ShapeDtypeStruct((count, width), F32),
            jax.ShapeDtypeStruct((heads, count, count), F32),
            jax.ShapeDtypeStruct((heads, DH, count), F32),
        ],
        in_specs=in_vmem(1),
        out_specs=in_vmem(4),
        scratch_shapes=[pltpu.VMEM((heads, count, DH), F32)],
        compiler_params=compiler_params(),
        cost_estimate=cost(6),
        name="house_chain",
    )(house_all)


def rotate_kernel(
    heads,
    blocks,
    ints_ref,
    after_ref,
    rows_ref,
    unit_t_ref,
    query_ref,
    key_ref,
    qrot_ref,
    krot_ref,
    local_ref,
    list_hi_ref,
    list_lo_ref,
):
    count = rows_ref.shape[0]
    entries = blocks * MAXL
    eye = (iota((DH, DH), 0) == iota((DH, DH), 1)).astype(F32)

    def cumulative(h, block):
        kept = jnp.where(iota((DH, count), 1) <= block, unit_t_ref[h], 0.0)
        return split(eye - 2.0 * nn_high(kept, rows_ref[:, head(h)]))

    base = ints_ref[0] * blocks

    def local_block(b, carry):
        here = pl.ds(pl.multiple_of(b * BLK, BLK), BLK)
        for h in range(heads):
            hi, lo = cumulative(h, base + b)
            local_ref[b, h] = hi
            query, key = query_ref[here, head(h)], key_ref[here, head(h)]
            qrot_ref[here, head(h)] = (nn(query, hi) + nn(query, lo)).astype(BF16)
            krot_ref[here, head(h)] = (nn(key, hi) + nn(key, lo)).astype(BF16)
        return carry

    lax.fori_loop(0, blocks, local_block, 0)

    def listed_block(e, carry):
        owner, offset = listed(ints_ref, e, entries)
        for h in range(heads):
            hi, lo = cumulative(h, owner * blocks + offset)
            list_hi_ref[e, h] = hi
            list_lo_ref[e, h] = lo
        return carry

    lax.fori_loop(0, entries, listed_block, 0)


def run_rotate(ints, after, house_rows, unit_t, query_rows, key_rows, heads, blocks):
    rows, width = query_rows.shape
    entries = blocks * MAXL
    return pl.pallas_call(
        functools.partial(rotate_kernel, heads, blocks),
        out_shape=[
            jax.ShapeDtypeStruct((rows, width), BF16),
            jax.ShapeDtypeStruct((rows, width), BF16),
            jax.ShapeDtypeStruct((blocks, heads, DH, DH), BF16),
            jax.ShapeDtypeStruct((entries, heads, DH, DH), BF16),
            jax.ShapeDtypeStruct((entries, heads, DH, DH), BF16),
        ],
        in_specs=in_smem(1) + [pl.BlockSpec(memory_space=pl.ANY)] + in_vmem(4),
        out_specs=in_vmem(5),
        compiler_params=compiler_params(),
        cost_estimate=cost(9),
        name="rotate",
    )(ints, after, house_rows, unit_t, query_rows, key_rows)


def attend_kernel(heads, blocks, places, pieces, *refs):
    ints_ref = refs[0]
    source_count = 1 + max(place[0] for pair in places for place in pair)
    sources = refs[1 : 1 + source_count]
    refs = refs[1 + source_count :]
    (query_ref, qrot_ref, krot_ref, value_ref, grad_ref, local_ref, hi_ref, lo_ref) = refs[:8]
    dq_ref, dcum_ref, dk_ref, dv_ref = refs[8:12]
    outs = refs[12 : 12 + max(pieces, 1)]
    refs = refs[12 + max(pieces, 1) :]
    far_keys, far_values, sems = refs[:3]
    entries = blocks * MAXL
    scaling = DH ** (-0.5)
    log_scale = scaling * math.log2(math.e)

    def start(e, src, kind, slot, where):
        pltpu.make_async_copy(src.at[where], slot.at[e], sems.at[kind, e]).start()

    for e in range(entries):
        owner, offset = listed(ints_ref, e, entries)
        row = pl.multiple_of(offset * BLK, BLK)
        if len(places) == 1:
            start(e, sources[0], 0, far_keys, (owner, pl.ds(row, BLK)))
            start(e, sources[1], 1, far_values, (owner, pl.ds(row, BLK)))
        else:
            distance = owner ^ ints_ref[0]
            for r, (key_place, value_place) in enumerate(places):

                @pl.when(distance == r)
                def _():
                    source, first = key_place
                    start(e, sources[source], 0, far_keys, pl.ds(first + row, BLK))
                    source, first = value_place
                    start(e, sources[source], 1, far_values, pl.ds(first + row, BLK))

    out_copies = []
    if pieces:
        payloads, out_sems = refs[3 : 3 + heads], refs[3 + heads]
        for payload in payloads:
            payload[...] = jnp.zeros_like(payload)
    for kind, slots in ((0, far_keys), (1, far_values)):
        for e in range(entries):
            pltpu.make_async_copy(slots.at[e], slots.at[e], sems.at[kind, e]).wait()

    later = iota((BLK, BLK), 0) > iota((BLK, BLK), 1)
    for h in range(heads):
        lanes = head(h)
        for a in range(blocks):
            here = slice(a * BLK, (a + 1) * BLK)
            qrot, grad = qrot_ref[here, lanes], grad_ref[here, lanes]
            keys = [krot_ref[b * BLK : (b + 1) * BLK, lanes] for b in range(a + 1)]
            values = [value_ref[b * BLK : (b + 1) * BLK, lanes] for b in range(a + 1)]
            for l in range(MAXL):
                e = a * MAXL + l
                raw = far_keys[e, :, lanes]
                keys.append((nn(raw, hi_ref[e, h]) + nn(raw, lo_ref[e, h])).astype(BF16))
                values.append(far_values[e, :, lanes])
            scores, top = [], None
            for b, key in enumerate(keys):
                part = nt(key, qrot) * log_scale
                if b == a:
                    part = jnp.where(later, -jnp.inf, part)
                scores.append(part)
                top = part if top is None else jnp.maximum(top, part)
            top = jnp.max(top, axis=0, keepdims=True)
            weights, dprobs, total, inner = [], [], None, None
            for part, value in zip(scores, values):
                weight = jnp.exp2(part - top)
                dprob = nt(value, grad)
                weights.append(weight)
                dprobs.append(dprob)
                product = weight * dprob
                total = weight if total is None else total + weight
                inner = product if inner is None else inner + product
            inverse = 1.0 / jnp.sum(total, axis=0, keepdims=True)
            delta = jnp.sum(inner, axis=0, keepdims=True) * inverse
            dscores = []
            for b in range(a + 1 + MAXL):
                probs = weights[b] * inverse
                probs_b = probs.astype(BF16)
                dscore = (probs * (dprobs[b] - delta)).astype(BF16)
                dscores.append(dscore)
                dkey, dvalue = nn(dscore, qrot) * scaling, nn(probs_b, grad)
                spot = slice(b * BLK, (b + 1) * BLK)
                if b < a:
                    dk_ref[spot, lanes] += dkey
                    dv_ref[spot, lanes] += dvalue
                elif b == a:
                    dk_ref[spot, lanes] = dkey
                    dv_ref[spot, lanes] = dvalue
                else:
                    e = a * MAXL + b - a - 1
                    dkey, dvalue = dkey.astype(BF16), dvalue.astype(BF16)
                    if pieces:
                        owner, offset = listed(ints_ref, e, entries)
                        distance = owner ^ ints_ref[0]
                        at = (distance & 1) * blocks + offset
                        payloads[h][at, distance >> 1, :, :DH] += dkey
                        payloads[h][at, distance >> 1, :, DH:] += dvalue
                    else:
                        outs[0][e, :, 2 * h * DH : (2 * h + 1) * DH] = dkey
                        outs[0][e, :, (2 * h + 1) * DH : (2 * h + 2) * DH] = dvalue
            dscores, keys = jnp.concatenate(dscores, axis=0), jnp.concatenate(keys, axis=0)
            dq_top, dq_low = split(tn(dscores, keys) * scaling)
            dq_ref[here, lanes] = nt(dq_top, local_ref[a, h]).astype(BF16)
            query = query_ref[here, lanes]
            dcum_ref[a, h] = tn(query, dq_top) + tn(query, dq_low)
        for i in range(pieces):
            where = outs[i].at[:, :, 2 * h * DH : (2 * h + 2) * DH]
            copy = pltpu.make_async_copy(payloads[h].at[i], where, out_sems.at[i, h])
            copy.start()
            out_copies.append(copy)
    for copy in out_copies:
        copy.wait()


def run_attend(ints, sources, places, arrays, heads, blocks, pieces):
    rows, width = arrays[0].shape
    entries = blocks * MAXL
    any_spec = pl.BlockSpec(memory_space=pl.ANY)
    scratch = [
        pltpu.VMEM((entries, BLK, width), BF16),
        pltpu.VMEM((entries, BLK, width), BF16),
        pltpu.SemaphoreType.DMA((2, entries)),
    ]
    if pieces:
        chips = len(places) // 2
        out_parts = [jax.ShapeDtypeStruct((chips, BLK, 2 * width), BF16)] * pieces
        part_specs = [any_spec] * pieces
        scratch += [pltpu.VMEM((pieces, chips, BLK, 2 * DH), BF16)] * heads
        scratch += [pltpu.SemaphoreType.DMA((pieces, heads))]
    else:
        out_parts = [jax.ShapeDtypeStruct((entries, BLK, 2 * width), BF16)]
        part_specs = in_vmem(1)
    return pl.pallas_call(
        functools.partial(attend_kernel, heads, blocks, places, pieces),
        out_shape=[
            jax.ShapeDtypeStruct((rows, width), BF16),
            jax.ShapeDtypeStruct((blocks, heads, DH, DH), F32),
            jax.ShapeDtypeStruct((rows, width), F32),
            jax.ShapeDtypeStruct((rows, width), F32),
        ]
        + out_parts,
        in_specs=in_smem(1) + [any_spec] * len(sources) + in_vmem(8),
        out_specs=in_vmem(4) + part_specs,
        scratch_shapes=scratch,
        compiler_params=compiler_params(),
        cost_estimate=cost(15),
        name="attend",
    )(ints, *sources, *arrays)


def merge_kernel(own_ref, got_ref, after_ref, *out_refs):
    for i, ref in enumerate(out_refs):
        total = own_ref[i + 1].astype(F32) + got_ref[i + 1].astype(F32)
        ref[...] = total.astype(BF16)


def run_merge(own, got, after):
    chips, rows, width = own.shape
    return pl.pallas_call(
        merge_kernel,
        out_shape=[jax.ShapeDtypeStruct((rows, width), BF16)] * (chips - 1),
        in_specs=in_vmem(2) + [pl.BlockSpec(memory_space=pl.ANY)],
        out_specs=in_vmem(chips - 1),
        compiler_params=compiler_params(),
        cost_estimate=cost(1.5),
        name="merge",
    )(own, got, after)


def project_kernel(heads, parts, per, flip_ref, *refs):
    part_refs = refs[:parts]
    dk_loc, dv_loc, dq_ref, key_ref, dcum_in, cum_ref, wq, wk, wv = refs[parts : parts + 9]
    first_ref, rest_ref, dcum_out, dk_ref, dv_ref = refs[parts + 9 :]
    step = pl.program_id(0)

    @pl.when(step == 0)
    def _():
        for h in range(heads):
            both = slice(2 * h * DH, (2 * h + 2) * DH)
            total = part_refs[0][0, :, both].astype(F32)
            for ref in part_refs[1:]:
                total = total + ref[0, :, both].astype(F32)
            dv_ref[:, head(h)] = (dv_loc[:, head(h)] + total[:, DH:]).astype(BF16)
            dk_top, dk_low = split(dk_loc[:, head(h)] + total[:, :DH])
            dk_ref[:, head(h)] = nt(dk_top, cum_ref[0, h]).astype(BF16)
            key = key_ref[:, head(h)]
            dcum_out[h] = dcum_in[0, h] + tn(key, dk_top) + tn(key, dk_low)

    term = nt(wq[...], dq_ref[...]) + nt(wk[...], dk_ref[...]) + nt(wv[...], dv_ref[...])
    term = term.T.astype(BF16)

    @pl.when(step < per)
    def _():
        first_ref[...] = term

    @pl.when(step >= per)
    def _():
        rest_ref[0] = term


def run_project(block, flip, parts, dk_loc, dv_loc, dq, key_rows, dcum, cum, weights, groups):
    width = dq.shape[1]
    heads = width // DH
    model = weights[0].shape[0]
    chunk = model // groups
    tile = min(512, chunk)
    per = chunk // tile

    def weight_tile(t, flip):
        m = t // per
        return (m + flip[0] * (groups - 1 - 2 * m)) * per + t % per, 0

    def rest_tile(t, flip):
        later = jnp.maximum(t - per, 0)
        return later // per, 0, later % per

    rows_spec = pl.BlockSpec((BLK, width), lambda t, flip: (block, 0))
    part_spec = pl.BlockSpec((1, BLK, 2 * width), lambda t, flip: (0, 0, 0))
    head_spec = pl.BlockSpec((1, heads, DH, DH), lambda t, flip: (block, 0, 0, 0))
    weight_spec = pl.BlockSpec((tile, width), weight_tile)
    return pl.pallas_call(
        functools.partial(project_kernel, heads, len(parts), per),
        grid_spec=pltpu.PrefetchScalarGridSpec(
            num_scalar_prefetch=1,
            grid=(model // tile,),
            in_specs=[part_spec] * len(parts)
            + [rows_spec] * 4
            + [head_spec] * 2
            + [weight_spec] * 3,
            out_specs=[
                pl.BlockSpec((BLK, tile), lambda t, flip: (0, jnp.minimum(t, per - 1))),
                pl.BlockSpec((1, BLK, tile), rest_tile),
                pl.BlockSpec((heads, DH, DH), lambda t, flip: (0, 0, 0)),
            ],
            scratch_shapes=[pltpu.VMEM((BLK, width), BF16), pltpu.VMEM((BLK, width), BF16)],
        ),
        out_shape=[
            jax.ShapeDtypeStruct((BLK, chunk), BF16),
            jax.ShapeDtypeStruct((groups - 1, BLK, chunk), BF16),
            jax.ShapeDtypeStruct((heads, DH, DH), F32),
        ],
        compiler_params=compiler_params(),
        cost_estimate=cost(5),
        name="project",
    )(flip, *parts, dk_loc, dv_loc, dq, key_rows, dcum, cum, *weights)


def adjoint_kernel(heads, blocks, base_ref, after_ref, *refs):
    dcums = refs[:blocks]
    unit_ref, rows_ref, inv_ref, out_ref = refs[blocks:]
    count, width = unit_ref.shape
    square = (count, count)
    eye = (iota(square, 0) == iota(square, 1)).astype(F32)
    row, col = iota(square, 0), iota(square, 1)
    for h in range(heads):
        units, rows, inverse = unit_ref[:, head(h)], rows_ref[:, head(h)], inv_ref[h]
        inverse_t = nt_high(eye, inverse)
        x_total = jnp.zeros((count, DH), F32)
        y_total = jnp.zeros((count, DH), F32)
        for j in range(blocks):
            mine = base_ref[0] * blocks + j
            dcum = dcums[j][h]
            live = iota((count, 1), 0) <= mine
            moved = nt_high(rows, dcum)
            overlap = jnp.where(col <= mine, nt_high(moved, units), 0.0)
            gamma = nn_high(overlap, inverse)
            gamma = jnp.where((row < col) & (col <= mine), gamma, 0.0)
            x_total += jnp.where(live, moved - 2.0 * nn_high(gamma, units), 0.0)
            beta = jnp.where(col <= mine, eye - inverse_t, 0.0)
            turned = jnp.where(live, units - nn_high(beta, units), 0.0)
            y_total += nn_high(turned, dcum)
        out_ref[:, head(h)] = x_total
        out_ref[:, slice(width + h * DH, width + (h + 1) * DH)] = y_total


def run_adjoint(ints, after, dcums, unit, rows, inverse, heads, blocks):
    count, width = unit.shape
    return pl.pallas_call(
        functools.partial(adjoint_kernel, heads, blocks),
        out_shape=jax.ShapeDtypeStruct((count, 2 * width), F32),
        in_specs=in_smem(1) + [pl.BlockSpec(memory_space=pl.ANY)] + in_vmem(blocks + 3),
        out_specs=pl.BlockSpec(memory_space=pltpu.VMEM),
        compiler_params=compiler_params(),
        cost_estimate=cost(11),
        name="adjoint",
    )(ints, after, *dcums, unit, rows, inverse)


def house_kernel(heads, blocks, base_ref, got_ref, unit_ref, rows_ref, house_ref, out_ref):
    count, width = unit_ref.shape
    total = jnp.sum(got_ref[...], axis=0)
    for h in range(heads):
        x_part = total[:, head(h)]
        y_part = total[:, slice(width + h * DH, width + (h + 1) * DH)]
        along = nt_high(y_part, rows_ref[:, head(h)])
        spot = iota((blocks, count), 0) + base_ref[0] * blocks
        along = jnp.where(iota((blocks, count), 1) < spot, along, 0.0)
        turned = y_part - 2.0 * nn_high(along, unit_ref[:, head(h)])
        dunit = -2.0 * (x_part + turned)
        house = house_ref[:, head(h)]
        lengths = jnp.sqrt(jnp.sum(house * house, axis=1, keepdims=True) + 1e-06)
        unit = house / lengths
        inner = jnp.sum(unit * dunit, axis=1, keepdims=True)
        out_ref[:, head(h)] = (dunit - unit * inner) / lengths


def run_house(ints, got, unit, rows, house_dirs, heads, blocks):
    return pl.pallas_call(
        functools.partial(house_kernel, heads, blocks),
        out_shape=jax.ShapeDtypeStruct(house_dirs.shape, F32),
        in_specs=[pl.BlockSpec(memory_space=pltpu.SMEM)] + in_vmem(4),
        out_specs=pl.BlockSpec(memory_space=pltpu.VMEM),
        compiler_params=compiler_params(),
        cost_estimate=cost(2),
        name="house_grad",
    )(ints, got, unit, rows, house_dirs)


def hop(value, distance, count):
    return lax.ppermute(value, "ctx", [(i, i ^ distance) for i in range(count)])


def slide(value, pairs):
    return lax.ppermute(value, "head", pairs)


def line_scatter(first, rest):
    place = lax.axis_index("head")
    ends = (place == 0) | (place == 3)
    inward = slide(rest, [(0, 1), (3, 2)])
    swapped = slide(rest[1:] + inward[1:], [(1, 2), (2, 1)])
    outward = slide(first + swapped[1], [(1, 0), (2, 3)])
    total = jnp.where(ends, first, rest[0]).astype(F32) + inward[0].astype(F32)
    total = total + swapped[0].astype(F32) + outward.astype(F32)
    return total.astype(BF16), inward


def shards(
    query_rows, key_rows, value_rows, grad_out, house_dirs, owners, offsets, w_query, w_key, w_value
):
    tok_rows, width = query_rows.shape
    heads, blocks = width // DH, tok_rows // BLK
    ctx_count, groups = lax.axis_size("ctx"), lax.axis_size("head")
    my_index = lax.axis_index("ctx").astype(jnp.int32)
    ints = jnp.concatenate([my_index.reshape(1), owners.reshape(-1), offsets.reshape(-1)])
    by_hand = ctx_count == 8
    core, across, along = 1, 2, 4

    if by_hand:
        house_all = house_dirs
        for distance in (core, across, along):
            other = hop(house_all, distance, 8)
            upper = (my_index & distance) != 0
            low, high = jnp.where(upper, other, house_all), jnp.where(upper, house_all, other)
            house_all = jnp.concatenate([low, high], axis=0)
        both = jnp.concatenate([key_rows, value_rows], axis=0)
        both_s, both_x, both_y = hop(both, core, 8), hop(both, across, 8), hop(both, along, 8)
        key_d, value_d = hop(both_y[:tok_rows], across, 8), hop(both_x[tok_rows:], along, 8)
        both_xs, both_ys = hop(both_x, core, 8), hop(both_y, core, 8)
        key_ds, value_ds = hop(key_d, core, 8), hop(value_d, core, 8)
        sources = [key_rows, value_rows, both_s, both_x, both_xs, both_y, both_ys]
        sources += [key_d, value_d, key_ds, value_ds]
        places = [((0, 0), (1, 0))] + [((i, 0), (i, tok_rows)) for i in range(2, 7)]
        places += [((7, 0), (8, 0)), ((9, 0), (10, 0))]
        after = both_x
    else:
        house_all = lax.all_gather(house_dirs, "ctx", axis=0, tiled=True)
        sources = [lax.all_gather(key_rows, "ctx"), lax.all_gather(value_rows, "ctx")]
        places = [((0, 0), (1, 0))]
        after = key_rows

    unit, rows, inverse, unit_t = run_chain(house_all, heads)
    qrot, krot, local, list_hi, list_lo = run_rotate(
        ints, after, rows, unit_t, query_rows, key_rows, heads, blocks
    )
    pieces = 2 * blocks if by_hand else 0
    dq, dcum, dk_loc, dv_loc, *outs = run_attend(
        ints,
        sources,
        places,
        (query_rows, qrot, krot, value_rows, grad_out, local, list_hi, list_lo),
        heads,
        blocks,
        pieces,
    )
    if not by_hand:
        spots = (owners * blocks + offsets).reshape(-1)
        empty = jnp.zeros((ctx_count * blocks, BLK, 2 * width), BF16)
        filled = empty.at[spots].add(outs[0])
        back = lax.psum_scatter(filled, "ctx", scatter_dimension=0, tiled=True)

    weights = (w_query, w_key, w_value)
    on_line = groups == 4
    flip = jnp.where(on_line & (lax.axis_index("head") >= 2), 1, 0).astype(jnp.int32).reshape(1)
    share = jnp.zeros((tok_rows, w_query.shape[0] // groups), BF16)
    dcums, after = [], key_rows
    for j in range(blocks):
        if by_hand:
            got = hop(outs[blocks + j], core, 8)
            to_x, to_y, to_d = run_merge(outs[j], got, after)
            parts = [outs[j], got, hop(to_x, across, 8)[None], hop(to_y, along, 8)[None]]
            after = hop(to_d, across + along, 8)
            parts.append(after[None])
        else:
            parts = [back[j : j + 1]]
        first, rest, dcum_j = run_project(
            j, flip, parts, dk_loc, dv_loc, dq, key_rows, dcum, local, weights, groups
        )
        dcums.append(dcum_j)
        if on_line:
            done, inward = line_scatter(first, rest)
            late = inward if j < blocks - 1 else late
        else:
            late = rest
            term = jnp.concatenate([first[None], rest], axis=0)
            done = lax.psum_scatter(term, "head", scatter_dimension=0, tiled=False)
        share = lax.dynamic_update_slice(share, done, (j * BLK, 0))

    sums = run_adjoint(ints, late, dcums, unit, rows, inverse, heads, blocks)
    sums = sums.reshape(ctx_count, blocks, 2 * width)
    got = lax.all_to_all(sums, "ctx", split_axis=0, concat_axis=0, tiled=True)
    house_grad = run_house(ints, got, unit, rows, house_dirs, heads, blocks)
    return (share, house_grad)


def solution(mesh):
    placed = (
        P("ctx", "head"),
        P("ctx", "head"),
        P("ctx", "head"),
        P("ctx", "head"),
        P("ctx", "head"),
        P("ctx", None),
        P("ctx", None),
        P(None, "head"),
        P(None, "head"),
        P(None, "head"),
    )
    return jax.shard_map(
        shards,
        mesh=mesh,
        in_specs=placed,
        out_specs=(P("ctx", "head"), P("ctx", "head")),
        check_vma=False,
    )
```

```python
import functools
import math

import jax
import jax.numpy as jnp
from jax import lax
from jax.experimental import pallas as pl
from jax.experimental.pallas import tpu as pltpu
from jax.sharding import PartitionSpec as P

DH = 128
BLK = 128
MAXL = 2
HIGH = lax.Precision.HIGHEST
F32 = jnp.float32
BF16 = jnp.bfloat16


def nn(a, b):
    return lax.dot_general(a, b, (((1,), (0,)), ((), ())), preferred_element_type=F32)


def nt(a, b):
    return lax.dot_general(a, b, (((1,), (1,)), ((), ())), preferred_element_type=F32)


def tn(a, b):
    return lax.dot_general(a, b, (((0,), (0,)), ((), ())), preferred_element_type=F32)


def nn_high(a, b):
    return lax.dot_general(
        a, b, (((1,), (0,)), ((), ())), precision=HIGH, preferred_element_type=F32
    )


def nt_high(a, b):
    return lax.dot_general(
        a, b, (((1,), (1,)), ((), ())), precision=HIGH, preferred_element_type=F32
    )


def split(value):
    top = value.astype(BF16)
    return top, (value - top.astype(F32)).astype(BF16)


def iota(shape, dim):
    return lax.broadcasted_iota(jnp.int32, shape, dim)


def head(h):
    return slice(h * DH, (h + 1) * DH)


def listed(ints_ref, entry, entries):
    return ints_ref[1 + entry], ints_ref[1 + entries + entry]


def grant(mebibytes):
    return pltpu.CompilerParams(vmem_limit_bytes=mebibytes * 1024 * 1024)


def cost(microseconds):
    return pl.CostEstimate(
        flops=int(microseconds * 1.15e9), bytes_accessed=1 << 20, transcendentals=0
    )


def in_smem(count):
    return [pl.BlockSpec(memory_space=pltpu.SMEM)] * count


def in_vmem(count):
    return [pl.BlockSpec(memory_space=pltpu.VMEM)] * count


def chain_kernel(heads, parts, ints_ref, *refs):
    house_refs = refs[:parts]
    unit_ref, rows_ref, inv_ref, unit_t_ref, unit_h, house_all = refs[parts:]
    count = unit_ref.shape[0]
    span = count // parts
    for t, ref in enumerate(house_refs):
        place = (ints_ref[0] // (8 // parts)) ^ t if parts > 1 else 0
        house_all[pl.ds(pl.multiple_of(place * span, span), span), :] = ref[...]
    eye = (iota((count, count), 0) == iota((count, count), 1)).astype(F32)
    for h in range(heads):
        house = house_all[:, head(h)]
        lengths = jnp.sqrt(jnp.sum(house * house, axis=1, keepdims=True) + 1e-06)
        unit_ref[:, head(h)] = house / lengths
        unit_h[h] = house / lengths
        inv_ref[h] = eye

    def eliminate(step, carry):
        below = iota((count, 1), 0) > step
        for h in range(heads):
            pivot = unit_h[h, pl.ds(step, 1), :]
            overlap = jnp.sum(unit_h[h] * pivot, axis=1, keepdims=True)
            factor = jnp.where(below, 2.0 * overlap, 0.0)
            inv_ref[h] = inv_ref[h] - factor * inv_ref[h, pl.ds(step, 1), :]
        return carry

    lax.fori_loop(0, count, eliminate, 0)
    eye_wide = (iota((DH, DH), 0) == iota((DH, DH), 1)).astype(F32)
    for h in range(heads):
        units = unit_ref[:, head(h)]
        rows_ref[:, head(h)] = nn_high(inv_ref[h], units)
        unit_t_ref[h] = nt_high(eye_wide, units)


def run_chain(ints, house_parts, heads):
    span, width = house_parts[0].shape
    parts = len(house_parts)
    count = span * parts
    return pl.pallas_call(
        functools.partial(chain_kernel, heads, parts),
        out_shape=[
            jax.ShapeDtypeStruct((count, width), F32),
            jax.ShapeDtypeStruct((count, width), F32),
            jax.ShapeDtypeStruct((heads, count, count), F32),
            jax.ShapeDtypeStruct((heads, DH, count), F32),
        ],
        in_specs=in_smem(1) + in_vmem(parts),
        out_specs=in_vmem(4),
        scratch_shapes=[pltpu.VMEM((heads, count, DH), F32), pltpu.VMEM((count, width), F32)],
        compiler_params=grant(16),
        cost_estimate=cost(6),
        name="house_chain",
    )(ints, *house_parts)


def rotate_kernel(
    heads,
    blocks,
    ints_ref,
    rows_ref,
    unit_t_ref,
    query_ref,
    key_ref,
    qrot_ref,
    krot_ref,
    local_ref,
    listed_ref,
):
    count = rows_ref.shape[0]
    entries = blocks * MAXL
    eye = (iota((DH, DH), 0) == iota((DH, DH), 1)).astype(F32)

    def cumulative(h, block):
        kept = jnp.where(iota((DH, count), 1) <= block, unit_t_ref[h], 0.0)
        return split(eye - 2.0 * nn_high(kept, rows_ref[:, head(h)]))

    base = ints_ref[0] * blocks

    def local_block(b, carry):
        here = pl.ds(pl.multiple_of(b * BLK, BLK), BLK)
        for h in range(heads):
            hi, lo = cumulative(h, base + b)
            local_ref[b, h] = hi
            query, key = query_ref[here, head(h)], key_ref[here, head(h)]
            qrot_ref[here, head(h)] = (nn(query, hi) + nn(query, lo)).astype(BF16)
            krot_ref[here, head(h)] = (nn(key, hi) + nn(key, lo)).astype(BF16)
        return carry

    lax.fori_loop(0, blocks, local_block, 0)

    def listed_block(e, carry):
        owner, offset = listed(ints_ref, e, entries)
        for h in range(heads):
            hi, lo = cumulative(h, owner * blocks + offset)
            listed_ref[e, h, :DH] = hi
            listed_ref[e, h, DH:] = lo
        return carry

    lax.fori_loop(0, entries, listed_block, 0)


def run_rotate(ints, house_rows, unit_t, query_rows, key_rows, heads, blocks):
    rows, width = query_rows.shape
    entries = blocks * MAXL
    return pl.pallas_call(
        functools.partial(rotate_kernel, heads, blocks),
        out_shape=[
            jax.ShapeDtypeStruct((rows, width), BF16),
            jax.ShapeDtypeStruct((rows, width), BF16),
            jax.ShapeDtypeStruct((blocks, heads, DH, DH), BF16),
            jax.ShapeDtypeStruct((entries, heads, 2 * DH, DH), BF16),
        ],
        in_specs=in_smem(1) + in_vmem(4),
        out_specs=in_vmem(4),
        compiler_params=grant(16),
        cost_estimate=cost(9),
        name="rotate",
    )(ints, house_rows, unit_t, query_rows, key_rows)


def attend_kernel(heads, blocks, places, pieces, *refs):
    ints_ref = refs[0]
    source_count = 1 + max(place[0] for pair in places for place in pair)
    sources = refs[1 : 1 + source_count]
    refs = refs[1 + source_count :]
    (query_ref, qrot_ref, krot_ref, value_ref, grad_ref, local_ref, listed_ref) = refs[:7]
    dq_ref, dcum_ref, dk_ref, dv_ref = refs[7:11]
    outs = refs[11 : 11 + max(len(pieces), 1)]
    refs = refs[11 + max(len(pieces), 1) :]
    far_keys, far_values, sems = refs[:3]
    entries = blocks * MAXL
    scaling = DH ** (-0.5)
    log_scale = scaling * math.log2(math.e)

    def start(e, src, kind, slot, where):
        pltpu.make_async_copy(src.at[where], slot.at[e], sems.at[kind, e]).start()

    for e in range(entries):
        owner, offset = listed(ints_ref, e, entries)
        row = pl.multiple_of(offset * BLK, BLK)
        if len(places) == 1:
            start(e, sources[0], 0, far_keys, (owner, pl.ds(row, BLK)))
            start(e, sources[1], 1, far_values, (owner, pl.ds(row, BLK)))
        else:
            distance = owner ^ ints_ref[0]
            for r, (key_place, value_place) in enumerate(places):

                @pl.when(distance == r)
                def _():
                    source, first = key_place
                    start(e, sources[source], 0, far_keys, pl.ds(first + row, BLK))
                    source, first = value_place
                    start(e, sources[source], 1, far_values, pl.ds(first + row, BLK))

    out_copies = []
    if pieces:
        payloads, out_sems = refs[3 : 3 + heads], refs[3 + heads]
        for payload in payloads:
            payload[...] = jnp.zeros_like(payload)
    for kind, slots in ((0, far_keys), (1, far_values)):
        for e in range(entries):
            pltpu.make_async_copy(slots.at[e], slots.at[e], sems.at[kind, e]).wait()

    later = iota((BLK, BLK), 0) > iota((BLK, BLK), 1)
    empty = jnp.zeros((BLK, DH), BF16)
    for h in range(heads):
        lanes = head(h)
        for a in range(blocks):
            here = slice(a * BLK, (a + 1) * BLK)
            qrot, grad = qrot_ref[here, lanes], grad_ref[here, lanes]
            both = jnp.concatenate(
                [
                    jnp.concatenate([qrot, empty], axis=1),
                    jnp.concatenate([empty, grad], axis=1),
                ],
                axis=0,
            )
            keys = [krot_ref[b * BLK : (b + 1) * BLK, lanes] for b in range(a + 1)]
            values = [value_ref[b * BLK : (b + 1) * BLK, lanes] for b in range(a + 1)]
            for l in range(MAXL):
                e = a * MAXL + l
                raw = far_keys[e, :, lanes]
                raw = jnp.concatenate([raw, raw], axis=1)
                keys.append(nn(raw, listed_ref[e, h]).astype(BF16))
                values.append(far_values[e, :, lanes])
            scores, dprobs, top = [], [], None
            for b in range(a + 1 + MAXL):
                pair = nt(jnp.concatenate([keys[b], values[b]], axis=1), both)
                part = pair[:, :BLK] * log_scale
                if b == a:
                    part = jnp.where(later, -jnp.inf, part)
                scores.append(part)
                dprobs.append(pair[:, BLK:])
                top = part if top is None else jnp.maximum(top, part)
            top = jnp.max(top, axis=0, keepdims=True)
            weights, total, inner = [], None, None
            for part, dprob in zip(scores, dprobs):
                weight = jnp.exp2(part - top)
                weights.append(weight)
                product = weight * dprob
                total = weight if total is None else total + weight
                inner = product if inner is None else inner + product
            inverse = 1.0 / jnp.sum(total, axis=0, keepdims=True)
            delta = jnp.sum(inner, axis=0, keepdims=True) * inverse
            dscores = []
            for b in range(a + 1 + MAXL):
                probs = weights[b] * inverse
                probs_b = probs.astype(BF16)
                dscore = (probs * (dprobs[b] - delta)).astype(BF16)
                dscores.append(dscore)
                pair = nn(jnp.concatenate([dscore, probs_b], axis=1), both)
                dkey, dvalue = pair[:, :DH] * scaling, pair[:, DH:]
                spot = slice(b * BLK, (b + 1) * BLK)
                if b < a:
                    dk_ref[spot, lanes] += dkey
                    dv_ref[spot, lanes] += dvalue
                elif b == a:
                    dk_ref[spot, lanes] = dkey
                    dv_ref[spot, lanes] = dvalue
                else:
                    e = a * MAXL + b - a - 1
                    dkey, dvalue = dkey.astype(BF16), dvalue.astype(BF16)
                    if pieces:
                        owner, offset = listed(ints_ref, e, entries)
                        distance = owner ^ ints_ref[0]
                        at = (distance & 1) * blocks + offset
                        payloads[h][at, distance >> 1, :, :DH] += dkey
                        payloads[h][at, distance >> 1, :, DH:] += dvalue
                    else:
                        outs[0][e, :, 2 * h * DH : (2 * h + 1) * DH] = dkey
                        outs[0][e, :, (2 * h + 1) * DH : (2 * h + 2) * DH] = dvalue
            dscores, keys = jnp.concatenate(dscores, axis=0), jnp.concatenate(keys, axis=0)
            dq_top, dq_low = split(tn(dscores, keys) * scaling)
            dq_ref[here, lanes] = nt(dq_top, local_ref[a, h]).astype(BF16)
            query = query_ref[here, lanes]
            query = jnp.concatenate([query, query], axis=0)
            dcum_ref[a, h] = tn(query, jnp.concatenate([dq_top, dq_low], axis=0))
        for i, (first, size) in enumerate(pieces):
            where = outs[i].at[:, :, :, 2 * h * DH : (2 * h + 2) * DH]
            source = payloads[h].at[pl.ds(first, size)]
            copy = pltpu.make_async_copy(source, where, out_sems.at[i, h])
            copy.start()
            out_copies.append(copy)
    for copy in out_copies:
        copy.wait()


def run_attend(ints, sources, places, arrays, heads, blocks, pieces):
    rows, width = arrays[0].shape
    entries = blocks * MAXL
    any_spec = pl.BlockSpec(memory_space=pl.ANY)
    scratch = [
        pltpu.VMEM((entries, BLK, width), BF16),
        pltpu.VMEM((entries, BLK, width), BF16),
        pltpu.SemaphoreType.DMA((2, entries)),
    ]
    if pieces:
        chips = len(places) // 2
        out_parts = [
            jax.ShapeDtypeStruct((size, chips, BLK, 2 * width), BF16) for _, size in pieces
        ]
        part_specs = [any_spec] * len(pieces)
        scratch += [pltpu.VMEM((2 * blocks, chips, BLK, 2 * DH), BF16)] * heads
        scratch += [pltpu.SemaphoreType.DMA((len(pieces), heads))]
    else:
        out_parts = [jax.ShapeDtypeStruct((entries, BLK, 2 * width), BF16)]
        part_specs = in_vmem(1)
    return pl.pallas_call(
        functools.partial(attend_kernel, heads, blocks, places, pieces),
        out_shape=[
            jax.ShapeDtypeStruct((rows, width), BF16),
            jax.ShapeDtypeStruct((blocks, heads, DH, DH), F32),
            jax.ShapeDtypeStruct((rows, width), F32),
            jax.ShapeDtypeStruct((rows, width), F32),
        ]
        + out_parts,
        in_specs=in_smem(1) + [any_spec] * len(sources) + in_vmem(7),
        out_specs=in_vmem(4) + part_specs,
        scratch_shapes=scratch,
        compiler_params=grant(36),
        cost_estimate=cost(15),
        name="attend",
    )(ints, *sources, *arrays)


def merge_kernel(own_ref, got_ref, after_ref, *out_refs):
    for i, ref in enumerate(out_refs):
        total = own_ref[0, i + 1].astype(F32) + got_ref[0, i + 1].astype(F32)
        ref[0] = total.astype(BF16)


def run_merge(own, got, first, size, after):
    _, chips, rows, width = own.shape
    cut = 2
    lanes = width // cut
    whole = pl.BlockSpec((1, chips, rows, lanes), lambda j, c: (first + j, 0, 0, c))
    return pl.pallas_call(
        merge_kernel,
        grid=(size, cut),
        out_shape=[jax.ShapeDtypeStruct((size, rows, width), BF16)] * (chips - 1),
        in_specs=[whole, whole, pl.BlockSpec((16, 128), lambda j, c: (0, 0))],
        out_specs=[pl.BlockSpec((1, rows, lanes), lambda j, c: (j, 0, c))] * (chips - 1),
        compiler_params=grant(16),
        cost_estimate=cost(2),
        name="merge",
    )(own, got, after)


def project_kernel(heads, parts, groups, flip_ref, after_ref, *refs):
    part_refs = refs[:parts]
    dk_loc, dv_loc, dq_ref, key_ref, dcum_in, cum_ref = refs[parts : parts + 6]
    weight_refs = refs[parts + 6 : parts + 9]
    first_ref, second_ref, rest_ref, dcum_out, tiles, sems = refs[parts + 9 :]
    count, _, tile, _ = tiles.shape
    per = count // groups
    copies = []
    for t in range(count):
        m = t // per
        row = ((m + flip_ref[0] * (groups - 1 - 2 * m)) * per + t % per) * tile
        rows = pl.ds(pl.multiple_of(row, tile), tile)
        for w, ref in enumerate(weight_refs):
            copy = pltpu.make_async_copy(ref.at[rows], tiles.at[t, w], sems.at[t, w])
            copy.start()
            copies.append(copy)

    dk, dv = [], []
    for h in range(heads):
        both = slice(2 * h * DH, (2 * h + 2) * DH)
        total = part_refs[0][0, :, both].astype(F32)
        for ref in part_refs[1:]:
            total = total + ref[0, :, both].astype(F32)
        dv.append((dv_loc[:, head(h)] + total[:, DH:]).astype(BF16))
        dk_top, dk_low = split(dk_loc[:, head(h)] + total[:, :DH])
        dk.append(nt(dk_top, cum_ref[0, h]).astype(BF16))
        key = key_ref[:, head(h)]
        key = jnp.concatenate([key, key], axis=0)
        dcum_out[h] = dcum_in[0, h] + tn(key, jnp.concatenate([dk_top, dk_low], axis=0))
    grads = (dq_ref[...], jnp.concatenate(dk, axis=1), jnp.concatenate(dv, axis=1))

    for t in range(count):
        term = None
        for w, grad in enumerate(grads):
            copies[3 * t + w].wait()
            part = nt(tiles[t, w], grad)
            term = part if term is None else term + part
        m, spot = t // per, slice(t % per * tile, (t % per + 1) * tile)
        out_ref, m = (first_ref, 0) if m == 0 else (second_ref, 0) if m == 1 else (rest_ref, m - 2)
        out_ref[m, :, spot] = term.T.astype(BF16)


def run_project(
    block, flip, after, parts, dk_loc, dv_loc, dq, key_rows, dcum, cum, weights, groups
):
    width = dq.shape[1]
    heads = width // DH
    model = weights[0].shape[0]
    chunk = model // groups
    tile = min(512, chunk)

    def part_spec(index):
        return pl.BlockSpec((1, BLK, 2 * width), lambda t: (index, 0, 0))

    def whole(*shape):
        return pl.BlockSpec(shape, lambda t: (0,) * len(shape))

    rows_spec = pl.BlockSpec((BLK, width), lambda t: (block, 0))
    head_spec = pl.BlockSpec((1, heads, DH, DH), lambda t: (block, 0, 0, 0))
    sizes = (1, 1, groups - 2)
    return pl.pallas_call(
        functools.partial(project_kernel, heads, len(parts), groups),
        grid=(1,),
        in_specs=in_smem(1)
        + [whole(16, 128)]
        + [part_spec(index) for _, index in parts]
        + [rows_spec] * 4
        + [head_spec] * 2
        + [pl.BlockSpec(memory_space=pl.ANY)] * 3,
        out_specs=[whole(size, BLK, chunk) for size in sizes] + [whole(heads, DH, DH)],
        scratch_shapes=[
            pltpu.VMEM((model // tile, 3, tile, width), BF16),
            pltpu.SemaphoreType.DMA((model // tile, 3)),
        ],
        out_shape=[jax.ShapeDtypeStruct((size, BLK, chunk), BF16) for size in sizes]
        + [jax.ShapeDtypeStruct((heads, DH, DH), F32)],
        compiler_params=grant(32),
        cost_estimate=cost(6),
        name="project",
    )(
        flip,
        after,
        *[part for part, _ in parts],
        dk_loc,
        dv_loc,
        dq,
        key_rows,
        dcum,
        cum,
        *weights,
    )


def adjoint_kernel(heads, blocks, ints_ref, after_ref, *refs):
    dcums = refs[:blocks]
    unit_ref, rows_ref, inv_ref, out_ref = refs[blocks:]
    count, width = unit_ref.shape
    stacked = (blocks * count, count)
    eye = (iota((count, count), 0) == iota((count, count), 1)).astype(F32)
    base = ints_ref[0] * blocks
    level, col = iota(stacked, 0), iota(stacked, 1)
    row = level % count
    mine = base + level // count
    alive = row[:, :1] <= mine[:, :1]
    for h in range(heads):
        units, rows, inverse = unit_ref[:, head(h)], rows_ref[:, head(h)], inv_ref[h]
        inverse_t = nt_high(eye, inverse)
        moved = jnp.concatenate([nt_high(rows, dcum[h]) for dcum in dcums], axis=0)
        overlap = jnp.where(col <= mine, nt_high(moved, units), 0.0)
        gamma = nn_high(overlap, inverse)
        gamma = jnp.where((row < col) & (col <= mine), gamma, 0.0)
        beta = jnp.concatenate([eye - inverse_t] * blocks, axis=0)
        beta = jnp.where(col <= mine, beta, 0.0)
        x_all = jnp.where(alive, moved - 2.0 * nn_high(gamma, units), 0.0)
        turned = jnp.concatenate([units] * blocks, axis=0) - nn_high(beta, units)
        turned = jnp.where(alive, turned, 0.0)
        x_total, y_total = None, None
        for j, dcum in enumerate(dcums):
            here = slice(j * count, (j + 1) * count)
            y_part = nn_high(turned[here], dcum[h])
            x_total = x_all[here] if j == 0 else x_total + x_all[here]
            y_total = y_part if j == 0 else y_total + y_part
        out_ref[:, head(h)] = x_total
        out_ref[:, slice(width + h * DH, width + (h + 1) * DH)] = y_total


def run_adjoint(ints, after, dcums, unit, rows, inverse, heads, blocks):
    count, width = unit.shape
    return pl.pallas_call(
        functools.partial(adjoint_kernel, heads, blocks),
        out_shape=jax.ShapeDtypeStruct((count, 2 * width), F32),
        in_specs=in_smem(1) + [pl.BlockSpec(memory_space=pl.ANY)] + in_vmem(blocks + 3),
        out_specs=pl.BlockSpec(memory_space=pltpu.VMEM),
        compiler_params=grant(16),
        cost_estimate=cost(11),
        name="adjoint",
    )(ints, after, *dcums, unit, rows, inverse)


def house_kernel(heads, blocks, base_ref, got_ref, unit_ref, rows_ref, house_ref, out_ref):
    count, width = unit_ref.shape
    total = jnp.sum(got_ref[...], axis=0)
    for h in range(heads):
        x_part = total[:, head(h)]
        y_part = total[:, slice(width + h * DH, width + (h + 1) * DH)]
        along = nt_high(y_part, rows_ref[:, head(h)])
        spot = iota((blocks, count), 0) + base_ref[0] * blocks
        along = jnp.where(iota((blocks, count), 1) < spot, along, 0.0)
        turned = y_part - 2.0 * nn_high(along, unit_ref[:, head(h)])
        dunit = -2.0 * (x_part + turned)
        house = house_ref[:, head(h)]
        lengths = jnp.sqrt(jnp.sum(house * house, axis=1, keepdims=True) + 1e-06)
        unit = house / lengths
        inner = jnp.sum(unit * dunit, axis=1, keepdims=True)
        out_ref[:, head(h)] = (dunit - unit * inner) / lengths


def run_house(ints, got, unit, rows, house_dirs, heads, blocks):
    return pl.pallas_call(
        functools.partial(house_kernel, heads, blocks),
        out_shape=jax.ShapeDtypeStruct(house_dirs.shape, F32),
        in_specs=[pl.BlockSpec(memory_space=pltpu.SMEM)] + in_vmem(4),
        out_specs=pl.BlockSpec(memory_space=pltpu.VMEM),
        compiler_params=grant(8),
        cost_estimate=cost(2),
        name="house_grad",
    )(ints, got, unit, rows, house_dirs)


def hop(value, distance, count):
    return lax.ppermute(value, "ctx", [(i, i ^ distance) for i in range(count)])


def slide(value, pairs):
    return lax.ppermute(value, "head", pairs)


def fold_kernel(rest_ref, inward_ref, after_ref, out_ref):
    out_ref[...] = (rest_ref[...].astype(F32) + inward_ref[...].astype(F32)).astype(BF16)


def run_fold(rest, inward, after):
    spec = pl.BlockSpec((1,) + rest.shape[1:], lambda t: (t, 0, 0))
    return pl.pallas_call(
        fold_kernel,
        grid=(rest.shape[0],),
        out_shape=jax.ShapeDtypeStruct(rest.shape, BF16),
        in_specs=[spec, spec, pl.BlockSpec((16, 128), lambda t: (0, 0))],
        out_specs=spec,
        compiler_params=grant(8),
        cost_estimate=cost(1),
        name="fold",
    )(rest, inward, after)


def line_scatter(first, second, rest, after):
    place = lax.axis_index("head")
    ends = (place == 0) | (place == 3)
    inward = slide(rest, [(0, 1), (3, 2)])
    inward_near = slide(second, [(0, 1), (3, 2)])
    swapped = slide(run_fold(rest, inward, after), [(1, 2), (2, 1)])
    outward = slide(first + swapped[1:], [(1, 0), (2, 3)])
    total = jnp.where(ends, first, second).astype(F32) + inward_near.astype(F32)
    total = total + swapped[:1].astype(F32) + outward.astype(F32)
    return total[0].astype(BF16), swapped


def shards(
    query_rows, key_rows, value_rows, grad_out, house_dirs, owners, offsets, w_query, w_key, w_value
):
    tok_rows, width = query_rows.shape
    heads, blocks = width // DH, tok_rows // BLK
    ctx_count, groups = lax.axis_size("ctx"), lax.axis_size("head")
    my_index = lax.axis_index("ctx").astype(jnp.int32)
    ints = jnp.concatenate([my_index.reshape(1), owners.reshape(-1), offsets.reshape(-1)])
    by_hand = ctx_count == 8
    core, across, along = 1, 2, 4

    if by_hand:
        other = hop(house_dirs, core, 8)
        upper = (my_index & core) != 0
        low, high = jnp.where(upper, other, house_dirs), jnp.where(upper, house_dirs, other)
        house_pair = jnp.concatenate([low, high], axis=0)
        house_parts = [house_pair] + [hop(house_pair, t, 8) for t in (2, 4, 6)]
        value_x, key_y = hop(value_rows, across, 8), hop(key_rows, along, 8)
        key_late, value_late, _ = lax.optimization_barrier((key_rows, value_rows, house_pair))
        key_x, value_y = hop(key_late, across, 8), hop(value_late, along, 8)
        key_d, value_d = hop(key_y, across, 8), hop(value_x, along, 8)
        sources, places = [], []
        for key, value in (
            (key_rows, value_rows),
            (key_x, value_x),
            (key_y, value_y),
            (key_d, value_d),
        ):
            for pair in ((key, value), (hop(key, core, 8), hop(value, core, 8))):
                places.append(((len(sources), 0), (len(sources) + 1, 0)))
                sources += pair
    else:
        house_parts = [lax.all_gather(house_dirs, "ctx", axis=0, tiled=True)]
        sources = [lax.all_gather(key_rows, "ctx"), lax.all_gather(value_rows, "ctx")]
        places = [((0, 0), (1, 0))]

    unit, rows, inverse, unit_t = run_chain(ints, house_parts, heads)
    qrot, krot, local, listed_cum = run_rotate(
        ints, rows, unit_t, query_rows, key_rows, heads, blocks
    )
    rounds = ((0, 1), (1, blocks - 1), (blocks, 1), (blocks + 1, blocks - 1))
    dq, dcum, dk_loc, dv_loc, *outs = run_attend(
        ints,
        sources,
        places,
        (query_rows, qrot, krot, value_rows, grad_out, local, listed_cum),
        heads,
        blocks,
        rounds if by_hand else (),
    )
    parts, merged = [], []
    if by_hand:
        got = [hop(outs[2], core, 8), hop(outs[3], core, 8)]
        flat = (-1, BLK, 2 * width)
        after = key_rows
        for j in range(blocks):
            source, first = min(j, 1), max(j - 1, 0)
            to_x, to_y, to_d = run_merge(outs[source], got[source], first, 1, after)
            merged.append(to_d[0])
            from_d = hop(to_d, across + along, 8)
            from_x, from_y = hop(to_x, across, 8), hop(to_y, along, 8)
            after = from_d[0]
            near = (outs[source].reshape(flat), got[source].reshape(flat))
            mine = [(part, 4 * first) for part in near]
            parts.append(mine + [(from_x, 0), (from_y, 0), (from_d, 0)])
    else:
        spots = (owners * blocks + offsets).reshape(-1)
        empty = jnp.zeros((ctx_count * blocks, BLK, 2 * width), BF16)
        filled = empty.at[spots].add(outs[0])
        back = lax.psum_scatter(filled, "ctx", scatter_dimension=0, tiled=True)
        parts = [[(back, j)] for j in range(blocks)]
        merged = [key_rows] * blocks

    weights = (w_query, w_key, w_value)
    on_line = groups == 4
    flip = jnp.where(on_line & (lax.axis_index("head") >= 2), 1, 0).astype(jnp.int32).reshape(1)
    share = jnp.zeros((tok_rows, w_query.shape[0] // groups), BF16)
    dcums = []
    for j in range(blocks):
        *terms, dcum_j = run_project(
            j, flip, merged[min(j + 1, blocks - 1)], parts[j], dk_loc, dv_loc, dq, key_rows, dcum, local, weights, groups
        )
        dcums.append(dcum_j)
        if on_line:
            done, swapped = line_scatter(*terms, merged[blocks - 1])
            late = swapped if j < blocks - 2 else late
        else:
            late = terms[0]
            term = jnp.concatenate(terms, axis=0)
            done = lax.psum_scatter(term, "head", scatter_dimension=0, tiled=False)
        share = lax.dynamic_update_slice(share, done, (j * BLK, 0))

    sums = run_adjoint(ints, late, dcums, unit, rows, inverse, heads, blocks)
    sums = sums.reshape(ctx_count, blocks, 2 * width)
    got = lax.all_to_all(sums, "ctx", split_axis=0, concat_axis=0, tiled=True)
    house_grad = run_house(ints, got, unit, rows, house_dirs, heads, blocks)
    return (share, house_grad)


def solution(mesh):
    placed = (
        P("ctx", "head"),
        P("ctx", "head"),
        P("ctx", "head"),
        P("ctx", "head"),
        P("ctx", "head"),
        P("ctx", None),
        P("ctx", None),
        P(None, "head"),
        P(None, "head"),
        P(None, "head"),
    )
    return jax.shard_map(
        shards,
        mesh=mesh,
        in_specs=placed,
        out_specs=(P("ctx", "head"), P("ctx", "head")),
        check_vma=False,
    )
```

```python
import functools
import math

import jax
import jax.numpy as jnp
from jax import lax
from jax.experimental import pallas as pl
from jax.experimental.pallas import tpu as pltpu
from jax.sharding import PartitionSpec as P

DH = 128
BLK = 128
MAXL = 2
HIGH = lax.Precision.HIGHEST
F32 = jnp.float32
BF16 = jnp.bfloat16


def nn(a, b):
    return lax.dot_general(a, b, (((1,), (0,)), ((), ())), preferred_element_type=F32)


def nt(a, b):
    return lax.dot_general(a, b, (((1,), (1,)), ((), ())), preferred_element_type=F32)


def tn(a, b):
    return lax.dot_general(a, b, (((0,), (0,)), ((), ())), preferred_element_type=F32)


def nn_high(a, b):
    return lax.dot_general(
        a, b, (((1,), (0,)), ((), ())), precision=HIGH, preferred_element_type=F32
    )


def nt_high(a, b):
    return lax.dot_general(
        a, b, (((1,), (1,)), ((), ())), precision=HIGH, preferred_element_type=F32
    )


def split(value):
    top = value.astype(BF16)
    return top, (value - top.astype(F32)).astype(BF16)


def iota(shape, dim):
    return lax.broadcasted_iota(jnp.int32, shape, dim)


def head(h):
    return slice(h * DH, (h + 1) * DH)


def listed(ints_ref, entry, entries):
    return ints_ref[1 + entry], ints_ref[1 + entries + entry]


def grant(mebibytes):
    return pltpu.CompilerParams(vmem_limit_bytes=mebibytes * 1024 * 1024)


def cost(microseconds):
    return pl.CostEstimate(
        flops=int(microseconds * 1.15e9), bytes_accessed=1 << 20, transcendentals=0
    )


def in_smem(count):
    return [pl.BlockSpec(memory_space=pltpu.SMEM)] * count


def in_vmem(count):
    return [pl.BlockSpec(memory_space=pltpu.VMEM)] * count


def chain_kernel(heads, parts, ints_ref, *refs):
    house_refs = refs[:parts]
    unit_ref, rows_ref, inv_ref, unit_t_ref, unit_h, house_all = refs[parts:]
    count = unit_ref.shape[0]
    span = count // parts
    for t, ref in enumerate(house_refs):
        place = (ints_ref[0] // (8 // parts)) ^ t if parts > 1 else 0
        house_all[pl.ds(pl.multiple_of(place * span, span), span), :] = ref[...]
    eye = (iota((count, count), 0) == iota((count, count), 1)).astype(F32)
    for h in range(heads):
        house = house_all[:, head(h)]
        lengths = jnp.sqrt(jnp.sum(house * house, axis=1, keepdims=True) + 1e-06)
        unit_ref[:, head(h)] = house / lengths
        unit_h[h] = house / lengths
        inv_ref[h] = eye

    def eliminate(step, carry):
        below = iota((count, 1), 0) > step
        for h in range(heads):
            pivot = unit_h[h, pl.ds(step, 1), :]
            overlap = jnp.sum(unit_h[h] * pivot, axis=1, keepdims=True)
            factor = jnp.where(below, 2.0 * overlap, 0.0)
            inv_ref[h] = inv_ref[h] - factor * inv_ref[h, pl.ds(step, 1), :]
        return carry

    lax.fori_loop(0, count, eliminate, 0)
    eye_wide = (iota((DH, DH), 0) == iota((DH, DH), 1)).astype(F32)
    for h in range(heads):
        units = unit_ref[:, head(h)]
        rows_ref[:, head(h)] = nn_high(inv_ref[h], units)
        unit_t_ref[h] = nt_high(eye_wide, units)


def run_chain(ints, house_parts, heads):
    span, width = house_parts[0].shape
    parts = len(house_parts)
    count = span * parts
    return pl.pallas_call(
        functools.partial(chain_kernel, heads, parts),
        out_shape=[
            jax.ShapeDtypeStruct((count, width), F32),
            jax.ShapeDtypeStruct((count, width), F32),
            jax.ShapeDtypeStruct((heads, count, count), F32),
            jax.ShapeDtypeStruct((heads, DH, count), F32),
        ],
        in_specs=in_smem(1) + in_vmem(parts),
        out_specs=in_vmem(4),
        scratch_shapes=[pltpu.VMEM((heads, count, DH), F32), pltpu.VMEM((count, width), F32)],
        compiler_params=grant(60),
        cost_estimate=cost(6),
        name="house_chain",
    )(ints, *house_parts)


def rotate_kernel(
    heads,
    blocks,
    ints_ref,
    rows_ref,
    unit_t_ref,
    query_ref,
    key_ref,
    qrot_ref,
    krot_ref,
    local_ref,
    listed_ref,
):
    count = rows_ref.shape[0]
    entries = blocks * MAXL
    eye = (iota((DH, DH), 0) == iota((DH, DH), 1)).astype(F32)

    def cumulative(h, block):
        kept = jnp.where(iota((DH, count), 1) <= block, unit_t_ref[h], 0.0)
        return split(eye - 2.0 * nn_high(kept, rows_ref[:, head(h)]))

    base = ints_ref[0] * blocks

    def local_block(b, carry):
        here = pl.ds(pl.multiple_of(b * BLK, BLK), BLK)
        for h in range(heads):
            hi, lo = cumulative(h, base + b)
            local_ref[b, h] = hi
            query, key = query_ref[here, head(h)], key_ref[here, head(h)]
            qrot_ref[here, head(h)] = (nn(query, hi) + nn(query, lo)).astype(BF16)
            krot_ref[here, head(h)] = (nn(key, hi) + nn(key, lo)).astype(BF16)
        return carry

    lax.fori_loop(0, blocks, local_block, 0)

    def listed_block(e, carry):
        owner, offset = listed(ints_ref, e, entries)
        for h in range(heads):
            hi, lo = cumulative(h, owner * blocks + offset)
            listed_ref[e, h, :DH] = hi
            listed_ref[e, h, DH:] = lo
        return carry

    lax.fori_loop(0, entries, listed_block, 0)


def run_rotate(ints, house_rows, unit_t, query_rows, key_rows, heads, blocks):
    rows, width = query_rows.shape
    entries = blocks * MAXL
    return pl.pallas_call(
        functools.partial(rotate_kernel, heads, blocks),
        out_shape=[
            jax.ShapeDtypeStruct((rows, width), BF16),
            jax.ShapeDtypeStruct((rows, width), BF16),
            jax.ShapeDtypeStruct((blocks, heads, DH, DH), BF16),
            jax.ShapeDtypeStruct((entries, heads, 2 * DH, DH), BF16),
        ],
        in_specs=in_smem(1) + in_vmem(4),
        out_specs=in_vmem(4),
        compiler_params=grant(60),
        cost_estimate=cost(9),
        name="rotate",
    )(ints, house_rows, unit_t, query_rows, key_rows)


def attend_kernel(heads, blocks, places, pieces, *refs):
    ints_ref = refs[0]
    source_count = 1 + max(place[0] for pair in places for place in pair)
    sources = refs[1 : 1 + source_count]
    refs = refs[1 + source_count :]
    (query_ref, qrot_ref, krot_ref, value_ref, grad_ref, local_ref, listed_ref) = refs[:7]
    dq_ref, dcum_ref, dk_ref, dv_ref = refs[7:11]
    outs = refs[11 : 11 + max(len(pieces), 1)]
    refs = refs[11 + max(len(pieces), 1) :]
    far_keys, far_values, sems = refs[:3]
    entries = blocks * MAXL
    scaling = DH ** (-0.5)
    log_scale = scaling * math.log2(math.e)

    def start(e, src, kind, slot, where):
        pltpu.make_async_copy(src.at[where], slot.at[e], sems.at[kind, e]).start()

    for e in range(entries):
        owner, offset = listed(ints_ref, e, entries)
        row = pl.multiple_of(offset * BLK, BLK)
        if len(places) == 1:
            start(e, sources[0], 0, far_keys, (owner, pl.ds(row, BLK)))
            start(e, sources[1], 1, far_values, (owner, pl.ds(row, BLK)))
        else:
            distance = owner ^ ints_ref[0]
            for r, (key_place, value_place) in enumerate(places):

                @pl.when(distance == r)
                def _():
                    source, first = key_place
                    start(e, sources[source], 0, far_keys, pl.ds(first + row, BLK))
                    source, first = value_place
                    start(e, sources[source], 1, far_values, pl.ds(first + row, BLK))

    out_copies = []
    if pieces:
        payloads, out_sems = refs[3 : 3 + heads], refs[3 + heads]
        for payload in payloads:
            payload[...] = jnp.zeros_like(payload)
    for kind, slots in ((0, far_keys), (1, far_values)):
        for e in range(entries):
            pltpu.make_async_copy(slots.at[e], slots.at[e], sems.at[kind, e]).wait()

    later = iota((BLK, BLK), 0) > iota((BLK, BLK), 1)
    empty = jnp.zeros((BLK, DH), BF16)
    steps = range(blocks)
    for h in range(heads):
        lanes = head(h)
        spans = [slice(a * BLK, (a + 1) * BLK) for a in steps]
        both, keys, values = [], [], []
        for a in steps:
            qrot, grad = qrot_ref[spans[a], lanes], grad_ref[spans[a], lanes]
            upper = jnp.concatenate([qrot, empty], axis=1)
            lower = jnp.concatenate([empty, grad], axis=1)
            both.append(jnp.concatenate([upper, lower], axis=0))
            keys.append([krot_ref[spans[b], lanes] for b in range(a + 1)])
            values.append([value_ref[spans[b], lanes] for b in range(a + 1)])
            for l in range(MAXL):
                e = a * MAXL + l
                raw = far_keys[e, :, lanes]
                raw = jnp.concatenate([raw, raw], axis=1)
                keys[a].append(nn(raw, listed_ref[e, h]).astype(BF16))
                values[a].append(far_values[e, :, lanes])
        scores, dprobs, tops = [], [], []
        for a in steps:
            scores.append([])
            dprobs.append([])
            top = None
            for b in range(a + 1 + MAXL):
                pair = nt(jnp.concatenate([keys[a][b], values[a][b]], axis=1), both[a])
                part = pair[:, :BLK] * log_scale
                if b == a:
                    part = jnp.where(later, -jnp.inf, part)
                scores[a].append(part)
                dprobs[a].append(pair[:, BLK:])
                top = part if top is None else jnp.maximum(top, part)
            tops.append(jnp.max(top, axis=0, keepdims=True))
        weights, inverses, deltas = [], [], []
        for a in steps:
            weights.append([])
            total, inner = None, None
            for part, dprob in zip(scores[a], dprobs[a]):
                weight = jnp.exp2(part - tops[a])
                weights[a].append(weight)
                product = weight * dprob
                total = weight if total is None else total + weight
                inner = product if inner is None else inner + product
            inverses.append(1.0 / jnp.sum(total, axis=0, keepdims=True))
            deltas.append(jnp.sum(inner, axis=0, keepdims=True) * inverses[a])
        dscores, pairs = [], []
        for a in steps:
            dscores.append([])
            pairs.append([])
            for b in range(a + 1 + MAXL):
                probs = weights[a][b] * inverses[a]
                dscore = (probs * (dprobs[a][b] - deltas[a])).astype(BF16)
                dscores[a].append(dscore)
                wide = jnp.concatenate([dscore, probs.astype(BF16)], axis=1)
                pairs[a].append(nn(wide, both[a]))
        for b in steps:
            total = pairs[b][b]
            for a in range(b + 1, blocks):
                total = total + pairs[a][b]
            dk_ref[spans[b], lanes] = total[:, :DH] * scaling
            dv_ref[spans[b], lanes] = total[:, DH:]
        for e in range(entries):
            pair = pairs[e // MAXL][e // MAXL + 1 + e % MAXL]
            dkey, dvalue = (pair[:, :DH] * scaling).astype(BF16), pair[:, DH:].astype(BF16)
            if pieces:
                owner, offset = listed(ints_ref, e, entries)
                distance = owner ^ ints_ref[0]
                at = (distance & 1) * blocks + offset
                payloads[h][at, distance >> 1, :, :DH] += dkey
                payloads[h][at, distance >> 1, :, DH:] += dvalue
            else:
                outs[0][e, :, 2 * h * DH : (2 * h + 1) * DH] = dkey
                outs[0][e, :, (2 * h + 1) * DH : (2 * h + 2) * DH] = dvalue
        halves = []
        for a in steps:
            wide, tall = jnp.concatenate(dscores[a], axis=0), jnp.concatenate(keys[a], axis=0)
            halves.append(split(tn(wide, tall) * scaling))
        for a in steps:
            dq_top, dq_low = halves[a]
            dq_ref[spans[a], lanes] = nt(dq_top, local_ref[a, h]).astype(BF16)
            query = query_ref[spans[a], lanes]
            query = jnp.concatenate([query, query], axis=0)
            dcum_ref[a, h] = tn(query, jnp.concatenate([dq_top, dq_low], axis=0))
        for i, (first, size) in enumerate(pieces):
            where = outs[i].at[:, :, :, 2 * h * DH : (2 * h + 2) * DH]
            source = payloads[h].at[pl.ds(first, size)]
            copy = pltpu.make_async_copy(source, where, out_sems.at[i, h])
            copy.start()
            out_copies.append(copy)
    for copy in out_copies:
        copy.wait()


def run_attend(ints, sources, places, arrays, heads, blocks, pieces):
    rows, width = arrays[0].shape
    entries = blocks * MAXL
    any_spec = pl.BlockSpec(memory_space=pl.ANY)
    scratch = [
        pltpu.VMEM((entries, BLK, width), BF16),
        pltpu.VMEM((entries, BLK, width), BF16),
        pltpu.SemaphoreType.DMA((2, entries)),
    ]
    if pieces:
        chips = len(places) // 2
        out_parts = [
            jax.ShapeDtypeStruct((size, chips, BLK, 2 * width), BF16) for _, size in pieces
        ]
        part_specs = [any_spec] * len(pieces)
        scratch += [pltpu.VMEM((2 * blocks, chips, BLK, 2 * DH), BF16)] * heads
        scratch += [pltpu.SemaphoreType.DMA((len(pieces), heads))]
    else:
        out_parts = [jax.ShapeDtypeStruct((entries, BLK, 2 * width), BF16)]
        part_specs = in_vmem(1)
    return pl.pallas_call(
        functools.partial(attend_kernel, heads, blocks, places, pieces),
        out_shape=[
            jax.ShapeDtypeStruct((rows, width), BF16),
            jax.ShapeDtypeStruct((blocks, heads, DH, DH), F32),
            jax.ShapeDtypeStruct((rows, width), F32),
            jax.ShapeDtypeStruct((rows, width), F32),
        ]
        + out_parts,
        in_specs=in_smem(1) + [any_spec] * len(sources) + in_vmem(7),
        out_specs=in_vmem(4) + part_specs,
        scratch_shapes=scratch,
        compiler_params=grant(60),
        cost_estimate=cost(15),
        name="attend",
    )(ints, *sources, *arrays)


def merge_kernel(own_ref, got_ref, *refs):
    for i, ref in enumerate(refs[-3:]):
        total = own_ref[0, i + 1].astype(F32) + got_ref[0, i + 1].astype(F32)
        ref[0] = total.astype(BF16)


def run_merge(own, got, first, size, afters):
    _, chips, rows, width = own.shape
    cut = 2
    lanes = width // cut
    whole = pl.BlockSpec((1, chips, rows, lanes), lambda j, c: (first + j, 0, 0, c))
    return pl.pallas_call(
        merge_kernel,
        grid=(size, cut),
        out_shape=[jax.ShapeDtypeStruct((size, rows, width), BF16)] * (chips - 1),
        in_specs=[whole] * 2 + [pl.BlockSpec((16, 128), lambda j, c: (0, 0))] * len(afters),
        out_specs=[pl.BlockSpec((1, rows, lanes), lambda j, c: (j, 0, c))] * (chips - 1),
        compiler_params=grant(60),
        cost_estimate=cost(2),
        name="merge",
    )(own, got, *afters)


def project_kernel(heads, parts, size, layout, flip_ref, after_ref, *refs):
    groups = sum(layout)
    part_refs = refs[: size * parts]
    dk_loc, dv_loc, dq_ref, key_ref, dcum_in, cum_ref = refs[size * parts : size * parts + 6]
    weight_refs = refs[size * parts + 6 : size * parts + 9]
    out_refs = refs[size * parts + 9 : -3]
    dcum_out, tiles, sems = refs[-3:]
    count, _, tile, _ = tiles.shape
    per = count // groups
    copies = []
    for t in range(count):
        m = t // per
        row = ((m + flip_ref[0] * (groups - 1 - 2 * m)) * per + t % per) * tile
        rows = pl.ds(pl.multiple_of(row, tile), tile)
        for w, ref in enumerate(weight_refs):
            copy = pltpu.make_async_copy(ref.at[rows], tiles.at[t, w], sems.at[t, w])
            copy.start()
            copies.append(copy)

    dk_rows, dv_rows = [], []
    for j in range(size):
        here = slice(j * BLK, (j + 1) * BLK)
        dk, dv = [], []
        for h in range(heads):
            both = slice(2 * h * DH, (2 * h + 2) * DH)
            total = part_refs[j * parts][0, :, both].astype(F32)
            for ref in part_refs[j * parts + 1 : (j + 1) * parts]:
                total = total + ref[0, :, both].astype(F32)
            dv.append((dv_loc[here, head(h)] + total[:, DH:]).astype(BF16))
            dk_top, dk_low = split(dk_loc[here, head(h)] + total[:, :DH])
            dk.append(nt(dk_top, cum_ref[j, h]).astype(BF16))
            key = key_ref[here, head(h)]
            key = jnp.concatenate([key, key], axis=0)
            dcum = tn(key, jnp.concatenate([dk_top, dk_low], axis=0))
            dcum_out[j, h] = dcum_in[j, h] + dcum
        dk_rows.append(jnp.concatenate(dk, axis=1))
        dv_rows.append(jnp.concatenate(dv, axis=1))
    grads = (dq_ref[...], jnp.concatenate(dk_rows, axis=0), jnp.concatenate(dv_rows, axis=0))

    for t in range(count):
        term = None
        for w, grad in enumerate(grads):
            copies[3 * t + w].wait()
            part = nt(tiles[t, w], grad)
            term = part if term is None else term + part
        term = term.T.astype(BF16)
        m, spot = t // per, slice(t % per * tile, (t % per + 1) * tile)
        ends = [sum(layout[: i + 1]) for i in range(len(layout))]
        at = next(i for i, end in enumerate(ends) if m < end)
        out_refs[at][m - ends[at] + layout[at], :, spot] = term


def run_project(
    block, layout, flip, after, parts, dk_loc, dv_loc, dq, key_rows, dcum, cum, weights
):
    size, groups = len(parts), sum(layout)
    width = dq.shape[1]
    heads = width // DH
    model = weights[0].shape[0]
    chunk = model // groups
    tile = min(512, chunk)

    def part_spec(index):
        return pl.BlockSpec((1, BLK, 2 * width), lambda t: (index, 0, 0))

    def whole(*shape):
        return pl.BlockSpec(shape, lambda t: (0,) * len(shape))

    rows_spec = pl.BlockSpec((size * BLK, width), lambda t: (block // size, 0))
    head_spec = pl.BlockSpec((size, heads, DH, DH), lambda t: (block // size, 0, 0, 0))
    flat = [part for row in parts for part in row]
    rows = size * BLK
    return pl.pallas_call(
        functools.partial(project_kernel, heads, len(parts[0]), size, layout),
        grid=(1,),
        in_specs=in_smem(1)
        + [whole(16, 128)]
        + [part_spec(index) for _, index in flat]
        + [rows_spec] * 4
        + [head_spec] * 2
        + [pl.BlockSpec(memory_space=pl.ANY)] * 3,
        out_specs=[whole(count, rows, chunk) for count in layout] + [whole(size, heads, DH, DH)],
        scratch_shapes=[
            pltpu.VMEM((model // tile, 3, tile, width), BF16),
            pltpu.SemaphoreType.DMA((model // tile, 3)),
        ],
        out_shape=[jax.ShapeDtypeStruct((count, rows, chunk), BF16) for count in layout]
        + [jax.ShapeDtypeStruct((size, heads, DH, DH), F32)],
        compiler_params=grant(60),
        cost_estimate=cost(12),
        name="project",
    )(
        flip,
        after,
        *[part for part, _ in flat],
        dk_loc,
        dv_loc,
        dq,
        key_rows,
        dcum,
        cum,
        *weights,
    )


def adjoint_kernel(heads, blocks, ints_ref, after_ref, *refs):
    dcums = [ref.at[j] for ref in refs[:-4] for j in range(ref.shape[0])]
    unit_ref, rows_ref, inv_ref, out_ref = refs[-4:]
    count, width = unit_ref.shape
    stacked = (blocks * count, count)
    eye = (iota((count, count), 0) == iota((count, count), 1)).astype(F32)
    base = ints_ref[0] * blocks
    level, col = iota(stacked, 0), iota(stacked, 1)
    row = level % count
    mine = base + level // count
    alive = row[:, :1] <= mine[:, :1]
    for h in range(heads):
        units, rows, inverse = unit_ref[:, head(h)], rows_ref[:, head(h)], inv_ref[h]
        inverse_t = nt_high(eye, inverse)
        moved = jnp.concatenate([nt_high(rows, dcum[h]) for dcum in dcums], axis=0)
        overlap = jnp.where(col <= mine, nt_high(moved, units), 0.0)
        gamma = nn_high(overlap, inverse)
        gamma = jnp.where((row < col) & (col <= mine), gamma, 0.0)
        beta = jnp.concatenate([eye - inverse_t] * blocks, axis=0)
        beta = jnp.where(col <= mine, beta, 0.0)
        x_all = jnp.where(alive, moved - 2.0 * nn_high(gamma, units), 0.0)
        turned = jnp.concatenate([units] * blocks, axis=0) - nn_high(beta, units)
        turned = jnp.where(alive, turned, 0.0)
        x_total, y_total = None, None
        for j, dcum in enumerate(dcums):
            here = slice(j * count, (j + 1) * count)
            y_part = nn_high(turned[here], dcum[h])
            x_total = x_all[here] if j == 0 else x_total + x_all[here]
            y_total = y_part if j == 0 else y_total + y_part
        out_ref[:, head(h)] = x_total
        out_ref[:, slice(width + h * DH, width + (h + 1) * DH)] = y_total


def run_adjoint(ints, after, dcums, unit, rows, inverse, heads, blocks):
    count, width = unit.shape
    return pl.pallas_call(
        functools.partial(adjoint_kernel, heads, blocks),
        out_shape=jax.ShapeDtypeStruct((count, 2 * width), F32),
        in_specs=in_smem(1) + [pl.BlockSpec(memory_space=pl.ANY)] + in_vmem(len(dcums) + 3),
        out_specs=pl.BlockSpec(memory_space=pltpu.VMEM),
        compiler_params=grant(60),
        cost_estimate=cost(2),
        name="adjoint",
    )(ints, after, *dcums, unit, rows, inverse)


def house_kernel(heads, blocks, base_ref, got_ref, unit_ref, rows_ref, house_ref, out_ref):
    count, width = unit_ref.shape
    total = jnp.sum(got_ref[...], axis=0)
    for h in range(heads):
        x_part = total[:, head(h)]
        y_part = total[:, slice(width + h * DH, width + (h + 1) * DH)]
        along = nt_high(y_part, rows_ref[:, head(h)])
        spot = iota((blocks, count), 0) + base_ref[0] * blocks
        along = jnp.where(iota((blocks, count), 1) < spot, along, 0.0)
        turned = y_part - 2.0 * nn_high(along, unit_ref[:, head(h)])
        dunit = -2.0 * (x_part + turned)
        house = house_ref[:, head(h)]
        lengths = jnp.sqrt(jnp.sum(house * house, axis=1, keepdims=True) + 1e-06)
        unit = house / lengths
        inner = jnp.sum(unit * dunit, axis=1, keepdims=True)
        out_ref[:, head(h)] = (dunit - unit * inner) / lengths


def run_house(ints, got, unit, rows, house_dirs, heads, blocks):
    return pl.pallas_call(
        functools.partial(house_kernel, heads, blocks),
        out_shape=jax.ShapeDtypeStruct(house_dirs.shape, F32),
        in_specs=[pl.BlockSpec(memory_space=pltpu.SMEM)] + in_vmem(4),
        out_specs=pl.BlockSpec(memory_space=pltpu.VMEM),
        compiler_params=grant(60),
        cost_estimate=cost(2),
        name="house_grad",
    )(ints, got, unit, rows, house_dirs)


def hop(value, distance, count):
    return lax.ppermute(value, "ctx", [(i, i ^ distance) for i in range(count)])


def slide(value, pairs):
    return lax.ppermute(value, "head", pairs)


def fold_kernel(rest_ref, inward_ref, after_ref, out_ref):
    out_ref[...] = (rest_ref[...].astype(F32) + inward_ref[...].astype(F32)).astype(BF16)


def run_fold(rest, inward, after):
    count, rows, width = rest.shape
    later = pl.BlockSpec((1, rows, width), lambda t: (t + 1, 0, 0))
    return pl.pallas_call(
        fold_kernel,
        grid=(count - 1,),
        out_shape=jax.ShapeDtypeStruct((count - 1, rows, width), BF16),
        in_specs=[later, later, pl.BlockSpec((16, 128), lambda t: (0, 0))],
        out_specs=pl.BlockSpec((1, rows, width), lambda t: (t, 0, 0)),
        compiler_params=grant(60),
        cost_estimate=cost(2),
        name="fold",
    )(rest, inward, after)


INWARD = [(0, 1), (3, 2)]
MIDDLE = [(1, 2), (2, 1)]
OUTWARD = [(1, 0), (2, 3)]


def line_scatter(first, rest, inward, after):
    place = lax.axis_index("head")
    ends = (place == 0) | (place == 3)
    swapped = slide(run_fold(rest, inward, after), MIDDLE)
    outward = slide(first + swapped[1:], OUTWARD)
    total = jnp.where(ends, first, rest[:1]).astype(F32) + inward[:1].astype(F32)
    total = total + swapped[:1].astype(F32) + outward.astype(F32)
    return total[0].astype(BF16), swapped


def line_scatter_apart(first, near, far, last):
    place = lax.axis_index("head")
    ends = (place == 0) | (place == 3)
    in_last, in_far, in_near = slide(last, INWARD), slide(far, INWARD), slide(near, INWARD)
    swap_last, swap_far = slide(last + in_last, MIDDLE), slide(far + in_far, MIDDLE)
    outward = slide(first + swap_last, OUTWARD)
    total = jnp.where(ends, first, near).astype(F32) + in_near.astype(F32)
    total = total + swap_far.astype(F32) + outward.astype(F32)
    return total[0].astype(BF16)


def shards(
    query_rows, key_rows, value_rows, grad_out, house_dirs, owners, offsets, w_query, w_key, w_value
):
    tok_rows, width = query_rows.shape
    heads, blocks = width // DH, tok_rows // BLK
    ctx_count, groups = lax.axis_size("ctx"), lax.axis_size("head")
    my_index = lax.axis_index("ctx").astype(jnp.int32)
    ints = jnp.concatenate([my_index.reshape(1), owners.reshape(-1), offsets.reshape(-1)])
    by_hand = ctx_count == 8 and groups == 4 and blocks == 4
    core, across, along = 1, 2, 4

    if by_hand:
        other = hop(house_dirs, core, 8)
        upper = (my_index & core) != 0
        low, high = jnp.where(upper, other, house_dirs), jnp.where(upper, house_dirs, other)
        house_pair = jnp.concatenate([low, high], axis=0)
        house_parts = [house_pair] + [hop(house_pair, t, 8) for t in (2, 4, 6)]
        value_x, key_y = hop(value_rows, across, 8), hop(key_rows, along, 8)
        key_late, value_late, *_ = lax.optimization_barrier((key_rows, value_rows, *house_parts))
        key_x, value_y = hop(key_late, across, 8), hop(value_late, along, 8)
        key_d, value_d = hop(key_y, across, 8), hop(value_x, along, 8)
    else:
        house_parts = [lax.all_gather(house_dirs, "ctx", axis=0, tiled=True)]

    unit, rows, inverse, unit_t = run_chain(ints, house_parts, heads)
    qrot, krot, local, listed_cum = run_rotate(
        ints, rows, unit_t, query_rows, key_rows, heads, blocks
    )
    if by_hand:
        late = lax.optimization_barrier((key_x, value_y, key_d, value_d, qrot))
        siblings = (key_late, value_late, late[0], value_x, key_y, late[1], late[2], late[3])
        siblings = [hop(part, core, 8) for part in siblings]
        own = (key_rows, value_rows, key_x, value_x, key_y, value_y, key_d, value_d)
        sources, places = [], []
        for t in range(4):
            for pair in (own[2 * t : 2 * t + 2], siblings[2 * t : 2 * t + 2]):
                places.append(((len(sources), 0), (len(sources) + 1, 0)))
                sources += pair
    else:
        sources = [lax.all_gather(key_rows, "ctx"), lax.all_gather(value_rows, "ctx")]
        places = [((0, 0), (1, 0))]

    rounds = ((0, 1), (1, blocks - 1), (blocks, 1), (blocks + 1, blocks - 1))
    dq, dcum, dk_loc, dv_loc, *outs = run_attend(
        ints,
        sources,
        places,
        (query_rows, qrot, krot, value_rows, grad_out, local, listed_cum),
        heads,
        blocks,
        rounds if by_hand else (),
    )
    weights = (w_query, w_key, w_value)
    flip = jnp.where(by_hand & (lax.axis_index("head") >= 2), 1, 0).astype(jnp.int32).reshape(1)

    def project(block, layout, after, parts):
        return run_project(
            block, layout, flip, after, parts, dk_loc, dv_loc, dq, key_rows, dcum, local, weights
        )

    share = jnp.zeros((tok_rows, w_query.shape[0] // groups), BF16)
    if by_hand:
        got = hop(outs[2], core, 8)
        got = [got, hop(lax.optimization_barrier((outs[3], got))[0], core, 8)]

        def give_back(j, afters):
            source, first = min(j, 1), max(j - 1, 0)
            sent = run_merge(outs[source], got[source], first, 1, [part[0] for part in afters])
            back = [hop(part, t, 8) for part, t in zip(sent, (across, along, across + along))]
            near = [part.reshape(-1, BLK, 2 * width) for part in (outs[source], got[source])]
            return [(part, 4 * first) for part in near] + [(part, 0) for part in back], sent, back

        joint, apart = (1, groups - 1), (1,) * groups
        parts_0, _, back_0 = give_back(0, [])
        parts_1, sent_1, back_1 = give_back(1, back_0)
        *terms_0, dcum_0 = project(0, joint, sent_1[2][0], [parts_0])
        inward_0 = slide(terms_0[1], INWARD)
        parts_2, sent_2, back_2 = give_back(2, back_1 + [terms_0[1]])
        *terms_1, dcum_1 = project(1, joint, sent_2[2][0], [parts_1])
        inward_1 = slide(terms_1[1], INWARD)
        parts_3, _, back_3 = give_back(3, back_2 + [terms_1[1], inward_0])
        *terms_2, dcum_2 = project(2, apart, inward_1[0], [parts_2, parts_3])
        done_0, _ = line_scatter(*terms_0, inward_0, back_3[2][0])
        done_1, swapped = line_scatter(*terms_1, inward_1, back_3[2][0])
        done_2 = line_scatter_apart(*terms_2)
        late = swapped[0]
        dcums = [dcum_0, dcum_1, dcum_2]
        for j, done in enumerate((done_0, done_1, done_2)):
            share = lax.dynamic_update_slice(share, done, (j * BLK, 0))
    else:
        spots = (owners * blocks + offsets).reshape(-1)
        empty = jnp.zeros((ctx_count * blocks, BLK, 2 * width), BF16)
        filled = empty.at[spots].add(outs[0])
        back = lax.psum_scatter(filled, "ctx", scatter_dimension=0, tiled=True)
        late, dcums = key_rows, []
        for j in range(blocks):
            *terms, dcum_out = project(j, (groups,), key_rows, [[(back, j)]])
            dcums.append(dcum_out)
            done = lax.psum_scatter(terms[0], "head", scatter_dimension=0, tiled=False)
            share = lax.dynamic_update_slice(share, done, (j * BLK, 0))

    sums = run_adjoint(ints, late, dcums, unit, rows, inverse, heads, blocks)
    sums = sums.reshape(ctx_count, blocks, 2 * width)
    got = lax.all_to_all(sums, "ctx", split_axis=0, concat_axis=0, tiled=True)
    house_grad = run_house(ints, got, unit, rows, house_dirs, heads, blocks)
    return (share, house_grad)


def solution(mesh):
    placed = (
        P("ctx", "head"),
        P("ctx", "head"),
        P("ctx", "head"),
        P("ctx", "head"),
        P("ctx", "head"),
        P("ctx", None),
        P("ctx", None),
        P(None, "head"),
        P(None, "head"),
        P(None, "head"),
    )
    return jax.shard_map(
        shards,
        mesh=mesh,
        in_specs=placed,
        out_specs=(P("ctx", "head"), P("ctx", "head")),
        check_vma=False,
    )
```

```python
import functools
import math

import jax
import jax.numpy as jnp
from jax import lax
from jax.experimental import pallas as pl
from jax.experimental.pallas import tpu as pltpu
from jax.sharding import PartitionSpec as P

DH = 128
BLK = 128
MAXL = 2
HIGH = lax.Precision.HIGHEST
F32 = jnp.float32
BF16 = jnp.bfloat16


def nn(a, b):
    return lax.dot_general(a, b, (((1,), (0,)), ((), ())), preferred_element_type=F32)


def nt(a, b):
    return lax.dot_general(a, b, (((1,), (1,)), ((), ())), preferred_element_type=F32)


def tn(a, b):
    return lax.dot_general(a, b, (((0,), (0,)), ((), ())), preferred_element_type=F32)


def nn_high(a, b):
    return lax.dot_general(
        a, b, (((1,), (0,)), ((), ())), precision=HIGH, preferred_element_type=F32
    )


def nt_high(a, b):
    return lax.dot_general(
        a, b, (((1,), (1,)), ((), ())), precision=HIGH, preferred_element_type=F32
    )


def split(value):
    top = value.astype(BF16)
    return top, (value - top.astype(F32)).astype(BF16)


def iota(shape, dim):
    return lax.broadcasted_iota(jnp.int32, shape, dim)


def head(h):
    return slice(h * DH, (h + 1) * DH)


def listed(ints_ref, entry, entries):
    return ints_ref[1 + entry], ints_ref[1 + entries + entry]


def grant(mebibytes):
    return pltpu.CompilerParams(vmem_limit_bytes=mebibytes * 1024 * 1024)


def cost(microseconds):
    return pl.CostEstimate(
        flops=int(microseconds * 1.15e9), bytes_accessed=1 << 20, transcendentals=0
    )


def in_smem(count):
    return [pl.BlockSpec(memory_space=pltpu.SMEM)] * count


def in_vmem(count):
    return [pl.BlockSpec(memory_space=pltpu.VMEM)] * count


def chain_kernel(heads, parts, ints_ref, *refs):
    house_refs = refs[:parts]
    unit_ref, rows_ref, inv_ref, unit_t_ref, unit_h, house_all = refs[parts:]
    count = unit_ref.shape[0]
    span = count // parts
    for t, ref in enumerate(house_refs):
        place = (ints_ref[0] // (8 // parts)) ^ t if parts > 1 else 0
        house_all[pl.ds(pl.multiple_of(place * span, span), span), :] = ref[...]
    eye = (iota((count, count), 0) == iota((count, count), 1)).astype(F32)
    for h in range(heads):
        house = house_all[:, head(h)]
        lengths = jnp.sqrt(jnp.sum(house * house, axis=1, keepdims=True) + 1e-06)
        unit_ref[:, head(h)] = house / lengths
        unit_h[h] = house / lengths
        inv_ref[h] = eye

    def eliminate(step, carry):
        below = iota((count, 1), 0) > step
        for h in range(heads):
            pivot = unit_h[h, pl.ds(step, 1), :]
            overlap = jnp.sum(unit_h[h] * pivot, axis=1, keepdims=True)
            factor = jnp.where(below, 2.0 * overlap, 0.0)
            inv_ref[h] = inv_ref[h] - factor * inv_ref[h, pl.ds(step, 1), :]
        return carry

    lax.fori_loop(0, count, eliminate, 0)
    eye_wide = (iota((DH, DH), 0) == iota((DH, DH), 1)).astype(F32)
    for h in range(heads):
        units = unit_ref[:, head(h)]
        rows_ref[:, head(h)] = nn_high(inv_ref[h], units)
        unit_t_ref[h] = nt_high(eye_wide, units)


def run_chain(ints, house_parts, heads):
    span, width = house_parts[0].shape
    parts = len(house_parts)
    count = span * parts
    return pl.pallas_call(
        functools.partial(chain_kernel, heads, parts),
        out_shape=[
            jax.ShapeDtypeStruct((count, width), F32),
            jax.ShapeDtypeStruct((count, width), F32),
            jax.ShapeDtypeStruct((heads, count, count), F32),
            jax.ShapeDtypeStruct((heads, DH, count), F32),
        ],
        in_specs=in_smem(1) + in_vmem(parts),
        out_specs=in_vmem(4),
        scratch_shapes=[pltpu.VMEM((heads, count, DH), F32), pltpu.VMEM((count, width), F32)],
        compiler_params=grant(60),
        cost_estimate=cost(6),
        name="house_chain",
    )(ints, *house_parts)


def rotate_kernel(
    heads,
    blocks,
    ints_ref,
    rows_ref,
    unit_t_ref,
    query_ref,
    key_ref,
    qrot_ref,
    krot_ref,
    local_ref,
    listed_ref,
):
    count = rows_ref.shape[0]
    entries = blocks * MAXL
    eye = (iota((DH, DH), 0) == iota((DH, DH), 1)).astype(F32)

    def cumulative(h, block):
        kept = jnp.where(iota((DH, count), 1) <= block, unit_t_ref[h], 0.0)
        return split(eye - 2.0 * nn_high(kept, rows_ref[:, head(h)]))

    base = ints_ref[0] * blocks

    def local_block(b, carry):
        here = pl.ds(pl.multiple_of(b * BLK, BLK), BLK)
        for h in range(heads):
            hi, lo = cumulative(h, base + b)
            local_ref[b, h] = hi
            query, key = query_ref[here, head(h)], key_ref[here, head(h)]
            qrot_ref[here, head(h)] = (nn(query, hi) + nn(query, lo)).astype(BF16)
            krot_ref[here, head(h)] = (nn(key, hi) + nn(key, lo)).astype(BF16)
        return carry

    lax.fori_loop(0, blocks, local_block, 0)

    def listed_block(e, carry):
        owner, offset = listed(ints_ref, e, entries)
        for h in range(heads):
            hi, lo = cumulative(h, owner * blocks + offset)
            listed_ref[e, h, :DH] = hi
            listed_ref[e, h, DH:] = lo
        return carry

    lax.fori_loop(0, entries, listed_block, 0)


def run_rotate(ints, house_rows, unit_t, query_rows, key_rows, heads, blocks):
    rows, width = query_rows.shape
    entries = blocks * MAXL
    return pl.pallas_call(
        functools.partial(rotate_kernel, heads, blocks),
        out_shape=[
            jax.ShapeDtypeStruct((rows, width), BF16),
            jax.ShapeDtypeStruct((rows, width), BF16),
            jax.ShapeDtypeStruct((blocks, heads, DH, DH), BF16),
            jax.ShapeDtypeStruct((entries, heads, 2 * DH, DH), BF16),
        ],
        in_specs=in_smem(1) + in_vmem(4),
        out_specs=in_vmem(4),
        compiler_params=grant(60),
        cost_estimate=cost(9),
        name="rotate",
    )(ints, house_rows, unit_t, query_rows, key_rows)


def attend_kernel(heads, blocks, places, pieces, *refs):
    ints_ref = refs[0]
    source_count = 1 + max(place[0] for pair in places for place in pair)
    sources = refs[1 : 1 + source_count]
    refs = refs[1 + source_count :]
    (query_ref, qrot_ref, krot_ref, value_ref, grad_ref, local_ref, listed_ref) = refs[:7]
    dq_ref, dcum_ref, dk_ref, dv_ref = refs[7:11]
    outs = refs[11 : 11 + max(len(pieces), 1)]
    refs = refs[11 + max(len(pieces), 1) :]
    far_keys, far_values, sems = refs[:3]
    entries = blocks * MAXL
    scaling = DH ** (-0.5)
    log_scale = scaling * math.log2(math.e)

    def start(e, src, kind, slot, where):
        pltpu.make_async_copy(src.at[where], slot.at[e], sems.at[kind, e]).start()

    for e in range(entries):
        owner, offset = listed(ints_ref, e, entries)
        row = pl.multiple_of(offset * BLK, BLK)
        if len(places) == 1:
            start(e, sources[0], 0, far_keys, (owner, pl.ds(row, BLK)))
            start(e, sources[1], 1, far_values, (owner, pl.ds(row, BLK)))
        else:
            distance = owner ^ ints_ref[0]
            for r, (key_place, value_place) in enumerate(places):

                @pl.when(distance == r)
                def _():
                    source, first = key_place
                    start(e, sources[source], 0, far_keys, pl.ds(first + row, BLK))
                    source, first = value_place
                    start(e, sources[source], 1, far_values, pl.ds(first + row, BLK))

    out_copies = []
    if pieces:
        payloads, out_sems = refs[3 : 3 + heads], refs[3 + heads]
        for payload in payloads:
            payload[...] = jnp.zeros_like(payload)
    for kind, slots in ((0, far_keys), (1, far_values)):
        for e in range(entries):
            pltpu.make_async_copy(slots.at[e], slots.at[e], sems.at[kind, e]).wait()

    later = iota((BLK, BLK), 0) > iota((BLK, BLK), 1)
    empty = jnp.zeros((BLK, DH), BF16)
    steps = range(blocks)
    for h in range(heads):
        lanes = head(h)
        spans = [slice(a * BLK, (a + 1) * BLK) for a in steps]
        both, keys, values = [], [], []
        for a in steps:
            qrot, grad = qrot_ref[spans[a], lanes], grad_ref[spans[a], lanes]
            upper = jnp.concatenate([qrot, empty], axis=1)
            lower = jnp.concatenate([empty, grad], axis=1)
            both.append(jnp.concatenate([upper, lower], axis=0))
            keys.append([krot_ref[spans[b], lanes] for b in range(a + 1)])
            values.append([value_ref[spans[b], lanes] for b in range(a + 1)])
            for l in range(MAXL):
                e = a * MAXL + l
                raw = far_keys[e, :, lanes]
                raw = jnp.concatenate([raw, raw], axis=1)
                keys[a].append(nn(raw, listed_ref[e, h]).astype(BF16))
                values[a].append(far_values[e, :, lanes])
        scores, dprobs, tops = [], [], []
        for a in steps:
            scores.append([])
            dprobs.append([])
            top = None
            for b in range(a + 1 + MAXL):
                pair = nt(jnp.concatenate([keys[a][b], values[a][b]], axis=1), both[a])
                part = pair[:, :BLK] * log_scale
                if b == a:
                    part = jnp.where(later, -jnp.inf, part)
                scores[a].append(part)
                dprobs[a].append(pair[:, BLK:])
                top = part if top is None else jnp.maximum(top, part)
            tops.append(jnp.max(top, axis=0, keepdims=True))
        weights, inverses, deltas = [], [], []
        for a in steps:
            weights.append([])
            total, inner = None, None
            for part, dprob in zip(scores[a], dprobs[a]):
                weight = jnp.exp2(part - tops[a])
                weights[a].append(weight)
                product = weight * dprob
                total = weight if total is None else total + weight
                inner = product if inner is None else inner + product
            inverses.append(1.0 / jnp.sum(total, axis=0, keepdims=True))
            deltas.append(jnp.sum(inner, axis=0, keepdims=True) * inverses[a])
        dscores, pairs = [], []
        for a in steps:
            dscores.append([])
            pairs.append([])
            for b in range(a + 1 + MAXL):
                probs = weights[a][b] * inverses[a]
                dscore = (probs * (dprobs[a][b] - deltas[a])).astype(BF16)
                dscores[a].append(dscore)
                wide = jnp.concatenate([dscore, probs.astype(BF16)], axis=1)
                pairs[a].append(nn(wide, both[a]))
        for b in steps:
            total = pairs[b][b]
            for a in range(b + 1, blocks):
                total = total + pairs[a][b]
            dk_ref[spans[b], lanes] = total[:, :DH] * scaling
            dv_ref[spans[b], lanes] = total[:, DH:]
        for e in range(entries):
            pair = pairs[e // MAXL][e // MAXL + 1 + e % MAXL]
            dkey, dvalue = (pair[:, :DH] * scaling).astype(BF16), pair[:, DH:].astype(BF16)
            if pieces:
                owner, offset = listed(ints_ref, e, entries)
                distance = owner ^ ints_ref[0]
                at = (distance & 1) * blocks + offset
                payloads[h][at, distance >> 1, :, :DH] += dkey
                payloads[h][at, distance >> 1, :, DH:] += dvalue
            else:
                outs[0][e, :, 2 * h * DH : (2 * h + 1) * DH] = dkey
                outs[0][e, :, (2 * h + 1) * DH : (2 * h + 2) * DH] = dvalue
        halves = []
        for a in steps:
            wide, tall = jnp.concatenate(dscores[a], axis=0), jnp.concatenate(keys[a], axis=0)
            halves.append(split(tn(wide, tall) * scaling))
        for a in steps:
            dq_top, dq_low = halves[a]
            dq_ref[spans[a], lanes] = nt(dq_top, local_ref[a, h]).astype(BF16)
            query = query_ref[spans[a], lanes]
            query = jnp.concatenate([query, query], axis=0)
            dcum_ref[a, h] = tn(query, jnp.concatenate([dq_top, dq_low], axis=0))
        for i, (first, size) in enumerate(pieces):
            where = outs[i].at[:, :, :, 2 * h * DH : (2 * h + 2) * DH]
            source = payloads[h].at[pl.ds(first, size)]
            copy = pltpu.make_async_copy(source, where, out_sems.at[i, h])
            copy.start()
            out_copies.append(copy)
    for copy in out_copies:
        copy.wait()


def run_attend(ints, sources, places, arrays, heads, blocks, pieces):
    rows, width = arrays[0].shape
    entries = blocks * MAXL
    any_spec = pl.BlockSpec(memory_space=pl.ANY)
    scratch = [
        pltpu.VMEM((entries, BLK, width), BF16),
        pltpu.VMEM((entries, BLK, width), BF16),
        pltpu.SemaphoreType.DMA((2, entries)),
    ]
    if pieces:
        chips = len(places) // 2
        out_parts = [
            jax.ShapeDtypeStruct((size, chips, BLK, 2 * width), BF16) for _, size in pieces
        ]
        part_specs = [any_spec] * len(pieces)
        scratch += [pltpu.VMEM((2 * blocks, chips, BLK, 2 * DH), BF16)] * heads
        scratch += [pltpu.SemaphoreType.DMA((len(pieces), heads))]
    else:
        out_parts = [jax.ShapeDtypeStruct((entries, BLK, 2 * width), BF16)]
        part_specs = in_vmem(1)
    return pl.pallas_call(
        functools.partial(attend_kernel, heads, blocks, places, pieces),
        out_shape=[
            jax.ShapeDtypeStruct((rows, width), BF16),
            jax.ShapeDtypeStruct((blocks, heads, DH, DH), F32),
            jax.ShapeDtypeStruct((rows, width), F32),
            jax.ShapeDtypeStruct((rows, width), F32),
        ]
        + out_parts,
        in_specs=in_smem(1) + [any_spec] * len(sources) + in_vmem(7),
        out_specs=in_vmem(4) + part_specs,
        scratch_shapes=scratch,
        compiler_params=grant(60),
        cost_estimate=cost(15),
        name="attend",
    )(ints, *sources, *arrays)


def merge_kernel(own_ref, got_ref, *refs):
    for i, ref in enumerate(refs[-3:]):
        total = own_ref[0, i + 1].astype(F32) + got_ref[0, i + 1].astype(F32)
        ref[0] = total.astype(BF16)


def run_merge(own, got, first, size, afters):
    _, chips, rows, width = own.shape
    cut = 2
    lanes = width // cut
    whole = pl.BlockSpec((1, chips, rows, lanes), lambda j, c: (first + j, 0, 0, c))
    return pl.pallas_call(
        merge_kernel,
        grid=(size, cut),
        out_shape=[jax.ShapeDtypeStruct((size, rows, width), BF16)] * (chips - 1),
        in_specs=[whole] * 2
        + [pl.BlockSpec((1, 16, 128), lambda j, c: (0, 0, 0))] * len(afters),
        out_specs=[pl.BlockSpec((1, rows, lanes), lambda j, c: (j, 0, c))] * (chips - 1),
        compiler_params=grant(60),
        cost_estimate=cost(2),
        name="merge",
    )(own, got, *afters)


def project_kernel(heads, parts, size, groups, chunks, flip_ref, after_ref, *refs):
    outs = len(chunks)
    tiles, sems = refs[-2:]
    per = tiles.shape[0] // outs
    tile = tiles.shape[2]
    if parts:
        part_refs, refs = refs[: size * parts], refs[size * parts :]
        dk_loc, dv_loc, dq_ref, key_ref, dcum_in, cum_ref = refs[:6]
        weight_refs, out_refs = refs[6:9], refs[9 : 9 + outs]
        dcum_out, dk_out, dv_out = refs[9 + outs : 12 + outs]
    else:
        dq_ref, dk_ref, dv_ref = refs[:3]
        weight_refs, out_refs = refs[3:6], refs[6 : 6 + outs]
    copies = []
    for t in range(outs * per):
        m = chunks[t // per]
        row = ((m + flip_ref[0] * (groups - 1 - 2 * m)) * per + t % per) * tile
        rows = pl.ds(pl.multiple_of(row, tile), tile)
        for w, ref in enumerate(weight_refs):
            copy = pltpu.make_async_copy(ref.at[rows], tiles.at[t, w], sems.at[t, w])
            copy.start()
            copies.append(copy)

    if parts:
        dk_rows, dv_rows = [], []
        for j in range(size):
            here = slice(j * BLK, (j + 1) * BLK)
            dk, dv = [], []
            for h in range(heads):
                both = slice(2 * h * DH, (2 * h + 2) * DH)
                total = part_refs[j * parts][0, :, both].astype(F32)
                for ref in part_refs[j * parts + 1 : (j + 1) * parts]:
                    total = total + ref[0, :, both].astype(F32)
                dv.append((dv_loc[here, head(h)] + total[:, DH:]).astype(BF16))
                dk_top, dk_low = split(dk_loc[here, head(h)] + total[:, :DH])
                dk.append(nt(dk_top, cum_ref[j, h]).astype(BF16))
                key = key_ref[here, head(h)]
                key = jnp.concatenate([key, key], axis=0)
                dcum = tn(key, jnp.concatenate([dk_top, dk_low], axis=0))
                dcum_out[j, h] = dcum_in[j, h] + dcum
            dk_rows.append(jnp.concatenate(dk, axis=1))
            dv_rows.append(jnp.concatenate(dv, axis=1))
        dk_all, dv_all = jnp.concatenate(dk_rows, axis=0), jnp.concatenate(dv_rows, axis=0)
        dk_out[...] = dk_all
        dv_out[...] = dv_all
        grads = (dq_ref[...], dk_all, dv_all)
    else:
        grads = (dq_ref[...], dk_ref[...], dv_ref[...])

    for t in range(outs * per):
        term = None
        for w, grad in enumerate(grads):
            copies[3 * t + w].wait()
            part = nt(tiles[t, w], grad)
            term = part if term is None else term + part
        spot = slice(t % per * tile, (t % per + 1) * tile)
        out_refs[t // per][0, :, spot] = term.T.astype(BF16)


def run_project(block, size, groups, chunks, flip, after, parts, finished, arrays, weights):
    dk_loc, dv_loc, dq, key_rows, dcum, cum = arrays
    width = dq.shape[1]
    heads = width // DH
    model = weights[0].shape[0]
    chunk = model // groups
    tile = min(512, chunk)
    rows = size * BLK
    tile_count = len(chunks) * chunk // tile

    def part_spec(index):
        return pl.BlockSpec((1, BLK, 2 * width), lambda t: (index, 0, 0))

    def whole(*shape):
        return pl.BlockSpec(shape, lambda t: (0,) * len(shape))

    rows_spec = pl.BlockSpec((rows, width), lambda t: (block // size, 0))
    head_spec = pl.BlockSpec((size, heads, DH, DH), lambda t: (block // size, 0, 0, 0))
    flat = [part for row in parts for part in row]
    out_specs = [whole(1, rows, chunk)] * len(chunks)
    out_shape = [jax.ShapeDtypeStruct((1, rows, chunk), BF16)] * len(chunks)
    if parts:
        in_specs = [part_spec(index) for _, index in flat] + [rows_spec] * 4 + [head_spec] * 2
        inputs = [part for part, _ in flat] + [dk_loc, dv_loc, dq, key_rows, dcum, cum]
        out_specs += [whole(size, heads, DH, DH)] + [whole(rows, width)] * 2
        out_shape += [jax.ShapeDtypeStruct((size, heads, DH, DH), F32)]
        out_shape += [jax.ShapeDtypeStruct((rows, width), BF16)] * 2
    else:
        in_specs = [rows_spec] + [whole(rows, width)] * 2
        inputs = [dq, *finished]
    return pl.pallas_call(
        functools.partial(
            project_kernel, heads, len(parts[0]) if parts else 0, size, groups, chunks
        ),
        grid=(1,),
        in_specs=in_smem(1)
        + [whole(1, 16, 128)]
        + in_specs
        + [pl.BlockSpec(memory_space=pl.ANY)] * 3,
        out_specs=out_specs,
        scratch_shapes=[
            pltpu.VMEM((tile_count, 3, tile, width), BF16),
            pltpu.SemaphoreType.DMA((tile_count, 3)),
        ],
        out_shape=out_shape,
        compiler_params=grant(60),
        cost_estimate=cost(3 * len(chunks)),
        name="project",
    )(flip, after, *inputs, *weights)


def adjoint_kernel(heads, blocks, ints_ref, after_ref, *refs):
    dcums = [ref.at[j] for ref in refs[:-4] for j in range(ref.shape[0])]
    unit_ref, rows_ref, inv_ref, out_ref = refs[-4:]
    count, width = unit_ref.shape
    stacked = (blocks * count, count)
    eye = (iota((count, count), 0) == iota((count, count), 1)).astype(F32)
    base = ints_ref[0] * blocks
    level, col = iota(stacked, 0), iota(stacked, 1)
    row = level % count
    mine = base + level // count
    alive = row[:, :1] <= mine[:, :1]
    for h in range(heads):
        units, rows, inverse = unit_ref[:, head(h)], rows_ref[:, head(h)], inv_ref[h]
        inverse_t = nt_high(eye, inverse)
        moved = jnp.concatenate([nt_high(rows, dcum[h]) for dcum in dcums], axis=0)
        overlap = jnp.where(col <= mine, nt_high(moved, units), 0.0)
        gamma = nn_high(overlap, inverse)
        gamma = jnp.where((row < col) & (col <= mine), gamma, 0.0)
        beta = jnp.concatenate([eye - inverse_t] * blocks, axis=0)
        beta = jnp.where(col <= mine, beta, 0.0)
        x_all = jnp.where(alive, moved - 2.0 * nn_high(gamma, units), 0.0)
        turned = jnp.concatenate([units] * blocks, axis=0) - nn_high(beta, units)
        turned = jnp.where(alive, turned, 0.0)
        x_total, y_total = None, None
        for j, dcum in enumerate(dcums):
            here = slice(j * count, (j + 1) * count)
            y_part = nn_high(turned[here], dcum[h])
            x_total = x_all[here] if j == 0 else x_total + x_all[here]
            y_total = y_part if j == 0 else y_total + y_part
        out_ref[:, head(h)] = x_total
        out_ref[:, slice(width + h * DH, width + (h + 1) * DH)] = y_total


def run_adjoint(ints, after, dcums, unit, rows, inverse, heads, blocks):
    count, width = unit.shape
    return pl.pallas_call(
        functools.partial(adjoint_kernel, heads, blocks),
        out_shape=jax.ShapeDtypeStruct((count, 2 * width), F32),
        in_specs=in_smem(1) + [pl.BlockSpec(memory_space=pl.ANY)] + in_vmem(len(dcums) + 3),
        out_specs=pl.BlockSpec(memory_space=pltpu.VMEM),
        compiler_params=grant(60),
        cost_estimate=cost(2),
        name="adjoint",
    )(ints, after, *dcums, unit, rows, inverse)


def house_kernel(heads, blocks, base_ref, got_ref, unit_ref, rows_ref, house_ref, out_ref):
    count, width = unit_ref.shape
    total = jnp.sum(got_ref[...], axis=0)
    for h in range(heads):
        x_part = total[:, head(h)]
        y_part = total[:, slice(width + h * DH, width + (h + 1) * DH)]
        along = nt_high(y_part, rows_ref[:, head(h)])
        spot = iota((blocks, count), 0) + base_ref[0] * blocks
        along = jnp.where(iota((blocks, count), 1) < spot, along, 0.0)
        turned = y_part - 2.0 * nn_high(along, unit_ref[:, head(h)])
        dunit = -2.0 * (x_part + turned)
        house = house_ref[:, head(h)]
        lengths = jnp.sqrt(jnp.sum(house * house, axis=1, keepdims=True) + 1e-06)
        unit = house / lengths
        inner = jnp.sum(unit * dunit, axis=1, keepdims=True)
        out_ref[:, head(h)] = (dunit - unit * inner) / lengths


def run_house(ints, got, unit, rows, house_dirs, heads, blocks):
    return pl.pallas_call(
        functools.partial(house_kernel, heads, blocks),
        out_shape=jax.ShapeDtypeStruct(house_dirs.shape, F32),
        in_specs=[pl.BlockSpec(memory_space=pltpu.SMEM)] + in_vmem(4),
        out_specs=pl.BlockSpec(memory_space=pltpu.VMEM),
        compiler_params=grant(60),
        cost_estimate=cost(2),
        name="house_grad",
    )(ints, got, unit, rows, house_dirs)


def hop(value, distance, count):
    return lax.ppermute(value, "ctx", [(i, i ^ distance) for i in range(count)])


def slide(value, pairs):
    return lax.ppermute(value, "head", pairs)


INWARD = [(0, 1), (3, 2)]
MIDDLE = [(1, 2), (2, 1)]
OUTWARD = [(1, 0), (2, 3)]


def near_kernel(ends_ref, first_ref, near_ref, inward_ref, out_ref):
    mine = jnp.where(ends_ref[0] > 0, first_ref[0], near_ref[0]).astype(F32)
    out_ref[...] = mine + inward_ref[0].astype(F32)


def run_near(ends, first, near, inward):
    return pl.pallas_call(
        near_kernel,
        out_shape=jax.ShapeDtypeStruct(first.shape[1:], F32),
        in_specs=in_smem(1) + in_vmem(3),
        out_specs=pl.BlockSpec(memory_space=pltpu.VMEM),
        compiler_params=grant(60),
        cost_estimate=cost(16),
        name="near_sum",
    )(ends, first, near, inward)


def line_scatter(share, first, near, far, last):
    place = lax.axis_index("head")
    ends = ((place == 0) | (place == 3)).astype(jnp.int32).reshape(1)
    in_last, in_far, in_near = slide(last, INWARD), slide(far, INWARD), slide(near, INWARD)
    swap_last, swap_far = slide(last + in_last, MIDDLE), slide(far + in_far, MIDDLE)
    outward = slide(first + swap_last, OUTWARD)
    total = run_near(ends, first, near, in_near)
    return run_share(share, total, swap_far, outward), swap_last


def share_kernel(*refs):
    total_ref, far_ref, outward_ref, out_ref = refs[-4:]
    far = far_ref[0].astype(F32) + outward_ref[0].astype(F32)
    out_ref[...] = (total_ref[...] + far).astype(BF16)


def run_share(share, total, far, outward):
    rows, width = total.shape
    place = 0 if share is None else 1
    tile = min(512, width)
    part = pl.BlockSpec((1, rows, tile), lambda t: (0, 0, t))
    given = [] if share is None else [share]
    return pl.pallas_call(
        share_kernel,
        grid=(width // tile,),
        out_shape=jax.ShapeDtypeStruct((2 * rows, width), BF16),
        in_specs=[pl.BlockSpec(memory_space=pl.ANY)] * len(given)
        + [pl.BlockSpec((rows, tile), lambda t: (0, t)), part, part],
        out_specs=pl.BlockSpec((rows, tile), lambda t: (place, t)),
        input_output_aliases={0: 0} if given else {},
        compiler_params=grant(60),
        cost_estimate=cost(2),
        name="share",
    )(*given, total, far, outward)


def shards(
    query_rows, key_rows, value_rows, grad_out, house_dirs, owners, offsets, w_query, w_key, w_value
):
    tok_rows, width = query_rows.shape
    heads, blocks = width // DH, tok_rows // BLK
    ctx_count, groups = lax.axis_size("ctx"), lax.axis_size("head")
    my_index = lax.axis_index("ctx").astype(jnp.int32)
    ints = jnp.concatenate([my_index.reshape(1), owners.reshape(-1), offsets.reshape(-1)])
    by_hand = ctx_count == 8 and groups == 4 and blocks == 4
    core, across, along = 1, 2, 4

    if by_hand:
        other = hop(house_dirs, core, 8)
        upper = (my_index & core) != 0
        low, high = jnp.where(upper, other, house_dirs), jnp.where(upper, house_dirs, other)
        house_pair = jnp.concatenate([low, high], axis=0)
        house_parts = [house_pair] + [hop(house_pair, t, 8) for t in (2, 4, 6)]
        value_x, key_y = hop(value_rows, across, 8), hop(key_rows, along, 8)
        key_late, value_late, *_ = lax.optimization_barrier((key_rows, value_rows, *house_parts))
        key_x, value_y = hop(key_late, across, 8), hop(value_late, along, 8)
        key_d, value_d = hop(key_y, across, 8), hop(value_x, along, 8)
    else:
        house_parts = [lax.all_gather(house_dirs, "ctx", axis=0, tiled=True)]

    unit, rows, inverse, unit_t = run_chain(ints, house_parts, heads)
    qrot, krot, local, listed_cum = run_rotate(
        ints, rows, unit_t, query_rows, key_rows, heads, blocks
    )
    if by_hand:
        late = lax.optimization_barrier((key_x, value_y, key_d, value_d, qrot))
        siblings = (key_late, value_late, late[0], value_x, key_y, late[1], late[2], late[3])
        siblings = [hop(part, core, 8) for part in siblings]
        own = (key_rows, value_rows, key_x, value_x, key_y, value_y, key_d, value_d)
        sources, places = [], []
        for t in range(4):
            for pair in (own[2 * t : 2 * t + 2], siblings[2 * t : 2 * t + 2]):
                places.append(((len(sources), 0), (len(sources) + 1, 0)))
                sources += pair
    else:
        sources = [lax.all_gather(key_rows, "ctx"), lax.all_gather(value_rows, "ctx")]
        places = [((0, 0), (1, 0))]

    half = blocks // 2
    rounds = tuple((first, half) for first in range(0, 2 * blocks, half))
    dq, dcum, dk_loc, dv_loc, *outs = run_attend(
        ints,
        sources,
        places,
        (query_rows, qrot, krot, value_rows, grad_out, local, listed_cum),
        heads,
        blocks,
        rounds if by_hand else (),
    )
    weights = (w_query, w_key, w_value)
    flip = jnp.where(by_hand & (lax.axis_index("head") >= 2), 1, 0).astype(jnp.int32).reshape(1)

    arrays = (dk_loc, dv_loc, dq, key_rows, dcum, local)

    def project(block, size, chunks, after, parts, finished=()):
        return run_project(
            block, size, groups, chunks, flip, after, parts, finished, arrays, weights
        )

    if by_hand:
        got_0 = hop(outs[2], core, 8)
        got_1 = hop(lax.optimization_barrier((outs[3], got_0))[0], core, 8)
        sent_0 = run_merge(outs[0], got_0, 0, half, [])
        sent_1 = run_merge(outs[1], got_1, 0, half, [sent_0[0]])

        def give_back(own, got, sent):
            back = [hop(part, t, 8) for part, t in zip(sent, (across, along, across + along))]
            near = [part.reshape(-1, BLK, 2 * width) for part in (own, got)]
            parts = [
                [(part, 4 * j) for part in near] + [(part, j) for part in back]
                for j in range(half)
            ]
            return parts, back

        parts_0, back_0 = give_back(outs[0], got_0, sent_0)
        *sent_1, _ = lax.optimization_barrier((*sent_1, back_0))
        parts_1, back_1 = give_back(outs[1], got_1, sent_1)
        far_0, last_0, dcum_0, *finished = project(0, half, (2, 3), sent_1[0], parts_0)
        first_0, near_0 = project(0, half, (0, 1), far_0, (), finished)
        share, late = line_scatter(None, first_0, near_0, far_0, last_0)
        *terms_1, dcum_1, _, _ = project(half, half, (0, 1, 2, 3), key_rows[None], parts_1)
        share, _ = line_scatter(share, *terms_1)
        dcums = [dcum_0, dcum_1]
    else:
        spots = (owners * blocks + offsets).reshape(-1)
        empty = jnp.zeros((ctx_count * blocks, BLK, 2 * width), BF16)
        filled = empty.at[spots].add(outs[0])
        back = lax.psum_scatter(filled, "ctx", scatter_dimension=0, tiled=True)
        late, dcums = key_rows, []
        share = jnp.zeros((tok_rows, w_query.shape[0] // groups), BF16)
        for j in range(blocks):
            *terms, dcum_out, _, _ = project(
                j, 1, tuple(range(groups)), key_rows[None], [[(back, j)]]
            )
            dcums.append(dcum_out)
            term = jnp.concatenate(terms, axis=0)
            done = lax.psum_scatter(term, "head", scatter_dimension=0, tiled=False)
            share = lax.dynamic_update_slice(share, done, (j * BLK, 0))

    sums = run_adjoint(ints, late, dcums, unit, rows, inverse, heads, blocks)
    sums = sums.reshape(ctx_count, blocks, 2 * width)
    got = lax.all_to_all(sums, "ctx", split_axis=0, concat_axis=0, tiled=True)
    house_grad = run_house(ints, got, unit, rows, house_dirs, heads, blocks)
    return (share, house_grad)


def solution(mesh):
    placed = (
        P("ctx", "head"),
        P("ctx", "head"),
        P("ctx", "head"),
        P("ctx", "head"),
        P("ctx", "head"),
        P("ctx", None),
        P("ctx", None),
        P(None, "head"),
        P(None, "head"),
        P(None, "head"),
    )
    return jax.shard_map(
        shards,
        mesh=mesh,
        in_specs=placed,
        out_specs=(P("ctx", "head"), P("ctx", "head")),
        check_vma=False,
    )
```

```python
import functools
import math

import jax
import jax.numpy as jnp
from jax import lax
from jax.experimental import pallas as pl
from jax.experimental.pallas import tpu as pltpu
from jax.sharding import PartitionSpec as P

DH = 128
BLK = 128
MAXL = 2
HIGH = lax.Precision.HIGHEST
F32 = jnp.float32
BF16 = jnp.bfloat16


def nn(a, b):
    return lax.dot_general(a, b, (((1,), (0,)), ((), ())), preferred_element_type=F32)


def nt(a, b):
    return lax.dot_general(a, b, (((1,), (1,)), ((), ())), preferred_element_type=F32)


def tn(a, b):
    return lax.dot_general(a, b, (((0,), (0,)), ((), ())), preferred_element_type=F32)


def nn_high(a, b):
    return lax.dot_general(
        a, b, (((1,), (0,)), ((), ())), precision=HIGH, preferred_element_type=F32
    )


def nt_high(a, b):
    return lax.dot_general(
        a, b, (((1,), (1,)), ((), ())), precision=HIGH, preferred_element_type=F32
    )


def split(value):
    top = value.astype(BF16)
    return top, (value - top.astype(F32)).astype(BF16)


def iota(shape, dim):
    return lax.broadcasted_iota(jnp.int32, shape, dim)


def head(h):
    return slice(h * DH, (h + 1) * DH)


def listed(ints_ref, entry, entries):
    return ints_ref[1 + entry], ints_ref[1 + entries + entry]


def grant(mebibytes):
    return pltpu.CompilerParams(vmem_limit_bytes=mebibytes * 1024 * 1024)


def cost(microseconds):
    return pl.CostEstimate(
        flops=int(microseconds * 1.15e9), bytes_accessed=1 << 20, transcendentals=0
    )


def in_smem(count):
    return [pl.BlockSpec(memory_space=pltpu.SMEM)] * count


def in_vmem(count):
    return [pl.BlockSpec(memory_space=pltpu.VMEM)] * count


def chain_kernel(heads, parts, ints_ref, *refs):
    house_refs = refs[:parts]
    unit_ref, rows_ref, inv_ref, unit_t_ref, unit_h, house_all = refs[parts:]
    count = unit_ref.shape[0]
    span = count // parts
    for t, ref in enumerate(house_refs):
        place = (ints_ref[0] // (8 // parts)) ^ t if parts > 1 else 0
        house_all[pl.ds(pl.multiple_of(place * span, span), span), :] = ref[...]
    eye = (iota((count, count), 0) == iota((count, count), 1)).astype(F32)
    for h in range(heads):
        house = house_all[:, head(h)]
        lengths = jnp.sqrt(jnp.sum(house * house, axis=1, keepdims=True) + 1e-06)
        unit_ref[:, head(h)] = house / lengths
        unit_h[h] = house / lengths
        inv_ref[h] = eye

    def eliminate(step, carry):
        below = iota((count, 1), 0) > step
        for h in range(heads):
            pivot = unit_h[h, pl.ds(step, 1), :]
            overlap = jnp.sum(unit_h[h] * pivot, axis=1, keepdims=True)
            factor = jnp.where(below, 2.0 * overlap, 0.0)
            inv_ref[h] = inv_ref[h] - factor * inv_ref[h, pl.ds(step, 1), :]
        return carry

    lax.fori_loop(0, count, eliminate, 0)
    eye_wide = (iota((DH, DH), 0) == iota((DH, DH), 1)).astype(F32)
    for h in range(heads):
        units = unit_ref[:, head(h)]
        rows_ref[:, head(h)] = nn_high(inv_ref[h], units)
        unit_t_ref[h] = nt_high(eye_wide, units)


def run_chain(ints, house_parts, heads):
    span, width = house_parts[0].shape
    parts = len(house_parts)
    count = span * parts
    return pl.pallas_call(
        functools.partial(chain_kernel, heads, parts),
        out_shape=[
            jax.ShapeDtypeStruct((count, width), F32),
            jax.ShapeDtypeStruct((count, width), F32),
            jax.ShapeDtypeStruct((heads, count, count), F32),
            jax.ShapeDtypeStruct((heads, DH, count), F32),
        ],
        in_specs=in_smem(1) + in_vmem(parts),
        out_specs=in_vmem(4),
        scratch_shapes=[pltpu.VMEM((heads, count, DH), F32), pltpu.VMEM((count, width), F32)],
        compiler_params=grant(12),
        cost_estimate=cost(6),
        name="house_chain",
    )(ints, *house_parts)


def rotate_kernel(
    heads,
    blocks,
    ints_ref,
    rows_ref,
    unit_t_ref,
    query_ref,
    key_ref,
    qrot_ref,
    krot_ref,
    local_ref,
    listed_ref,
):
    count = rows_ref.shape[0]
    entries = blocks * MAXL
    eye = (iota((DH, DH), 0) == iota((DH, DH), 1)).astype(F32)

    def cumulative(h, block):
        kept = jnp.where(iota((DH, count), 1) <= block, unit_t_ref[h], 0.0)
        return split(eye - 2.0 * nn_high(kept, rows_ref[:, head(h)]))

    base = ints_ref[0] * blocks

    def local_block(b, carry):
        here = pl.ds(pl.multiple_of(b * BLK, BLK), BLK)
        for h in range(heads):
            hi, lo = cumulative(h, base + b)
            local_ref[b, h] = hi
            query, key = query_ref[here, head(h)], key_ref[here, head(h)]
            qrot_ref[here, head(h)] = (nn(query, hi) + nn(query, lo)).astype(BF16)
            krot_ref[here, head(h)] = (nn(key, hi) + nn(key, lo)).astype(BF16)
        return carry

    lax.fori_loop(0, blocks, local_block, 0)

    def listed_block(e, carry):
        owner, offset = listed(ints_ref, e, entries)
        for h in range(heads):
            hi, lo = cumulative(h, owner * blocks + offset)
            listed_ref[e, h, :DH] = hi
            listed_ref[e, h, DH:] = lo
        return carry

    lax.fori_loop(0, entries, listed_block, 0)


def run_rotate(ints, house_rows, unit_t, query_rows, key_rows, heads, blocks):
    rows, width = query_rows.shape
    entries = blocks * MAXL
    return pl.pallas_call(
        functools.partial(rotate_kernel, heads, blocks),
        out_shape=[
            jax.ShapeDtypeStruct((rows, width), BF16),
            jax.ShapeDtypeStruct((rows, width), BF16),
            jax.ShapeDtypeStruct((blocks, heads, DH, DH), BF16),
            jax.ShapeDtypeStruct((entries, heads, 2 * DH, DH), BF16),
        ],
        in_specs=in_smem(1) + in_vmem(4),
        out_specs=in_vmem(4),
        compiler_params=grant(16),
        cost_estimate=cost(9),
        name="rotate",
    )(ints, house_rows, unit_t, query_rows, key_rows)


def attend_kernel(heads, blocks, places, pieces, *refs):
    ints_ref = refs[0]
    source_count = 1 + max(place[0] for pair in places for place in pair)
    sources = refs[1 : 1 + source_count]
    refs = refs[1 + source_count :]
    (query_ref, qrot_ref, krot_ref, value_ref, grad_ref, local_ref, listed_ref) = refs[:7]
    dq_ref, dcum_ref, dk_ref, dv_ref = refs[7:11]
    outs = refs[11 : 11 + max(len(pieces), 1)]
    refs = refs[11 + max(len(pieces), 1) :]
    far_keys, far_values, sems = refs[:3]
    entries = blocks * MAXL
    scaling = DH ** (-0.5)
    log_scale = scaling * math.log2(math.e)

    def start(e, src, kind, slot, where):
        pltpu.make_async_copy(src.at[where], slot.at[e], sems.at[kind, e]).start()

    for e in range(entries):
        owner, offset = listed(ints_ref, e, entries)
        row = pl.multiple_of(offset * BLK, BLK)
        if len(places) == 1:
            start(e, sources[0], 0, far_keys, (owner, pl.ds(row, BLK)))
            start(e, sources[1], 1, far_values, (owner, pl.ds(row, BLK)))
        else:
            distance = owner ^ ints_ref[0]
            for r, (key_place, value_place) in enumerate(places):

                @pl.when(distance == r)
                def _():
                    source, first = key_place
                    start(e, sources[source], 0, far_keys, pl.ds(first + row, BLK))
                    source, first = value_place
                    start(e, sources[source], 1, far_values, pl.ds(first + row, BLK))

    out_copies = []
    if pieces:
        payloads, out_sems = refs[3 : 3 + heads], refs[3 + heads]
        for payload in payloads:
            payload[...] = jnp.zeros_like(payload)
    for kind, slots in ((0, far_keys), (1, far_values)):
        for e in range(entries):
            pltpu.make_async_copy(slots.at[e], slots.at[e], sems.at[kind, e]).wait()

    later = iota((BLK, BLK), 0) > iota((BLK, BLK), 1)
    empty = jnp.zeros((BLK, DH), BF16)
    steps = range(blocks)
    for h in range(heads):
        lanes = head(h)
        spans = [slice(a * BLK, (a + 1) * BLK) for a in steps]
        both, keys, values = [], [], []
        for a in steps:
            qrot, grad = qrot_ref[spans[a], lanes], grad_ref[spans[a], lanes]
            upper = jnp.concatenate([qrot, empty], axis=1)
            lower = jnp.concatenate([empty, grad], axis=1)
            both.append(jnp.concatenate([upper, lower], axis=0))
            keys.append([krot_ref[spans[b], lanes] for b in range(a + 1)])
            values.append([value_ref[spans[b], lanes] for b in range(a + 1)])
            for l in range(MAXL):
                e = a * MAXL + l
                raw = far_keys[e, :, lanes]
                raw = jnp.concatenate([raw, raw], axis=1)
                keys[a].append(nn(raw, listed_ref[e, h]).astype(BF16))
                values[a].append(far_values[e, :, lanes])
        scores, dprobs, tops = [], [], []
        for a in steps:
            scores.append([])
            dprobs.append([])
            top = None
            for b in range(a + 1 + MAXL):
                pair = nt(jnp.concatenate([keys[a][b], values[a][b]], axis=1), both[a])
                part = pair[:, :BLK] * log_scale
                if b == a:
                    part = jnp.where(later, -jnp.inf, part)
                scores[a].append(part)
                dprobs[a].append(pair[:, BLK:])
                top = part if top is None else jnp.maximum(top, part)
            tops.append(jnp.max(top, axis=0, keepdims=True))
        weights, inverses, deltas = [], [], []
        for a in steps:
            weights.append([])
            total, inner = None, None
            for part, dprob in zip(scores[a], dprobs[a]):
                weight = jnp.exp2(part - tops[a])
                weights[a].append(weight)
                product = weight * dprob
                total = weight if total is None else total + weight
                inner = product if inner is None else inner + product
            inverses.append(1.0 / jnp.sum(total, axis=0, keepdims=True))
            deltas.append(jnp.sum(inner, axis=0, keepdims=True) * inverses[a])
        dscores, pairs = [], []
        for a in steps:
            dscores.append([])
            pairs.append([])
            for b in range(a + 1 + MAXL):
                probs = weights[a][b] * inverses[a]
                dscore = (probs * (dprobs[a][b] - deltas[a])).astype(BF16)
                dscores[a].append(dscore)
                wide = jnp.concatenate([dscore, probs.astype(BF16)], axis=1)
                pairs[a].append(nn(wide, both[a]))
        for b in steps:
            total = pairs[b][b]
            for a in range(b + 1, blocks):
                total = total + pairs[a][b]
            dk_ref[spans[b], lanes] = total[:, :DH] * scaling
            dv_ref[spans[b], lanes] = total[:, DH:]
        for e in range(entries):
            pair = pairs[e // MAXL][e // MAXL + 1 + e % MAXL]
            dkey, dvalue = (pair[:, :DH] * scaling).astype(BF16), pair[:, DH:].astype(BF16)
            if pieces:
                owner, offset = listed(ints_ref, e, entries)
                distance = owner ^ ints_ref[0]
                at = (distance & 1) * blocks + offset
                payloads[h][at, distance >> 1, :, :DH] += dkey
                payloads[h][at, distance >> 1, :, DH:] += dvalue
            else:
                outs[0][e, :, 2 * h * DH : (2 * h + 1) * DH] = dkey
                outs[0][e, :, (2 * h + 1) * DH : (2 * h + 2) * DH] = dvalue
        halves = []
        for a in steps:
            wide, tall = jnp.concatenate(dscores[a], axis=0), jnp.concatenate(keys[a], axis=0)
            halves.append(split(tn(wide, tall) * scaling))
        for a in steps:
            dq_top, dq_low = halves[a]
            dq_ref[spans[a], lanes] = nt(dq_top, local_ref[a, h]).astype(BF16)
            query = query_ref[spans[a], lanes]
            query = jnp.concatenate([query, query], axis=0)
            dcum_ref[a, h] = tn(query, jnp.concatenate([dq_top, dq_low], axis=0))
        for i, (first, size) in enumerate(pieces):
            where = outs[i].at[:, :, :, 2 * h * DH : (2 * h + 2) * DH]
            source = payloads[h].at[pl.ds(first, size)]
            copy = pltpu.make_async_copy(source, where, out_sems.at[i, h])
            copy.start()
            out_copies.append(copy)
    for copy in out_copies:
        copy.wait()


def run_attend(ints, sources, places, arrays, heads, blocks, pieces):
    rows, width = arrays[0].shape
    entries = blocks * MAXL
    any_spec = pl.BlockSpec(memory_space=pl.ANY)
    scratch = [
        pltpu.VMEM((entries, BLK, width), BF16),
        pltpu.VMEM((entries, BLK, width), BF16),
        pltpu.SemaphoreType.DMA((2, entries)),
    ]
    if pieces:
        chips = len(places) // 2
        out_parts = [
            jax.ShapeDtypeStruct((size, chips, BLK, 2 * width), BF16) for _, size in pieces
        ]
        part_specs = [any_spec] * len(pieces)
        scratch += [pltpu.VMEM((2 * blocks, chips, BLK, 2 * DH), BF16)] * heads
        scratch += [pltpu.SemaphoreType.DMA((len(pieces), heads))]
    else:
        out_parts = [jax.ShapeDtypeStruct((entries, BLK, 2 * width), BF16)]
        part_specs = in_vmem(1)
    return pl.pallas_call(
        functools.partial(attend_kernel, heads, blocks, places, pieces),
        out_shape=[
            jax.ShapeDtypeStruct((rows, width), BF16),
            jax.ShapeDtypeStruct((blocks, heads, DH, DH), F32),
            jax.ShapeDtypeStruct((rows, width), F32),
            jax.ShapeDtypeStruct((rows, width), F32),
        ]
        + out_parts,
        in_specs=in_smem(1) + [any_spec] * len(sources) + in_vmem(7),
        out_specs=in_vmem(4) + part_specs,
        scratch_shapes=scratch,
        compiler_params=grant(30),
        cost_estimate=cost(15),
        name="attend",
    )(ints, *sources, *arrays)


def merge_kernel(own_ref, got_ref, *refs):
    for i, ref in enumerate(refs[-3:]):
        total = own_ref[0, i + 1].astype(F32) + got_ref[0, i + 1].astype(F32)
        ref[0] = total.astype(BF16)


def run_merge(own, got, first, size, afters):
    _, chips, rows, width = own.shape
    cut = 2
    lanes = width // cut
    whole = pl.BlockSpec((1, chips, rows, lanes), lambda j, c: (first + j, 0, 0, c))
    return pl.pallas_call(
        merge_kernel,
        grid=(size, cut),
        out_shape=[jax.ShapeDtypeStruct((size, rows, width), BF16)] * (chips - 1),
        in_specs=[whole] * 2
        + [pl.BlockSpec((1, 16, 128), lambda j, c: (0, 0, 0))] * len(afters),
        out_specs=[pl.BlockSpec((1, rows, lanes), lambda j, c: (j, 0, c))] * (chips - 1),
        compiler_params=grant(12),
        cost_estimate=cost(2),
        name="merge",
    )(own, got, *afters)


def project_kernel(heads, parts, size, groups, layout, flip_ref, after_ref, *refs):
    outs = len(layout)
    chunks = [(m, i, at) for i, row in enumerate(layout) for at, m in enumerate(row)]
    tiles, sems = refs[-2:]
    per = tiles.shape[0] // len(chunks)
    tile = tiles.shape[2]
    if parts:
        part_refs, refs = refs[: size * parts], refs[size * parts :]
        dk_loc, dv_loc, dq_ref, key_ref, dcum_in, cum_ref = refs[:6]
        weight_refs, out_refs = refs[6:9], refs[9 : 9 + outs]
        dcum_out, dk_out, dv_out = refs[9 + outs : 12 + outs]
    else:
        dq_ref, dk_ref, dv_ref = refs[:3]
        weight_refs, out_refs = refs[3:6], refs[6 : 6 + outs]
    copies = []
    for t in range(len(chunks) * per):
        m = chunks[t // per][0]
        row = ((m + flip_ref[0] * (groups - 1 - 2 * m)) * per + t % per) * tile
        rows = pl.ds(pl.multiple_of(row, tile), tile)
        for w, ref in enumerate(weight_refs):
            copy = pltpu.make_async_copy(ref.at[rows], tiles.at[t, w], sems.at[t, w])
            copy.start()
            copies.append(copy)

    if parts:
        dk_rows, dv_rows = [], []
        for j in range(size):
            here = slice(j * BLK, (j + 1) * BLK)
            dk, dv = [], []
            for h in range(heads):
                both = slice(2 * h * DH, (2 * h + 2) * DH)
                total = part_refs[j * parts][0, :, both].astype(F32)
                for ref in part_refs[j * parts + 1 : (j + 1) * parts]:
                    total = total + ref[0, :, both].astype(F32)
                dv.append((dv_loc[here, head(h)] + total[:, DH:]).astype(BF16))
                dk_top, dk_low = split(dk_loc[here, head(h)] + total[:, :DH])
                dk.append(nt(dk_top, cum_ref[j, h]).astype(BF16))
                key = key_ref[here, head(h)]
                key = jnp.concatenate([key, key], axis=0)
                dcum = tn(key, jnp.concatenate([dk_top, dk_low], axis=0))
                dcum_out[j, h] = dcum_in[j, h] + dcum
            dk_rows.append(jnp.concatenate(dk, axis=1))
            dv_rows.append(jnp.concatenate(dv, axis=1))
        dk_all, dv_all = jnp.concatenate(dk_rows, axis=0), jnp.concatenate(dv_rows, axis=0)
        dk_out[...] = dk_all
        dv_out[...] = dv_all
        grads = (dq_ref[...], dk_all, dv_all)
    else:
        grads = (dq_ref[...], dk_ref[...], dv_ref[...])

    for t in range(len(chunks) * per):
        term = None
        for w, grad in enumerate(grads):
            copies[3 * t + w].wait()
            part = nt(tiles[t, w], grad)
            term = part if term is None else term + part
        spot = slice(t % per * tile, (t % per + 1) * tile)
        _, out, at = chunks[t // per]
        out_refs[out][at, :, spot] = term.T.astype(BF16)


def run_project(block, size, groups, layout, flip, after, parts, finished, arrays, weights):
    dk_loc, dv_loc, dq, key_rows, dcum, cum = arrays
    width = dq.shape[1]
    heads = width // DH
    model = weights[0].shape[0]
    chunk = model // groups
    tile = min(512, chunk)
    rows = size * BLK
    tile_count = sum(map(len, layout)) * chunk // tile

    def part_spec(index):
        return pl.BlockSpec((1, BLK, 2 * width), lambda t: (index, 0, 0))

    def whole(*shape):
        return pl.BlockSpec(shape, lambda t: (0,) * len(shape))

    rows_spec = pl.BlockSpec((rows, width), lambda t: (block // size, 0))
    head_spec = pl.BlockSpec((size, heads, DH, DH), lambda t: (block // size, 0, 0, 0))
    flat = [part for row in parts for part in row]
    out_specs = [whole(len(row), rows, chunk) for row in layout]
    out_shape = [jax.ShapeDtypeStruct((len(row), rows, chunk), BF16) for row in layout]
    if parts:
        in_specs = [part_spec(index) for _, index in flat] + [rows_spec] * 4 + [head_spec] * 2
        inputs = [part for part, _ in flat] + [dk_loc, dv_loc, dq, key_rows, dcum, cum]
        out_specs += [whole(size, heads, DH, DH)] + [whole(rows, width)] * 2
        out_shape += [jax.ShapeDtypeStruct((size, heads, DH, DH), F32)]
        out_shape += [jax.ShapeDtypeStruct((rows, width), BF16)] * 2
    else:
        in_specs = [rows_spec] + [whole(rows, width)] * 2
        inputs = [dq, *finished]
    return pl.pallas_call(
        functools.partial(
            project_kernel, heads, len(parts[0]) if parts else 0, size, groups, layout
        ),
        grid=(1,),
        in_specs=in_smem(1)
        + [whole(1, 16, 128)]
        + in_specs
        + [pl.BlockSpec(memory_space=pl.ANY)] * 3,
        out_specs=out_specs,
        scratch_shapes=[
            pltpu.VMEM((tile_count, 3, tile, width), BF16),
            pltpu.SemaphoreType.DMA((tile_count, 3)),
        ],
        out_shape=out_shape,
        compiler_params=grant(60),
        cost_estimate=cost(3 * sum(map(len, layout))),
        name="project",
    )(flip, after, *inputs, *weights)


def adjoint_kernel(heads, blocks, ints_ref, after_ref, *refs):
    dcums = [ref.at[j] for ref in refs[:-4] for j in range(ref.shape[0])]
    unit_ref, rows_ref, inv_ref, out_ref = refs[-4:]
    count, width = unit_ref.shape
    stacked = (blocks * count, count)
    eye = (iota((count, count), 0) == iota((count, count), 1)).astype(F32)
    base = ints_ref[0] * blocks
    level, col = iota(stacked, 0), iota(stacked, 1)
    row = level % count
    mine = base + level // count
    alive = row[:, :1] <= mine[:, :1]
    for h in range(heads):
        units, rows, inverse = unit_ref[:, head(h)], rows_ref[:, head(h)], inv_ref[h]
        inverse_t = nt_high(eye, inverse)
        moved = jnp.concatenate([nt_high(rows, dcum[h]) for dcum in dcums], axis=0)
        overlap = jnp.where(col <= mine, nt_high(moved, units), 0.0)
        gamma = nn_high(overlap, inverse)
        gamma = jnp.where((row < col) & (col <= mine), gamma, 0.0)
        beta = jnp.concatenate([eye - inverse_t] * blocks, axis=0)
        beta = jnp.where(col <= mine, beta, 0.0)
        x_all = jnp.where(alive, moved - 2.0 * nn_high(gamma, units), 0.0)
        turned = jnp.concatenate([units] * blocks, axis=0) - nn_high(beta, units)
        turned = jnp.where(alive, turned, 0.0)
        x_total, y_total = None, None
        for j, dcum in enumerate(dcums):
            here = slice(j * count, (j + 1) * count)
            y_part = nn_high(turned[here], dcum[h])
            x_total = x_all[here] if j == 0 else x_total + x_all[here]
            y_total = y_part if j == 0 else y_total + y_part
        out_ref[:, head(h)] = x_total
        out_ref[:, slice(width + h * DH, width + (h + 1) * DH)] = y_total


def run_adjoint(ints, after, dcums, unit, rows, inverse, heads, blocks):
    count, width = unit.shape
    return pl.pallas_call(
        functools.partial(adjoint_kernel, heads, blocks),
        out_shape=jax.ShapeDtypeStruct((count, 2 * width), F32),
        in_specs=in_smem(1) + [pl.BlockSpec(memory_space=pl.ANY)] + in_vmem(len(dcums) + 3),
        out_specs=pl.BlockSpec(memory_space=pltpu.VMEM),
        compiler_params=grant(60),
        cost_estimate=cost(2),
        name="adjoint",
    )(ints, after, *dcums, unit, rows, inverse)


def house_kernel(heads, blocks, base_ref, after_ref, got_ref, unit_ref, rows_ref, house_ref, out_ref):
    count, width = unit_ref.shape
    total = jnp.sum(got_ref[...], axis=0)
    for h in range(heads):
        x_part = total[:, head(h)]
        y_part = total[:, slice(width + h * DH, width + (h + 1) * DH)]
        along = nt_high(y_part, rows_ref[:, head(h)])
        spot = iota((blocks, count), 0) + base_ref[0] * blocks
        along = jnp.where(iota((blocks, count), 1) < spot, along, 0.0)
        turned = y_part - 2.0 * nn_high(along, unit_ref[:, head(h)])
        dunit = -2.0 * (x_part + turned)
        house = house_ref[:, head(h)]
        lengths = jnp.sqrt(jnp.sum(house * house, axis=1, keepdims=True) + 1e-06)
        unit = house / lengths
        inner = jnp.sum(unit * dunit, axis=1, keepdims=True)
        out_ref[:, head(h)] = (dunit - unit * inner) / lengths


def run_house(ints, after, got, unit, rows, house_dirs, heads, blocks):
    return pl.pallas_call(
        functools.partial(house_kernel, heads, blocks),
        out_shape=jax.ShapeDtypeStruct(house_dirs.shape, F32),
        in_specs=in_smem(1) + [pl.BlockSpec(memory_space=pl.ANY)] + in_vmem(4),
        out_specs=pl.BlockSpec(memory_space=pltpu.VMEM),
        compiler_params=grant(60),
        cost_estimate=cost(2),
        name="house_grad",
    )(ints, after, got, unit, rows, house_dirs)


def hop(value, distance, count):
    return lax.ppermute(value, "ctx", [(i, i ^ distance) for i in range(count)])


def slide(value, pairs):
    return lax.ppermute(value, "head", pairs)


INWARD = [(0, 1), (3, 2)]
MIDDLE = [(1, 2), (2, 1)]
OUTWARD = [(1, 0), (2, 3)]


def near_kernel(ends_ref, first_ref, near_ref, inward_ref, out_ref):
    mine = jnp.where(ends_ref[0] > 0, first_ref[0], near_ref[0]).astype(F32)
    out_ref[...] = mine + inward_ref[0].astype(F32)


def run_near(ends, first, near, inward):
    _, rows, width = first.shape
    return pl.pallas_call(
        near_kernel,
        grid=(1,),
        out_shape=jax.ShapeDtypeStruct((rows, width), F32),
        in_specs=in_smem(1) + [pl.BlockSpec((1, rows, width), lambda t: (0, 0, 0))] * 3,
        out_specs=pl.BlockSpec((rows, width), lambda t: (0, 0)),
        compiler_params=grant(60),
        cost_estimate=cost(16),
        name="near_sum",
    )(ends, first, near, inward)


def share_kernel(*refs):
    total_ref, far_ref, outward_ref, out_ref = refs[-4:]
    far = far_ref[0].astype(F32) + outward_ref[0].astype(F32)
    out_ref[...] = (total_ref[...] + far).astype(BF16)


def run_share(share, band, bands, total, far, outward):
    rows, width = total.shape
    tile = min(512, width)
    part = pl.BlockSpec((1, rows, tile), lambda t: (0, 0, t))
    given = [] if share is None else [share]
    return pl.pallas_call(
        share_kernel,
        grid=(width // tile,),
        out_shape=jax.ShapeDtypeStruct((bands * rows, width), BF16),
        in_specs=[pl.BlockSpec(memory_space=pl.ANY)] * len(given)
        + [pl.BlockSpec((rows, tile), lambda t: (0, t)), part, part],
        out_specs=pl.BlockSpec((rows, tile), lambda t: (band, t)),
        input_output_aliases={0: 0} if given else {},
        compiler_params=grant(60),
        cost_estimate=cost(2),
        name="share",
    )(*given, total, far, outward)


def line_ends():
    place = lax.axis_index("head")
    return ((place == 0) | (place == 3)).astype(jnp.int32).reshape(1)


def line_scatter(share, band, bands, first, rest):
    inward = slide(rest, INWARD)
    swapped = slide(rest[1:] + inward[1:], MIDDLE)
    outward = slide(first + swapped[1:], OUTWARD)
    total = run_near(line_ends(), first, rest, inward)
    return run_share(share, band, bands, total, swapped, outward), outward


def line_scatter_apart(share, band, bands, first, near, far, last):
    in_last, in_far, in_near = slide(last, INWARD), slide(far, INWARD), slide(near, INWARD)
    swap_last, swap_far = slide(last + in_last, MIDDLE), slide(far + in_far, MIDDLE)
    outward = slide(first + swap_last, OUTWARD)
    total = run_near(line_ends(), first, near, in_near)
    return run_share(share, band, bands, total, swap_far, outward)


def shards(
    query_rows, key_rows, value_rows, grad_out, house_dirs, owners, offsets, w_query, w_key, w_value
):
    tok_rows, width = query_rows.shape
    heads, blocks = width // DH, tok_rows // BLK
    ctx_count, groups = lax.axis_size("ctx"), lax.axis_size("head")
    my_index = lax.axis_index("ctx").astype(jnp.int32)
    ints = jnp.concatenate([my_index.reshape(1), owners.reshape(-1), offsets.reshape(-1)])
    by_hand = ctx_count == 8 and groups == 4 and blocks == 4
    core, across, along = 1, 2, 4

    if by_hand:
        other = hop(house_dirs, core, 8)
        upper = (my_index & core) != 0
        low, high = jnp.where(upper, other, house_dirs), jnp.where(upper, house_dirs, other)
        house_pair = jnp.concatenate([low, high], axis=0)
        house_parts = [house_pair] + [hop(house_pair, t, 8) for t in (2, 4, 6)]
        value_x, key_y = hop(value_rows, across, 8), hop(key_rows, along, 8)
        key_late, value_late, *_ = lax.optimization_barrier((key_rows, value_rows, *house_parts))
        key_x, value_y = hop(key_late, across, 8), hop(value_late, along, 8)
        key_d, value_d = hop(key_y, across, 8), hop(value_x, along, 8)
    else:
        house_parts = [lax.all_gather(house_dirs, "ctx", axis=0, tiled=True)]

    unit, rows, inverse, unit_t = run_chain(ints, house_parts, heads)
    qrot, krot, local, listed_cum = run_rotate(
        ints, rows, unit_t, query_rows, key_rows, heads, blocks
    )
    if by_hand:
        late = lax.optimization_barrier((key_x, value_y, key_d, value_d, qrot))
        siblings = (key_late, value_late, late[0], value_x, key_y, late[1], late[2], late[3])
        siblings = [hop(part, core, 8) for part in siblings]
        own = (key_rows, value_rows, key_x, value_x, key_y, value_y, key_d, value_d)
        sources, places = [], []
        for t in range(4):
            for pair in (own[2 * t : 2 * t + 2], siblings[2 * t : 2 * t + 2]):
                places.append(((len(sources), 0), (len(sources) + 1, 0)))
                sources += pair
    else:
        sources = [lax.all_gather(key_rows, "ctx"), lax.all_gather(value_rows, "ctx")]
        places = [((0, 0), (1, 0))]

    rounds = ((0, 1), (1, blocks - 1), (blocks, 1), (blocks + 1, blocks - 1))
    dq, dcum, dk_loc, dv_loc, *outs = run_attend(
        ints,
        sources,
        places,
        (query_rows, qrot, krot, value_rows, grad_out, local, listed_cum),
        heads,
        blocks,
        rounds if by_hand else (),
    )
    weights = (w_query, w_key, w_value)
    flip = jnp.where(by_hand & (lax.axis_index("head") >= 2), 1, 0).astype(jnp.int32).reshape(1)

    arrays = (dk_loc, dv_loc, dq, key_rows, dcum, local)

    def project(block, layout, after, parts):
        size = len(parts)
        return run_project(block, size, groups, layout, flip, after, parts, (), arrays, weights)

    if by_hand:
        got_0 = hop(outs[2], core, 8)
        got_1 = hop(lax.optimization_barrier((outs[3], got_0))[0], core, 8)
        sent_0 = run_merge(outs[0], got_0, 0, 1, [])
        sent_1 = run_merge(outs[1], got_1, 0, 1, [sent_0[0]])
        sent_2 = run_merge(outs[1], got_1, 1, 2, [sent_1[0]])

        def give_back(own, got, first, sent):
            back = [hop(part, t, 8) for part, t in zip(sent, (across, along, across + along))]
            near = [part.reshape(-1, BLK, 2 * width) for part in (own, got)]
            parts = []
            for j in range(sent[0].shape[0]):
                mine = [(part, 4 * (first + j)) for part in near]
                parts.append(mine + [(part, j) for part in back])
            return parts, back

        parts_0, back_0 = give_back(outs[0], got_0, 0, sent_0)
        *sent_1, _ = lax.optimization_barrier((*sent_1, back_0))
        parts_1, back_1 = give_back(outs[1], got_1, 0, sent_1)
        *sent_2, _ = lax.optimization_barrier((*sent_2, back_1))
        parts_2, _ = give_back(outs[1], got_1, 1, sent_2)
        joint, apart = ((0,), (1, 2, 3)), ((0,), (1,), (2,), (3,))
        *terms_0, dcum_0, _, _ = project(0, joint, sent_1[0], parts_0)
        *terms_1, dcum_1, _, _ = project(1, joint, sent_2[0], parts_1)
        *terms_2, dcum_2, _, _ = project(2, apart, terms_1[0], parts_2)
        share, late = line_scatter(None, 0, 4, *terms_0)
        share, later = line_scatter(share, 1, 4, *terms_1)
        share = line_scatter_apart(share, 1, 2, *terms_2)
        dcums = [dcum_0, dcum_1, dcum_2]
    else:
        spots = (owners * blocks + offsets).reshape(-1)
        empty = jnp.zeros((ctx_count * blocks, BLK, 2 * width), BF16)
        filled = empty.at[spots].add(outs[0])
        back = lax.psum_scatter(filled, "ctx", scatter_dimension=0, tiled=True)
        late, later, dcums = key_rows, key_rows, []
        share = jnp.zeros((tok_rows, w_query.shape[0] // groups), BF16)
        for j in range(blocks):
            term, dcum_out, _, _ = project(
                j, (tuple(range(groups)),), key_rows[None], [[(back, j)]]
            )
            dcums.append(dcum_out)
            done = lax.psum_scatter(term, "head", scatter_dimension=0, tiled=False)
            share = lax.dynamic_update_slice(share, done, (j * BLK, 0))

    sums = run_adjoint(ints, late, dcums, unit, rows, inverse, heads, blocks)
    sums = sums.reshape(ctx_count, blocks, 2 * width)
    got = lax.all_to_all(sums, "ctx", split_axis=0, concat_axis=0, tiled=True)
    house_grad = run_house(ints, later, got, unit, rows, house_dirs, heads, blocks)
    return (share, house_grad)


def solution(mesh):
    placed = (
        P("ctx", "head"),
        P("ctx", "head"),
        P("ctx", "head"),
        P("ctx", "head"),
        P("ctx", "head"),
        P("ctx", None),
        P("ctx", None),
        P(None, "head"),
        P(None, "head"),
        P(None, "head"),
    )
    return jax.shard_map(
        shards,
        mesh=mesh,
        in_specs=placed,
        out_specs=(P("ctx", "head"), P("ctx", "head")),
        check_vma=False,
    )
```

```python
import functools
import math

import jax
import jax.numpy as jnp
from jax import lax
from jax.experimental import pallas as pl
from jax.experimental.pallas import tpu as pltpu
from jax.sharding import PartitionSpec as P

DH = 128
BLK = 128
MAXL = 2
HIGH = lax.Precision.HIGHEST
F32 = jnp.float32
BF16 = jnp.bfloat16


def nn(a, b):
    return lax.dot_general(a, b, (((1,), (0,)), ((), ())), preferred_element_type=F32)


def nt(a, b):
    return lax.dot_general(a, b, (((1,), (1,)), ((), ())), preferred_element_type=F32)


def tn(a, b):
    return lax.dot_general(a, b, (((0,), (0,)), ((), ())), preferred_element_type=F32)


def nn_high(a, b):
    return lax.dot_general(
        a, b, (((1,), (0,)), ((), ())), precision=HIGH, preferred_element_type=F32
    )


def nt_high(a, b):
    return lax.dot_general(
        a, b, (((1,), (1,)), ((), ())), precision=HIGH, preferred_element_type=F32
    )


def split(value):
    top = value.astype(BF16)
    return top, (value - top.astype(F32)).astype(BF16)


def iota(shape, dim):
    return lax.broadcasted_iota(jnp.int32, shape, dim)


def head(h):
    return slice(h * DH, (h + 1) * DH)


def listed(ints_ref, entry, entries):
    return ints_ref[1 + entry], ints_ref[1 + entries + entry]


def grant(mebibytes):
    return pltpu.CompilerParams(vmem_limit_bytes=mebibytes * 1024 * 1024)


def cost(microseconds):
    return pl.CostEstimate(
        flops=int(microseconds * 1.15e9), bytes_accessed=1 << 20, transcendentals=0
    )


def in_smem(count):
    return [pl.BlockSpec(memory_space=pltpu.SMEM)] * count


def in_vmem(count):
    return [pl.BlockSpec(memory_space=pltpu.VMEM)] * count


def chain_kernel(heads, parts, ints_ref, *refs):
    house_refs = refs[:parts]
    unit_ref, rows_ref, inv_ref, wide_ref, tall_ref, unit_h, house_all = refs[parts:]
    count = unit_ref.shape[0]
    span = count // parts
    for t, ref in enumerate(house_refs):
        place = (ints_ref[0] // (8 // parts)) ^ t if parts > 1 else 0
        house_all[pl.ds(pl.multiple_of(place * span, span), span), :] = ref[...]
    eye = (iota((count, count), 0) == iota((count, count), 1)).astype(F32)
    for h in range(heads):
        house = house_all[:, head(h)]
        lengths = jnp.sqrt(jnp.sum(house * house, axis=1, keepdims=True) + 1e-06)
        unit_ref[:, head(h)] = house / lengths
        unit_h[h] = house / lengths
        inv_ref[h] = eye

    def eliminate(step, carry):
        below = iota((count, 1), 0) > step
        for h in range(heads):
            pivot = unit_h[h, pl.ds(step, 1), :]
            overlap = jnp.sum(unit_h[h] * pivot, axis=1, keepdims=True)
            factor = jnp.where(below, 2.0 * overlap, 0.0)
            inv_ref[h] = inv_ref[h] - factor * inv_ref[h, pl.ds(step, 1), :]
        return carry

    lax.fori_loop(0, count, eliminate, 0)
    eye_wide = (iota((DH, DH), 0) == iota((DH, DH), 1)).astype(F32)
    for h in range(heads):
        units = unit_ref[:, head(h)]
        rows = nn_high(inv_ref[h], units)
        rows_ref[:, head(h)] = rows
        unit_hi, unit_lo = split(nt_high(eye_wide, units))
        rows_hi, rows_lo = split(rows)
        wide_ref[h] = jnp.concatenate([unit_hi, unit_hi, unit_lo], axis=1)
        tall_ref[h] = jnp.concatenate([rows_hi, rows_lo, rows_hi], axis=0)


def run_chain(ints, house_parts, heads):
    span, width = house_parts[0].shape
    parts = len(house_parts)
    count = span * parts
    return pl.pallas_call(
        functools.partial(chain_kernel, heads, parts),
        out_shape=[
            jax.ShapeDtypeStruct((count, width), F32),
            jax.ShapeDtypeStruct((count, width), F32),
            jax.ShapeDtypeStruct((heads, count, count), F32),
            jax.ShapeDtypeStruct((heads, DH, 3 * count), BF16),
            jax.ShapeDtypeStruct((heads, 3 * count, DH), BF16),
        ],
        in_specs=in_smem(1) + in_vmem(parts),
        out_specs=in_vmem(5),
        scratch_shapes=[pltpu.VMEM((heads, count, DH), F32), pltpu.VMEM((count, width), F32)],
        compiler_params=grant(12),
        cost_estimate=cost(6),
        name="house_chain",
    )(ints, *house_parts)


def rotate_kernel(
    heads,
    blocks,
    ints_ref,
    wide_ref,
    tall_ref,
    query_ref,
    key_ref,
    qrot_ref,
    krot_ref,
    local_ref,
    listed_ref,
):
    count = wide_ref.shape[2] // 3
    entries = blocks * MAXL
    column = iota((DH, 3 * count), 1) % count
    eye = (iota((DH, DH), 0) == iota((DH, DH), 1)).astype(F32)

    def cumulative(h, block):
        kept = jnp.where(column <= block, wide_ref[h].astype(F32), 0.0).astype(BF16)
        return split(eye - 2.0 * nn(kept, tall_ref[h]))

    base = ints_ref[0] * blocks

    def local_block(b, carry):
        here = pl.ds(pl.multiple_of(b * BLK, BLK), BLK)
        for h in range(heads):
            hi, lo = cumulative(h, base + b)
            local_ref[b, h] = hi
            query, key = query_ref[here, head(h)], key_ref[here, head(h)]
            qrot_ref[here, head(h)] = (nn(query, hi) + nn(query, lo)).astype(BF16)
            krot_ref[here, head(h)] = (nn(key, hi) + nn(key, lo)).astype(BF16)
        return carry

    lax.fori_loop(0, blocks, local_block, 0)

    def listed_block(e, carry):
        owner, offset = listed(ints_ref, e, entries)
        for h in range(heads):
            hi, lo = cumulative(h, owner * blocks + offset)
            listed_ref[e, h, :DH] = hi
            listed_ref[e, h, DH:] = lo
        return carry

    lax.fori_loop(0, entries, listed_block, 0)


def run_rotate(ints, wide, tall, query_rows, key_rows, heads, blocks):
    rows, width = query_rows.shape
    entries = blocks * MAXL
    return pl.pallas_call(
        functools.partial(rotate_kernel, heads, blocks),
        out_shape=[
            jax.ShapeDtypeStruct((rows, width), BF16),
            jax.ShapeDtypeStruct((rows, width), BF16),
            jax.ShapeDtypeStruct((blocks, heads, DH, DH), BF16),
            jax.ShapeDtypeStruct((entries, heads, 2 * DH, DH), BF16),
        ],
        in_specs=in_smem(1) + in_vmem(4),
        out_specs=in_vmem(4),
        compiler_params=grant(16),
        cost_estimate=cost(9),
        name="rotate",
    )(ints, wide, tall, query_rows, key_rows)


def attend_kernel(heads, blocks, places, pieces, *refs):
    ints_ref = refs[0]
    source_count = 1 + max(place[0] for pair in places for place in pair)
    sources = refs[1 : 1 + source_count]
    refs = refs[1 + source_count :]
    (query_ref, qrot_ref, krot_ref, value_ref, grad_ref, local_ref, listed_ref) = refs[:7]
    dq_ref, dcum_ref, dk_ref, dv_ref = refs[7:11]
    outs = refs[11 : 11 + max(len(pieces), 1)]
    refs = refs[11 + max(len(pieces), 1) :]
    far_keys, far_values, sems = refs[:3]
    entries = blocks * MAXL
    scaling = DH ** (-0.5)
    log_scale = scaling * math.log2(math.e)

    def start(e, src, kind, slot, where):
        pltpu.make_async_copy(src.at[where], slot.at[e], sems.at[kind, e]).start()

    for e in range(entries):
        owner, offset = listed(ints_ref, e, entries)
        row = pl.multiple_of(offset * BLK, BLK)
        if len(places) == 1:
            start(e, sources[0], 0, far_keys, (owner, pl.ds(row, BLK)))
            start(e, sources[1], 1, far_values, (owner, pl.ds(row, BLK)))
        else:
            distance = owner ^ ints_ref[0]
            for r, (key_place, value_place) in enumerate(places):

                @pl.when(distance == r)
                def _():
                    source, first = key_place
                    start(e, sources[source], 0, far_keys, pl.ds(first + row, BLK))
                    source, first = value_place
                    start(e, sources[source], 1, far_values, pl.ds(first + row, BLK))

    out_copies = []
    if pieces:
        payloads, out_sems = refs[3 : 3 + heads], refs[3 + heads]
        for payload in payloads:
            payload[...] = jnp.zeros_like(payload)
    for kind, slots in ((0, far_keys), (1, far_values)):
        for e in range(entries):
            pltpu.make_async_copy(slots.at[e], slots.at[e], sems.at[kind, e]).wait()

    later = iota((BLK, BLK), 0) > iota((BLK, BLK), 1)
    empty = jnp.zeros((BLK, DH), BF16)
    steps = range(blocks)
    for h in range(heads):
        lanes = head(h)
        spans = [slice(a * BLK, (a + 1) * BLK) for a in steps]
        both, keys, values = [], [], []
        for a in steps:
            qrot, grad = qrot_ref[spans[a], lanes], grad_ref[spans[a], lanes]
            upper = jnp.concatenate([qrot, empty], axis=1)
            lower = jnp.concatenate([empty, grad], axis=1)
            both.append(jnp.concatenate([upper, lower], axis=0))
            keys.append([krot_ref[spans[b], lanes] for b in range(a + 1)])
            values.append([value_ref[spans[b], lanes] for b in range(a + 1)])
            for l in range(MAXL):
                e = a * MAXL + l
                raw = far_keys[e, :, lanes]
                raw = jnp.concatenate([raw, raw], axis=1)
                keys[a].append(nn(raw, listed_ref[e, h]).astype(BF16))
                values[a].append(far_values[e, :, lanes])
        scores, dprobs, tops = [], [], []
        for a in steps:
            scores.append([])
            dprobs.append([])
            top = None
            for b in range(a + 1 + MAXL):
                pair = nt(jnp.concatenate([keys[a][b], values[a][b]], axis=1), both[a])
                part = pair[:, :BLK] * log_scale
                if b == a:
                    part = jnp.where(later, -jnp.inf, part)
                scores[a].append(part)
                dprobs[a].append(pair[:, BLK:])
                top = part if top is None else jnp.maximum(top, part)
            tops.append(jnp.max(top, axis=0, keepdims=True))
        weights, inverses, deltas = [], [], []
        for a in steps:
            weights.append([])
            total, inner = None, None
            for part, dprob in zip(scores[a], dprobs[a]):
                weight = jnp.exp2(part - tops[a])
                weights[a].append(weight)
                product = weight * dprob
                total = weight if total is None else total + weight
                inner = product if inner is None else inner + product
            inverses.append(1.0 / jnp.sum(total, axis=0, keepdims=True))
            deltas.append(jnp.sum(inner, axis=0, keepdims=True) * inverses[a])
        dscores, pairs = [], []
        for a in steps:
            dscores.append([])
            pairs.append([])
            for b in range(a + 1 + MAXL):
                probs = weights[a][b] * inverses[a]
                dscore = (probs * (dprobs[a][b] - deltas[a])).astype(BF16)
                dscores[a].append(dscore)
                wide = jnp.concatenate([dscore, probs.astype(BF16)], axis=1)
                pairs[a].append(nn(wide, both[a]))
        for b in steps:
            total = pairs[b][b]
            for a in range(b + 1, blocks):
                total = total + pairs[a][b]
            dk_ref[spans[b], lanes] = total[:, :DH] * scaling
            dv_ref[spans[b], lanes] = total[:, DH:]
        for e in range(entries):
            pair = pairs[e // MAXL][e // MAXL + 1 + e % MAXL]
            dkey, dvalue = (pair[:, :DH] * scaling).astype(BF16), pair[:, DH:].astype(BF16)
            if pieces:
                owner, offset = listed(ints_ref, e, entries)
                distance = owner ^ ints_ref[0]
                at = (distance & 1) * blocks + offset
                payloads[h][at, distance >> 1, :, :DH] += dkey
                payloads[h][at, distance >> 1, :, DH:] += dvalue
            else:
                outs[0][e, :, 2 * h * DH : (2 * h + 1) * DH] = dkey
                outs[0][e, :, (2 * h + 1) * DH : (2 * h + 2) * DH] = dvalue
        halves = []
        for a in steps:
            wide, tall = jnp.concatenate(dscores[a], axis=0), jnp.concatenate(keys[a], axis=0)
            halves.append(split(tn(wide, tall) * scaling))
        for a in steps:
            dq_top, dq_low = halves[a]
            dq_ref[spans[a], lanes] = nt(dq_top, local_ref[a, h]).astype(BF16)
            query = query_ref[spans[a], lanes]
            query = jnp.concatenate([query, query], axis=0)
            dcum_ref[a, h] = tn(query, jnp.concatenate([dq_top, dq_low], axis=0))
        for i, (first, size) in enumerate(pieces):
            where = outs[i].at[:, :, :, 2 * h * DH : (2 * h + 2) * DH]
            source = payloads[h].at[pl.ds(first, size)]
            copy = pltpu.make_async_copy(source, where, out_sems.at[i, h])
            copy.start()
            out_copies.append(copy)
    for copy in out_copies:
        copy.wait()


def run_attend(ints, sources, places, arrays, heads, blocks, pieces):
    rows, width = arrays[0].shape
    entries = blocks * MAXL
    any_spec = pl.BlockSpec(memory_space=pl.ANY)
    scratch = [
        pltpu.VMEM((entries, BLK, width), BF16),
        pltpu.VMEM((entries, BLK, width), BF16),
        pltpu.SemaphoreType.DMA((2, entries)),
    ]
    if pieces:
        chips = len(places) // 2
        out_parts = [
            jax.ShapeDtypeStruct((size, chips, BLK, 2 * width), BF16) for _, size in pieces
        ]
        part_specs = [any_spec] * len(pieces)
        scratch += [pltpu.VMEM((2 * blocks, chips, BLK, 2 * DH), BF16)] * heads
        scratch += [pltpu.SemaphoreType.DMA((len(pieces), heads))]
    else:
        out_parts = [jax.ShapeDtypeStruct((entries, BLK, 2 * width), BF16)]
        part_specs = in_vmem(1)
    return pl.pallas_call(
        functools.partial(attend_kernel, heads, blocks, places, pieces),
        out_shape=[
            jax.ShapeDtypeStruct((rows, width), BF16),
            jax.ShapeDtypeStruct((blocks, heads, DH, DH), F32),
            jax.ShapeDtypeStruct((rows, width), F32),
            jax.ShapeDtypeStruct((rows, width), F32),
        ]
        + out_parts,
        in_specs=in_smem(1) + [any_spec] * len(sources) + in_vmem(7),
        out_specs=in_vmem(4) + part_specs,
        scratch_shapes=scratch,
        compiler_params=grant(30),
        cost_estimate=cost(15),
        name="attend",
    )(ints, *sources, *arrays)


def merge_kernel(own_ref, got_ref, *refs):
    for i, ref in enumerate(refs[-3:]):
        total = own_ref[0, i + 1].astype(F32) + got_ref[0, i + 1].astype(F32)
        ref[0] = total.astype(BF16)


def run_merge(own, got, first, size, afters):
    _, chips, rows, width = own.shape
    cut = 2
    lanes = width // cut
    whole = pl.BlockSpec((1, chips, rows, lanes), lambda j, c: (first + j, 0, 0, c))
    return pl.pallas_call(
        merge_kernel,
        grid=(size, cut),
        out_shape=[jax.ShapeDtypeStruct((size, rows, width), BF16)] * (chips - 1),
        in_specs=[whole] * 2
        + [pl.BlockSpec((1, 16, 128), lambda j, c: (0, 0, 0))] * len(afters),
        out_specs=[pl.BlockSpec((1, rows, lanes), lambda j, c: (j, 0, c))] * (chips - 1),
        compiler_params=grant(12),
        cost_estimate=cost(2),
        name="merge",
    )(own, got, *afters)


def project_kernel(heads, parts, size, groups, before, layout, afters, flip_ref, *refs):
    refs = refs[afters:]
    outs = len(layout)
    chunks = [(m, i, at) for i, row in enumerate(layout) for at, m in enumerate(row)]
    tiles, sems = refs[-2:]
    per = tiles.shape[0] // len(chunks)
    tile = tiles.shape[2]
    part_refs, refs = refs[: size * parts], refs[size * parts :]
    before_refs, refs = refs[:before], refs[before:]
    dk_loc, dv_loc, dq_ref, key_ref, dcum_in, cum_ref = refs[:6]
    weight_refs, out_refs = refs[6:9], refs[9 : 9 + outs]
    dcum_out, dk_out, dv_out = refs[9 + outs : 12 + outs]
    copies = []
    for t in range(len(chunks) * per):
        m = chunks[t // per][0]
        row = ((m + flip_ref[0] * (groups - 1 - 2 * m)) * per + t % per) * tile
        rows = pl.ds(pl.multiple_of(row, tile), tile)
        for w, ref in enumerate(weight_refs):
            copy = pltpu.make_async_copy(ref.at[rows], tiles.at[t, w], sems.at[t, w])
            copy.start()
            copies.append(copy)

    earlier = ()
    dk_rows, dv_rows = [], []
    for j in range(size):
        here = slice(j * BLK, (j + 1) * BLK)
        dk, dv = [], []
        for h in range(heads):
            both = slice(2 * h * DH, (2 * h + 2) * DH)
            total = part_refs[j * parts][0, :, both].astype(F32)
            for ref in part_refs[j * parts + 1 : (j + 1) * parts]:
                total = total + ref[0, :, both].astype(F32)
            dv.append((dv_loc[here, head(h)] + total[:, DH:]).astype(BF16))
            dk_top, dk_low = split(dk_loc[here, head(h)] + total[:, :DH])
            dk.append(nt(dk_top, cum_ref[j, h]).astype(BF16))
            key = key_ref[here, head(h)]
            key = jnp.concatenate([key, key], axis=0)
            dcum = tn(key, jnp.concatenate([dk_top, dk_low], axis=0))
            dcum_out[j, h] = dcum_in[j, h] + dcum
        dk_rows.append(jnp.concatenate(dk, axis=1))
        dv_rows.append(jnp.concatenate(dv, axis=1))
    dk_all, dv_all = jnp.concatenate(dk_rows, axis=0), jnp.concatenate(dv_rows, axis=0)
    dk_out[...] = dk_all
    dv_out[...] = dv_all
    grads = (dq_ref[...], dk_all, dv_all)
    if before:
        earlier = [
            jnp.concatenate([old[...], new], axis=0) for old, new in zip(before_refs, grads)
        ]

    for t in range(len(chunks) * per):
        term = None
        m, out, at = chunks[t // per]
        for w, grad in enumerate(earlier if before and m == 0 else grads):
            copies[3 * t + w].wait()
            part = nt(tiles[t, w], grad)
            term = part if term is None else term + part
        spot = slice(t % per * tile, (t % per + 1) * tile)
        out_refs[out][at, :, spot] = term.T.astype(BF16)


def run_project(block, groups, layout, flip, afters, parts, before, arrays, weights):
    dk_loc, dv_loc, dq, key_rows, dcum, cum = arrays
    size, width = len(parts), dq.shape[1]
    heads = width // DH
    model = weights[0].shape[0]
    chunk = model // groups
    tile = min(512, chunk)
    rows = size * BLK
    tile_count = sum(map(len, layout)) * chunk // tile

    def part_spec(index):
        return pl.BlockSpec((1, BLK, 2 * width), lambda t: (index, 0, 0))

    def whole(*shape):
        return pl.BlockSpec(shape, lambda t: (0,) * len(shape))

    rows_spec = pl.BlockSpec((rows, width), lambda t: (block // size, 0))
    head_spec = pl.BlockSpec((size, heads, DH, DH), lambda t: (block // size, 0, 0, 0))
    flat = [part for row in parts for part in row]
    heights = [2 * rows if before and row == (0,) else rows for row in layout]
    shapes = [(len(row), height, chunk) for row, height in zip(layout, heights)]
    return pl.pallas_call(
        functools.partial(
            project_kernel,
            heads,
            len(parts[0]),
            size,
            groups,
            len(before),
            layout,
            len(afters),
        ),
        grid=(1,),
        in_specs=in_smem(1)
        + [whole(1, 16, 128)] * len(afters)
        + [part_spec(index) for _, index in flat]
        + [whole(rows, width)] * len(before)
        + [rows_spec] * 4
        + [head_spec] * 2
        + [pl.BlockSpec(memory_space=pl.ANY)] * 3,
        out_specs=[whole(*shape) for shape in shapes]
        + [whole(size, heads, DH, DH)]
        + [whole(rows, width)] * 2,
        scratch_shapes=[
            pltpu.VMEM((tile_count, 3, tile, width), BF16),
            pltpu.SemaphoreType.DMA((tile_count, 3)),
        ],
        out_shape=[jax.ShapeDtypeStruct(shape, BF16) for shape in shapes]
        + [jax.ShapeDtypeStruct((size, heads, DH, DH), F32)]
        + [jax.ShapeDtypeStruct((rows, width), BF16)] * 2,
        compiler_params=grant(60),
        cost_estimate=cost(3 * sum(map(len, layout))),
        name="project",
    )(
        flip,
        *afters,
        *[part for part, _ in flat],
        *before,
        dk_loc,
        dv_loc,
        dq,
        key_rows,
        dcum,
        cum,
        *weights,
    )


def adjoint_kernel(heads, blocks, afters, ints_ref, *refs):
    refs = refs[afters:]
    dcums = [ref.at[j] for ref in refs[:-4] for j in range(ref.shape[0])]
    unit_ref, rows_ref, inv_ref, out_ref = refs[-4:]
    count, width = unit_ref.shape
    stacked = (blocks * count, count)
    eye = (iota((count, count), 0) == iota((count, count), 1)).astype(F32)
    base = ints_ref[0] * blocks
    level, col = iota(stacked, 0), iota(stacked, 1)
    row = level % count
    mine = base + level // count
    alive = row[:, :1] <= mine[:, :1]
    for h in range(heads):
        units, rows, inverse = unit_ref[:, head(h)], rows_ref[:, head(h)], inv_ref[h]
        inverse_t = nt_high(eye, inverse)
        moved = jnp.concatenate([nt_high(rows, dcum[h]) for dcum in dcums], axis=0)
        overlap = jnp.where(col <= mine, nt_high(moved, units), 0.0)
        gamma = nn_high(overlap, inverse)
        gamma = jnp.where((row < col) & (col <= mine), gamma, 0.0)
        beta = jnp.concatenate([eye - inverse_t] * blocks, axis=0)
        beta = jnp.where(col <= mine, beta, 0.0)
        x_all = jnp.where(alive, moved - 2.0 * nn_high(gamma, units), 0.0)
        turned = jnp.concatenate([units] * blocks, axis=0) - nn_high(beta, units)
        turned = jnp.where(alive, turned, 0.0)
        x_total, y_total = None, None
        for j, dcum in enumerate(dcums):
            here = slice(j * count, (j + 1) * count)
            y_part = nn_high(turned[here], dcum[h])
            x_total = x_all[here] if j == 0 else x_total + x_all[here]
            y_total = y_part if j == 0 else y_total + y_part
        out_ref[:, head(h)] = x_total
        out_ref[:, slice(width + h * DH, width + (h + 1) * DH)] = y_total


def run_adjoint(ints, afters, dcums, unit, rows, inverse, heads, blocks):
    count, width = unit.shape
    return pl.pallas_call(
        functools.partial(adjoint_kernel, heads, blocks, len(afters)),
        out_shape=jax.ShapeDtypeStruct((count, 2 * width), F32),
        in_specs=in_smem(1)
        + [pl.BlockSpec(memory_space=pl.ANY)] * len(afters)
        + in_vmem(len(dcums) + 3),
        out_specs=pl.BlockSpec(memory_space=pltpu.VMEM),
        compiler_params=grant(60),
        cost_estimate=cost(2),
        name="adjoint",
    )(ints, *afters, *dcums, unit, rows, inverse)


def house_kernel(heads, blocks, base_ref, after_ref, got_ref, unit_ref, rows_ref, house_ref, out_ref):
    count, width = unit_ref.shape
    total = jnp.sum(got_ref[...], axis=0)
    for h in range(heads):
        x_part = total[:, head(h)]
        y_part = total[:, slice(width + h * DH, width + (h + 1) * DH)]
        along = nt_high(y_part, rows_ref[:, head(h)])
        spot = iota((blocks, count), 0) + base_ref[0] * blocks
        along = jnp.where(iota((blocks, count), 1) < spot, along, 0.0)
        turned = y_part - 2.0 * nn_high(along, unit_ref[:, head(h)])
        dunit = -2.0 * (x_part + turned)
        house = house_ref[:, head(h)]
        lengths = jnp.sqrt(jnp.sum(house * house, axis=1, keepdims=True) + 1e-06)
        unit = house / lengths
        inner = jnp.sum(unit * dunit, axis=1, keepdims=True)
        out_ref[:, head(h)] = (dunit - unit * inner) / lengths


def run_house(ints, after, got, unit, rows, house_dirs, heads, blocks):
    return pl.pallas_call(
        functools.partial(house_kernel, heads, blocks),
        out_shape=jax.ShapeDtypeStruct(house_dirs.shape, F32),
        in_specs=in_smem(1) + [pl.BlockSpec(memory_space=pl.ANY)] + in_vmem(4),
        out_specs=pl.BlockSpec(memory_space=pltpu.VMEM),
        compiler_params=grant(60),
        cost_estimate=cost(2),
        name="house_grad",
    )(ints, after, got, unit, rows, house_dirs)


def hop(value, distance, count):
    return lax.ppermute(value, "ctx", [(i, i ^ distance) for i in range(count)])


def slide(value, pairs):
    return lax.ppermute(value, "head", pairs)


INWARD = [(0, 1), (3, 2)]
MIDDLE = [(1, 2), (2, 1)]
OUTWARD = [(1, 0), (2, 3)]


def near_kernel(ends_ref, first_ref, near_ref, inward_ref, out_ref):
    mine = jnp.where(ends_ref[0] > 0, first_ref[0], near_ref[0]).astype(F32)
    out_ref[...] = mine + inward_ref[0].astype(F32)


def run_near(ends, first, near, inward):
    _, rows, width = first.shape
    return pl.pallas_call(
        near_kernel,
        grid=(1,),
        out_shape=jax.ShapeDtypeStruct((rows, width), F32),
        in_specs=in_smem(1) + [pl.BlockSpec((1, rows, width), lambda t: (0, 0, 0))] * 3,
        out_specs=pl.BlockSpec((rows, width), lambda t: (0, 0)),
        compiler_params=grant(60),
        cost_estimate=cost(5),
        name="near_sum",
    )(ends, first, near, inward)


def share_kernel(*refs):
    total_ref, far_ref, outward_ref, out_ref = refs[-4:]
    far = far_ref[0].astype(F32) + outward_ref[0].astype(F32)
    out_ref[...] = (total_ref[...] + far).astype(BF16)


def run_share(share, band, bands, total, far, outward):
    rows, width = total.shape
    tile = min(512, width)
    part = pl.BlockSpec((1, rows, tile), lambda t: (0, 0, t))
    given = [] if share is None else [share]
    return pl.pallas_call(
        share_kernel,
        grid=(width // tile,),
        out_shape=jax.ShapeDtypeStruct((bands * rows, width), BF16),
        in_specs=[pl.BlockSpec(memory_space=pl.ANY)] * len(given)
        + [pl.BlockSpec((rows, tile), lambda t: (0, t)), part, part],
        out_specs=pl.BlockSpec((rows, tile), lambda t: (band, t)),
        input_output_aliases={0: 0} if given else {},
        compiler_params=grant(60),
        cost_estimate=cost(2),
        name="share",
    )(*given, total, far, outward)


def line_ends():
    place = lax.axis_index("head")
    return ((place == 0) | (place == 3)).astype(jnp.int32).reshape(1)


def line_scatter(share, band, bands, first, rest, inward, inner):
    swapped = slide(inner, MIDDLE)
    outward = slide(first + swapped[1:], OUTWARD)
    total = run_near(line_ends(), first, rest, inward)
    return run_share(share, band, bands, total, swapped, outward), outward


def line_scatter_apart(share, band, bands, first, near, far, last, meanwhile):
    in_last, in_far, in_near = slide(last, INWARD), slide(far, INWARD), slide(near, INWARD)
    sum_last = last + in_last
    swap_last = slide(sum_last, MIDDLE)
    other = meanwhile(sum_last)
    sum_far, _ = lax.optimization_barrier((far + in_far, other))
    swap_far = slide(sum_far, MIDDLE)
    outward = slide(first + swap_last, OUTWARD)
    total = run_near(line_ends(), first, near, in_near)
    return run_share(share, band, bands, total, swap_far, outward), other


def shards(
    query_rows, key_rows, value_rows, grad_out, house_dirs, owners, offsets, w_query, w_key, w_value
):
    tok_rows, width = query_rows.shape
    heads, blocks = width // DH, tok_rows // BLK
    ctx_count, groups = lax.axis_size("ctx"), lax.axis_size("head")
    my_index = lax.axis_index("ctx").astype(jnp.int32)
    ints = jnp.concatenate([my_index.reshape(1), owners.reshape(-1), offsets.reshape(-1)])
    by_hand = ctx_count == 8 and groups == 4 and blocks == 4
    core, across, along = 1, 2, 4

    if by_hand:
        other = hop(house_dirs, core, 8)
        upper = (my_index & core) != 0
        low, high = jnp.where(upper, other, house_dirs), jnp.where(upper, house_dirs, other)
        house_pair = jnp.concatenate([low, high], axis=0)
        value_x, key_y = hop(value_rows, across, 8), hop(key_rows, along, 8)
        key_x, value_y = hop(key_rows, across, 8), hop(value_rows, along, 8)
        house_late, *_ = lax.optimization_barrier((house_pair, value_x, key_y))
        house_parts = [house_pair] + [hop(house_late, t, 8) for t in (2, 4, 6)]
        key_d, value_d = hop(key_y, across, 8), hop(value_x, along, 8)
    else:
        house_parts = [lax.all_gather(house_dirs, "ctx", axis=0, tiled=True)]

    unit, rows, inverse, wide, tall = run_chain(ints, house_parts, heads)
    qrot, krot, local, listed_cum = run_rotate(
        ints, wide, tall, query_rows, key_rows, heads, blocks
    )
    if by_hand:
        own = (key_rows, value_rows, key_x, value_x, key_y, value_y, key_d, value_d)
        early = lax.optimization_barrier((*own[:6], *house_parts))[:6]
        late = lax.optimization_barrier((*own[6:], qrot))[:2]
        siblings = [hop(part, core, 8) for part in (*early, *late)]
        sources, places = [], []
        for t in range(4):
            for pair in (own[2 * t : 2 * t + 2], siblings[2 * t : 2 * t + 2]):
                places.append(((len(sources), 0), (len(sources) + 1, 0)))
                sources += pair
    else:
        sources = [lax.all_gather(key_rows, "ctx"), lax.all_gather(value_rows, "ctx")]
        places = [((0, 0), (1, 0))]

    rounds = ((0, 1), (1, blocks - 1), (blocks, 1), (blocks + 1, blocks - 1))
    dq, dcum, dk_loc, dv_loc, *outs = run_attend(
        ints,
        sources,
        places,
        (query_rows, qrot, krot, value_rows, grad_out, local, listed_cum),
        heads,
        blocks,
        rounds if by_hand else (),
    )
    weights = (w_query, w_key, w_value)
    flip = jnp.where(by_hand & (lax.axis_index("head") >= 2), 1, 0).astype(jnp.int32).reshape(1)

    arrays = (dk_loc, dv_loc, dq, key_rows, dcum, local)

    def project(block, layout, afters, parts, before=()):
        return run_project(block, groups, layout, flip, afters, parts, before, arrays, weights)

    if by_hand:
        got_0 = hop(outs[2], core, 8)
        got_1 = hop(lax.optimization_barrier((outs[3], got_0))[0], core, 8)
        sent_0 = run_merge(outs[0], got_0, 0, 1, [])
        sent_1 = run_merge(outs[1], got_1, 0, 1, [sent_0[0]])
        sent_2 = run_merge(outs[1], got_1, 1, 2, [sent_1[0]])

        def give_back(own, got, first, sent):
            back = [hop(part, t, 8) for part, t in zip(sent, (across, along, across + along))]
            near = [part.reshape(-1, BLK, 2 * width) for part in (own, got)]
            parts = []
            for j in range(sent[0].shape[0]):
                mine = [(part, 4 * (first + j)) for part in near]
                parts.append(mine + [(part, j) for part in back])
            return parts, back

        parts_0, back_0 = give_back(outs[0], got_0, 0, sent_0)
        *later_1, _, _ = lax.optimization_barrier((*sent_1, back_0, sent_2))
        parts_1, back_1 = give_back(outs[1], got_1, 0, later_1)
        *later_2, _ = lax.optimization_barrier((*sent_2, back_1))
        parts_2, _ = give_back(outs[1], got_1, 1, later_2)
        rest_0, dcum_0, *grads_0 = project(0, ((1, 2, 3),), [sent_2[0]], parts_0)
        before = (dq, *grads_0)
        split_off = ((0,), (1, 2, 3))
        firsts, rest_1, dcum_1, *_ = project(1, split_off, [rest_0], parts_1, before)
        inward_0, inward_1 = slide(rest_0, INWARD), slide(rest_1, INWARD)
        sum_0, sum_1 = rest_0[1:] + inward_0[1:], rest_1[1:] + inward_1[1:]
        apart = ((0,), (1,), (2,), (3,))
        *terms, dcum_2, _, _ = project(2, apart, [rest_1, sum_0], parts_2)
        share, earlier = line_scatter(None, 0, 4, firsts[:, :BLK], rest_0, inward_0, sum_0)
        share, later = line_scatter(share, 1, 4, firsts[:, BLK:], rest_1, inward_1, sum_1)

        def adjoint_sums(after):
            dcums = [dcum_0, dcum_1, dcum_2]
            afters = (after, earlier)
            return run_adjoint(ints, afters, dcums, unit, rows, inverse, heads, blocks)

        share, sums = line_scatter_apart(share, 1, 2, *terms, adjoint_sums)
    else:
        spots = (owners * blocks + offsets).reshape(-1)
        empty = jnp.zeros((ctx_count * blocks, BLK, 2 * width), BF16)
        filled = empty.at[spots].add(outs[0])
        back = lax.psum_scatter(filled, "ctx", scatter_dimension=0, tiled=True)
        dcums = []
        share = jnp.zeros((tok_rows, w_query.shape[0] // groups), BF16)
        for j in range(blocks):
            term, dcum_out, _, _ = project(
                j, (tuple(range(groups)),), [], [[(back, j)]]
            )
            dcums.append(dcum_out)
            done = lax.psum_scatter(term, "head", scatter_dimension=0, tiled=False)
            share = lax.dynamic_update_slice(share, done, (j * BLK, 0))

        sums = run_adjoint(ints, (), dcums, unit, rows, inverse, heads, blocks)
        later = key_rows

    sums = sums.reshape(ctx_count, blocks, 2 * width)
    got = lax.all_to_all(sums, "ctx", split_axis=0, concat_axis=0, tiled=True)
    house_grad = run_house(ints, later, got, unit, rows, house_dirs, heads, blocks)
    return (share, house_grad)


def solution(mesh):
    placed = (
        P("ctx", "head"),
        P("ctx", "head"),
        P("ctx", "head"),
        P("ctx", "head"),
        P("ctx", "head"),
        P("ctx", None),
        P("ctx", None),
        P(None, "head"),
        P(None, "head"),
        P(None, "head"),
    )
    return jax.shard_map(
        shards,
        mesh=mesh,
        in_specs=placed,
        out_specs=(P("ctx", "head"), P("ctx", "head")),
        check_vma=False,
    )
```

```python
import functools
import math

import jax
import jax.numpy as jnp
from jax import lax
from jax.experimental import pallas as pl
from jax.experimental.pallas import tpu as pltpu
from jax.sharding import PartitionSpec as P

DH = 128
BLK = 128
MAXL = 2
HIGH = lax.Precision.HIGHEST
F32 = jnp.float32
BF16 = jnp.bfloat16


def nn(a, b):
    return lax.dot_general(a, b, (((1,), (0,)), ((), ())), preferred_element_type=F32)


def nt(a, b):
    return lax.dot_general(a, b, (((1,), (1,)), ((), ())), preferred_element_type=F32)


def tn(a, b):
    return lax.dot_general(a, b, (((0,), (0,)), ((), ())), preferred_element_type=F32)


def nn_high(a, b):
    return lax.dot_general(
        a, b, (((1,), (0,)), ((), ())), precision=HIGH, preferred_element_type=F32
    )


def nt_high(a, b):
    return lax.dot_general(
        a, b, (((1,), (1,)), ((), ())), precision=HIGH, preferred_element_type=F32
    )


def split(value):
    top = value.astype(BF16)
    return top, (value - top.astype(F32)).astype(BF16)


def iota(shape, dim):
    return lax.broadcasted_iota(jnp.int32, shape, dim)


def head(h):
    return slice(h * DH, (h + 1) * DH)


def listed(ints_ref, entry, entries):
    return ints_ref[1 + entry], ints_ref[1 + entries + entry]


def grant(mebibytes):
    return pltpu.CompilerParams(vmem_limit_bytes=mebibytes * 1024 * 1024)


def cost(microseconds):
    return pl.CostEstimate(
        flops=int(microseconds * 1.15e9), bytes_accessed=1 << 20, transcendentals=0
    )


def in_smem(count):
    return [pl.BlockSpec(memory_space=pltpu.SMEM)] * count


def in_vmem(count):
    return [pl.BlockSpec(memory_space=pltpu.VMEM)] * count


def chain_kernel(heads, parts, ints_ref, *refs):
    house_refs = refs[:parts]
    unit_ref, rows_ref, inv_ref, wide_ref, tall_ref, unit_h, house_all = refs[parts:]
    count = unit_ref.shape[0]
    span = count // parts
    for t, ref in enumerate(house_refs):
        place = (ints_ref[0] // (8 // parts)) ^ t if parts > 1 else 0
        house_all[pl.ds(pl.multiple_of(place * span, span), span), :] = ref[...]
    eye = (iota((count, count), 0) == iota((count, count), 1)).astype(F32)
    for h in range(heads):
        house = house_all[:, head(h)]
        lengths = jnp.sqrt(jnp.sum(house * house, axis=1, keepdims=True) + 1e-06)
        unit_ref[:, head(h)] = house / lengths
        unit_h[h] = house / lengths
        inv_ref[h] = eye

    def eliminate(step, carry):
        below = iota((count, 1), 0) > step
        for h in range(heads):
            pivot = unit_h[h, pl.ds(step, 1), :]
            overlap = jnp.sum(unit_h[h] * pivot, axis=1, keepdims=True)
            factor = jnp.where(below, 2.0 * overlap, 0.0)
            inv_ref[h] = inv_ref[h] - factor * inv_ref[h, pl.ds(step, 1), :]
        return carry

    lax.fori_loop(0, count, eliminate, 0)
    eye_wide = (iota((DH, DH), 0) == iota((DH, DH), 1)).astype(F32)
    for h in range(heads):
        units = unit_ref[:, head(h)]
        rows = nn_high(inv_ref[h], units)
        rows_ref[:, head(h)] = rows
        unit_hi, unit_lo = split(nt_high(eye_wide, units))
        rows_hi, rows_lo = split(rows)
        wide_ref[h] = jnp.concatenate([unit_hi, unit_hi, unit_lo], axis=1)
        tall_ref[h] = jnp.concatenate([rows_hi, rows_lo, rows_hi], axis=0)


def run_chain(ints, house_parts, heads):
    span, width = house_parts[0].shape
    parts = len(house_parts)
    count = span * parts
    return pl.pallas_call(
        functools.partial(chain_kernel, heads, parts),
        out_shape=[
            jax.ShapeDtypeStruct((count, width), F32),
            jax.ShapeDtypeStruct((count, width), F32),
            jax.ShapeDtypeStruct((heads, count, count), F32),
            jax.ShapeDtypeStruct((heads, DH, 3 * count), BF16),
            jax.ShapeDtypeStruct((heads, 3 * count, DH), BF16),
        ],
        in_specs=in_smem(1) + in_vmem(parts),
        out_specs=in_vmem(5),
        scratch_shapes=[pltpu.VMEM((heads, count, DH), F32), pltpu.VMEM((count, width), F32)],
        compiler_params=grant(12),
        cost_estimate=cost(6),
        name="house_chain",
    )(ints, *house_parts)


def rotate_kernel(
    heads,
    blocks,
    ints_ref,
    wide_ref,
    tall_ref,
    query_ref,
    key_ref,
    qrot_ref,
    krot_ref,
    local_ref,
    listed_ref,
):
    count = wide_ref.shape[2] // 3
    entries = blocks * MAXL
    column = iota((DH, 3 * count), 1) % count
    eye = (iota((DH, DH), 0) == iota((DH, DH), 1)).astype(F32)

    def cumulative(h, block):
        kept = jnp.where(column <= block, wide_ref[h].astype(F32), 0.0).astype(BF16)
        return split(eye - 2.0 * nn(kept, tall_ref[h]))

    base = ints_ref[0] * blocks

    def local_block(b, carry):
        here = pl.ds(pl.multiple_of(b * BLK, BLK), BLK)
        for h in range(heads):
            hi, lo = cumulative(h, base + b)
            local_ref[b, h] = hi
            query, key = query_ref[here, head(h)], key_ref[here, head(h)]
            qrot_ref[here, head(h)] = (nn(query, hi) + nn(query, lo)).astype(BF16)
            krot_ref[here, head(h)] = (nn(key, hi) + nn(key, lo)).astype(BF16)
        return carry

    lax.fori_loop(0, blocks, local_block, 0)

    def listed_block(e, carry):
        owner, offset = listed(ints_ref, e, entries)
        for h in range(heads):
            hi, lo = cumulative(h, owner * blocks + offset)
            listed_ref[e, h, :DH] = hi
            listed_ref[e, h, DH:] = lo
        return carry

    lax.fori_loop(0, entries, listed_block, 0)


def run_rotate(ints, wide, tall, query_rows, key_rows, heads, blocks):
    rows, width = query_rows.shape
    entries = blocks * MAXL
    return pl.pallas_call(
        functools.partial(rotate_kernel, heads, blocks),
        out_shape=[
            jax.ShapeDtypeStruct((rows, width), BF16),
            jax.ShapeDtypeStruct((rows, width), BF16),
            jax.ShapeDtypeStruct((blocks, heads, DH, DH), BF16),
            jax.ShapeDtypeStruct((entries, heads, 2 * DH, DH), BF16),
        ],
        in_specs=in_smem(1) + in_vmem(4),
        out_specs=in_vmem(4),
        compiler_params=grant(16),
        cost_estimate=cost(9),
        name="rotate",
    )(ints, wide, tall, query_rows, key_rows)


def attend_kernel(heads, blocks, places, pieces, *refs):
    ints_ref = refs[0]
    source_count = 1 + max(place[0] for pair in places for place in pair)
    sources = refs[1 : 1 + source_count]
    refs = refs[1 + source_count :]
    (query_ref, qrot_ref, krot_ref, value_ref, grad_ref, local_ref, listed_ref) = refs[:7]
    dq_ref, dcum_ref, dk_ref, dv_ref = refs[7:11]
    outs = refs[11 : 11 + max(len(pieces), 1)]
    refs = refs[11 + max(len(pieces), 1) :]
    dq_all, dcum_all, dk_all, dv_all, grad_sems, far_keys, far_values, sems = refs[:8]
    entries = blocks * MAXL
    scaling = DH ** (-0.5)
    log_scale = scaling * math.log2(math.e)

    def start(e, src, kind, slot, where):
        pltpu.make_async_copy(src.at[where], slot.at[e], sems.at[kind, e]).start()

    for e in range(entries):
        owner, offset = listed(ints_ref, e, entries)
        row = pl.multiple_of(offset * BLK, BLK)
        if len(places) == 1:
            start(e, sources[0], 0, far_keys, (owner, pl.ds(row, BLK)))
            start(e, sources[1], 1, far_values, (owner, pl.ds(row, BLK)))
        else:
            distance = owner ^ ints_ref[0]
            for r, (key_place, value_place) in enumerate(places):

                @pl.when(distance == r)
                def _():
                    source, first = key_place
                    start(e, sources[source], 0, far_keys, pl.ds(first + row, BLK))
                    source, first = value_place
                    start(e, sources[source], 1, far_values, pl.ds(first + row, BLK))

    out_copies = []
    if pieces:
        payloads, out_sems = refs[8 : 8 + heads], refs[8 + heads]
        for payload in payloads:
            payload[...] = jnp.zeros_like(payload)
    for kind, slots in ((0, far_keys), (1, far_values)):
        for e in range(entries):
            pltpu.make_async_copy(slots.at[e], slots.at[e], sems.at[kind, e]).wait()

    later = iota((BLK, BLK), 0) > iota((BLK, BLK), 1)
    empty = jnp.zeros((BLK, DH), BF16)
    steps = range(blocks)
    for h in range(heads):
        lanes = head(h)
        spans = [slice(a * BLK, (a + 1) * BLK) for a in steps]
        both, keys, values = [], [], []
        for a in steps:
            qrot, grad = qrot_ref[spans[a], lanes], grad_ref[spans[a], lanes]
            upper = jnp.concatenate([qrot, empty], axis=1)
            lower = jnp.concatenate([empty, grad], axis=1)
            both.append(jnp.concatenate([upper, lower], axis=0))
            keys.append([krot_ref[spans[b], lanes] for b in range(a + 1)])
            values.append([value_ref[spans[b], lanes] for b in range(a + 1)])
            for l in range(MAXL):
                e = a * MAXL + l
                raw = far_keys[e, :, lanes]
                raw = jnp.concatenate([raw, raw], axis=1)
                keys[a].append(nn(raw, listed_ref[e, h]).astype(BF16))
                values[a].append(far_values[e, :, lanes])
        scores, dprobs, tops = [], [], []
        for a in steps:
            scores.append([])
            dprobs.append([])
            top = None
            for b in range(a + 1 + MAXL):
                pair = nt(jnp.concatenate([keys[a][b], values[a][b]], axis=1), both[a])
                part = pair[:, :BLK] * log_scale
                if b == a:
                    part = jnp.where(later, -jnp.inf, part)
                scores[a].append(part)
                dprobs[a].append(pair[:, BLK:])
                top = part if top is None else jnp.maximum(top, part)
            tops.append(jnp.max(top, axis=0, keepdims=True))
        weights, inverses, deltas = [], [], []
        for a in steps:
            weights.append([])
            total, inner = None, None
            for part, dprob in zip(scores[a], dprobs[a]):
                weight = jnp.exp2(part - tops[a])
                weights[a].append(weight)
                product = weight * dprob
                total = weight if total is None else total + weight
                inner = product if inner is None else inner + product
            inverses.append(1.0 / jnp.sum(total, axis=0, keepdims=True))
            deltas.append(jnp.sum(inner, axis=0, keepdims=True) * inverses[a])
        dscores, pairs = [], []
        for a in steps:
            dscores.append([])
            pairs.append([])
            for b in range(a + 1 + MAXL):
                probs = weights[a][b] * inverses[a]
                dscore = (probs * (dprobs[a][b] - deltas[a])).astype(BF16)
                dscores[a].append(dscore)
                wide = jnp.concatenate([dscore, probs.astype(BF16)], axis=1)
                pairs[a].append(nn(wide, both[a]))
        for b in steps:
            total = pairs[b][b]
            for a in range(b + 1, blocks):
                total = total + pairs[a][b]
            dk_all[h, spans[b]] = total[:, :DH] * scaling
            dv_all[h, spans[b]] = total[:, DH:]
        for e in range(entries):
            pair = pairs[e // MAXL][e // MAXL + 1 + e % MAXL]
            dkey, dvalue = (pair[:, :DH] * scaling).astype(BF16), pair[:, DH:].astype(BF16)
            if pieces:
                owner, offset = listed(ints_ref, e, entries)
                distance = owner ^ ints_ref[0]
                at = (distance & 1) * blocks + offset
                payloads[h][at, distance >> 1, :, :DH] += dkey
                payloads[h][at, distance >> 1, :, DH:] += dvalue
            else:
                outs[0][e, :, 2 * h * DH : (2 * h + 1) * DH] = dkey
                outs[0][e, :, (2 * h + 1) * DH : (2 * h + 2) * DH] = dvalue
        halves = []
        for a in steps:
            wide, tall = jnp.concatenate(dscores[a], axis=0), jnp.concatenate(keys[a], axis=0)
            halves.append(split(tn(wide, tall) * scaling))
        for a in steps:
            dq_top, dq_low = halves[a]
            dq_all[h, spans[a]] = nt(dq_top, local_ref[a, h]).astype(BF16)
            query = query_ref[spans[a], lanes]
            query = jnp.concatenate([query, query], axis=0)
            dcum_all[h, a] = tn(query, jnp.concatenate([dq_top, dq_low], axis=0))
        for i, (source, where) in enumerate(
            (
                (dk_all.at[h], dk_ref.at[:, lanes]),
                (dv_all.at[h], dv_ref.at[:, lanes]),
                (dq_all.at[h], dq_ref.at[:, lanes]),
                (dcum_all.at[h], dcum_ref.at[:, h]),
            )
        ):
            copy = pltpu.make_async_copy(source, where, grad_sems.at[i, h])
            copy.start()
            out_copies.append(copy)
        for i, (first, size) in enumerate(pieces):
            where = outs[i].at[:, :, :, 2 * h * DH : (2 * h + 2) * DH]
            source = payloads[h].at[pl.ds(first, size)]
            copy = pltpu.make_async_copy(source, where, out_sems.at[i, h])
            copy.start()
            out_copies.append(copy)
    for copy in out_copies:
        copy.wait()


def run_attend(ints, sources, places, arrays, heads, blocks, pieces):
    rows, width = arrays[0].shape
    entries = blocks * MAXL
    any_spec = pl.BlockSpec(memory_space=pl.ANY)
    scratch = [
        pltpu.VMEM((heads, rows, DH), BF16),
        pltpu.VMEM((heads, blocks, DH, DH), F32),
        pltpu.VMEM((heads, rows, DH), F32),
        pltpu.VMEM((heads, rows, DH), F32),
        pltpu.SemaphoreType.DMA((4, heads)),
        pltpu.VMEM((entries, BLK, width), BF16),
        pltpu.VMEM((entries, BLK, width), BF16),
        pltpu.SemaphoreType.DMA((2, entries)),
    ]
    if pieces:
        chips = len(places) // 2
        out_parts = [
            jax.ShapeDtypeStruct((size, chips, BLK, 2 * width), BF16) for _, size in pieces
        ]
        part_specs = [any_spec] * len(pieces)
        scratch += [pltpu.VMEM((2 * blocks, chips, BLK, 2 * DH), BF16)] * heads
        scratch += [pltpu.SemaphoreType.DMA((len(pieces), heads))]
    else:
        out_parts = [jax.ShapeDtypeStruct((entries, BLK, 2 * width), BF16)]
        part_specs = in_vmem(1)
    return pl.pallas_call(
        functools.partial(attend_kernel, heads, blocks, places, pieces),
        out_shape=[
            jax.ShapeDtypeStruct((rows, width), BF16),
            jax.ShapeDtypeStruct((blocks, heads, DH, DH), F32),
            jax.ShapeDtypeStruct((rows, width), F32),
            jax.ShapeDtypeStruct((rows, width), F32),
        ]
        + out_parts,
        in_specs=in_smem(1) + [any_spec] * len(sources) + in_vmem(7),
        out_specs=[pl.BlockSpec(memory_space=pltpu.HBM)] * 4 + part_specs,
        scratch_shapes=scratch,
        compiler_params=grant(58),
        cost_estimate=cost(15),
        name="attend",
    )(ints, *sources, *arrays)


def merge_kernel(own_ref, got_ref, *refs):
    for i, ref in enumerate(refs[-3:]):
        total = own_ref[0, i + 1].astype(F32) + got_ref[0, i + 1].astype(F32)
        ref[0] = total.astype(BF16)


def run_merge(own, got, first, size, afters):
    _, chips, rows, width = own.shape
    cut = 2
    lanes = width // cut
    whole = pl.BlockSpec((1, chips, rows, lanes), lambda j, c: (first + j, 0, 0, c))
    return pl.pallas_call(
        merge_kernel,
        grid=(size, cut),
        out_shape=[jax.ShapeDtypeStruct((size, rows, width), BF16)] * (chips - 1),
        in_specs=[whole] * 2
        + [pl.BlockSpec((1, 16, 128), lambda j, c: (0, 0, 0))] * len(afters),
        out_specs=[pl.BlockSpec((1, rows, lanes), lambda j, c: (j, 0, c))] * (chips - 1),
        compiler_params=grant(12),
        cost_estimate=cost(2),
        name="merge",
    )(own, got, *afters)


def project_kernel(heads, parts, size, groups, before, layout, afters, flip_ref, *refs):
    refs = refs[afters:]
    outs = len(layout)
    chunks = [(m, i, at) for i, row in enumerate(layout) for at, m in enumerate(row)]
    tiles, sems = refs[-2:]
    per = tiles.shape[0] // len(chunks)
    tile = tiles.shape[2]
    part_refs, refs = refs[: size * parts], refs[size * parts :]
    before_refs, refs = refs[:before], refs[before:]
    dk_loc, dv_loc, dq_ref, key_ref, dcum_in, cum_ref = refs[:6]
    weight_refs, out_refs = refs[6:9], refs[9 : 9 + outs]
    dcum_out, dk_out, dv_out = refs[9 + outs : 12 + outs]
    copies = []
    for t in range(len(chunks) * per):
        m = chunks[t // per][0]
        row = ((m + flip_ref[0] * (groups - 1 - 2 * m)) * per + t % per) * tile
        rows = pl.ds(pl.multiple_of(row, tile), tile)
        for w, ref in enumerate(weight_refs):
            copy = pltpu.make_async_copy(ref.at[rows], tiles.at[t, w], sems.at[t, w])
            copy.start()
            copies.append(copy)

    earlier = ()
    dk_rows, dv_rows = [], []
    for j in range(size):
        here = slice(j * BLK, (j + 1) * BLK)
        dk, dv = [], []
        for h in range(heads):
            both = slice(2 * h * DH, (2 * h + 2) * DH)
            total = part_refs[j * parts][0, :, both].astype(F32)
            for ref in part_refs[j * parts + 1 : (j + 1) * parts]:
                total = total + ref[0, :, both].astype(F32)
            dv.append((dv_loc[here, head(h)] + total[:, DH:]).astype(BF16))
            dk_top, dk_low = split(dk_loc[here, head(h)] + total[:, :DH])
            dk.append(nt(dk_top, cum_ref[j, h]).astype(BF16))
            key = key_ref[here, head(h)]
            key = jnp.concatenate([key, key], axis=0)
            dcum = tn(key, jnp.concatenate([dk_top, dk_low], axis=0))
            dcum_out[j, h] = dcum_in[j, h] + dcum
        dk_rows.append(jnp.concatenate(dk, axis=1))
        dv_rows.append(jnp.concatenate(dv, axis=1))
    dk_all, dv_all = jnp.concatenate(dk_rows, axis=0), jnp.concatenate(dv_rows, axis=0)
    dk_out[...] = dk_all
    dv_out[...] = dv_all
    grads = (dq_ref[...], dk_all, dv_all)
    if before:
        earlier = [
            jnp.concatenate([old[...], new], axis=0) for old, new in zip(before_refs, grads)
        ]

    for t in range(len(chunks) * per):
        term = None
        m, out, at = chunks[t // per]
        for w, grad in enumerate(earlier if before and m == 0 else grads):
            copies[3 * t + w].wait()
            part = nt(tiles[t, w], grad)
            term = part if term is None else term + part
        spot = slice(t % per * tile, (t % per + 1) * tile)
        out_refs[out][at, :, spot] = term.T.astype(BF16)


def run_project(block, groups, layout, flip, afters, parts, before, arrays, weights):
    dk_loc, dv_loc, dq, key_rows, dcum, cum = arrays
    size, width = len(parts), dq.shape[1]
    heads = width // DH
    model = weights[0].shape[0]
    chunk = model // groups
    tile = min(512, chunk)
    rows = size * BLK
    tile_count = sum(map(len, layout)) * chunk // tile

    def part_spec(index):
        return pl.BlockSpec((1, BLK, 2 * width), lambda t: (index, 0, 0))

    def whole(*shape):
        return pl.BlockSpec(shape, lambda t: (0,) * len(shape))

    rows_spec = pl.BlockSpec((rows, width), lambda t: (block // size, 0))
    head_spec = pl.BlockSpec((size, heads, DH, DH), lambda t: (block // size, 0, 0, 0))
    flat = [part for row in parts for part in row]
    heights = [2 * rows if before and row == (0,) else rows for row in layout]
    shapes = [(len(row), height, chunk) for row, height in zip(layout, heights)]
    return pl.pallas_call(
        functools.partial(
            project_kernel,
            heads,
            len(parts[0]),
            size,
            groups,
            len(before),
            layout,
            len(afters),
        ),
        grid=(1,),
        in_specs=in_smem(1)
        + [whole(1, 16, 128)] * len(afters)
        + [part_spec(index) for _, index in flat]
        + [whole(rows, width)] * len(before)
        + [rows_spec] * 4
        + [head_spec] * 2
        + [pl.BlockSpec(memory_space=pl.ANY)] * 3,
        out_specs=[whole(*shape) for shape in shapes]
        + [whole(size, heads, DH, DH)]
        + [whole(rows, width)] * 2,
        scratch_shapes=[
            pltpu.VMEM((tile_count, 3, tile, width), BF16),
            pltpu.SemaphoreType.DMA((tile_count, 3)),
        ],
        out_shape=[jax.ShapeDtypeStruct(shape, BF16) for shape in shapes]
        + [jax.ShapeDtypeStruct((size, heads, DH, DH), F32)]
        + [jax.ShapeDtypeStruct((rows, width), BF16)] * 2,
        compiler_params=grant(60),
        cost_estimate=cost(3 * sum(map(len, layout))),
        name="project",
    )(
        flip,
        *afters,
        *[part for part, _ in flat],
        *before,
        dk_loc,
        dv_loc,
        dq,
        key_rows,
        dcum,
        cum,
        *weights,
    )


def adjoint_kernel(heads, blocks, afters, ints_ref, *refs):
    refs = refs[afters:]
    dcums = [ref.at[j] for ref in refs[:-4] for j in range(ref.shape[0])]
    unit_ref, rows_ref, inv_ref, out_ref = refs[-4:]
    count, width = unit_ref.shape
    stacked = (blocks * count, count)
    eye = (iota((count, count), 0) == iota((count, count), 1)).astype(F32)
    base = ints_ref[0] * blocks
    level, col = iota(stacked, 0), iota(stacked, 1)
    row = level % count
    mine = base + level // count
    alive = row[:, :1] <= mine[:, :1]
    for h in range(heads):
        units, rows, inverse = unit_ref[:, head(h)], rows_ref[:, head(h)], inv_ref[h]
        inverse_t = nt_high(eye, inverse)
        moved = jnp.concatenate([nt_high(rows, dcum[h]) for dcum in dcums], axis=0)
        overlap = jnp.where(col <= mine, nt_high(moved, units), 0.0)
        gamma = nn_high(overlap, inverse)
        gamma = jnp.where((row < col) & (col <= mine), gamma, 0.0)
        beta = jnp.concatenate([eye - inverse_t] * blocks, axis=0)
        beta = jnp.where(col <= mine, beta, 0.0)
        x_all = jnp.where(alive, moved - 2.0 * nn_high(gamma, units), 0.0)
        turned = jnp.concatenate([units] * blocks, axis=0) - nn_high(beta, units)
        turned = jnp.where(alive, turned, 0.0)
        x_total, y_total = None, None
        for j, dcum in enumerate(dcums):
            here = slice(j * count, (j + 1) * count)
            y_part = nn_high(turned[here], dcum[h])
            x_total = x_all[here] if j == 0 else x_total + x_all[here]
            y_total = y_part if j == 0 else y_total + y_part
        out_ref[:, head(h)] = x_total
        out_ref[:, slice(width + h * DH, width + (h + 1) * DH)] = y_total


def run_adjoint(ints, afters, dcums, unit, rows, inverse, heads, blocks):
    count, width = unit.shape
    return pl.pallas_call(
        functools.partial(adjoint_kernel, heads, blocks, len(afters)),
        out_shape=jax.ShapeDtypeStruct((count, 2 * width), F32),
        in_specs=in_smem(1)
        + [pl.BlockSpec(memory_space=pl.ANY)] * len(afters)
        + in_vmem(len(dcums) + 3),
        out_specs=pl.BlockSpec(memory_space=pltpu.VMEM),
        compiler_params=grant(60),
        cost_estimate=cost(2),
        name="adjoint",
    )(ints, *afters, *dcums, unit, rows, inverse)


def house_kernel(heads, blocks, base_ref, got_ref, unit_ref, rows_ref, house_ref, out_ref):
    count, width = unit_ref.shape
    total = jnp.sum(got_ref[...], axis=0)
    for h in range(heads):
        x_part = total[:, head(h)]
        y_part = total[:, slice(width + h * DH, width + (h + 1) * DH)]
        along = nt_high(y_part, rows_ref[:, head(h)])
        spot = iota((blocks, count), 0) + base_ref[0] * blocks
        along = jnp.where(iota((blocks, count), 1) < spot, along, 0.0)
        turned = y_part - 2.0 * nn_high(along, unit_ref[:, head(h)])
        dunit = -2.0 * (x_part + turned)
        house = house_ref[:, head(h)]
        lengths = jnp.sqrt(jnp.sum(house * house, axis=1, keepdims=True) + 1e-06)
        unit = house / lengths
        inner = jnp.sum(unit * dunit, axis=1, keepdims=True)
        out_ref[:, head(h)] = (dunit - unit * inner) / lengths


def run_house(ints, got, unit, rows, house_dirs, heads, blocks):
    return pl.pallas_call(
        functools.partial(house_kernel, heads, blocks),
        out_shape=jax.ShapeDtypeStruct(house_dirs.shape, F32),
        in_specs=in_smem(1) + in_vmem(4),
        out_specs=pl.BlockSpec(memory_space=pltpu.VMEM),
        compiler_params=grant(60),
        cost_estimate=cost(2),
        name="house_grad",
    )(ints, got, unit, rows, house_dirs)


def hop(value, distance, count):
    return lax.ppermute(value, "ctx", [(i, i ^ distance) for i in range(count)])


def slide(value, pairs):
    return lax.ppermute(value, "head", pairs)


INWARD = [(0, 1), (3, 2)]
MIDDLE = [(1, 2), (2, 1)]
OUTWARD = [(1, 0), (2, 3)]


def near_kernel(ends_ref, first_ref, near_ref, inward_ref, out_ref):
    mine = jnp.where(ends_ref[0] > 0, first_ref[0], near_ref[0]).astype(F32)
    out_ref[...] = mine + inward_ref[0].astype(F32)


def run_near(ends, first, near, inward):
    _, rows, width = first.shape
    return pl.pallas_call(
        near_kernel,
        grid=(1,),
        out_shape=jax.ShapeDtypeStruct((rows, width), F32),
        in_specs=in_smem(1) + [pl.BlockSpec((1, rows, width), lambda t: (0, 0, 0))] * 3,
        out_specs=pl.BlockSpec((rows, width), lambda t: (0, 0)),
        compiler_params=grant(60),
        cost_estimate=cost(5),
        name="near_sum",
    )(ends, first, near, inward)


def share_kernel(*refs):
    total_ref, far_ref, outward_ref, out_ref = refs[-4:]
    far = far_ref[0].astype(F32) + outward_ref[0].astype(F32)
    out_ref[...] = (total_ref[...] + far).astype(BF16)


def run_share(share, band, bands, total, far, outward):
    rows, width = total.shape
    tile = min(512, width)
    part = pl.BlockSpec((1, rows, tile), lambda t: (0, 0, t))
    given = [] if share is None else [share]
    return pl.pallas_call(
        share_kernel,
        grid=(width // tile,),
        out_shape=jax.ShapeDtypeStruct((bands * rows, width), BF16),
        in_specs=[pl.BlockSpec(memory_space=pl.ANY)] * len(given)
        + [pl.BlockSpec((rows, tile), lambda t: (0, t)), part, part],
        out_specs=pl.BlockSpec((rows, tile), lambda t: (band, t)),
        input_output_aliases={0: 0} if given else {},
        compiler_params=grant(60),
        cost_estimate=cost(2),
        name="share",
    )(*given, total, far, outward)


def line_ends():
    place = lax.axis_index("head")
    return ((place == 0) | (place == 3)).astype(jnp.int32).reshape(1)


def line_scatter(share, band, bands, first, rest, inward, inner):
    swapped = slide(inner, MIDDLE)
    outer = first + swapped[1:]
    outward = slide(outer, OUTWARD)
    total = run_near(line_ends(), first, rest, inward)
    return run_share(share, band, bands, total, swapped, outward), swapped, outer


def line_scatter_apart(share, band, bands, first, near, far, last, ready, exchange, earlier):
    in_last, in_far, in_near = slide(last, INWARD), slide(far, INWARD), slide(near, INWARD)
    in_last, ready = lax.optimization_barrier((in_last, ready))
    sum_last = last + in_last
    ready, *_ = lax.optimization_barrier((ready, sum_last, earlier))
    got = exchange(ready)
    swap_last = slide(sum_last, MIDDLE)
    in_far, got = lax.optimization_barrier((in_far, got))
    swap_far = slide(far + in_far, MIDDLE)
    outward = slide(first + swap_last, OUTWARD)
    total = run_near(line_ends(), first, near, in_near)
    return run_share(share, band, bands, total, swap_far, outward), got


def shards(
    query_rows, key_rows, value_rows, grad_out, house_dirs, owners, offsets, w_query, w_key, w_value
):
    tok_rows, width = query_rows.shape
    heads, blocks = width // DH, tok_rows // BLK
    ctx_count, groups = lax.axis_size("ctx"), lax.axis_size("head")
    my_index = lax.axis_index("ctx").astype(jnp.int32)
    ints = jnp.concatenate([my_index.reshape(1), owners.reshape(-1), offsets.reshape(-1)])
    by_hand = ctx_count == 8 and groups == 4 and blocks == 4
    core, across, along = 1, 2, 4

    if by_hand:
        other = hop(house_dirs, core, 8)
        upper = (my_index & core) != 0
        low, high = jnp.where(upper, other, house_dirs), jnp.where(upper, house_dirs, other)
        house_pair = jnp.concatenate([low, high], axis=0)
        value_x, key_y = hop(value_rows, across, 8), hop(key_rows, along, 8)
        key_x, value_y = hop(key_rows, across, 8), hop(value_rows, along, 8)
        house_late, *_ = lax.optimization_barrier((house_pair, value_x, key_y))
        house_parts = [house_pair] + [hop(house_late, t, 8) for t in (2, 4, 6)]
        key_d, value_d = hop(key_y, across, 8), hop(value_x, along, 8)
    else:
        house_parts = [lax.all_gather(house_dirs, "ctx", axis=0, tiled=True)]

    unit, rows, inverse, wide, tall = run_chain(ints, house_parts, heads)
    qrot, krot, local, listed_cum = run_rotate(
        ints, wide, tall, query_rows, key_rows, heads, blocks
    )
    if by_hand:
        own = (key_rows, value_rows, key_x, value_x, key_y, value_y, key_d, value_d)
        early = lax.optimization_barrier((*own[:6], *house_parts))[:6]
        late = lax.optimization_barrier((*own[6:], qrot))[:2]
        siblings = [hop(part, core, 8) for part in (*early, *late)]
        sources, places = [], []
        for t in range(4):
            for pair in (own[2 * t : 2 * t + 2], siblings[2 * t : 2 * t + 2]):
                places.append(((len(sources), 0), (len(sources) + 1, 0)))
                sources += pair
    else:
        sources = [lax.all_gather(key_rows, "ctx"), lax.all_gather(value_rows, "ctx")]
        places = [((0, 0), (1, 0))]

    rounds = ((0, 1), (1, blocks - 1), (blocks, 1), (blocks + 1, blocks - 1))
    dq, dcum, dk_loc, dv_loc, *outs = run_attend(
        ints,
        sources,
        places,
        (query_rows, qrot, krot, value_rows, grad_out, local, listed_cum),
        heads,
        blocks,
        rounds if by_hand else (),
    )
    weights = (w_query, w_key, w_value)
    flip = jnp.where(by_hand & (lax.axis_index("head") >= 2), 1, 0).astype(jnp.int32).reshape(1)

    arrays = (dk_loc, dv_loc, dq, key_rows, dcum, local)

    def project(block, layout, afters, parts, before=()):
        return run_project(block, groups, layout, flip, afters, parts, before, arrays, weights)

    def share_sums(sums):
        sums = sums.reshape(ctx_count, blocks, 2 * width)
        return lax.all_to_all(sums, "ctx", split_axis=0, concat_axis=0, tiled=True)

    if by_hand:
        got_0 = hop(outs[2], core, 8)
        got_1 = hop(lax.optimization_barrier((outs[3], got_0))[0], core, 8)
        sent_0 = run_merge(outs[0], got_0, 0, 1, [])
        sent_1 = run_merge(outs[1], got_1, 0, 1, [sent_0[0]])
        sent_2 = run_merge(outs[1], got_1, 1, 2, [sent_1[0]])

        def give_back(own, got, first, sent):
            back = [hop(part, t, 8) for part, t in zip(sent, (across, along, across + along))]
            near = [part.reshape(-1, BLK, 2 * width) for part in (own, got)]
            parts = []
            for j in range(sent[0].shape[0]):
                mine = [(part, 4 * (first + j)) for part in near]
                parts.append(mine + [(part, j) for part in back])
            return parts, back

        parts_0, back_0 = give_back(outs[0], got_0, 0, sent_0)
        *later_1, _, _ = lax.optimization_barrier((*sent_1, back_0, sent_2))
        parts_1, back_1 = give_back(outs[1], got_1, 0, later_1)
        *later_2, _ = lax.optimization_barrier((*sent_2, back_1))
        parts_2, _ = give_back(outs[1], got_1, 1, later_2)
        rest_0, dcum_0, *grads_0 = project(0, ((1, 2, 3),), [sent_2[0]], parts_0)
        before = (dq, *grads_0)
        split_off = ((0,), (1, 2, 3))
        firsts, rest_1, dcum_1, *_ = project(1, split_off, [rest_0], parts_1, before)
        inward_0, inward_1 = slide(rest_0, INWARD), slide(rest_1, INWARD)
        apart = ((0,), (1,), (2,), (3,))
        *terms, dcum_2, _, _ = project(2, apart, [rest_1], parts_2)
        share, swapped_0, outer_0 = line_scatter(
            None, 0, 4, firsts[:, :BLK], rest_0, inward_0, rest_0[1:] + inward_0[1:]
        )
        inward_1, _ = lax.optimization_barrier((inward_1, swapped_0))
        sum_1 = rest_1[1:] + inward_1[1:]
        share, _, outer_1 = line_scatter(
            share, 1, 4, firsts[:, BLK:], rest_1, inward_1, sum_1
        )
        dcums = [dcum_0, dcum_1, dcum_2]
        sums = run_adjoint(ints, (sum_1, outer_0), dcums, unit, rows, inverse, heads, blocks)
        share, got = line_scatter_apart(
            share, 1, 2, *terms, sums, share_sums, outer_1
        )
    else:
        spots = (owners * blocks + offsets).reshape(-1)
        empty = jnp.zeros((ctx_count * blocks, BLK, 2 * width), BF16)
        filled = empty.at[spots].add(outs[0])
        back = lax.psum_scatter(filled, "ctx", scatter_dimension=0, tiled=True)
        dcums = []
        share = jnp.zeros((tok_rows, w_query.shape[0] // groups), BF16)
        for j in range(blocks):
            term, dcum_out, _, _ = project(
                j, (tuple(range(groups)),), [], [[(back, j)]]
            )
            dcums.append(dcum_out)
            done = lax.psum_scatter(term, "head", scatter_dimension=0, tiled=False)
            share = lax.dynamic_update_slice(share, done, (j * BLK, 0))

        got = share_sums(run_adjoint(ints, (), dcums, unit, rows, inverse, heads, blocks))

    house_grad = run_house(ints, got, unit, rows, house_dirs, heads, blocks)
    return (share, house_grad)


def solution(mesh):
    placed = (
        P("ctx", "head"),
        P("ctx", "head"),
        P("ctx", "head"),
        P("ctx", "head"),
        P("ctx", "head"),
        P("ctx", None),
        P("ctx", None),
        P(None, "head"),
        P(None, "head"),
        P(None, "head"),
    )
    return jax.shard_map(
        shards,
        mesh=mesh,
        in_specs=placed,
        out_specs=(P("ctx", "head"), P("ctx", "head")),
        check_vma=False,
    )
```

```python
import functools
import math

import jax
import jax.numpy as jnp
from jax import lax
from jax.experimental import pallas as pl
from jax.experimental.pallas import tpu as pltpu
from jax.sharding import PartitionSpec as P

DH = 128
BLK = 128
MAXL = 2
HIGH = lax.Precision.HIGHEST
F32 = jnp.float32
BF16 = jnp.bfloat16


def nn(a, b):
    return lax.dot_general(a, b, (((1,), (0,)), ((), ())), preferred_element_type=F32)


def nt(a, b):
    return lax.dot_general(a, b, (((1,), (1,)), ((), ())), preferred_element_type=F32)


def tn(a, b):
    return lax.dot_general(a, b, (((0,), (0,)), ((), ())), preferred_element_type=F32)


def nn_high(a, b):
    return lax.dot_general(
        a, b, (((1,), (0,)), ((), ())), precision=HIGH, preferred_element_type=F32
    )


def nt_high(a, b):
    return lax.dot_general(
        a, b, (((1,), (1,)), ((), ())), precision=HIGH, preferred_element_type=F32
    )


def split(value):
    top = value.astype(BF16)
    return top, (value - top.astype(F32)).astype(BF16)


def iota(shape, dim):
    return lax.broadcasted_iota(jnp.int32, shape, dim)


def head(h):
    return slice(h * DH, (h + 1) * DH)


def listed(ints_ref, entry, entries):
    return ints_ref[1 + entry], ints_ref[1 + entries + entry]


def grant(mebibytes):
    return pltpu.CompilerParams(vmem_limit_bytes=mebibytes * 1024 * 1024)


def cost(microseconds):
    return pl.CostEstimate(
        flops=int(microseconds * 1.15e9), bytes_accessed=1 << 20, transcendentals=0
    )


def in_smem(count):
    return [pl.BlockSpec(memory_space=pltpu.SMEM)] * count


def in_vmem(count):
    return [pl.BlockSpec(memory_space=pltpu.VMEM)] * count


def chain_kernel(heads, parts, ints_ref, *refs):
    house_refs = refs[:parts]
    unit_ref, rows_ref, inv_ref, wide_ref, tall_ref, unit_h, house_all = refs[parts:]
    count = unit_ref.shape[0]
    span = count // parts
    for t, ref in enumerate(house_refs):
        place = (ints_ref[0] // (8 // parts)) ^ t if parts > 1 else 0
        house_all[pl.ds(pl.multiple_of(place * span, span), span), :] = ref[...]
    eye = (iota((count, count), 0) == iota((count, count), 1)).astype(F32)
    for h in range(heads):
        house = house_all[:, head(h)]
        lengths = jnp.sqrt(jnp.sum(house * house, axis=1, keepdims=True) + 1e-06)
        unit_ref[:, head(h)] = house / lengths
        unit_h[h] = house / lengths
        inv_ref[h] = eye

    def eliminate(step, carry):
        below = iota((count, 1), 0) > step
        for h in range(heads):
            pivot = unit_h[h, pl.ds(step, 1), :]
            overlap = jnp.sum(unit_h[h] * pivot, axis=1, keepdims=True)
            factor = jnp.where(below, 2.0 * overlap, 0.0)
            inv_ref[h] = inv_ref[h] - factor * inv_ref[h, pl.ds(step, 1), :]
        return carry

    lax.fori_loop(0, count, eliminate, 0)
    eye_wide = (iota((DH, DH), 0) == iota((DH, DH), 1)).astype(F32)
    for h in range(heads):
        units = unit_ref[:, head(h)]
        rows = nn_high(inv_ref[h], units)
        rows_ref[:, head(h)] = rows
        unit_hi, unit_lo = split(nt_high(eye_wide, units))
        rows_hi, rows_lo = split(rows)
        wide_ref[h] = jnp.concatenate([unit_hi, unit_hi, unit_lo], axis=1)
        tall_ref[h] = jnp.concatenate([rows_hi, rows_lo, rows_hi], axis=0)


def run_chain(ints, house_parts, heads):
    span, width = house_parts[0].shape
    parts = len(house_parts)
    count = span * parts
    return pl.pallas_call(
        functools.partial(chain_kernel, heads, parts),
        out_shape=[
            jax.ShapeDtypeStruct((count, width), F32),
            jax.ShapeDtypeStruct((count, width), F32),
            jax.ShapeDtypeStruct((heads, count, count), F32),
            jax.ShapeDtypeStruct((heads, DH, 3 * count), BF16),
            jax.ShapeDtypeStruct((heads, 3 * count, DH), BF16),
        ],
        in_specs=in_smem(1) + in_vmem(parts),
        out_specs=in_vmem(5),
        scratch_shapes=[pltpu.VMEM((heads, count, DH), F32), pltpu.VMEM((count, width), F32)],
        compiler_params=grant(12),
        cost_estimate=cost(6),
        name="house_chain",
    )(ints, *house_parts)


def rotate_kernel(
    heads,
    blocks,
    ints_ref,
    wide_ref,
    tall_ref,
    query_ref,
    key_ref,
    qrot_ref,
    krot_ref,
    local_ref,
    listed_ref,
):
    count = wide_ref.shape[2] // 3
    entries = blocks * MAXL
    column = iota((DH, 3 * count), 1) % count
    eye = (iota((DH, DH), 0) == iota((DH, DH), 1)).astype(F32)

    def cumulative(h, block):
        kept = jnp.where(column <= block, wide_ref[h].astype(F32), 0.0).astype(BF16)
        return split(eye - 2.0 * nn(kept, tall_ref[h]))

    base = ints_ref[0] * blocks

    def local_block(b, carry):
        here = pl.ds(pl.multiple_of(b * BLK, BLK), BLK)
        for h in range(heads):
            hi, lo = cumulative(h, base + b)
            local_ref[b, h] = hi
            query, key = query_ref[here, head(h)], key_ref[here, head(h)]
            qrot_ref[here, head(h)] = (nn(query, hi) + nn(query, lo)).astype(BF16)
            krot_ref[here, head(h)] = (nn(key, hi) + nn(key, lo)).astype(BF16)
        return carry

    lax.fori_loop(0, blocks, local_block, 0)

    def listed_block(e, carry):
        owner, offset = listed(ints_ref, e, entries)
        for h in range(heads):
            hi, lo = cumulative(h, owner * blocks + offset)
            listed_ref[e, h, :DH] = hi
            listed_ref[e, h, DH:] = lo
        return carry

    lax.fori_loop(0, entries, listed_block, 0)


def run_rotate(ints, wide, tall, query_rows, key_rows, heads, blocks):
    rows, width = query_rows.shape
    entries = blocks * MAXL
    return pl.pallas_call(
        functools.partial(rotate_kernel, heads, blocks),
        out_shape=[
            jax.ShapeDtypeStruct((rows, width), BF16),
            jax.ShapeDtypeStruct((rows, width), BF16),
            jax.ShapeDtypeStruct((blocks, heads, DH, DH), BF16),
            jax.ShapeDtypeStruct((entries, heads, 2 * DH, DH), BF16),
        ],
        in_specs=in_smem(1) + in_vmem(4),
        out_specs=in_vmem(4),
        compiler_params=grant(16),
        cost_estimate=cost(9),
        name="rotate",
    )(ints, wide, tall, query_rows, key_rows)


def attend_kernel(heads, blocks, places, pieces, *refs):
    ints_ref = refs[0]
    source_count = 1 + max(place[0] for pair in places for place in pair)
    sources = refs[1 : 1 + source_count]
    refs = refs[1 + source_count :]
    (query_ref, qrot_ref, krot_ref, value_ref, grad_ref, local_ref, listed_ref) = refs[:7]
    dq_ref, dcum_ref, dk_ref, dv_ref = refs[7:11]
    outs = refs[11 : 11 + max(len(pieces), 1)]
    refs = refs[11 + max(len(pieces), 1) :]
    dq_all, dcum_all, dk_all, dv_all, grad_sems, far_keys, far_values, sems = refs[:8]
    entries = blocks * MAXL
    scaling = DH ** (-0.5)
    log_scale = scaling * math.log2(math.e)

    def start(e, src, kind, slot, where):
        pltpu.make_async_copy(src.at[where], slot.at[e], sems.at[kind, e]).start()

    for e in range(entries):
        owner, offset = listed(ints_ref, e, entries)
        row = pl.multiple_of(offset * BLK, BLK)
        if len(places) == 1:
            start(e, sources[0], 0, far_keys, (owner, pl.ds(row, BLK)))
            start(e, sources[1], 1, far_values, (owner, pl.ds(row, BLK)))
        else:
            distance = owner ^ ints_ref[0]
            for r, (key_place, value_place) in enumerate(places):

                @pl.when(distance == r)
                def _():
                    source, first = key_place
                    start(e, sources[source], 0, far_keys, pl.ds(first + row, BLK))
                    source, first = value_place
                    start(e, sources[source], 1, far_values, pl.ds(first + row, BLK))

    out_copies = []
    if pieces:
        payloads, out_sems = refs[8 : 8 + heads], refs[8 + heads]
        for payload in payloads:
            payload[...] = jnp.zeros_like(payload)
    for kind, slots in ((0, far_keys), (1, far_values)):
        for e in range(entries):
            pltpu.make_async_copy(slots.at[e], slots.at[e], sems.at[kind, e]).wait()

    later = iota((BLK, BLK), 0) > iota((BLK, BLK), 1)
    empty = jnp.zeros((BLK, DH), BF16)
    steps = range(blocks)
    for h in range(heads):
        lanes = head(h)
        spans = [slice(a * BLK, (a + 1) * BLK) for a in steps]
        both, keys, values = [], [], []
        for a in steps:
            qrot, grad = qrot_ref[spans[a], lanes], grad_ref[spans[a], lanes]
            upper = jnp.concatenate([qrot, empty], axis=1)
            lower = jnp.concatenate([empty, grad], axis=1)
            both.append(jnp.concatenate([upper, lower], axis=0))
            keys.append([krot_ref[spans[b], lanes] for b in range(a + 1)])
            values.append([value_ref[spans[b], lanes] for b in range(a + 1)])
            for l in range(MAXL):
                e = a * MAXL + l
                raw = far_keys[e, :, lanes]
                raw = jnp.concatenate([raw, raw], axis=1)
                keys[a].append(nn(raw, listed_ref[e, h]).astype(BF16))
                values[a].append(far_values[e, :, lanes])
        scores, dprobs, tops = [], [], []
        for a in steps:
            scores.append([])
            dprobs.append([])
            top = None
            for b in range(a + 1 + MAXL):
                pair = nt(jnp.concatenate([keys[a][b], values[a][b]], axis=1), both[a])
                part = pair[:, :BLK] * log_scale
                if b == a:
                    part = jnp.where(later, -jnp.inf, part)
                scores[a].append(part)
                dprobs[a].append(pair[:, BLK:])
                top = part if top is None else jnp.maximum(top, part)
            tops.append(jnp.max(top, axis=0, keepdims=True))
        weights, inverses, deltas = [], [], []
        for a in steps:
            weights.append([])
            total, inner = None, None
            for part, dprob in zip(scores[a], dprobs[a]):
                weight = jnp.exp2(part - tops[a])
                weights[a].append(weight)
                product = weight * dprob
                total = weight if total is None else total + weight
                inner = product if inner is None else inner + product
            inverses.append(1.0 / jnp.sum(total, axis=0, keepdims=True))
            deltas.append(jnp.sum(inner, axis=0, keepdims=True) * inverses[a])
        dscores, pairs = [], []
        for a in steps:
            dscores.append([])
            pairs.append([])
            for b in range(a + 1 + MAXL):
                probs = weights[a][b] * inverses[a]
                dscore = (probs * (dprobs[a][b] - deltas[a])).astype(BF16)
                dscores[a].append(dscore)
                wide = jnp.concatenate([dscore, probs.astype(BF16)], axis=1)
                pairs[a].append(nn(wide, both[a]))
        for b in steps:
            total = pairs[b][b]
            for a in range(b + 1, blocks):
                total = total + pairs[a][b]
            dk_all[h, spans[b]] = total[:, :DH] * scaling
            dv_all[h, spans[b]] = total[:, DH:]
        for e in range(entries):
            pair = pairs[e // MAXL][e // MAXL + 1 + e % MAXL]
            dkey, dvalue = (pair[:, :DH] * scaling).astype(BF16), pair[:, DH:].astype(BF16)
            if pieces:
                owner, offset = listed(ints_ref, e, entries)
                distance = owner ^ ints_ref[0]
                at = (distance & 1) * blocks + offset
                payloads[h][at, distance >> 1, :, :DH] += dkey
                payloads[h][at, distance >> 1, :, DH:] += dvalue
            else:
                outs[0][e, :, 2 * h * DH : (2 * h + 1) * DH] = dkey
                outs[0][e, :, (2 * h + 1) * DH : (2 * h + 2) * DH] = dvalue
        halves = []
        for a in steps:
            wide, tall = jnp.concatenate(dscores[a], axis=0), jnp.concatenate(keys[a], axis=0)
            halves.append(split(tn(wide, tall) * scaling))
        for a in steps:
            dq_top, dq_low = halves[a]
            dq_all[h, spans[a]] = nt(dq_top, local_ref[a, h]).astype(BF16)
            query = query_ref[spans[a], lanes]
            query = jnp.concatenate([query, query], axis=0)
            dcum_all[h, a] = tn(query, jnp.concatenate([dq_top, dq_low], axis=0))
        for i, (source, where) in enumerate(
            (
                (dk_all.at[h], dk_ref.at[:, lanes]),
                (dv_all.at[h], dv_ref.at[:, lanes]),
                (dq_all.at[h], dq_ref.at[:, lanes]),
                (dcum_all.at[h], dcum_ref.at[:, h]),
            )
        ):
            copy = pltpu.make_async_copy(source, where, grad_sems.at[i, h])
            copy.start()
            out_copies.append(copy)
        for i, (first, size) in enumerate(pieces):
            where = outs[i].at[:, :, :, 2 * h * DH : (2 * h + 2) * DH]
            source = payloads[h].at[pl.ds(first, size)]
            copy = pltpu.make_async_copy(source, where, out_sems.at[i, h])
            copy.start()
            out_copies.append(copy)
    for copy in out_copies:
        copy.wait()


def run_attend(ints, sources, places, arrays, heads, blocks, pieces):
    rows, width = arrays[0].shape
    entries = blocks * MAXL
    any_spec = pl.BlockSpec(memory_space=pl.ANY)
    scratch = [
        pltpu.VMEM((heads, rows, DH), BF16),
        pltpu.VMEM((heads, blocks, DH, DH), F32),
        pltpu.VMEM((heads, rows, DH), F32),
        pltpu.VMEM((heads, rows, DH), F32),
        pltpu.SemaphoreType.DMA((4, heads)),
        pltpu.VMEM((entries, BLK, width), BF16),
        pltpu.VMEM((entries, BLK, width), BF16),
        pltpu.SemaphoreType.DMA((2, entries)),
    ]
    if pieces:
        chips = len(places) // 2
        out_parts = [
            pltpu.HBM((size, chips, BLK, 2 * width), BF16) for _, size in pieces
        ]
        part_specs = [any_spec] * len(pieces)
        scratch += [pltpu.VMEM((2 * blocks, chips, BLK, 2 * DH), BF16)] * heads
        scratch += [pltpu.SemaphoreType.DMA((len(pieces), heads))]
    else:
        out_parts = [jax.ShapeDtypeStruct((entries, BLK, 2 * width), BF16)]
        part_specs = in_vmem(1)
    return pl.pallas_call(
        functools.partial(attend_kernel, heads, blocks, places, pieces),
        out_shape=[
            pltpu.HBM((rows, width), BF16),
            pltpu.HBM((blocks, heads, DH, DH), F32),
            pltpu.HBM((rows, width), F32),
            pltpu.HBM((rows, width), F32),
        ]
        + out_parts,
        in_specs=in_smem(1) + [any_spec] * len(sources) + in_vmem(7),
        out_specs=[pl.BlockSpec(memory_space=pltpu.HBM)] * 4 + part_specs,
        scratch_shapes=scratch,
        compiler_params=grant(36),
        cost_estimate=cost(15),
        name="attend",
    )(ints, *sources, *arrays)


def merge_kernel(own_ref, got_ref, *refs):
    for i, ref in enumerate(refs[-3:]):
        total = own_ref[0, i + 1].astype(F32) + got_ref[0, i + 1].astype(F32)
        ref[0] = total.astype(BF16)


def run_merge(own, got, first, size, afters):
    _, chips, rows, width = own.shape
    cut = 2
    lanes = width // cut
    whole = pl.BlockSpec((1, chips, rows, lanes), lambda j, c: (first + j, 0, 0, c))
    return pl.pallas_call(
        merge_kernel,
        grid=(size, cut),
        out_shape=[jax.ShapeDtypeStruct((size, rows, width), BF16)] * (chips - 1),
        in_specs=[whole] * 2
        + [pl.BlockSpec((1, 16, 128), lambda j, c: (0, 0, 0))] * len(afters),
        out_specs=[pl.BlockSpec((1, rows, lanes), lambda j, c: (j, 0, c))] * (chips - 1),
        compiler_params=grant(60),
        cost_estimate=cost(2),
        name="merge",
    )(own, got, *afters)


def project_kernel(heads, parts, size, groups, before, layout, afters, flip_ref, *refs):
    refs = refs[afters:]
    outs = len(layout)
    chunks = [(m, i, at) for i, row in enumerate(layout) for at, m in enumerate(row)]
    tiles, sems = refs[-2:]
    per = tiles.shape[0] // len(chunks)
    tile = tiles.shape[2]
    part_refs, refs = refs[: size * parts], refs[size * parts :]
    before_refs, refs = refs[:before], refs[before:]
    dk_loc, dv_loc, dq_ref, key_ref, dcum_in, cum_ref = refs[:6]
    weight_refs, out_refs = refs[6:9], refs[9 : 9 + outs]
    dcum_out, dk_out, dv_out = refs[9 + outs : 12 + outs]
    copies = []
    for t in range(len(chunks) * per):
        m = chunks[t // per][0]
        row = ((m + flip_ref[0] * (groups - 1 - 2 * m)) * per + t % per) * tile
        rows = pl.ds(pl.multiple_of(row, tile), tile)
        for w, ref in enumerate(weight_refs):
            copy = pltpu.make_async_copy(ref.at[rows], tiles.at[t, w], sems.at[t, w])
            copy.start()
            copies.append(copy)

    earlier = ()
    dk_rows, dv_rows = [], []
    for j in range(size):
        here = slice(j * BLK, (j + 1) * BLK)
        dk, dv = [], []
        for h in range(heads):
            both = slice(2 * h * DH, (2 * h + 2) * DH)
            total = part_refs[j * parts][0, :, both].astype(F32)
            for ref in part_refs[j * parts + 1 : (j + 1) * parts]:
                total = total + ref[0, :, both].astype(F32)
            dv.append((dv_loc[here, head(h)] + total[:, DH:]).astype(BF16))
            dk_top, dk_low = split(dk_loc[here, head(h)] + total[:, :DH])
            dk.append(nt(dk_top, cum_ref[j, h]).astype(BF16))
            key = key_ref[here, head(h)]
            key = jnp.concatenate([key, key], axis=0)
            dcum = tn(key, jnp.concatenate([dk_top, dk_low], axis=0))
            dcum_out[j, h] = dcum_in[j, h] + dcum
        dk_rows.append(jnp.concatenate(dk, axis=1))
        dv_rows.append(jnp.concatenate(dv, axis=1))
    dk_all, dv_all = jnp.concatenate(dk_rows, axis=0), jnp.concatenate(dv_rows, axis=0)
    dk_out[...] = dk_all
    dv_out[...] = dv_all
    grads = (dq_ref[...], dk_all, dv_all)
    if before:
        earlier = [
            jnp.concatenate([old[...], new], axis=0) for old, new in zip(before_refs, grads)
        ]

    for t in range(len(chunks) * per):
        term = None
        m, out, at = chunks[t // per]
        for w, grad in enumerate(earlier if before and m == 0 else grads):
            copies[3 * t + w].wait()
            part = nt(tiles[t, w], grad)
            term = part if term is None else term + part
        spot = slice(t % per * tile, (t % per + 1) * tile)
        out_refs[out][at, :, spot] = term.T.astype(BF16)


def run_project(block, groups, layout, flip, afters, parts, before, arrays, weights):
    dk_loc, dv_loc, dq, key_rows, dcum, cum = arrays
    size, width = len(parts), dq.shape[1]
    heads = width // DH
    model = weights[0].shape[0]
    chunk = model // groups
    tile = min(512, chunk)
    rows = size * BLK
    tile_count = sum(map(len, layout)) * chunk // tile

    def part_spec(index):
        return pl.BlockSpec((1, BLK, 2 * width), lambda t: (index, 0, 0))

    def whole(*shape):
        return pl.BlockSpec(shape, lambda t: (0,) * len(shape))

    rows_spec = pl.BlockSpec((rows, width), lambda t: (block // size, 0))
    head_spec = pl.BlockSpec((size, heads, DH, DH), lambda t: (block // size, 0, 0, 0))
    flat = [part for row in parts for part in row]
    heights = [2 * rows if before and row == (0,) else rows for row in layout]
    shapes = [(len(row), height, chunk) for row, height in zip(layout, heights)]
    return pl.pallas_call(
        functools.partial(
            project_kernel,
            heads,
            len(parts[0]),
            size,
            groups,
            len(before),
            layout,
            len(afters),
        ),
        grid=(1,),
        in_specs=in_smem(1)
        + [whole(1, 16, 128)] * len(afters)
        + [part_spec(index) for _, index in flat]
        + [whole(rows, width)] * len(before)
        + [rows_spec] * 4
        + [head_spec] * 2
        + [pl.BlockSpec(memory_space=pl.ANY)] * 3,
        out_specs=[whole(*shape) for shape in shapes]
        + [whole(size, heads, DH, DH)]
        + [whole(rows, width)] * 2,
        scratch_shapes=[
            pltpu.VMEM((tile_count, 3, tile, width), BF16),
            pltpu.SemaphoreType.DMA((tile_count, 3)),
        ],
        out_shape=[jax.ShapeDtypeStruct(shape, BF16) for shape in shapes]
        + [jax.ShapeDtypeStruct((size, heads, DH, DH), F32)]
        + [jax.ShapeDtypeStruct((rows, width), BF16)] * 2,
        compiler_params=grant(60),
        cost_estimate=cost(3 * sum(map(len, layout))),
        name="project",
    )(
        flip,
        *afters,
        *[part for part, _ in flat],
        *before,
        dk_loc,
        dv_loc,
        dq,
        key_rows,
        dcum,
        cum,
        *weights,
    )


def adjoint_kernel(heads, blocks, afters, ints_ref, *refs):
    refs = refs[afters:]
    dcums = [ref.at[j] for ref in refs[:-4] for j in range(ref.shape[0])]
    unit_ref, rows_ref, inv_ref, out_ref = refs[-4:]
    count, width = unit_ref.shape
    stacked = (blocks * count, count)
    eye = (iota((count, count), 0) == iota((count, count), 1)).astype(F32)
    base = ints_ref[0] * blocks
    level, col = iota(stacked, 0), iota(stacked, 1)
    row = level % count
    mine = base + level // count
    alive = row[:, :1] <= mine[:, :1]
    for h in range(heads):
        units, rows, inverse = unit_ref[:, head(h)], rows_ref[:, head(h)], inv_ref[h]
        inverse_t = nt_high(eye, inverse)
        moved = jnp.concatenate([nt_high(rows, dcum[h]) for dcum in dcums], axis=0)
        overlap = jnp.where(col <= mine, nt_high(moved, units), 0.0)
        gamma = nn_high(overlap, inverse)
        gamma = jnp.where((row < col) & (col <= mine), gamma, 0.0)
        beta = jnp.concatenate([eye - inverse_t] * blocks, axis=0)
        beta = jnp.where(col <= mine, beta, 0.0)
        x_all = jnp.where(alive, moved - 2.0 * nn_high(gamma, units), 0.0)
        turned = jnp.concatenate([units] * blocks, axis=0) - nn_high(beta, units)
        turned = jnp.where(alive, turned, 0.0)
        x_total, y_total = None, None
        for j, dcum in enumerate(dcums):
            here = slice(j * count, (j + 1) * count)
            y_part = nn_high(turned[here], dcum[h])
            x_total = x_all[here] if j == 0 else x_total + x_all[here]
            y_total = y_part if j == 0 else y_total + y_part
        out_ref[:, head(h)] = x_total
        out_ref[:, slice(width + h * DH, width + (h + 1) * DH)] = y_total


def run_adjoint(ints, afters, dcums, unit, rows, inverse, heads, blocks):
    count, width = unit.shape
    return pl.pallas_call(
        functools.partial(adjoint_kernel, heads, blocks, len(afters)),
        out_shape=jax.ShapeDtypeStruct((count, 2 * width), F32),
        in_specs=in_smem(1)
        + [pl.BlockSpec(memory_space=pl.ANY)] * len(afters)
        + in_vmem(len(dcums) + 3),
        out_specs=pl.BlockSpec(memory_space=pltpu.VMEM),
        compiler_params=grant(60),
        cost_estimate=cost(2),
        name="adjoint",
    )(ints, *afters, *dcums, unit, rows, inverse)


def house_kernel(heads, blocks, base_ref, got_ref, unit_ref, rows_ref, house_ref, out_ref):
    count, width = unit_ref.shape
    total = jnp.sum(got_ref[...], axis=0)
    for h in range(heads):
        x_part = total[:, head(h)]
        y_part = total[:, slice(width + h * DH, width + (h + 1) * DH)]
        along = nt_high(y_part, rows_ref[:, head(h)])
        spot = iota((blocks, count), 0) + base_ref[0] * blocks
        along = jnp.where(iota((blocks, count), 1) < spot, along, 0.0)
        turned = y_part - 2.0 * nn_high(along, unit_ref[:, head(h)])
        dunit = -2.0 * (x_part + turned)
        house = house_ref[:, head(h)]
        lengths = jnp.sqrt(jnp.sum(house * house, axis=1, keepdims=True) + 1e-06)
        unit = house / lengths
        inner = jnp.sum(unit * dunit, axis=1, keepdims=True)
        out_ref[:, head(h)] = (dunit - unit * inner) / lengths


def run_house(ints, got, unit, rows, house_dirs, heads, blocks):
    return pl.pallas_call(
        functools.partial(house_kernel, heads, blocks),
        out_shape=jax.ShapeDtypeStruct(house_dirs.shape, F32),
        in_specs=in_smem(1) + in_vmem(4),
        out_specs=pl.BlockSpec(memory_space=pltpu.VMEM),
        compiler_params=grant(60),
        cost_estimate=cost(2),
        name="house_grad",
    )(ints, got, unit, rows, house_dirs)


def hop(value, distance, count):
    return lax.ppermute(value, "ctx", [(i, i ^ distance) for i in range(count)])


def slide(value, pairs):
    return lax.ppermute(value, "head", pairs)


INWARD = [(0, 1), (3, 2)]
MIDDLE = [(1, 2), (2, 1)]
OUTWARD = [(1, 0), (2, 3)]


def near_kernel(ends_ref, first_ref, near_ref, inward_ref, out_ref):
    mine = jnp.where(ends_ref[0] > 0, first_ref[0], near_ref[0]).astype(F32)
    out_ref[...] = mine + inward_ref[0].astype(F32)


def run_near(ends, first, near, inward):
    _, rows, width = first.shape
    return pl.pallas_call(
        near_kernel,
        grid=(1,),
        out_shape=jax.ShapeDtypeStruct((rows, width), F32),
        in_specs=in_smem(1) + [pl.BlockSpec((1, rows, width), lambda t: (0, 0, 0))] * 3,
        out_specs=pl.BlockSpec((rows, width), lambda t: (0, 0)),
        compiler_params=grant(60),
        cost_estimate=cost(5),
        name="near_sum",
    )(ends, first, near, inward)


def share_kernel(*refs):
    total_ref, far_ref, outward_ref, out_ref = refs[-4:]
    far = far_ref[0].astype(F32) + outward_ref[0].astype(F32)
    out_ref[...] = (total_ref[...] + far).astype(BF16)


def run_share(share, band, bands, total, far, outward):
    rows, width = total.shape
    tile = min(512, width)
    part = pl.BlockSpec((1, rows, tile), lambda t: (0, 0, t))
    given = [] if share is None else [share]
    return pl.pallas_call(
        share_kernel,
        grid=(width // tile,),
        out_shape=jax.ShapeDtypeStruct((bands * rows, width), BF16),
        in_specs=[pl.BlockSpec(memory_space=pl.ANY)] * len(given)
        + [pl.BlockSpec((rows, tile), lambda t: (0, t)), part, part],
        out_specs=pl.BlockSpec((rows, tile), lambda t: (band, t)),
        input_output_aliases={0: 0} if given else {},
        compiler_params=grant(60),
        cost_estimate=cost(2),
        name="share",
    )(*given, total, far, outward)


def line_ends():
    place = lax.axis_index("head")
    return ((place == 0) | (place == 3)).astype(jnp.int32).reshape(1)


def line_scatter(share, band, bands, first, rest, inward, inner):
    swapped = slide(inner, MIDDLE)
    outer = first + swapped[1:]
    outward = slide(outer, OUTWARD)
    total = run_near(line_ends(), first, rest, inward)
    return run_share(share, band, bands, total, swapped, outward), swapped, outer


def line_scatter_apart(share, band, bands, first, near, far, last, ready, exchange, earlier):
    in_last, in_far, in_near = slide(last, INWARD), slide(far, INWARD), slide(near, INWARD)
    in_last, ready = lax.optimization_barrier((in_last, ready))
    sum_last = last + in_last
    ready, *_ = lax.optimization_barrier((ready, sum_last, earlier))
    got = exchange(ready)
    swap_last = slide(sum_last, MIDDLE)
    in_far, got = lax.optimization_barrier((in_far, got))
    sum_far = far + in_far
    swap_far = slide(sum_far, MIDDLE)
    outward = slide(first + swap_last, OUTWARD)
    in_near, _ = lax.optimization_barrier((in_near, sum_far))
    total = run_near(line_ends(), first, near, in_near)
    return run_share(share, band, bands, total, swap_far, outward), got


def shards(
    query_rows, key_rows, value_rows, grad_out, house_dirs, owners, offsets, w_query, w_key, w_value
):
    tok_rows, width = query_rows.shape
    heads, blocks = width // DH, tok_rows // BLK
    ctx_count, groups = lax.axis_size("ctx"), lax.axis_size("head")
    my_index = lax.axis_index("ctx").astype(jnp.int32)
    ints = jnp.concatenate([my_index.reshape(1), owners.reshape(-1), offsets.reshape(-1)])
    by_hand = ctx_count == 8 and groups == 4 and blocks == 4
    core, across, along = 1, 2, 4

    if by_hand:
        other = hop(house_dirs, core, 8)
        upper = (my_index & core) != 0
        low, high = jnp.where(upper, other, house_dirs), jnp.where(upper, house_dirs, other)
        house_pair = jnp.concatenate([low, high], axis=0)
        value_x, key_y = hop(value_rows, across, 8), hop(key_rows, along, 8)
        key_x, value_y = hop(key_rows, across, 8), hop(value_rows, along, 8)
        house_late, *_ = lax.optimization_barrier((house_pair, value_x, key_y))
        house_parts = [house_pair] + [hop(house_late, t, 8) for t in (2, 4, 6)]
        key_d, value_d = hop(key_y, across, 8), hop(value_x, along, 8)
    else:
        house_parts = [lax.all_gather(house_dirs, "ctx", axis=0, tiled=True)]

    unit, rows, inverse, wide, tall = run_chain(ints, house_parts, heads)
    ready = query_rows
    if by_hand:
        own = (key_rows, value_rows, key_x, value_x, key_y, value_y, key_d, value_d)
        early = lax.optimization_barrier((*own[:6], *house_parts))[:6]
        siblings = [hop(part, core, 8) for part in early]
        ready, *_ = lax.optimization_barrier((query_rows, *siblings[:3]))
    qrot, krot, local, listed_cum = run_rotate(ints, wide, tall, ready, key_rows, heads, blocks)
    if by_hand:
        late = lax.optimization_barrier((*own[6:], qrot))[:2]
        siblings += [hop(part, core, 8) for part in late]
        sources, places = [], []
        for t in range(4):
            for pair in (own[2 * t : 2 * t + 2], siblings[2 * t : 2 * t + 2]):
                places.append(((len(sources), 0), (len(sources) + 1, 0)))
                sources += pair
    else:
        sources = [lax.all_gather(key_rows, "ctx"), lax.all_gather(value_rows, "ctx")]
        places = [((0, 0), (1, 0))]

    rounds = ((0, 1), (1, blocks - 1), (blocks, 1), (blocks + 1, blocks - 1))
    dq, dcum, dk_loc, dv_loc, *outs = run_attend(
        ints,
        sources,
        places,
        (query_rows, qrot, krot, value_rows, grad_out, local, listed_cum),
        heads,
        blocks,
        rounds if by_hand else (),
    )
    weights = (w_query, w_key, w_value)
    flip = jnp.where(by_hand & (lax.axis_index("head") >= 2), 1, 0).astype(jnp.int32).reshape(1)

    arrays = (dk_loc, dv_loc, dq, key_rows, dcum, local)

    def project(block, layout, afters, parts, before=()):
        return run_project(block, groups, layout, flip, afters, parts, before, arrays, weights)

    def share_sums(sums):
        sums = sums.reshape(ctx_count, blocks, 2 * width)
        return lax.all_to_all(sums, "ctx", split_axis=0, concat_axis=0, tiled=True)

    if by_hand:
        got_0 = hop(outs[2], core, 8)
        got_1 = hop(lax.optimization_barrier((outs[3], got_0))[0], core, 8)
        sent_0 = run_merge(outs[0], got_0, 0, 1, [])
        sent_1 = run_merge(outs[1], got_1, 0, 1, [sent_0[0]])
        sent_2 = run_merge(outs[1], got_1, 1, 2, [sent_1[0]])

        def give_back(own, got, first, sent):
            back = [hop(part, t, 8) for part, t in zip(sent, (across, along, across + along))]
            near = [part.reshape(-1, BLK, 2 * width) for part in (own, got)]
            parts = []
            for j in range(sent[0].shape[0]):
                mine = [(part, 4 * (first + j)) for part in near]
                parts.append(mine + [(part, j) for part in back])
            return parts, back

        parts_0, back_0 = give_back(outs[0], got_0, 0, sent_0)
        *later_1, _, _ = lax.optimization_barrier((*sent_1, back_0, sent_2))
        parts_1, back_1 = give_back(outs[1], got_1, 0, later_1)
        *later_2, _ = lax.optimization_barrier((*sent_2, back_1))
        parts_2, _ = give_back(outs[1], got_1, 1, later_2)
        rest_0, dcum_0, *grads_0 = project(0, ((1, 2, 3),), [sent_2[0]], parts_0)
        before = (dq, *grads_0)
        split_off = ((0,), (1, 2, 3))
        firsts, rest_1, dcum_1, *_ = project(1, split_off, [rest_0], parts_1, before)
        inward_0, inward_1 = slide(rest_0, INWARD), slide(rest_1, INWARD)
        apart = ((0,), (1,), (2,), (3,))
        *terms, dcum_2, _, _ = project(2, apart, [rest_1], parts_2)
        share, swapped_0, outer_0 = line_scatter(
            None, 0, 4, firsts[:, :BLK], rest_0, inward_0, rest_0[1:] + inward_0[1:]
        )
        inward_1, *_ = lax.optimization_barrier((inward_1, swapped_0, dcum_2))
        sum_1 = rest_1[1:] + inward_1[1:]
        share, _, outer_1 = line_scatter(
            share, 1, 4, firsts[:, BLK:], rest_1, inward_1, sum_1
        )
        dcums = [dcum_0, dcum_1, dcum_2]
        sums = run_adjoint(ints, (sum_1, outer_0), dcums, unit, rows, inverse, heads, blocks)
        share, got = line_scatter_apart(
            share, 1, 2, *terms, sums, share_sums, outer_1
        )
    else:
        spots = (owners * blocks + offsets).reshape(-1)
        empty = jnp.zeros((ctx_count * blocks, BLK, 2 * width), BF16)
        filled = empty.at[spots].add(outs[0])
        back = lax.psum_scatter(filled, "ctx", scatter_dimension=0, tiled=True)
        dcums = []
        share = jnp.zeros((tok_rows, w_query.shape[0] // groups), BF16)
        for j in range(blocks):
            term, dcum_out, _, _ = project(
                j, (tuple(range(groups)),), [], [[(back, j)]]
            )
            dcums.append(dcum_out)
            done = lax.psum_scatter(term, "head", scatter_dimension=0, tiled=False)
            share = lax.dynamic_update_slice(share, done, (j * BLK, 0))

        got = share_sums(run_adjoint(ints, (), dcums, unit, rows, inverse, heads, blocks))

    house_grad = run_house(ints, got, unit, rows, house_dirs, heads, blocks)
    return (share, house_grad)


def solution(mesh):
    placed = (
        P("ctx", "head"),
        P("ctx", "head"),
        P("ctx", "head"),
        P("ctx", "head"),
        P("ctx", "head"),
        P("ctx", None),
        P("ctx", None),
        P(None, "head"),
        P(None, "head"),
        P(None, "head"),
    )
    return jax.shard_map(
        shards,
        mesh=mesh,
        in_specs=placed,
        out_specs=(P("ctx", "head"), P("ctx", "head")),
        check_vma=False,
    )
```

```python
import functools
import math

import jax
import jax.numpy as jnp
from jax import lax
from jax.experimental import pallas as pl
from jax.experimental.pallas import tpu as pltpu
from jax.sharding import PartitionSpec as P

DH = 128
BLK = 128
MAXL = 2
HIGH = lax.Precision.HIGHEST
F32 = jnp.float32
BF16 = jnp.bfloat16


def nn(a, b):
    return lax.dot_general(a, b, (((1,), (0,)), ((), ())), preferred_element_type=F32)


def nt(a, b):
    return lax.dot_general(a, b, (((1,), (1,)), ((), ())), preferred_element_type=F32)


def tn(a, b):
    return lax.dot_general(a, b, (((0,), (0,)), ((), ())), preferred_element_type=F32)


def nn_high(a, b):
    return lax.dot_general(
        a, b, (((1,), (0,)), ((), ())), precision=HIGH, preferred_element_type=F32
    )


def nt_high(a, b):
    return lax.dot_general(
        a, b, (((1,), (1,)), ((), ())), precision=HIGH, preferred_element_type=F32
    )


def split(value):
    top = value.astype(BF16)
    return top, (value - top.astype(F32)).astype(BF16)


def iota(shape, dim):
    return lax.broadcasted_iota(jnp.int32, shape, dim)


def head(h):
    return slice(h * DH, (h + 1) * DH)


def listed(ints_ref, entry, entries):
    return ints_ref[1 + entry], ints_ref[1 + entries + entry]


def grant(mebibytes):
    return pltpu.CompilerParams(vmem_limit_bytes=mebibytes * 1024 * 1024)


def cost(microseconds):
    return pl.CostEstimate(
        flops=int(microseconds * 1.15e9), bytes_accessed=1 << 20, transcendentals=0
    )


def in_smem(count):
    return [pl.BlockSpec(memory_space=pltpu.SMEM)] * count


def in_vmem(count):
    return [pl.BlockSpec(memory_space=pltpu.VMEM)] * count


def chain_kernel(heads, parts, ints_ref, *refs):
    house_refs = refs[:parts]
    unit_ref, rows_ref, inv_ref, wide_ref, tall_ref, unit_h, house_all = refs[parts:]
    count = unit_ref.shape[0]
    span = count // parts
    for t, ref in enumerate(house_refs):
        place = (ints_ref[0] // (8 // parts)) ^ t if parts > 1 else 0
        house_all[pl.ds(pl.multiple_of(place * span, span), span), :] = ref[...]
    eye = (iota((count, count), 0) == iota((count, count), 1)).astype(F32)
    for h in range(heads):
        house = house_all[:, head(h)]
        lengths = jnp.sqrt(jnp.sum(house * house, axis=1, keepdims=True) + 1e-06)
        unit_ref[:, head(h)] = house / lengths
        unit_h[h] = house / lengths
        inv_ref[h] = eye

    def eliminate(step, carry):
        below = iota((count, 1), 0) > step
        for h in range(heads):
            pivot = unit_h[h, pl.ds(step, 1), :]
            overlap = jnp.sum(unit_h[h] * pivot, axis=1, keepdims=True)
            factor = jnp.where(below, 2.0 * overlap, 0.0)
            inv_ref[h] = inv_ref[h] - factor * inv_ref[h, pl.ds(step, 1), :]
        return carry

    lax.fori_loop(0, count, eliminate, 0)
    eye_wide = (iota((DH, DH), 0) == iota((DH, DH), 1)).astype(F32)
    for h in range(heads):
        units = unit_ref[:, head(h)]
        rows = nn_high(inv_ref[h], units)
        rows_ref[:, head(h)] = rows
        unit_hi, unit_lo = split(nt_high(eye_wide, units))
        rows_hi, rows_lo = split(rows)
        wide_ref[h] = jnp.concatenate([unit_hi, unit_hi, unit_lo], axis=1)
        tall_ref[h] = jnp.concatenate([rows_hi, rows_lo, rows_hi], axis=0)


def run_chain(ints, house_parts, heads):
    span, width = house_parts[0].shape
    parts = len(house_parts)
    count = span * parts
    return pl.pallas_call(
        functools.partial(chain_kernel, heads, parts),
        out_shape=[
            jax.ShapeDtypeStruct((count, width), F32),
            jax.ShapeDtypeStruct((count, width), F32),
            jax.ShapeDtypeStruct((heads, count, count), F32),
            jax.ShapeDtypeStruct((heads, DH, 3 * count), BF16),
            jax.ShapeDtypeStruct((heads, 3 * count, DH), BF16),
        ],
        in_specs=in_smem(1) + in_vmem(parts),
        out_specs=in_vmem(5),
        scratch_shapes=[pltpu.VMEM((heads, count, DH), F32), pltpu.VMEM((count, width), F32)],
        compiler_params=grant(12),
        cost_estimate=cost(6),
        name="house_chain",
    )(ints, *house_parts)


def rotate_kernel(
    heads,
    blocks,
    ints_ref,
    wide_ref,
    tall_ref,
    query_ref,
    key_ref,
    qrot_ref,
    krot_ref,
    local_ref,
    listed_ref,
):
    count = wide_ref.shape[2] // 3
    entries = blocks * MAXL
    column = iota((DH, 3 * count), 1) % count
    eye = (iota((DH, DH), 0) == iota((DH, DH), 1)).astype(F32)

    def cumulative(h, block):
        kept = jnp.where(column <= block, wide_ref[h].astype(F32), 0.0).astype(BF16)
        return split(eye - 2.0 * nn(kept, tall_ref[h]))

    base = ints_ref[0] * blocks

    def local_block(b, carry):
        here = pl.ds(pl.multiple_of(b * BLK, BLK), BLK)
        for h in range(heads):
            hi, lo = cumulative(h, base + b)
            local_ref[b, h] = hi
            query, key = query_ref[here, head(h)], key_ref[here, head(h)]
            qrot_ref[here, head(h)] = (nn(query, hi) + nn(query, lo)).astype(BF16)
            krot_ref[here, head(h)] = (nn(key, hi) + nn(key, lo)).astype(BF16)
        return carry

    lax.fori_loop(0, blocks, local_block, 0)

    def listed_block(e, carry):
        owner, offset = listed(ints_ref, e, entries)
        for h in range(heads):
            hi, lo = cumulative(h, owner * blocks + offset)
            listed_ref[e, h, :DH] = hi
            listed_ref[e, h, DH:] = lo
        return carry

    lax.fori_loop(0, entries, listed_block, 0)


def run_rotate(ints, wide, tall, query_rows, key_rows, heads, blocks):
    rows, width = query_rows.shape
    entries = blocks * MAXL
    return pl.pallas_call(
        functools.partial(rotate_kernel, heads, blocks),
        out_shape=[
            jax.ShapeDtypeStruct((rows, width), BF16),
            jax.ShapeDtypeStruct((rows, width), BF16),
            jax.ShapeDtypeStruct((blocks, heads, DH, DH), BF16),
            jax.ShapeDtypeStruct((entries, heads, 2 * DH, DH), BF16),
        ],
        in_specs=in_smem(1) + in_vmem(4),
        out_specs=in_vmem(4),
        compiler_params=grant(16),
        cost_estimate=cost(9),
        name="rotate",
    )(ints, wide, tall, query_rows, key_rows)


def attend_kernel(heads, blocks, places, pieces, *refs):
    ints_ref = refs[0]
    source_count = 1 + max(place[0] for pair in places for place in pair)
    sources = refs[1 : 1 + source_count]
    refs = refs[1 + source_count :]
    (query_ref, qrot_ref, krot_ref, value_ref, grad_ref, local_ref, listed_ref) = refs[:7]
    dq_ref, dcum_ref, dk_ref, dv_ref = refs[7:11]
    outs = refs[11 : 11 + max(len(pieces), 1)]
    refs = refs[11 + max(len(pieces), 1) :]
    dq_all, dcum_all, dk_all, dv_all, grad_sems, far_keys, far_values, sems = refs[:8]
    entries = blocks * MAXL
    scaling = DH ** (-0.5)
    log_scale = scaling * math.log2(math.e)

    def start(e, src, kind, slot, where):
        pltpu.make_async_copy(src.at[where], slot.at[e], sems.at[kind, e]).start()

    for e in range(entries):
        owner, offset = listed(ints_ref, e, entries)
        row = pl.multiple_of(offset * BLK, BLK)
        if len(places) == 1:
            start(e, sources[0], 0, far_keys, (owner, pl.ds(row, BLK)))
            start(e, sources[1], 1, far_values, (owner, pl.ds(row, BLK)))
        else:
            distance = owner ^ ints_ref[0]
            for r, (key_place, value_place) in enumerate(places):

                @pl.when(distance == r)
                def _():
                    source, first = key_place
                    start(e, sources[source], 0, far_keys, pl.ds(first + row, BLK))
                    source, first = value_place
                    start(e, sources[source], 1, far_values, pl.ds(first + row, BLK))

    out_copies = []
    if pieces:
        payloads, out_sems = refs[8 : 8 + heads], refs[8 + heads]
        for payload in payloads:
            payload[...] = jnp.zeros_like(payload)
    later = iota((BLK, BLK), 0) > iota((BLK, BLK), 1)
    empty = jnp.zeros((BLK, DH), BF16)
    def wait_far():
        for kind, slots in ((0, far_keys), (1, far_values)):
            for e in range(entries):
                pltpu.make_async_copy(slots.at[e], slots.at[e], sems.at[kind, e]).wait()

    spans = [slice(a * BLK, (a + 1) * BLK) for a in range(blocks)]
    group = 2 if heads % 2 == 0 else 1
    for start_head in range(0, heads, group):
        steps = [(h, a) for h in range(start_head, start_head + group) for a in range(blocks)]
        both, keys, values, scores, dprobs, tops = {}, {}, {}, {}, {}, {}

        def score(step, b, key, value):
            pair = nt(jnp.concatenate([key, value], axis=1), both[step])
            part = pair[:, :BLK] * log_scale
            if b == step[1]:
                part = jnp.where(later, -jnp.inf, part)
            keys[step].append(key)
            scores[step].append(part)
            dprobs[step].append(pair[:, BLK:])
            tops[step] = part if b == 0 else jnp.maximum(tops[step], part)

        for step in steps:
            h, a = step
            lanes = head(h)
            qrot, grad = qrot_ref[spans[a], lanes], grad_ref[spans[a], lanes]
            upper = jnp.concatenate([qrot, empty], axis=1)
            lower = jnp.concatenate([empty, grad], axis=1)
            both[step] = jnp.concatenate([upper, lower], axis=0)
            keys[step], scores[step], dprobs[step] = [], [], []
            for b in range(a + 1):
                score(step, b, krot_ref[spans[b], lanes], value_ref[spans[b], lanes])
        if start_head == 0:
            wait_far()
        for step in steps:
            h, a = step
            for l in range(MAXL):
                e = a * MAXL + l
                raw = far_keys[e, :, head(h)]
                raw = jnp.concatenate([raw, raw], axis=1)
                key = nn(raw, listed_ref[e, h]).astype(BF16)
                score(step, a + 1 + l, key, far_values[e, :, head(h)])
        weights, inverses, deltas = {}, {}, {}
        for step in steps:
            top = jnp.max(tops[step], axis=0, keepdims=True)
            weights[step] = []
            total, inner = None, None
            for part, dprob in zip(scores[step], dprobs[step]):
                weight = jnp.exp2(part - top)
                weights[step].append(weight)
                product = weight * dprob
                total = weight if total is None else total + weight
                inner = product if inner is None else inner + product
            inverses[step] = 1.0 / jnp.sum(total, axis=0, keepdims=True)
            deltas[step] = jnp.sum(inner, axis=0, keepdims=True) * inverses[step]
        dscores, pairs = {}, {}
        for step in steps:
            dscores[step], pairs[step] = [], []
            for weight, dprob in zip(weights[step], dprobs[step]):
                probs = weight * inverses[step]
                dscore = (probs * (dprob - deltas[step])).astype(BF16)
                dscores[step].append(dscore)
                wide = jnp.concatenate([dscore, probs.astype(BF16)], axis=1)
                pairs[step].append(nn(wide, both[step]))
        for h, b in steps:
            total = pairs[h, b][b]
            for a in range(b + 1, blocks):
                total = total + pairs[h, a][b]
            dk_all[h, spans[b]] = total[:, :DH] * scaling
            dv_all[h, spans[b]] = total[:, DH:]
        for h, a in steps:
            for l in range(MAXL):
                e = a * MAXL + l
                pair = pairs[h, a][a + 1 + l]
                dkey, dvalue = (pair[:, :DH] * scaling).astype(BF16), pair[:, DH:].astype(BF16)
                if pieces:
                    owner, offset = listed(ints_ref, e, entries)
                    distance = owner ^ ints_ref[0]
                    at = (distance & 1) * blocks + offset
                    payloads[h][at, distance >> 1, :, :DH] += dkey
                    payloads[h][at, distance >> 1, :, DH:] += dvalue
                else:
                    outs[0][e, :, 2 * h * DH : (2 * h + 1) * DH] = dkey
                    outs[0][e, :, (2 * h + 1) * DH : (2 * h + 2) * DH] = dvalue
        halves = {}
        for step in steps:
            wide = jnp.concatenate(dscores[step], axis=0)
            tall = jnp.concatenate(keys[step], axis=0)
            halves[step] = split(tn(wide, tall) * scaling)
        for h, a in steps:
            dq_top, dq_low = halves[h, a]
            dq_all[h, spans[a]] = nt(dq_top, local_ref[a, h]).astype(BF16)
            query = query_ref[spans[a], head(h)]
            query = jnp.concatenate([query, query], axis=0)
            dcum_all[h, a] = tn(query, jnp.concatenate([dq_top, dq_low], axis=0))
        for h in range(start_head, start_head + group):
            moves = [
                (payloads[h].at[pl.ds(first, size)], outs[i], out_sems.at[i, h])
                for i, (first, size) in enumerate(pieces)
            ]
            moves = [
                (source, where.at[:, :, :, 2 * h * DH : (2 * h + 2) * DH], sem)
                for source, where, sem in moves
            ]
            moves += [
                (dk_all.at[h], dk_ref.at[:, head(h)], grad_sems.at[0, h]),
                (dv_all.at[h], dv_ref.at[:, head(h)], grad_sems.at[1, h]),
                (dq_all.at[h], dq_ref.at[:, head(h)], grad_sems.at[2, h]),
                (dcum_all.at[h], dcum_ref.at[:, h], grad_sems.at[3, h]),
            ]
            for source, where, sem in moves:
                copy = pltpu.make_async_copy(source, where, sem)
                copy.start()
                out_copies.append(copy)
    for copy in out_copies:
        copy.wait()


def run_attend(ints, sources, places, arrays, heads, blocks, pieces):
    rows, width = arrays[0].shape
    entries = blocks * MAXL
    any_spec = pl.BlockSpec(memory_space=pl.ANY)
    scratch = [
        pltpu.VMEM((heads, rows, DH), BF16),
        pltpu.VMEM((heads, blocks, DH, DH), F32),
        pltpu.VMEM((heads, rows, DH), F32),
        pltpu.VMEM((heads, rows, DH), F32),
        pltpu.SemaphoreType.DMA((4, heads)),
        pltpu.VMEM((entries, BLK, width), BF16),
        pltpu.VMEM((entries, BLK, width), BF16),
        pltpu.SemaphoreType.DMA((2, entries)),
    ]
    if pieces:
        chips = len(places) // 2
        out_parts = [
            pltpu.HBM((size, chips, BLK, 2 * width), BF16) for _, size in pieces
        ]
        part_specs = [any_spec] * len(pieces)
        scratch += [pltpu.VMEM((2 * blocks, chips, BLK, 2 * DH), BF16)] * heads
        scratch += [pltpu.SemaphoreType.DMA((len(pieces), heads))]
    else:
        out_parts = [jax.ShapeDtypeStruct((entries, BLK, 2 * width), BF16)]
        part_specs = in_vmem(1)
    return pl.pallas_call(
        functools.partial(attend_kernel, heads, blocks, places, pieces),
        out_shape=[
            pltpu.HBM((rows, width), BF16),
            pltpu.HBM((blocks, heads, DH, DH), F32),
            pltpu.HBM((rows, width), F32),
            pltpu.HBM((rows, width), F32),
        ]
        + out_parts,
        in_specs=in_smem(1) + [any_spec] * len(sources) + in_vmem(7),
        out_specs=[pl.BlockSpec(memory_space=pltpu.HBM)] * 4 + part_specs,
        scratch_shapes=scratch,
        compiler_params=grant(36),
        cost_estimate=cost(15),
        name="attend",
    )(ints, *sources, *arrays)


def merge_kernel(own_ref, got_ref, *refs):
    for i, ref in enumerate(refs[-3:]):
        total = own_ref[0, i + 1].astype(F32) + got_ref[0, i + 1].astype(F32)
        ref[0] = total.astype(BF16)


def run_merge(own, got, first, size, afters):
    _, chips, rows, width = own.shape
    cut = 2
    lanes = width // cut
    whole = pl.BlockSpec((1, chips, rows, lanes), lambda j, c: (first + j, 0, 0, c))
    return pl.pallas_call(
        merge_kernel,
        grid=(size, cut),
        out_shape=[jax.ShapeDtypeStruct((size, rows, width), BF16)] * (chips - 1),
        in_specs=[whole] * 2
        + [pl.BlockSpec((1, 16, 128), lambda j, c: (0, 0, 0))] * len(afters),
        out_specs=[pl.BlockSpec((1, rows, lanes), lambda j, c: (j, 0, c))] * (chips - 1),
        compiler_params=grant(60),
        cost_estimate=cost(2),
        name="merge",
    )(own, got, *afters)


def project_kernel(heads, parts, size, groups, before, layout, afters, flip_ref, *refs):
    refs = refs[afters:]
    outs = len(layout)
    chunks = [(m, i, at) for i, row in enumerate(layout) for at, m in enumerate(row)]
    tiles, sems = refs[-2:]
    per = tiles.shape[0] // len(chunks)
    tile = tiles.shape[2]
    part_refs, refs = refs[: size * parts], refs[size * parts :]
    before_refs, refs = refs[:before], refs[before:]
    dk_loc, dv_loc, dq_ref, key_ref, dcum_in, cum_ref = refs[:6]
    weight_refs, out_refs = refs[6:9], refs[9 : 9 + outs]
    dcum_out, dk_out, dv_out = refs[9 + outs : 12 + outs]
    copies = []
    for t in range(len(chunks) * per):
        m = chunks[t // per][0]
        row = ((m + flip_ref[0] * (groups - 1 - 2 * m)) * per + t % per) * tile
        rows = pl.ds(pl.multiple_of(row, tile), tile)
        for w, ref in enumerate(weight_refs):
            copy = pltpu.make_async_copy(ref.at[rows], tiles.at[t, w], sems.at[t, w])
            copy.start()
            copies.append(copy)

    earlier = ()
    dk_rows, dv_rows = [], []
    for j in range(size):
        here = slice(j * BLK, (j + 1) * BLK)
        dk, dv = [], []
        for h in range(heads):
            both = slice(2 * h * DH, (2 * h + 2) * DH)
            total = part_refs[j * parts][0, :, both].astype(F32)
            for ref in part_refs[j * parts + 1 : (j + 1) * parts]:
                total = total + ref[0, :, both].astype(F32)
            dv.append((dv_loc[here, head(h)] + total[:, DH:]).astype(BF16))
            dk_top, dk_low = split(dk_loc[here, head(h)] + total[:, :DH])
            dk.append(nt(dk_top, cum_ref[j, h]).astype(BF16))
            key = key_ref[here, head(h)]
            key = jnp.concatenate([key, key], axis=0)
            dcum = tn(key, jnp.concatenate([dk_top, dk_low], axis=0))
            dcum_out[j, h] = dcum_in[j, h] + dcum
        dk_rows.append(jnp.concatenate(dk, axis=1))
        dv_rows.append(jnp.concatenate(dv, axis=1))
    dk_all, dv_all = jnp.concatenate(dk_rows, axis=0), jnp.concatenate(dv_rows, axis=0)
    dk_out[...] = dk_all
    dv_out[...] = dv_all
    grads = (dq_ref[...], dk_all, dv_all)
    if before:
        earlier = [
            jnp.concatenate([old[...], new], axis=0) for old, new in zip(before_refs, grads)
        ]

    for t in range(len(chunks) * per):
        term = None
        m, out, at = chunks[t // per]
        for w, grad in enumerate(earlier if before and m == 0 else grads):
            copies[3 * t + w].wait()
            part = nt(tiles[t, w], grad)
            term = part if term is None else term + part
        spot = slice(t % per * tile, (t % per + 1) * tile)
        out_refs[out][at, :, spot] = term.T.astype(BF16)


def run_project(block, groups, layout, flip, afters, parts, before, arrays, weights):
    dk_loc, dv_loc, dq, key_rows, dcum, cum = arrays
    size, width = len(parts), dq.shape[1]
    heads = width // DH
    model = weights[0].shape[0]
    chunk = model // groups
    tile = min(512, chunk)
    rows = size * BLK
    tile_count = sum(map(len, layout)) * chunk // tile

    def part_spec(index):
        return pl.BlockSpec((1, BLK, 2 * width), lambda t: (index, 0, 0))

    def whole(*shape):
        return pl.BlockSpec(shape, lambda t: (0,) * len(shape))

    rows_spec = pl.BlockSpec((rows, width), lambda t: (block // size, 0))
    head_spec = pl.BlockSpec((size, heads, DH, DH), lambda t: (block // size, 0, 0, 0))
    flat = [part for row in parts for part in row]
    heights = [2 * rows if before and row == (0,) else rows for row in layout]
    shapes = [(len(row), height, chunk) for row, height in zip(layout, heights)]
    return pl.pallas_call(
        functools.partial(
            project_kernel,
            heads,
            len(parts[0]),
            size,
            groups,
            len(before),
            layout,
            len(afters),
        ),
        grid=(1,),
        in_specs=in_smem(1)
        + [whole(1, 16, 128)] * len(afters)
        + [part_spec(index) for _, index in flat]
        + [whole(rows, width)] * len(before)
        + [rows_spec] * 4
        + [head_spec] * 2
        + [pl.BlockSpec(memory_space=pl.ANY)] * 3,
        out_specs=[whole(*shape) for shape in shapes]
        + [whole(size, heads, DH, DH)]
        + [whole(rows, width)] * 2,
        scratch_shapes=[
            pltpu.VMEM((tile_count, 3, tile, width), BF16),
            pltpu.SemaphoreType.DMA((tile_count, 3)),
        ],
        out_shape=[jax.ShapeDtypeStruct(shape, BF16) for shape in shapes]
        + [jax.ShapeDtypeStruct((size, heads, DH, DH), F32)]
        + [jax.ShapeDtypeStruct((rows, width), BF16)] * 2,
        compiler_params=grant(60),
        cost_estimate=cost(3 * sum(map(len, layout))),
        name="project",
    )(
        flip,
        *afters,
        *[part for part, _ in flat],
        *before,
        dk_loc,
        dv_loc,
        dq,
        key_rows,
        dcum,
        cum,
        *weights,
    )


def adjoint_kernel(heads, blocks, afters, ints_ref, *refs):
    refs = refs[afters:]
    dcums = [ref.at[j] for ref in refs[:-4] for j in range(ref.shape[0])]
    unit_ref, rows_ref, inv_ref, out_ref = refs[-4:]
    count, width = unit_ref.shape
    stacked = (blocks * count, count)
    eye = (iota((count, count), 0) == iota((count, count), 1)).astype(F32)
    base = ints_ref[0] * blocks
    level, col = iota(stacked, 0), iota(stacked, 1)
    row = level % count
    mine = base + level // count
    alive = row[:, :1] <= mine[:, :1]
    for h in range(heads):
        units, rows, inverse = unit_ref[:, head(h)], rows_ref[:, head(h)], inv_ref[h]
        inverse_t = nt_high(eye, inverse)
        moved = jnp.concatenate([nt_high(rows, dcum[h]) for dcum in dcums], axis=0)
        overlap = jnp.where(col <= mine, nt_high(moved, units), 0.0)
        gamma = nn_high(overlap, inverse)
        gamma = jnp.where((row < col) & (col <= mine), gamma, 0.0)
        beta = jnp.concatenate([eye - inverse_t] * blocks, axis=0)
        beta = jnp.where(col <= mine, beta, 0.0)
        x_all = jnp.where(alive, moved - 2.0 * nn_high(gamma, units), 0.0)
        turned = jnp.concatenate([units] * blocks, axis=0) - nn_high(beta, units)
        turned = jnp.where(alive, turned, 0.0)
        x_total, y_total = None, None
        for j, dcum in enumerate(dcums):
            here = slice(j * count, (j + 1) * count)
            y_part = nn_high(turned[here], dcum[h])
            x_total = x_all[here] if j == 0 else x_total + x_all[here]
            y_total = y_part if j == 0 else y_total + y_part
        out_ref[:, head(h)] = x_total
        out_ref[:, slice(width + h * DH, width + (h + 1) * DH)] = y_total


def run_adjoint(ints, afters, dcums, unit, rows, inverse, heads, blocks):
    count, width = unit.shape
    return pl.pallas_call(
        functools.partial(adjoint_kernel, heads, blocks, len(afters)),
        out_shape=jax.ShapeDtypeStruct((count, 2 * width), F32),
        in_specs=in_smem(1)
        + [pl.BlockSpec(memory_space=pl.ANY)] * len(afters)
        + in_vmem(len(dcums) + 3),
        out_specs=pl.BlockSpec(memory_space=pltpu.VMEM),
        compiler_params=grant(60),
        cost_estimate=cost(0.2),
        name="adjoint",
    )(ints, *afters, *dcums, unit, rows, inverse)


def house_kernel(heads, blocks, base_ref, got_ref, unit_ref, rows_ref, house_ref, out_ref):
    count, width = unit_ref.shape
    total = jnp.sum(got_ref[...], axis=0)
    for h in range(heads):
        x_part = total[:, head(h)]
        y_part = total[:, slice(width + h * DH, width + (h + 1) * DH)]
        along = nt_high(y_part, rows_ref[:, head(h)])
        spot = iota((blocks, count), 0) + base_ref[0] * blocks
        along = jnp.where(iota((blocks, count), 1) < spot, along, 0.0)
        turned = y_part - 2.0 * nn_high(along, unit_ref[:, head(h)])
        dunit = -2.0 * (x_part + turned)
        house = house_ref[:, head(h)]
        lengths = jnp.sqrt(jnp.sum(house * house, axis=1, keepdims=True) + 1e-06)
        unit = house / lengths
        inner = jnp.sum(unit * dunit, axis=1, keepdims=True)
        out_ref[:, head(h)] = (dunit - unit * inner) / lengths


def run_house(ints, got, unit, rows, house_dirs, heads, blocks):
    return pl.pallas_call(
        functools.partial(house_kernel, heads, blocks),
        out_shape=jax.ShapeDtypeStruct(house_dirs.shape, F32),
        in_specs=in_smem(1) + in_vmem(4),
        out_specs=pl.BlockSpec(memory_space=pltpu.VMEM),
        compiler_params=grant(60),
        cost_estimate=cost(2),
        name="house_grad",
    )(ints, got, unit, rows, house_dirs)


def hop(value, distance, count):
    return lax.ppermute(value, "ctx", [(i, i ^ distance) for i in range(count)])


def slide(value, pairs):
    return lax.ppermute(value, "head", pairs)


INWARD = [(0, 1), (3, 2)]
MIDDLE = [(1, 2), (2, 1)]
OUTWARD = [(1, 0), (2, 3)]


def near_kernel(ends_ref, first_ref, near_ref, inward_ref, out_ref):
    mine = jnp.where(ends_ref[0] > 0, first_ref[0], near_ref[0]).astype(F32)
    out_ref[...] = mine + inward_ref[0].astype(F32)


def run_near(ends, first, band, near, inward):
    _, rows, width = near.shape
    return pl.pallas_call(
        near_kernel,
        grid=(1,),
        out_shape=jax.ShapeDtypeStruct((rows, width), F32),
        in_specs=in_smem(1)
        + [pl.BlockSpec((1, rows, width), lambda t: (0, band, 0))]
        + [pl.BlockSpec((1, rows, width), lambda t: (0, 0, 0))] * 2,
        out_specs=pl.BlockSpec((rows, width), lambda t: (0, 0)),
        compiler_params=grant(60),
        cost_estimate=cost(5),
        name="near_sum",
    )(ends, first, near, inward)


def share_kernel(*refs):
    total_ref, far_ref, outward_ref, out_ref = refs[-4:]
    far = far_ref[0].astype(F32) + outward_ref[0].astype(F32)
    out_ref[...] = (total_ref[...] + far).astype(BF16)


def run_share(share, band, bands, total, far, outward):
    rows, width = total.shape
    tile = min(512, width)
    part = pl.BlockSpec((1, rows, tile), lambda t: (0, 0, t))
    given = [] if share is None else [share]
    return pl.pallas_call(
        share_kernel,
        grid=(width // tile,),
        out_shape=jax.ShapeDtypeStruct((bands * rows, width), BF16),
        in_specs=[pl.BlockSpec(memory_space=pl.ANY)] * len(given)
        + [pl.BlockSpec((rows, tile), lambda t: (0, t)), part, part],
        out_specs=pl.BlockSpec((rows, tile), lambda t: (band, t)),
        input_output_aliases={0: 0} if given else {},
        compiler_params=grant(60),
        cost_estimate=cost(2),
        name="share",
    )(*given, total, far, outward)


def line_ends():
    place = lax.axis_index("head")
    return ((place == 0) | (place == 3)).astype(jnp.int32).reshape(1)


def line_scatter(share, band, bands, firsts, rest, inward, inner):
    swapped = slide(inner, MIDDLE)
    firsts, swapped = lax.optimization_barrier((firsts, swapped))
    rows = rest.shape[1]
    outer = firsts[:, band * rows : (band + 1) * rows] + swapped[1:]
    outward = slide(outer, OUTWARD)
    total = run_near(line_ends(), firsts, band, rest, inward)
    return run_share(share, band, bands, total, swapped, outward), swapped, outer


def line_scatter_apart(share, band, bands, first, near, far, last, ready, exchange, earlier):
    in_last, in_far, in_near = slide(last, INWARD), slide(far, INWARD), slide(near, INWARD)
    in_last, ready = lax.optimization_barrier((in_last, ready))
    sum_last = last + in_last
    ready, *_ = lax.optimization_barrier((ready, sum_last, earlier))
    got = exchange(ready)
    swap_last = slide(sum_last, MIDDLE)
    sum_far = far + in_far
    swap_far = slide(sum_far, MIDDLE)
    outward = slide(first + swap_last, OUTWARD)
    in_near, _ = lax.optimization_barrier((in_near, sum_far))
    total = run_near(line_ends(), first, 0, near, in_near)
    return run_share(share, band, bands, total, swap_far, outward), got


def shards(
    query_rows, key_rows, value_rows, grad_out, house_dirs, owners, offsets, w_query, w_key, w_value
):
    tok_rows, width = query_rows.shape
    heads, blocks = width // DH, tok_rows // BLK
    ctx_count, groups = lax.axis_size("ctx"), lax.axis_size("head")
    my_index = lax.axis_index("ctx").astype(jnp.int32)
    ints = jnp.concatenate([my_index.reshape(1), owners.reshape(-1), offsets.reshape(-1)])
    by_hand = ctx_count == 8 and groups == 4 and blocks == 4
    core, across, along = 1, 2, 4

    if by_hand:
        other = hop(house_dirs, core, 8)
        upper = (my_index & core) != 0
        low, high = jnp.where(upper, other, house_dirs), jnp.where(upper, house_dirs, other)
        house_pair = jnp.concatenate([low, high], axis=0)
        value_x, key_y = hop(value_rows, across, 8), hop(key_rows, along, 8)
        key_x, value_y = hop(key_rows, across, 8), hop(value_rows, along, 8)
        house_late, *_ = lax.optimization_barrier((house_pair, value_x, key_y))
        house_parts = [house_pair] + [hop(house_late, t, 8) for t in (2, 4, 6)]
        key_d, value_d = hop(key_y, across, 8), hop(value_x, along, 8)
    else:
        house_parts = [lax.all_gather(house_dirs, "ctx", axis=0, tiled=True)]

    unit, rows, inverse, wide, tall = run_chain(ints, house_parts, heads)
    ready = query_rows
    if by_hand:
        own = (key_rows, value_rows, key_x, value_x, key_y, value_y, key_d, value_d)
        early = lax.optimization_barrier((*own[:6], *house_parts))[:6]
        siblings = [hop(part, core, 8) for part in early]
        ready, *_ = lax.optimization_barrier((query_rows, *siblings[:3]))
    qrot, krot, local, listed_cum = run_rotate(ints, wide, tall, ready, key_rows, heads, blocks)
    if by_hand:
        late = lax.optimization_barrier((*own[6:], qrot))[:2]
        siblings += [hop(part, core, 8) for part in late]
        sources, places = [], []
        for t in range(4):
            for pair in (own[2 * t : 2 * t + 2], siblings[2 * t : 2 * t + 2]):
                places.append(((len(sources), 0), (len(sources) + 1, 0)))
                sources += pair
    else:
        sources = [lax.all_gather(key_rows, "ctx"), lax.all_gather(value_rows, "ctx")]
        places = [((0, 0), (1, 0))]

    rounds = ((0, 1), (1, blocks - 1), (blocks, 1), (blocks + 1, blocks - 1))
    dq, dcum, dk_loc, dv_loc, *outs = run_attend(
        ints,
        sources,
        places,
        (query_rows, qrot, krot, value_rows, grad_out, local, listed_cum),
        heads,
        blocks,
        rounds if by_hand else (),
    )
    weights = (w_query, w_key, w_value)
    flip = jnp.where(by_hand & (lax.axis_index("head") >= 2), 1, 0).astype(jnp.int32).reshape(1)

    arrays = (dk_loc, dv_loc, dq, key_rows, dcum, local)

    def project(block, layout, afters, parts, before=()):
        return run_project(block, groups, layout, flip, afters, parts, before, arrays, weights)

    def share_sums(sums):
        sums = sums.reshape(ctx_count, blocks, 2 * width)
        return lax.all_to_all(sums, "ctx", split_axis=0, concat_axis=0, tiled=True)

    if by_hand:
        got_0 = hop(outs[2], core, 8)
        got_1 = hop(lax.optimization_barrier((outs[3], got_0))[0], core, 8)
        sent_0 = run_merge(outs[0], got_0, 0, 1, [])
        sent_1 = run_merge(outs[1], got_1, 0, 1, [sent_0[0]])
        sent_2 = run_merge(outs[1], got_1, 1, 2, [sent_1[0]])

        def give_back(own, got, first, sent):
            back = [hop(part, t, 8) for part, t in zip(sent, (across, along, across + along))]
            near = [part.reshape(-1, BLK, 2 * width) for part in (own, got)]
            parts = []
            for j in range(sent[0].shape[0]):
                mine = [(part, 4 * (first + j)) for part in near]
                parts.append(mine + [(part, j) for part in back])
            return parts, back

        parts_0, back_0 = give_back(outs[0], got_0, 0, sent_0)
        *later_1, _, _ = lax.optimization_barrier((*sent_1, back_0, sent_2))
        parts_1, back_1 = give_back(outs[1], got_1, 0, later_1)
        *later_2, _ = lax.optimization_barrier((*sent_2, back_1))
        parts_2, _ = give_back(outs[1], got_1, 1, later_2)
        rest_0, dcum_0, *grads_0 = project(0, ((1, 2, 3),), [sent_2[0]], parts_0)
        before = (dq, *grads_0)
        split_off = ((0,), (1, 2, 3))
        firsts, rest_1, dcum_1, *_ = project(1, split_off, [rest_0], parts_1, before)
        inward_0, inward_1 = slide(rest_0, INWARD), slide(rest_1, INWARD)
        apart = ((0,), (1,), (2,), (3,))
        *terms, dcum_2, _, _ = project(2, apart, [rest_1], parts_2)
        share, swapped_0, outer_0 = line_scatter(
            None, 0, 4, firsts, rest_0, inward_0, rest_0[1:] + inward_0[1:]
        )
        inward_1, *_ = lax.optimization_barrier((inward_1, swapped_0, dcum_2))
        sum_1 = rest_1[1:] + inward_1[1:]
        share, _, outer_1 = line_scatter(
            share, 1, 4, firsts, rest_1, inward_1, sum_1
        )
        dcums = [dcum_0, dcum_1, dcum_2]
        sums = run_adjoint(ints, (sum_1, outer_0), dcums, unit, rows, inverse, heads, blocks)
        share, got = line_scatter_apart(
            share, 1, 2, *terms, sums, share_sums, outer_1
        )
    else:
        spots = (owners * blocks + offsets).reshape(-1)
        empty = jnp.zeros((ctx_count * blocks, BLK, 2 * width), BF16)
        filled = empty.at[spots].add(outs[0])
        back = lax.psum_scatter(filled, "ctx", scatter_dimension=0, tiled=True)
        dcums = []
        share = jnp.zeros((tok_rows, w_query.shape[0] // groups), BF16)
        for j in range(blocks):
            term, dcum_out, _, _ = project(
                j, (tuple(range(groups)),), [], [[(back, j)]]
            )
            dcums.append(dcum_out)
            done = lax.psum_scatter(term, "head", scatter_dimension=0, tiled=False)
            share = lax.dynamic_update_slice(share, done, (j * BLK, 0))

        got = share_sums(run_adjoint(ints, (), dcums, unit, rows, inverse, heads, blocks))

    house_grad = run_house(ints, got, unit, rows, house_dirs, heads, blocks)
    return (share, house_grad)


def solution(mesh):
    placed = (
        P("ctx", "head"),
        P("ctx", "head"),
        P("ctx", "head"),
        P("ctx", "head"),
        P("ctx", "head"),
        P("ctx", None),
        P("ctx", None),
        P(None, "head"),
        P(None, "head"),
        P(None, "head"),
    )
    return jax.shard_map(
        shards,
        mesh=mesh,
        in_specs=placed,
        out_specs=(P("ctx", "head"), P("ctx", "head")),
        check_vma=False,
    )
```

```python
import functools
import math

import jax
import jax.numpy as jnp
from jax import lax
from jax.experimental import pallas as pl
from jax.experimental.pallas import tpu as pltpu
from jax.sharding import PartitionSpec as P

DH = 128
BLK = 128
MAXL = 2
HIGH = lax.Precision.HIGHEST
F32 = jnp.float32
BF16 = jnp.bfloat16


def nn(a, b):
    return lax.dot_general(a, b, (((1,), (0,)), ((), ())), preferred_element_type=F32)


def nt(a, b):
    return lax.dot_general(a, b, (((1,), (1,)), ((), ())), preferred_element_type=F32)


def tn(a, b):
    return lax.dot_general(a, b, (((0,), (0,)), ((), ())), preferred_element_type=F32)


def nn_high(a, b):
    return lax.dot_general(
        a, b, (((1,), (0,)), ((), ())), precision=HIGH, preferred_element_type=F32
    )


def nt_high(a, b):
    return lax.dot_general(
        a, b, (((1,), (1,)), ((), ())), precision=HIGH, preferred_element_type=F32
    )


def split(value):
    top = value.astype(BF16)
    return top, (value - top.astype(F32)).astype(BF16)


def iota(shape, dim):
    return lax.broadcasted_iota(jnp.int32, shape, dim)


def head(h):
    return slice(h * DH, (h + 1) * DH)


def listed(ints_ref, entry, entries):
    return ints_ref[1 + entry], ints_ref[1 + entries + entry]


def grant(mebibytes):
    return pltpu.CompilerParams(vmem_limit_bytes=mebibytes * 1024 * 1024)


def cost(microseconds):
    return pl.CostEstimate(
        flops=int(microseconds * 1.15e9), bytes_accessed=1 << 20, transcendentals=0
    )


def in_smem(count):
    return [pl.BlockSpec(memory_space=pltpu.SMEM)] * count


def in_vmem(count):
    return [pl.BlockSpec(memory_space=pltpu.VMEM)] * count


def chain_kernel(heads, parts, ints_ref, *refs):
    house_refs = refs[:parts]
    unit_ref, rows_ref, inv_ref, wide_ref, tall_ref, unit_h, house_all = refs[parts:]
    count = unit_ref.shape[0]
    span = count // parts
    for t, ref in enumerate(house_refs):
        place = (ints_ref[0] // (8 // parts)) ^ t if parts > 1 else 0
        house_all[pl.ds(pl.multiple_of(place * span, span), span), :] = ref[...]
    eye = (iota((count, count), 0) == iota((count, count), 1)).astype(F32)
    for h in range(heads):
        house = house_all[:, head(h)]
        lengths = jnp.sqrt(jnp.sum(house * house, axis=1, keepdims=True) + 1e-06)
        unit_ref[:, head(h)] = house / lengths
        unit_h[h] = house / lengths
        inv_ref[h] = eye

    def eliminate(step, carry):
        below = iota((count, 1), 0) > step
        for h in range(heads):
            pivot = unit_h[h, pl.ds(step, 1), :]
            overlap = jnp.sum(unit_h[h] * pivot, axis=1, keepdims=True)
            factor = jnp.where(below, 2.0 * overlap, 0.0)
            inv_ref[h] = inv_ref[h] - factor * inv_ref[h, pl.ds(step, 1), :]
        return carry

    lax.fori_loop(0, count, eliminate, 0)
    eye_wide = (iota((DH, DH), 0) == iota((DH, DH), 1)).astype(F32)
    for h in range(heads):
        units = unit_ref[:, head(h)]
        rows = nn_high(inv_ref[h], units)
        rows_ref[:, head(h)] = rows
        unit_hi, unit_lo = split(nt_high(eye_wide, units))
        rows_hi, rows_lo = split(rows)
        wide_ref[h] = jnp.concatenate([unit_hi, unit_hi, unit_lo], axis=1)
        tall_ref[h] = jnp.concatenate([rows_hi, rows_lo, rows_hi], axis=0)


def run_chain(ints, house_parts, heads):
    span, width = house_parts[0].shape
    parts = len(house_parts)
    count = span * parts
    return pl.pallas_call(
        functools.partial(chain_kernel, heads, parts),
        out_shape=[
            jax.ShapeDtypeStruct((count, width), F32),
            jax.ShapeDtypeStruct((count, width), F32),
            jax.ShapeDtypeStruct((heads, count, count), F32),
            jax.ShapeDtypeStruct((heads, DH, 3 * count), BF16),
            jax.ShapeDtypeStruct((heads, 3 * count, DH), BF16),
        ],
        in_specs=in_smem(1) + in_vmem(parts),
        out_specs=in_vmem(5),
        scratch_shapes=[pltpu.VMEM((heads, count, DH), F32), pltpu.VMEM((count, width), F32)],
        compiler_params=grant(12),
        cost_estimate=cost(6),
        name="house_chain",
    )(ints, *house_parts)


def rotate_kernel(
    heads,
    blocks,
    ints_ref,
    wide_ref,
    tall_ref,
    query_ref,
    key_ref,
    qrot_ref,
    krot_ref,
    local_ref,
    listed_ref,
):
    count = wide_ref.shape[2] // 3
    entries = blocks * MAXL
    column = iota((DH, 3 * count), 1) % count
    eye = (iota((DH, DH), 0) == iota((DH, DH), 1)).astype(F32)

    def cumulative(h, block):
        kept = jnp.where(column <= block, wide_ref[h].astype(F32), 0.0).astype(BF16)
        return split(eye - 2.0 * nn(kept, tall_ref[h]))

    base = ints_ref[0] * blocks

    def local_block(b, carry):
        here = pl.ds(pl.multiple_of(b * BLK, BLK), BLK)
        for h in range(heads):
            hi, lo = cumulative(h, base + b)
            local_ref[b, h] = hi
            query, key = query_ref[here, head(h)], key_ref[here, head(h)]
            qrot_ref[here, head(h)] = (nn(query, hi) + nn(query, lo)).astype(BF16)
            krot_ref[here, head(h)] = (nn(key, hi) + nn(key, lo)).astype(BF16)
        return carry

    lax.fori_loop(0, blocks, local_block, 0)

    def listed_block(e, carry):
        owner, offset = listed(ints_ref, e, entries)
        for h in range(heads):
            hi, lo = cumulative(h, owner * blocks + offset)
            listed_ref[e, h, :DH] = hi
            listed_ref[e, h, DH:] = lo
        return carry

    lax.fori_loop(0, entries, listed_block, 0)


def run_rotate(ints, wide, tall, query_rows, key_rows, heads, blocks):
    rows, width = query_rows.shape
    entries = blocks * MAXL
    return pl.pallas_call(
        functools.partial(rotate_kernel, heads, blocks),
        out_shape=[
            jax.ShapeDtypeStruct((rows, width), BF16),
            jax.ShapeDtypeStruct((rows, width), BF16),
            jax.ShapeDtypeStruct((blocks, heads, DH, DH), BF16),
            jax.ShapeDtypeStruct((entries, heads, 2 * DH, DH), BF16),
        ],
        in_specs=in_smem(1) + in_vmem(4),
        out_specs=in_vmem(4),
        compiler_params=grant(16),
        cost_estimate=cost(9),
        name="rotate",
    )(ints, wide, tall, query_rows, key_rows)


def attend_kernel(heads, blocks, places, pieces, *refs):
    ints_ref = refs[0]
    source_count = 1 + max(place[0] for pair in places for place in pair)
    sources = refs[1 : 1 + source_count]
    refs = refs[1 + source_count :]
    (query_ref, qrot_ref, krot_ref, value_ref, grad_ref, local_ref, listed_ref) = refs[:7]
    dq_ref, dcum_ref, dk_ref, dv_ref = refs[7:11]
    outs = refs[11 : 11 + max(len(pieces), 1)]
    refs = refs[11 + max(len(pieces), 1) :]
    dq_all, dcum_all, dk_all, dv_all, grad_sems, far_keys, far_values, sems = refs[:8]
    entries = blocks * MAXL
    scaling = DH ** (-0.5)
    log_scale = scaling * math.log2(math.e)

    def start(e, src, kind, slot, where):
        pltpu.make_async_copy(src.at[where], slot.at[e], sems.at[kind, e]).start()

    for e in range(entries):
        owner, offset = listed(ints_ref, e, entries)
        row = pl.multiple_of(offset * BLK, BLK)
        if len(places) == 1:
            start(e, sources[0], 0, far_keys, (owner, pl.ds(row, BLK)))
            start(e, sources[1], 1, far_values, (owner, pl.ds(row, BLK)))
        else:
            distance = owner ^ ints_ref[0]
            for r, (key_place, value_place) in enumerate(places):

                @pl.when(distance == r)
                def _():
                    source, first = key_place
                    start(e, sources[source], 0, far_keys, pl.ds(first + row, BLK))
                    source, first = value_place
                    start(e, sources[source], 1, far_values, pl.ds(first + row, BLK))

    out_copies = []
    if pieces:
        payloads, out_sems = refs[8 : 8 + heads], refs[8 + heads]
        for payload in payloads:
            payload[...] = jnp.zeros_like(payload)
    later = iota((BLK, BLK), 0) > iota((BLK, BLK), 1)
    empty = jnp.zeros((BLK, DH), BF16)
    def wait_far():
        for kind, slots in ((0, far_keys), (1, far_values)):
            for e in range(entries):
                pltpu.make_async_copy(slots.at[e], slots.at[e], sems.at[kind, e]).wait()

    spans = [slice(a * BLK, (a + 1) * BLK) for a in range(blocks)]
    group = 1
    for start_head in range(0, heads, group):
        steps = [(h, a) for h in range(start_head, start_head + group) for a in range(blocks)]
        both, keys, values, scores, dprobs, tops = {}, {}, {}, {}, {}, {}

        def score(step, b, key, value):
            pair = nt(jnp.concatenate([key, value], axis=1), both[step])
            part = pair[:, :BLK] * log_scale
            if b == step[1]:
                part = jnp.where(later, -jnp.inf, part)
            keys[step].append(key)
            scores[step].append(part)
            dprobs[step].append(pair[:, BLK:])
            tops[step] = part if b == 0 else jnp.maximum(tops[step], part)

        for step in steps:
            h, a = step
            lanes = head(h)
            qrot, grad = qrot_ref[spans[a], lanes], grad_ref[spans[a], lanes]
            upper = jnp.concatenate([qrot, empty], axis=1)
            lower = jnp.concatenate([empty, grad], axis=1)
            both[step] = jnp.concatenate([upper, lower], axis=0)
            keys[step], scores[step], dprobs[step] = [], [], []
            for b in range(a + 1):
                score(step, b, krot_ref[spans[b], lanes], value_ref[spans[b], lanes])
        if start_head == 0:
            wait_far()
        for step in steps:
            h, a = step
            for l in range(MAXL):
                e = a * MAXL + l
                raw = far_keys[e, :, head(h)]
                raw = jnp.concatenate([raw, raw], axis=1)
                key = nn(raw, listed_ref[e, h]).astype(BF16)
                score(step, a + 1 + l, key, far_values[e, :, head(h)])
        weights, inverses, deltas = {}, {}, {}
        for step in steps:
            top = jnp.max(tops[step], axis=0, keepdims=True)
            weights[step] = []
            total, inner = None, None
            for part, dprob in zip(scores[step], dprobs[step]):
                weight = jnp.exp2(part - top)
                weights[step].append(weight)
                product = weight * dprob
                total = weight if total is None else total + weight
                inner = product if inner is None else inner + product
            inverses[step] = 1.0 / jnp.sum(total, axis=0, keepdims=True)
            deltas[step] = jnp.sum(inner, axis=0, keepdims=True) * inverses[step]
        dscores, pairs = {}, {}
        for step in steps:
            dscores[step], pairs[step] = [], []
            for weight, dprob in zip(weights[step], dprobs[step]):
                probs = weight * inverses[step]
                dscore = (probs * (dprob - deltas[step])).astype(BF16)
                dscores[step].append(dscore)
                wide = jnp.concatenate([dscore, probs.astype(BF16)], axis=1)
                pairs[step].append(nn(wide, both[step]))
        for h, b in steps:
            total = pairs[h, b][b]
            for a in range(b + 1, blocks):
                total = total + pairs[h, a][b]
            dk_all[h, spans[b]] = total[:, :DH] * scaling
            dv_all[h, spans[b]] = total[:, DH:]
        for h, a in steps:
            for l in range(MAXL):
                e = a * MAXL + l
                pair = pairs[h, a][a + 1 + l]
                dkey, dvalue = (pair[:, :DH] * scaling).astype(BF16), pair[:, DH:].astype(BF16)
                if pieces:
                    owner, offset = listed(ints_ref, e, entries)
                    distance = owner ^ ints_ref[0]
                    at = (distance & 1) * blocks + offset
                    payloads[h][at, distance >> 1, :, :DH] += dkey
                    payloads[h][at, distance >> 1, :, DH:] += dvalue
                else:
                    outs[0][e, :, 2 * h * DH : (2 * h + 1) * DH] = dkey
                    outs[0][e, :, (2 * h + 1) * DH : (2 * h + 2) * DH] = dvalue
        halves = {}
        for step in steps:
            wide = jnp.concatenate(dscores[step], axis=0)
            tall = jnp.concatenate(keys[step], axis=0)
            halves[step] = split(tn(wide, tall) * scaling)
        for h, a in steps:
            dq_top, dq_low = halves[h, a]
            dq_all[h, spans[a]] = nt(dq_top, local_ref[a, h]).astype(BF16)
            query = query_ref[spans[a], head(h)]
            query = jnp.concatenate([query, query], axis=0)
            dcum_all[h, a] = tn(query, jnp.concatenate([dq_top, dq_low], axis=0))
        for h in range(start_head, start_head + group):
            moves = [
                (payloads[h].at[pl.ds(first, size)], outs[i], out_sems.at[i, h])
                for i, (first, size) in enumerate(pieces)
            ]
            moves = [
                (source, where.at[:, :, :, 2 * h * DH : (2 * h + 2) * DH], sem)
                for source, where, sem in moves
            ]
            moves += [
                (dk_all.at[h], dk_ref.at[:, head(h)], grad_sems.at[0, h]),
                (dv_all.at[h], dv_ref.at[:, head(h)], grad_sems.at[1, h]),
                (dq_all.at[h], dq_ref.at[:, head(h)], grad_sems.at[2, h]),
                (dcum_all.at[h], dcum_ref.at[:, h], grad_sems.at[3, h]),
            ]
            for source, where, sem in moves:
                copy = pltpu.make_async_copy(source, where, sem)
                copy.start()
                out_copies.append(copy)
    for copy in out_copies:
        copy.wait()


def run_attend(ints, sources, places, arrays, heads, blocks, pieces):
    rows, width = arrays[0].shape
    entries = blocks * MAXL
    any_spec = pl.BlockSpec(memory_space=pl.ANY)
    scratch = [
        pltpu.VMEM((heads, rows, DH), BF16),
        pltpu.VMEM((heads, blocks, DH, DH), F32),
        pltpu.VMEM((heads, rows, DH), F32),
        pltpu.VMEM((heads, rows, DH), F32),
        pltpu.SemaphoreType.DMA((4, heads)),
        pltpu.VMEM((entries, BLK, width), BF16),
        pltpu.VMEM((entries, BLK, width), BF16),
        pltpu.SemaphoreType.DMA((2, entries)),
    ]
    if pieces:
        chips = len(places) // 2
        out_parts = [
            pltpu.HBM((size, chips, BLK, 2 * width), BF16) for _, size in pieces
        ]
        part_specs = [any_spec] * len(pieces)
        scratch += [pltpu.VMEM((2 * blocks, chips, BLK, 2 * DH), BF16)] * heads
        scratch += [pltpu.SemaphoreType.DMA((len(pieces), heads))]
    else:
        out_parts = [jax.ShapeDtypeStruct((entries, BLK, 2 * width), BF16)]
        part_specs = in_vmem(1)
    return pl.pallas_call(
        functools.partial(attend_kernel, heads, blocks, places, pieces),
        out_shape=[
            pltpu.HBM((rows, width), BF16),
            pltpu.HBM((blocks, heads, DH, DH), F32),
            pltpu.HBM((rows, width), F32),
            pltpu.HBM((rows, width), F32),
        ]
        + out_parts,
        in_specs=in_smem(1) + [any_spec] * len(sources) + in_vmem(7),
        out_specs=[pl.BlockSpec(memory_space=pltpu.HBM)] * 4 + part_specs,
        scratch_shapes=scratch,
        compiler_params=grant(36),
        cost_estimate=cost(15),
        name="attend",
    )(ints, *sources, *arrays)


def merge_kernel(own_ref, got_ref, *refs):
    for i, ref in enumerate(refs[-3:]):
        total = own_ref[0, i + 1].astype(F32) + got_ref[0, i + 1].astype(F32)
        ref[0] = total.astype(BF16)


def run_merge(own, got, first, size, afters):
    _, chips, rows, width = own.shape
    cut = 2
    lanes = width // cut
    whole = pl.BlockSpec((1, chips, rows, lanes), lambda j, c: (first + j, 0, 0, c))
    return pl.pallas_call(
        merge_kernel,
        grid=(size, cut),
        out_shape=[jax.ShapeDtypeStruct((size, rows, width), BF16)] * (chips - 1),
        in_specs=[whole] * 2
        + [pl.BlockSpec((1, 16, 128), lambda j, c: (0, 0, 0))] * len(afters),
        out_specs=[pl.BlockSpec((1, rows, lanes), lambda j, c: (j, 0, c))] * (chips - 1),
        compiler_params=grant(60),
        cost_estimate=cost(2),
        name="merge",
    )(own, got, *afters)


def start_tiles(chunks, groups, flip_ref, weight_refs, tiles, sems):
    count, _, tile, _ = tiles.shape
    per = count // len(chunks)
    copies = []
    for t in range(count):
        m = chunks[t // per][0]
        row = ((m + flip_ref[0] * (groups - 1 - 2 * m)) * per + t % per) * tile
        rows = pl.ds(pl.multiple_of(row, tile), tile)
        for w, ref in enumerate(weight_refs):
            copy = pltpu.make_async_copy(ref.at[rows], tiles.at[t, w], sems.at[t, w])
            copy.start()
            copies.append(copy)
    return copies


def multiply_tiles(chunks, copies, tiles, out_refs, grads_of):
    count, _, tile, _ = tiles.shape
    per = count // len(chunks)
    for t in range(count):
        term = None
        m, out, at = chunks[t // per]
        for w, grad in enumerate(grads_of(m)):
            copies[3 * t + w].wait()
            part = nt(tiles[t, w], grad)
            term = part if term is None else term + part
        spot = slice(t % per * tile, (t % per + 1) * tile)
        out_refs[out][at, :, spot] = term.T.astype(BF16)


def project_kernel(heads, parts, size, groups, before, layout, afters, flip_ref, *refs):
    refs = refs[afters:]
    outs = len(layout)
    chunks = [(m, i, at) for i, row in enumerate(layout) for at, m in enumerate(row)]
    tiles, sems = refs[-2:]
    part_refs, refs = refs[: size * parts], refs[size * parts :]
    before_refs, refs = refs[:before], refs[before:]
    dk_loc, dv_loc, dq_ref, key_ref, dcum_in, cum_ref = refs[:6]
    weight_refs, out_refs = refs[6:9], refs[9 : 9 + outs]
    dcum_out, dk_out, dv_out = refs[9 + outs : 12 + outs]
    copies = start_tiles(chunks, groups, flip_ref, weight_refs, tiles, sems)
    earlier = ()
    dk_rows, dv_rows = [], []
    for j in range(size):
        here = slice(j * BLK, (j + 1) * BLK)
        dk, dv = [], []
        for h in range(heads):
            both = slice(2 * h * DH, (2 * h + 2) * DH)
            total = part_refs[j * parts][0, :, both].astype(F32)
            for ref in part_refs[j * parts + 1 : (j + 1) * parts]:
                total = total + ref[0, :, both].astype(F32)
            dv.append((dv_loc[here, head(h)] + total[:, DH:]).astype(BF16))
            dk_top, dk_low = split(dk_loc[here, head(h)] + total[:, :DH])
            dk.append(nt(dk_top, cum_ref[j, h]).astype(BF16))
            key = key_ref[here, head(h)]
            key = jnp.concatenate([key, key], axis=0)
            dcum = tn(key, jnp.concatenate([dk_top, dk_low], axis=0))
            dcum_out[j, h] = dcum_in[j, h] + dcum
        dk_rows.append(jnp.concatenate(dk, axis=1))
        dv_rows.append(jnp.concatenate(dv, axis=1))
    dk_all, dv_all = jnp.concatenate(dk_rows, axis=0), jnp.concatenate(dv_rows, axis=0)
    dk_out[...] = dk_all
    dv_out[...] = dv_all
    grads = (dq_ref[...], dk_all, dv_all)
    if before:
        earlier = [
            jnp.concatenate([old[...], new], axis=0) for old, new in zip(before_refs, grads)
        ]

    multiply_tiles(
        chunks, copies, tiles, out_refs, lambda m: earlier if before and m == 0 else grads
    )


def project_more_kernel(groups, layout, afters, flip_ref, *refs):
    refs = refs[afters:]
    chunks = [(m, i, at) for i, row in enumerate(layout) for at, m in enumerate(row)]
    tiles, sems = refs[-2:]
    copies = start_tiles(chunks, groups, flip_ref, refs[3:6], tiles, sems)
    grads = [ref[...] for ref in refs[:3]]
    multiply_tiles(chunks, copies, tiles, refs[6:-2], lambda m: grads)


def run_project_more(block, groups, layout, flip, afters, dq, dk, dv, weights):
    rows, width = dk.shape
    model = weights[0].shape[0]
    chunk = model // groups
    tile = min(512, chunk)
    tile_count = sum(map(len, layout)) * chunk // tile

    def whole(*shape):
        return pl.BlockSpec(shape, lambda t: (0,) * len(shape))

    shapes = [(len(row), rows, chunk) for row in layout]
    return pl.pallas_call(
        functools.partial(project_more_kernel, groups, layout, len(afters)),
        grid=(1,),
        in_specs=in_smem(1)
        + [whole(1, 16, 128)] * len(afters)
        + [pl.BlockSpec((rows, width), lambda t: (block * BLK // rows, 0))]
        + [whole(rows, width)] * 2
        + [pl.BlockSpec(memory_space=pl.ANY)] * 3,
        out_specs=[whole(*shape) for shape in shapes],
        scratch_shapes=[
            pltpu.VMEM((tile_count, 3, tile, width), BF16),
            pltpu.SemaphoreType.DMA((tile_count, 3)),
        ],
        out_shape=[jax.ShapeDtypeStruct(shape, BF16) for shape in shapes],
        compiler_params=grant(60),
        cost_estimate=cost(3 * sum(map(len, layout))),
        name="project_more",
    )(flip, *afters, dq, dk, dv, *weights)


def run_project(block, groups, layout, flip, afters, parts, before, arrays, weights):
    dk_loc, dv_loc, dq, key_rows, dcum, cum = arrays
    size, width = len(parts), dq.shape[1]
    heads = width // DH
    model = weights[0].shape[0]
    chunk = model // groups
    tile = min(512, chunk)
    rows = size * BLK
    tile_count = sum(map(len, layout)) * chunk // tile

    def part_spec(index):
        return pl.BlockSpec((1, BLK, 2 * width), lambda t: (index, 0, 0))

    def whole(*shape):
        return pl.BlockSpec(shape, lambda t: (0,) * len(shape))

    rows_spec = pl.BlockSpec((rows, width), lambda t: (block // size, 0))
    head_spec = pl.BlockSpec((size, heads, DH, DH), lambda t: (block // size, 0, 0, 0))
    flat = [part for row in parts for part in row]
    heights = [2 * rows if before and row == (0,) else rows for row in layout]
    shapes = [(len(row), height, chunk) for row, height in zip(layout, heights)]
    return pl.pallas_call(
        functools.partial(
            project_kernel,
            heads,
            len(parts[0]),
            size,
            groups,
            len(before),
            layout,
            len(afters),
        ),
        grid=(1,),
        in_specs=in_smem(1)
        + [whole(1, 16, 128)] * len(afters)
        + [part_spec(index) for _, index in flat]
        + [whole(rows, width)] * len(before)
        + [rows_spec] * 4
        + [head_spec] * 2
        + [pl.BlockSpec(memory_space=pl.ANY)] * 3,
        out_specs=[whole(*shape) for shape in shapes]
        + [whole(size, heads, DH, DH)]
        + [whole(rows, width)] * 2,
        scratch_shapes=[
            pltpu.VMEM((tile_count, 3, tile, width), BF16),
            pltpu.SemaphoreType.DMA((tile_count, 3)),
        ],
        out_shape=[jax.ShapeDtypeStruct(shape, BF16) for shape in shapes]
        + [jax.ShapeDtypeStruct((size, heads, DH, DH), F32)]
        + [jax.ShapeDtypeStruct((rows, width), BF16)] * 2,
        compiler_params=grant(60),
        cost_estimate=cost(3 * sum(map(len, layout))),
        name="project",
    )(
        flip,
        *afters,
        *[part for part, _ in flat],
        *before,
        dk_loc,
        dv_loc,
        dq,
        key_rows,
        dcum,
        cum,
        *weights,
    )


def adjoint_kernel(heads, blocks, afters, ints_ref, *refs):
    refs = refs[afters:]
    dcums = [ref.at[j] for ref in refs[:-4] for j in range(ref.shape[0])]
    unit_ref, rows_ref, inv_ref, out_ref = refs[-4:]
    count, width = unit_ref.shape
    stacked = (blocks * count, count)
    eye = (iota((count, count), 0) == iota((count, count), 1)).astype(F32)
    base = ints_ref[0] * blocks
    level, col = iota(stacked, 0), iota(stacked, 1)
    row = level % count
    mine = base + level // count
    alive = row[:, :1] <= mine[:, :1]
    for h in range(heads):
        units, rows, inverse = unit_ref[:, head(h)], rows_ref[:, head(h)], inv_ref[h]
        inverse_t = nt_high(eye, inverse)
        moved = jnp.concatenate([nt_high(rows, dcum[h]) for dcum in dcums], axis=0)
        overlap = jnp.where(col <= mine, nt_high(moved, units), 0.0)
        gamma = nn_high(overlap, inverse)
        gamma = jnp.where((row < col) & (col <= mine), gamma, 0.0)
        beta = jnp.concatenate([eye - inverse_t] * blocks, axis=0)
        beta = jnp.where(col <= mine, beta, 0.0)
        x_all = jnp.where(alive, moved - 2.0 * nn_high(gamma, units), 0.0)
        turned = jnp.concatenate([units] * blocks, axis=0) - nn_high(beta, units)
        turned = jnp.where(alive, turned, 0.0)
        x_total, y_total = None, None
        for j, dcum in enumerate(dcums):
            here = slice(j * count, (j + 1) * count)
            y_part = nn_high(turned[here], dcum[h])
            x_total = x_all[here] if j == 0 else x_total + x_all[here]
            y_total = y_part if j == 0 else y_total + y_part
        out_ref[:, head(h)] = x_total
        out_ref[:, slice(width + h * DH, width + (h + 1) * DH)] = y_total


def run_adjoint(ints, afters, dcums, unit, rows, inverse, heads, blocks):
    count, width = unit.shape
    return pl.pallas_call(
        functools.partial(adjoint_kernel, heads, blocks, len(afters)),
        out_shape=jax.ShapeDtypeStruct((count, 2 * width), F32),
        in_specs=in_smem(1)
        + [pl.BlockSpec(memory_space=pl.ANY)] * len(afters)
        + in_vmem(len(dcums) + 3),
        out_specs=pl.BlockSpec(memory_space=pltpu.VMEM),
        compiler_params=grant(60),
        cost_estimate=cost(0.2),
        name="adjoint",
    )(ints, *afters, *dcums, unit, rows, inverse)


def house_kernel(heads, blocks, base_ref, got_ref, unit_ref, rows_ref, house_ref, out_ref):
    count, width = unit_ref.shape
    total = jnp.sum(got_ref[...], axis=0)
    for h in range(heads):
        x_part = total[:, head(h)]
        y_part = total[:, slice(width + h * DH, width + (h + 1) * DH)]
        along = nt_high(y_part, rows_ref[:, head(h)])
        spot = iota((blocks, count), 0) + base_ref[0] * blocks
        along = jnp.where(iota((blocks, count), 1) < spot, along, 0.0)
        turned = y_part - 2.0 * nn_high(along, unit_ref[:, head(h)])
        dunit = -2.0 * (x_part + turned)
        house = house_ref[:, head(h)]
        lengths = jnp.sqrt(jnp.sum(house * house, axis=1, keepdims=True) + 1e-06)
        unit = house / lengths
        inner = jnp.sum(unit * dunit, axis=1, keepdims=True)
        out_ref[:, head(h)] = (dunit - unit * inner) / lengths


def run_house(ints, got, unit, rows, house_dirs, heads, blocks):
    return pl.pallas_call(
        functools.partial(house_kernel, heads, blocks),
        out_shape=jax.ShapeDtypeStruct(house_dirs.shape, F32),
        in_specs=in_smem(1) + in_vmem(4),
        out_specs=pl.BlockSpec(memory_space=pltpu.VMEM),
        compiler_params=grant(60),
        cost_estimate=cost(2),
        name="house_grad",
    )(ints, got, unit, rows, house_dirs)


def hop(value, distance, count):
    return lax.ppermute(value, "ctx", [(i, i ^ distance) for i in range(count)])


def slide(value, pairs):
    return lax.ppermute(value, "head", pairs)


INWARD = [(0, 1), (3, 2)]
MIDDLE = [(1, 2), (2, 1)]
OUTWARD = [(1, 0), (2, 3)]


def near_kernel(ends_ref, first_ref, near_ref, inward_ref, out_ref):
    mine = jnp.where(ends_ref[0] > 0, first_ref[0], near_ref[0]).astype(F32)
    out_ref[...] = mine + inward_ref[0].astype(F32)


def run_near(ends, first, band, near, inward):
    _, rows, width = near.shape
    return pl.pallas_call(
        near_kernel,
        grid=(1,),
        out_shape=jax.ShapeDtypeStruct((rows, width), F32),
        in_specs=in_smem(1)
        + [pl.BlockSpec((1, rows, width), lambda t: (0, band, 0))]
        + [pl.BlockSpec((1, rows, width), lambda t: (0, 0, 0))] * 2,
        out_specs=pl.BlockSpec((rows, width), lambda t: (0, 0)),
        compiler_params=grant(60),
        cost_estimate=cost(5),
        name="near_sum",
    )(ends, first, near, inward)


def share_kernel(*refs):
    total_ref, far_ref, outward_ref, out_ref = refs[-4:]
    far = far_ref[0].astype(F32) + outward_ref[0].astype(F32)
    out_ref[...] = (total_ref[...] + far).astype(BF16)


def run_share(share, band, bands, total, far, outward):
    rows, width = total.shape
    tile = min(512, width)
    part = pl.BlockSpec((1, rows, tile), lambda t: (0, 0, t))
    given = [] if share is None else [share]
    return pl.pallas_call(
        share_kernel,
        grid=(width // tile,),
        out_shape=jax.ShapeDtypeStruct((bands * rows, width), BF16),
        in_specs=[pl.BlockSpec(memory_space=pl.ANY)] * len(given)
        + [pl.BlockSpec((rows, tile), lambda t: (0, t)), part, part],
        out_specs=pl.BlockSpec((rows, tile), lambda t: (band, t)),
        input_output_aliases={0: 0} if given else {},
        compiler_params=grant(60),
        cost_estimate=cost(2),
        name="share",
    )(*given, total, far, outward)


def line_ends():
    place = lax.axis_index("head")
    return ((place == 0) | (place == 3)).astype(jnp.int32).reshape(1)


def line_scatter(share, band, bands, firsts, rest, inward, inner):
    swapped = slide(inner, MIDDLE)
    firsts, swapped = lax.optimization_barrier((firsts, swapped))
    rows = rest.shape[1]
    outer = firsts[:, band * rows : (band + 1) * rows] + swapped[1:]
    outward = slide(outer, OUTWARD)
    total = run_near(line_ends(), firsts, band, rest, inward)
    return run_share(share, band, bands, total, swapped, outward), swapped, outer


def line_scatter_apart(share, band, bands, first, near, far, last, meanwhile, earlier):
    in_last, in_far, in_near = slide(last, INWARD), slide(far, INWARD), slide(near, INWARD)
    in_last, first = lax.optimization_barrier((in_last, first))
    sum_last = last + in_last
    swap_last = slide(sum_last, MIDDLE)
    other = meanwhile(sum_last)
    in_far, *_ = lax.optimization_barrier((in_far, other, earlier))
    swap_far = slide(far + in_far, MIDDLE)
    outer = first + swap_last
    outward = slide(outer, OUTWARD)
    in_near, _ = lax.optimization_barrier((in_near, outer))
    total = run_near(line_ends(), first, 0, near, in_near)
    return run_share(share, band, bands, total, swap_far, outward), other


def shards(
    query_rows, key_rows, value_rows, grad_out, house_dirs, owners, offsets, w_query, w_key, w_value
):
    tok_rows, width = query_rows.shape
    heads, blocks = width // DH, tok_rows // BLK
    ctx_count, groups = lax.axis_size("ctx"), lax.axis_size("head")
    my_index = lax.axis_index("ctx").astype(jnp.int32)
    ints = jnp.concatenate([my_index.reshape(1), owners.reshape(-1), offsets.reshape(-1)])
    by_hand = ctx_count == 8 and groups == 4 and blocks == 4
    core, across, along = 1, 2, 4

    if by_hand:
        other = hop(house_dirs, core, 8)
        upper = (my_index & core) != 0
        low, high = jnp.where(upper, other, house_dirs), jnp.where(upper, house_dirs, other)
        house_pair = jnp.concatenate([low, high], axis=0)
        value_x, key_y = hop(value_rows, across, 8), hop(key_rows, along, 8)
        key_x, value_y = hop(key_rows, across, 8), hop(value_rows, along, 8)
        house_late, *_ = lax.optimization_barrier((house_pair, value_x, key_y))
        house_parts = [house_pair] + [hop(house_late, t, 8) for t in (2, 4, 6)]
        key_d, value_d = hop(key_y, across, 8), hop(value_x, along, 8)
    else:
        house_parts = [lax.all_gather(house_dirs, "ctx", axis=0, tiled=True)]

    unit, rows, inverse, wide, tall = run_chain(ints, house_parts, heads)
    ready = query_rows
    if by_hand:
        own = (key_rows, value_rows, key_x, value_x, key_y, value_y, key_d, value_d)
        early = lax.optimization_barrier((*own[:6], *house_parts))[:6]
        siblings = [hop(part, core, 8) for part in early]
        ready, *_ = lax.optimization_barrier((query_rows, *siblings[:3]))
    qrot, krot, local, listed_cum = run_rotate(ints, wide, tall, ready, key_rows, heads, blocks)
    if by_hand:
        late = lax.optimization_barrier((*own[6:], qrot))[:2]
        siblings += [hop(part, core, 8) for part in late]
        sources, places = [], []
        for t in range(4):
            for pair in (own[2 * t : 2 * t + 2], siblings[2 * t : 2 * t + 2]):
                places.append(((len(sources), 0), (len(sources) + 1, 0)))
                sources += pair
    else:
        sources = [lax.all_gather(key_rows, "ctx"), lax.all_gather(value_rows, "ctx")]
        places = [((0, 0), (1, 0))]

    rounds = ((0, 1), (1, blocks - 1), (blocks, 1), (blocks + 1, blocks - 1))
    dq, dcum, dk_loc, dv_loc, *outs = run_attend(
        ints,
        sources,
        places,
        (query_rows, qrot, krot, value_rows, grad_out, local, listed_cum),
        heads,
        blocks,
        rounds if by_hand else (),
    )
    weights = (w_query, w_key, w_value)
    flip = jnp.where(by_hand & (lax.axis_index("head") >= 2), 1, 0).astype(jnp.int32).reshape(1)

    arrays = (dk_loc, dv_loc, dq, key_rows, dcum, local)

    def project(block, layout, afters, parts, before=()):
        return run_project(block, groups, layout, flip, afters, parts, before, arrays, weights)

    def share_sums(sums):
        sums = sums.reshape(ctx_count, blocks, 2 * width)
        return lax.all_to_all(sums, "ctx", split_axis=0, concat_axis=0, tiled=True)

    if by_hand:
        got_0 = hop(outs[2], core, 8)
        got_1 = hop(lax.optimization_barrier((outs[3], got_0))[0], core, 8)
        sent_0 = run_merge(outs[0], got_0, 0, 1, [])
        sent_1 = run_merge(outs[1], got_1, 0, 1, [sent_0[0]])
        sent_2 = run_merge(outs[1], got_1, 1, 2, [sent_1[0]])

        def give_back(own, got, first, sent):
            back = [hop(part, t, 8) for part, t in zip(sent, (across, along, across + along))]
            near = [part.reshape(-1, BLK, 2 * width) for part in (own, got)]
            parts = []
            for j in range(sent[0].shape[0]):
                mine = [(part, 4 * (first + j)) for part in near]
                parts.append(mine + [(part, j) for part in back])
            return parts, back

        parts_0, back_0 = give_back(outs[0], got_0, 0, sent_0)
        *later_1, _, _ = lax.optimization_barrier((*sent_1, back_0, sent_2))
        parts_1, back_1 = give_back(outs[1], got_1, 0, later_1)
        *later_2, _ = lax.optimization_barrier((*sent_2, back_1))
        parts_2, _ = give_back(outs[1], got_1, 1, later_2)
        rest_0, dcum_0, *grads_0 = project(0, ((1, 2, 3),), [sent_2[0]], parts_0)
        before = (dq, *grads_0)
        split_off = ((0,), (1, 2, 3))
        firsts, rest_1, dcum_1, *_ = project(1, split_off, [rest_0], parts_1, before)
        inward_0, inward_1 = slide(rest_0, INWARD), slide(rest_1, INWARD)
        far, last, dcum_2, *grads_2 = project(2, ((2,), (3,)), [rest_1], parts_2)
        share, swapped_0, outer_0 = line_scatter(
            None, 0, 4, firsts, rest_0, inward_0, rest_0[1:] + inward_0[1:]
        )
        inward_1, *_ = lax.optimization_barrier((inward_1, swapped_0, dcum_2))
        sum_1 = rest_1[1:] + inward_1[1:]
        share, _, outer_1 = line_scatter(
            share, 1, 4, firsts, rest_1, inward_1, sum_1
        )
        first, near = run_project_more(
            2, groups, ((0,), (1,)), flip, [sum_1], dq, *grads_2, weights
        )

        def meanwhile(after):
            dcums = [dcum_0, dcum_1, dcum_2]
            return run_adjoint(ints, (after, outer_0), dcums, unit, rows, inverse, heads, blocks)

        share, sums = line_scatter_apart(
            share, 1, 2, first, near, far, last, meanwhile, outer_1
        )
        got = share_sums(sums)
    else:
        spots = (owners * blocks + offsets).reshape(-1)
        empty = jnp.zeros((ctx_count * blocks, BLK, 2 * width), BF16)
        filled = empty.at[spots].add(outs[0])
        back = lax.psum_scatter(filled, "ctx", scatter_dimension=0, tiled=True)
        dcums = []
        share = jnp.zeros((tok_rows, w_query.shape[0] // groups), BF16)
        for j in range(blocks):
            term, dcum_out, _, _ = project(
                j, (tuple(range(groups)),), [], [[(back, j)]]
            )
            dcums.append(dcum_out)
            done = lax.psum_scatter(term, "head", scatter_dimension=0, tiled=False)
            share = lax.dynamic_update_slice(share, done, (j * BLK, 0))

        got = share_sums(run_adjoint(ints, (), dcums, unit, rows, inverse, heads, blocks))

    house_grad = run_house(ints, got, unit, rows, house_dirs, heads, blocks)
    return (share, house_grad)


def solution(mesh):
    placed = (
        P("ctx", "head"),
        P("ctx", "head"),
        P("ctx", "head"),
        P("ctx", "head"),
        P("ctx", "head"),
        P("ctx", None),
        P("ctx", None),
        P(None, "head"),
        P(None, "head"),
        P(None, "head"),
    )
    return jax.shard_map(
        shards,
        mesh=mesh,
        in_specs=placed,
        out_specs=(P("ctx", "head"), P("ctx", "head")),
        check_vma=False,
    )
```

```python
import functools
import math

import jax
import jax.numpy as jnp
from jax import lax
from jax.experimental import pallas as pl
from jax.experimental.pallas import tpu as pltpu
from jax.sharding import PartitionSpec as P

DH = 128
BLK = 128
MAXL = 2
HIGH = lax.Precision.HIGHEST
F32 = jnp.float32
BF16 = jnp.bfloat16


def nn(a, b):
    return lax.dot_general(a, b, (((1,), (0,)), ((), ())), preferred_element_type=F32)


def nt(a, b):
    return lax.dot_general(a, b, (((1,), (1,)), ((), ())), preferred_element_type=F32)


def tn(a, b):
    return lax.dot_general(a, b, (((0,), (0,)), ((), ())), preferred_element_type=F32)


def nn_high(a, b):
    return lax.dot_general(
        a, b, (((1,), (0,)), ((), ())), precision=HIGH, preferred_element_type=F32
    )


def nt_high(a, b):
    return lax.dot_general(
        a, b, (((1,), (1,)), ((), ())), precision=HIGH, preferred_element_type=F32
    )


def split(value):
    top = value.astype(BF16)
    return top, (value - top.astype(F32)).astype(BF16)


def iota(shape, dim):
    return lax.broadcasted_iota(jnp.int32, shape, dim)


def head(h):
    return slice(h * DH, (h + 1) * DH)


def listed(ints_ref, entry, entries):
    return ints_ref[1 + entry], ints_ref[1 + entries + entry]


def grant(mebibytes):
    return pltpu.CompilerParams(vmem_limit_bytes=mebibytes * 1024 * 1024)


def cost(microseconds):
    return pl.CostEstimate(
        flops=int(microseconds * 1.15e9), bytes_accessed=1 << 20, transcendentals=0
    )


def in_smem(count):
    return [pl.BlockSpec(memory_space=pltpu.SMEM)] * count


def in_vmem(count):
    return [pl.BlockSpec(memory_space=pltpu.VMEM)] * count


def chain_kernel(heads, parts, ints_ref, *refs):
    house_refs = refs[:parts]
    unit_ref, rows_ref, inv_ref, wide_ref, tall_ref, unit_h, house_all = refs[parts:]
    count = unit_ref.shape[0]
    span = count // parts
    for t, ref in enumerate(house_refs):
        place = (ints_ref[0] // (8 // parts)) ^ t if parts > 1 else 0
        house_all[pl.ds(pl.multiple_of(place * span, span), span), :] = ref[...]
    eye = (iota((count, count), 0) == iota((count, count), 1)).astype(F32)
    for h in range(heads):
        house = house_all[:, head(h)]
        lengths = jnp.sqrt(jnp.sum(house * house, axis=1, keepdims=True) + 1e-06)
        unit_ref[:, head(h)] = house / lengths
        unit_h[h] = house / lengths
        inv_ref[h] = eye

    def eliminate(step, carry):
        below = iota((count, 1), 0) > step
        for h in range(heads):
            pivot = unit_h[h, pl.ds(step, 1), :]
            overlap = jnp.sum(unit_h[h] * pivot, axis=1, keepdims=True)
            factor = jnp.where(below, 2.0 * overlap, 0.0)
            inv_ref[h] = inv_ref[h] - factor * inv_ref[h, pl.ds(step, 1), :]
        return carry

    lax.fori_loop(0, count, eliminate, 0)
    eye_wide = (iota((DH, DH), 0) == iota((DH, DH), 1)).astype(F32)
    for h in range(heads):
        units = unit_ref[:, head(h)]
        rows = nn_high(inv_ref[h], units)
        rows_ref[:, head(h)] = rows
        unit_hi, unit_lo = split(nt_high(eye_wide, units))
        rows_hi, rows_lo = split(rows)
        wide_ref[h] = jnp.concatenate([unit_hi, unit_hi, unit_lo], axis=1)
        tall_ref[h] = jnp.concatenate([rows_hi, rows_lo, rows_hi], axis=0)


def run_chain(ints, house_parts, heads):
    span, width = house_parts[0].shape
    parts = len(house_parts)
    count = span * parts
    return pl.pallas_call(
        functools.partial(chain_kernel, heads, parts),
        out_shape=[
            jax.ShapeDtypeStruct((count, width), F32),
            jax.ShapeDtypeStruct((count, width), F32),
            jax.ShapeDtypeStruct((heads, count, count), F32),
            jax.ShapeDtypeStruct((heads, DH, 3 * count), BF16),
            jax.ShapeDtypeStruct((heads, 3 * count, DH), BF16),
        ],
        in_specs=in_smem(1) + in_vmem(parts),
        out_specs=in_vmem(5),
        scratch_shapes=[pltpu.VMEM((heads, count, DH), F32), pltpu.VMEM((count, width), F32)],
        compiler_params=grant(12),
        cost_estimate=cost(6),
        name="house_chain",
    )(ints, *house_parts)


def rotate_kernel(
    heads,
    blocks,
    ints_ref,
    wide_ref,
    tall_ref,
    query_ref,
    key_ref,
    qrot_ref,
    krot_ref,
    local_ref,
    listed_ref,
):
    count = wide_ref.shape[2] // 3
    entries = blocks * MAXL
    column = iota((DH, 3 * count), 1) % count
    eye = (iota((DH, DH), 0) == iota((DH, DH), 1)).astype(F32)

    def cumulative(h, block):
        kept = jnp.where(column <= block, wide_ref[h].astype(F32), 0.0).astype(BF16)
        return split(eye - 2.0 * nn(kept, tall_ref[h]))

    base = ints_ref[0] * blocks

    def local_block(b, carry):
        here = pl.ds(pl.multiple_of(b * BLK, BLK), BLK)
        for h in range(heads):
            hi, lo = cumulative(h, base + b)
            local_ref[b, h] = hi
            query, key = query_ref[here, head(h)], key_ref[here, head(h)]
            qrot_ref[here, head(h)] = (nn(query, hi) + nn(query, lo)).astype(BF16)
            krot_ref[here, head(h)] = (nn(key, hi) + nn(key, lo)).astype(BF16)
        return carry

    lax.fori_loop(0, blocks, local_block, 0)

    def listed_block(e, carry):
        owner, offset = listed(ints_ref, e, entries)
        for h in range(heads):
            hi, lo = cumulative(h, owner * blocks + offset)
            listed_ref[e, h, :DH] = hi
            listed_ref[e, h, DH:] = lo
        return carry

    lax.fori_loop(0, entries, listed_block, 0)


def run_rotate(ints, wide, tall, query_rows, key_rows, heads, blocks):
    rows, width = query_rows.shape
    entries = blocks * MAXL
    return pl.pallas_call(
        functools.partial(rotate_kernel, heads, blocks),
        out_shape=[
            jax.ShapeDtypeStruct((rows, width), BF16),
            jax.ShapeDtypeStruct((rows, width), BF16),
            jax.ShapeDtypeStruct((blocks, heads, DH, DH), BF16),
            jax.ShapeDtypeStruct((entries, heads, 2 * DH, DH), BF16),
        ],
        in_specs=in_smem(1) + in_vmem(4),
        out_specs=in_vmem(4),
        compiler_params=grant(16),
        cost_estimate=cost(9),
        name="rotate",
    )(ints, wide, tall, query_rows, key_rows)


def attend_kernel(heads, blocks, places, pieces, *refs):
    ints_ref = refs[0]
    source_count = 1 + max(place[0] for pair in places for place in pair)
    sources = refs[1 : 1 + source_count]
    refs = refs[1 + source_count :]
    (query_ref, qrot_ref, krot_ref, value_ref, grad_ref, local_ref, listed_ref) = refs[:7]
    dq_ref, dcum_ref, dk_ref, dv_ref = refs[7:11]
    outs = refs[11 : 11 + max(len(pieces), 1)]
    refs = refs[11 + max(len(pieces), 1) :]
    dq_all, dcum_all, dk_all, dv_all, grad_sems, far_keys, far_values, sems = refs[:8]
    entries = blocks * MAXL
    scaling = DH ** (-0.5)
    log_scale = scaling * math.log2(math.e)

    def start(e, src, kind, slot, where):
        pltpu.make_async_copy(src.at[where], slot.at[e], sems.at[kind, e]).start()

    for e in range(entries):
        owner, offset = listed(ints_ref, e, entries)
        row = pl.multiple_of(offset * BLK, BLK)
        if len(places) == 1:
            start(e, sources[0], 0, far_keys, (owner, pl.ds(row, BLK)))
            start(e, sources[1], 1, far_values, (owner, pl.ds(row, BLK)))
        else:
            distance = owner ^ ints_ref[0]
            for r, (key_place, value_place) in enumerate(places):

                @pl.when(distance == r)
                def _():
                    source, first = key_place
                    start(e, sources[source], 0, far_keys, pl.ds(first + row, BLK))
                    source, first = value_place
                    start(e, sources[source], 1, far_values, pl.ds(first + row, BLK))

    out_copies = []
    if pieces:
        payloads, out_sems = refs[8 : 8 + heads], refs[8 + heads]
        for payload in payloads:
            payload[...] = jnp.zeros_like(payload)
    for kind, slots in ((0, far_keys), (1, far_values)):
        for e in range(entries):
            pltpu.make_async_copy(slots.at[e], slots.at[e], sems.at[kind, e]).wait()

    later = iota((BLK, BLK), 0) > iota((BLK, BLK), 1)
    empty = jnp.zeros((BLK, DH), BF16)
    steps = range(blocks)
    for h in range(heads):
        lanes = head(h)
        spans = [slice(a * BLK, (a + 1) * BLK) for a in steps]
        both, keys, values = [], [], []
        for a in steps:
            qrot, grad = qrot_ref[spans[a], lanes], grad_ref[spans[a], lanes]
            upper = jnp.concatenate([qrot, empty], axis=1)
            lower = jnp.concatenate([empty, grad], axis=1)
            both.append(jnp.concatenate([upper, lower], axis=0))
            keys.append([krot_ref[spans[b], lanes] for b in range(a + 1)])
            values.append([value_ref[spans[b], lanes] for b in range(a + 1)])
            for l in range(MAXL):
                e = a * MAXL + l
                raw = far_keys[e, :, lanes]
                raw = jnp.concatenate([raw, raw], axis=1)
                keys[a].append(nn(raw, listed_ref[e, h]).astype(BF16))
                values[a].append(far_values[e, :, lanes])
        scores, dprobs, tops = [], [], []
        for a in steps:
            scores.append([])
            dprobs.append([])
            top = None
            for b in range(a + 1 + MAXL):
                pair = nt(jnp.concatenate([keys[a][b], values[a][b]], axis=1), both[a])
                part = pair[:, :BLK] * log_scale
                if b == a:
                    part = jnp.where(later, -jnp.inf, part)
                scores[a].append(part)
                dprobs[a].append(pair[:, BLK:])
                top = part if top is None else jnp.maximum(top, part)
            tops.append(jnp.max(top, axis=0, keepdims=True))
        weights, inverses, deltas = [], [], []
        for a in steps:
            weights.append([])
            total, inner = None, None
            for part, dprob in zip(scores[a], dprobs[a]):
                weight = jnp.exp2(part - tops[a])
                weights[a].append(weight)
                product = weight * dprob
                total = weight if total is None else total + weight
                inner = product if inner is None else inner + product
            inverses.append(1.0 / jnp.sum(total, axis=0, keepdims=True))
            deltas.append(jnp.sum(inner, axis=0, keepdims=True) * inverses[a])
        dscores, pairs = [], []
        for a in steps:
            dscores.append([])
            pairs.append([])
            for b in range(a + 1 + MAXL):
                probs = weights[a][b] * inverses[a]
                dscore = (probs * (dprobs[a][b] - deltas[a])).astype(BF16)
                dscores[a].append(dscore)
                wide = jnp.concatenate([dscore, probs.astype(BF16)], axis=1)
                pairs[a].append(nn(wide, both[a]))
        for b in steps:
            total = pairs[b][b]
            for a in range(b + 1, blocks):
                total = total + pairs[a][b]
            dk_all[h, spans[b]] = total[:, :DH] * scaling
            dv_all[h, spans[b]] = total[:, DH:]
        for e in range(entries):
            pair = pairs[e // MAXL][e // MAXL + 1 + e % MAXL]
            dkey, dvalue = (pair[:, :DH] * scaling).astype(BF16), pair[:, DH:].astype(BF16)
            if pieces:
                owner, offset = listed(ints_ref, e, entries)
                distance = owner ^ ints_ref[0]
                at = (distance & 1) * blocks + offset
                payloads[h][at, distance >> 1, :, :DH] += dkey
                payloads[h][at, distance >> 1, :, DH:] += dvalue
            else:
                outs[0][e, :, 2 * h * DH : (2 * h + 1) * DH] = dkey
                outs[0][e, :, (2 * h + 1) * DH : (2 * h + 2) * DH] = dvalue
        halves = []
        for a in steps:
            wide, tall = jnp.concatenate(dscores[a], axis=0), jnp.concatenate(keys[a], axis=0)
            halves.append(split(tn(wide, tall) * scaling))
        for a in steps:
            dq_top, dq_low = halves[a]
            dq_all[h, spans[a]] = nt(dq_top, local_ref[a, h]).astype(BF16)
            query = query_ref[spans[a], lanes]
            query = jnp.concatenate([query, query], axis=0)
            dcum_all[h, a] = tn(query, jnp.concatenate([dq_top, dq_low], axis=0))
        for i, (source, where) in enumerate(
            (
                (dk_all.at[h], dk_ref.at[:, lanes]),
                (dv_all.at[h], dv_ref.at[:, lanes]),
                (dq_all.at[h], dq_ref.at[:, lanes]),
                (dcum_all.at[h], dcum_ref.at[:, h]),
            )
        ):
            copy = pltpu.make_async_copy(source, where, grad_sems.at[i, h])
            copy.start()
            out_copies.append(copy)
        for i, (first, size) in enumerate(pieces):
            where = outs[i].at[:, :, :, 2 * h * DH : (2 * h + 2) * DH]
            source = payloads[h].at[pl.ds(first, size)]
            copy = pltpu.make_async_copy(source, where, out_sems.at[i, h])
            copy.start()
            out_copies.append(copy)
    for copy in out_copies:
        copy.wait()


def run_attend(ints, sources, places, arrays, heads, blocks, pieces):
    rows, width = arrays[0].shape
    entries = blocks * MAXL
    any_spec = pl.BlockSpec(memory_space=pl.ANY)
    scratch = [
        pltpu.VMEM((heads, rows, DH), BF16),
        pltpu.VMEM((heads, blocks, DH, DH), F32),
        pltpu.VMEM((heads, rows, DH), F32),
        pltpu.VMEM((heads, rows, DH), F32),
        pltpu.SemaphoreType.DMA((4, heads)),
        pltpu.VMEM((entries, BLK, width), BF16),
        pltpu.VMEM((entries, BLK, width), BF16),
        pltpu.SemaphoreType.DMA((2, entries)),
    ]
    if pieces:
        chips = len(places) // 2
        out_parts = [
            pltpu.HBM((size, chips, BLK, 2 * width), BF16) for _, size in pieces
        ]
        part_specs = [any_spec] * len(pieces)
        scratch += [pltpu.VMEM((2 * blocks, chips, BLK, 2 * DH), BF16)] * heads
        scratch += [pltpu.SemaphoreType.DMA((len(pieces), heads))]
    else:
        out_parts = [jax.ShapeDtypeStruct((entries, BLK, 2 * width), BF16)]
        part_specs = in_vmem(1)
    return pl.pallas_call(
        functools.partial(attend_kernel, heads, blocks, places, pieces),
        out_shape=[
            pltpu.HBM((rows, width), BF16),
            pltpu.HBM((blocks, heads, DH, DH), F32),
            pltpu.HBM((rows, width), F32),
            pltpu.HBM((rows, width), F32),
        ]
        + out_parts,
        in_specs=in_smem(1) + [any_spec] * len(sources) + in_vmem(7),
        out_specs=[pl.BlockSpec(memory_space=pltpu.HBM)] * 4 + part_specs,
        scratch_shapes=scratch,
        compiler_params=grant(36),
        cost_estimate=cost(15),
        name="attend",
    )(ints, *sources, *arrays)


def merge_kernel(own_ref, got_ref, *refs):
    for i, ref in enumerate(refs[-3:]):
        total = own_ref[0, i + 1].astype(F32) + got_ref[0, i + 1].astype(F32)
        ref[0] = total.astype(BF16)


def run_merge(own, got, first, size, afters):
    _, chips, rows, width = own.shape
    cut = 2
    lanes = width // cut
    whole = pl.BlockSpec((1, chips, rows, lanes), lambda j, c: (first + j, 0, 0, c))
    return pl.pallas_call(
        merge_kernel,
        grid=(size, cut),
        out_shape=[jax.ShapeDtypeStruct((size, rows, width), BF16)] * (chips - 1),
        in_specs=[whole] * 2
        + [pl.BlockSpec((1, 16, 128), lambda j, c: (0, 0, 0))] * len(afters),
        out_specs=[pl.BlockSpec((1, rows, lanes), lambda j, c: (j, 0, c))] * (chips - 1),
        compiler_params=grant(60),
        cost_estimate=cost(2),
        name="merge",
    )(own, got, *afters)


def start_tiles(chunks, groups, flip_ref, weight_refs, tiles, sems):
    count, _, tile, _ = tiles.shape
    per = count // len(chunks)
    copies = []
    for t in range(count):
        m = chunks[t // per][0]
        row = ((m + flip_ref[0] * (groups - 1 - 2 * m)) * per + t % per) * tile
        rows = pl.ds(pl.multiple_of(row, tile), tile)
        for w, ref in enumerate(weight_refs):
            copy = pltpu.make_async_copy(ref.at[rows], tiles.at[t, w], sems.at[t, w])
            copy.start()
            copies.append(copy)
    return copies


def multiply_tiles(chunks, copies, tiles, out_refs, grads_of):
    count, _, tile, _ = tiles.shape
    per = count // len(chunks)
    for t in range(count):
        term = None
        m, out, at = chunks[t // per]
        for w, grad in enumerate(grads_of(m)):
            copies[3 * t + w].wait()
            part = nt(tiles[t, w], grad)
            term = part if term is None else term + part
        spot = slice(t % per * tile, (t % per + 1) * tile)
        out_refs[out][at, :, spot] = term.T.astype(BF16)


def project_kernel(heads, parts, size, groups, before, layout, afters, flip_ref, *refs):
    refs = refs[afters:]
    outs = len(layout)
    chunks = [(m, i, at) for i, row in enumerate(layout) for at, m in enumerate(row)]
    tiles, sems = refs[-2:]
    part_refs, refs = refs[: size * parts], refs[size * parts :]
    before_refs, refs = refs[:before], refs[before:]
    dk_loc, dv_loc, dq_ref, key_ref, dcum_in, cum_ref = refs[:6]
    weight_refs, out_refs = refs[6:9], refs[9 : 9 + outs]
    dcum_out, dk_out, dv_out = refs[9 + outs : 12 + outs]
    copies = start_tiles(chunks, groups, flip_ref, weight_refs, tiles, sems)
    earlier = ()
    dk_rows, dv_rows = [], []
    for j in range(size):
        here = slice(j * BLK, (j + 1) * BLK)
        dk, dv = [], []
        for h in range(heads):
            both = slice(2 * h * DH, (2 * h + 2) * DH)
            total = part_refs[j * parts][0, :, both].astype(F32)
            for ref in part_refs[j * parts + 1 : (j + 1) * parts]:
                total = total + ref[0, :, both].astype(F32)
            dv.append((dv_loc[here, head(h)] + total[:, DH:]).astype(BF16))
            dk_top, dk_low = split(dk_loc[here, head(h)] + total[:, :DH])
            dk.append(nt(dk_top, cum_ref[j, h]).astype(BF16))
            key = key_ref[here, head(h)]
            key = jnp.concatenate([key, key], axis=0)
            dcum = tn(key, jnp.concatenate([dk_top, dk_low], axis=0))
            dcum_out[j, h] = dcum_in[j, h] + dcum
        dk_rows.append(jnp.concatenate(dk, axis=1))
        dv_rows.append(jnp.concatenate(dv, axis=1))
    dk_all, dv_all = jnp.concatenate(dk_rows, axis=0), jnp.concatenate(dv_rows, axis=0)
    dk_out[...] = dk_all
    dv_out[...] = dv_all
    grads = (dq_ref[...], dk_all, dv_all)
    if before:
        earlier = [
            jnp.concatenate([old[...], new], axis=0) for old, new in zip(before_refs, grads)
        ]

    multiply_tiles(
        chunks, copies, tiles, out_refs, lambda m: earlier if before and m == 0 else grads
    )


def project_more_kernel(groups, layout, afters, flip_ref, *refs):
    refs = refs[afters:]
    chunks = [(m, i, at) for i, row in enumerate(layout) for at, m in enumerate(row)]
    tiles, sems = refs[-2:]
    copies = start_tiles(chunks, groups, flip_ref, refs[3:6], tiles, sems)
    grads = [ref[...] for ref in refs[:3]]
    multiply_tiles(chunks, copies, tiles, refs[6:-2], lambda m: grads)


def run_project_more(block, groups, layout, flip, afters, dq, dk, dv, weights):
    rows, width = dk.shape
    model = weights[0].shape[0]
    chunk = model // groups
    tile = min(512, chunk)
    tile_count = sum(map(len, layout)) * chunk // tile

    def whole(*shape):
        return pl.BlockSpec(shape, lambda t: (0,) * len(shape))

    shapes = [(len(row), rows, chunk) for row in layout]
    return pl.pallas_call(
        functools.partial(project_more_kernel, groups, layout, len(afters)),
        grid=(1,),
        in_specs=in_smem(1)
        + [whole(1, 16, 128)] * len(afters)
        + [pl.BlockSpec((rows, width), lambda t: (block * BLK // rows, 0))]
        + [whole(rows, width)] * 2
        + [pl.BlockSpec(memory_space=pl.ANY)] * 3,
        out_specs=[whole(*shape) for shape in shapes],
        scratch_shapes=[
            pltpu.VMEM((tile_count, 3, tile, width), BF16),
            pltpu.SemaphoreType.DMA((tile_count, 3)),
        ],
        out_shape=[jax.ShapeDtypeStruct(shape, BF16) for shape in shapes],
        compiler_params=grant(60),
        cost_estimate=cost(3 * sum(map(len, layout))),
        name="project_more",
    )(flip, *afters, dq, dk, dv, *weights)


def run_project(block, groups, layout, flip, afters, parts, before, arrays, weights):
    dk_loc, dv_loc, dq, key_rows, dcum, cum = arrays
    size, width = len(parts), dq.shape[1]
    heads = width // DH
    model = weights[0].shape[0]
    chunk = model // groups
    tile = min(512, chunk)
    rows = size * BLK
    tile_count = sum(map(len, layout)) * chunk // tile

    def part_spec(index):
        return pl.BlockSpec((1, BLK, 2 * width), lambda t: (index, 0, 0))

    def whole(*shape):
        return pl.BlockSpec(shape, lambda t: (0,) * len(shape))

    rows_spec = pl.BlockSpec((rows, width), lambda t: (block // size, 0))
    head_spec = pl.BlockSpec((size, heads, DH, DH), lambda t: (block // size, 0, 0, 0))
    flat = [part for row in parts for part in row]
    heights = [2 * rows if before and row == (0,) else rows for row in layout]
    shapes = [(len(row), height, chunk) for row, height in zip(layout, heights)]
    return pl.pallas_call(
        functools.partial(
            project_kernel,
            heads,
            len(parts[0]),
            size,
            groups,
            len(before),
            layout,
            len(afters),
        ),
        grid=(1,),
        in_specs=in_smem(1)
        + [whole(1, 16, 128)] * len(afters)
        + [part_spec(index) for _, index in flat]
        + [whole(rows, width)] * len(before)
        + [rows_spec] * 4
        + [head_spec] * 2
        + [pl.BlockSpec(memory_space=pl.ANY)] * 3,
        out_specs=[whole(*shape) for shape in shapes]
        + [whole(size, heads, DH, DH)]
        + [whole(rows, width)] * 2,
        scratch_shapes=[
            pltpu.VMEM((tile_count, 3, tile, width), BF16),
            pltpu.SemaphoreType.DMA((tile_count, 3)),
        ],
        out_shape=[jax.ShapeDtypeStruct(shape, BF16) for shape in shapes]
        + [jax.ShapeDtypeStruct((size, heads, DH, DH), F32)]
        + [jax.ShapeDtypeStruct((rows, width), BF16)] * 2,
        compiler_params=grant(60),
        cost_estimate=cost(3 * sum(map(len, layout))),
        name="project",
    )(
        flip,
        *afters,
        *[part for part, _ in flat],
        *before,
        dk_loc,
        dv_loc,
        dq,
        key_rows,
        dcum,
        cum,
        *weights,
    )


def adjoint_kernel(heads, blocks, afters, ints_ref, *refs):
    refs = refs[afters:]
    dcums = [ref.at[j] for ref in refs[:-4] for j in range(ref.shape[0])]
    unit_ref, rows_ref, inv_ref, out_ref = refs[-4:]
    count, width = unit_ref.shape
    stacked = (blocks * count, count)
    eye = (iota((count, count), 0) == iota((count, count), 1)).astype(F32)
    base = ints_ref[0] * blocks
    level, col = iota(stacked, 0), iota(stacked, 1)
    row = level % count
    mine = base + level // count
    alive = row[:, :1] <= mine[:, :1]
    for h in range(heads):
        units, rows, inverse = unit_ref[:, head(h)], rows_ref[:, head(h)], inv_ref[h]
        inverse_t = nt_high(eye, inverse)
        moved = jnp.concatenate([nt_high(rows, dcum[h]) for dcum in dcums], axis=0)
        overlap = jnp.where(col <= mine, nt_high(moved, units), 0.0)
        gamma = nn_high(overlap, inverse)
        gamma = jnp.where((row < col) & (col <= mine), gamma, 0.0)
        beta = jnp.concatenate([eye - inverse_t] * blocks, axis=0)
        beta = jnp.where(col <= mine, beta, 0.0)
        x_all = jnp.where(alive, moved - 2.0 * nn_high(gamma, units), 0.0)
        turned = jnp.concatenate([units] * blocks, axis=0) - nn_high(beta, units)
        turned = jnp.where(alive, turned, 0.0)
        x_total, y_total = None, None
        for j, dcum in enumerate(dcums):
            here = slice(j * count, (j + 1) * count)
            y_part = nn_high(turned[here], dcum[h])
            x_total = x_all[here] if j == 0 else x_total + x_all[here]
            y_total = y_part if j == 0 else y_total + y_part
        out_ref[:, head(h)] = x_total
        out_ref[:, slice(width + h * DH, width + (h + 1) * DH)] = y_total


def run_adjoint(ints, afters, dcums, unit, rows, inverse, heads, blocks):
    count, width = unit.shape
    return pl.pallas_call(
        functools.partial(adjoint_kernel, heads, blocks, len(afters)),
        out_shape=jax.ShapeDtypeStruct((count, 2 * width), F32),
        in_specs=in_smem(1)
        + [pl.BlockSpec(memory_space=pl.ANY)] * len(afters)
        + in_vmem(len(dcums) + 3),
        out_specs=pl.BlockSpec(memory_space=pltpu.VMEM),
        compiler_params=grant(60),
        cost_estimate=cost(0.2),
        name="adjoint",
    )(ints, *afters, *dcums, unit, rows, inverse)


def house_kernel(heads, blocks, base_ref, got_ref, unit_ref, rows_ref, house_ref, out_ref):
    count, width = unit_ref.shape
    total = jnp.sum(got_ref[...], axis=0)
    for h in range(heads):
        x_part = total[:, head(h)]
        y_part = total[:, slice(width + h * DH, width + (h + 1) * DH)]
        along = nt_high(y_part, rows_ref[:, head(h)])
        spot = iota((blocks, count), 0) + base_ref[0] * blocks
        along = jnp.where(iota((blocks, count), 1) < spot, along, 0.0)
        turned = y_part - 2.0 * nn_high(along, unit_ref[:, head(h)])
        dunit = -2.0 * (x_part + turned)
        house = house_ref[:, head(h)]
        lengths = jnp.sqrt(jnp.sum(house * house, axis=1, keepdims=True) + 1e-06)
        unit = house / lengths
        inner = jnp.sum(unit * dunit, axis=1, keepdims=True)
        out_ref[:, head(h)] = (dunit - unit * inner) / lengths


def run_house(ints, got, unit, rows, house_dirs, heads, blocks):
    return pl.pallas_call(
        functools.partial(house_kernel, heads, blocks),
        out_shape=jax.ShapeDtypeStruct(house_dirs.shape, F32),
        in_specs=in_smem(1) + in_vmem(4),
        out_specs=pl.BlockSpec(memory_space=pltpu.VMEM),
        compiler_params=grant(60),
        cost_estimate=cost(2),
        name="house_grad",
    )(ints, got, unit, rows, house_dirs)


def hop(value, distance, count):
    return lax.ppermute(value, "ctx", [(i, i ^ distance) for i in range(count)])


def slide(value, pairs):
    return lax.ppermute(value, "head", pairs)


INWARD = [(0, 1), (3, 2)]
MIDDLE = [(1, 2), (2, 1)]
OUTWARD = [(1, 0), (2, 3)]


def near_kernel(ends_ref, first_ref, near_ref, inward_ref, out_ref):
    mine = jnp.where(ends_ref[0] > 0, first_ref[0], near_ref[0]).astype(F32)
    out_ref[...] = mine + inward_ref[0].astype(F32)


def run_near(ends, first, band, near, inward):
    _, rows, width = near.shape
    return pl.pallas_call(
        near_kernel,
        grid=(1,),
        out_shape=jax.ShapeDtypeStruct((rows, width), F32),
        in_specs=in_smem(1)
        + [pl.BlockSpec((1, rows, width), lambda t: (0, band, 0))]
        + [pl.BlockSpec((1, rows, width), lambda t: (0, 0, 0))] * 2,
        out_specs=pl.BlockSpec((rows, width), lambda t: (0, 0)),
        compiler_params=grant(60),
        cost_estimate=cost(5),
        name="near_sum",
    )(ends, first, near, inward)


def share_kernel(*refs):
    total_ref, far_ref, outward_ref, out_ref = refs[-4:]
    far = far_ref[0].astype(F32) + outward_ref[0].astype(F32)
    out_ref[...] = (total_ref[...] + far).astype(BF16)


def run_share(share, band, bands, total, far, outward):
    rows, width = total.shape
    tile = min(512, width)
    part = pl.BlockSpec((1, rows, tile), lambda t: (0, 0, t))
    given = [] if share is None else [share]
    return pl.pallas_call(
        share_kernel,
        grid=(width // tile,),
        out_shape=jax.ShapeDtypeStruct((bands * rows, width), BF16),
        in_specs=[pl.BlockSpec(memory_space=pl.ANY)] * len(given)
        + [pl.BlockSpec((rows, tile), lambda t: (0, t)), part, part],
        out_specs=pl.BlockSpec((rows, tile), lambda t: (band, t)),
        input_output_aliases={0: 0} if given else {},
        compiler_params=grant(60),
        cost_estimate=cost(2),
        name="share",
    )(*given, total, far, outward)


def line_ends():
    place = lax.axis_index("head")
    return ((place == 0) | (place == 3)).astype(jnp.int32).reshape(1)


def line_scatter(band, firsts, rest, inward, inner):
    swapped = slide(inner, MIDDLE)
    firsts, swapped = lax.optimization_barrier((firsts, swapped))
    rows = rest.shape[1]
    outer = firsts[:, band * rows : (band + 1) * rows] + swapped[1:]
    outward = slide(outer, OUTWARD)
    return swapped, outward, outer


def line_scatter_apart(first, near, far, last, meanwhile, exchange, earlier):
    in_last, in_far, in_near = slide(last, INWARD), slide(far, INWARD), slide(near, INWARD)
    in_last, first = lax.optimization_barrier((in_last, first))
    sum_last = last + in_last
    swap_last = slide(sum_last, MIDDLE)
    other = meanwhile(sum_last)
    in_far, other = lax.optimization_barrier((in_far, other))
    sum_far = far + in_far
    swap_far = slide(sum_far, MIDDLE)
    other, _ = lax.optimization_barrier((other, sum_far))
    other = exchange(other)
    swap_last, _ = lax.optimization_barrier((swap_last, earlier))
    outer = first + swap_last
    outward = slide(outer, OUTWARD)
    other, in_near, _ = lax.optimization_barrier((other, in_near, outer))
    total = run_near(line_ends(), first, 0, near, in_near)
    return total, swap_far, outward, other, outer


def shards(
    query_rows, key_rows, value_rows, grad_out, house_dirs, owners, offsets, w_query, w_key, w_value
):
    tok_rows, width = query_rows.shape
    heads, blocks = width // DH, tok_rows // BLK
    ctx_count, groups = lax.axis_size("ctx"), lax.axis_size("head")
    my_index = lax.axis_index("ctx").astype(jnp.int32)
    ints = jnp.concatenate([my_index.reshape(1), owners.reshape(-1), offsets.reshape(-1)])
    by_hand = ctx_count == 8 and groups == 4 and blocks == 4
    core, across, along = 1, 2, 4

    if by_hand:
        other = hop(house_dirs, core, 8)
        upper = (my_index & core) != 0
        low, high = jnp.where(upper, other, house_dirs), jnp.where(upper, house_dirs, other)
        house_pair = jnp.concatenate([low, high], axis=0)
        value_x, key_y = hop(value_rows, across, 8), hop(key_rows, along, 8)
        key_x, value_y = hop(key_rows, across, 8), hop(value_rows, along, 8)
        house_late, *_ = lax.optimization_barrier((house_pair, value_x, key_y))
        house_parts = [house_pair] + [hop(house_late, t, 8) for t in (2, 4, 6)]
        key_d, value_d = hop(key_y, across, 8), hop(value_x, along, 8)
    else:
        house_parts = [lax.all_gather(house_dirs, "ctx", axis=0, tiled=True)]

    unit, rows, inverse, wide, tall = run_chain(ints, house_parts, heads)
    ready = query_rows
    if by_hand:
        own = (key_rows, value_rows, key_x, value_x, key_y, value_y, key_d, value_d)
        early = lax.optimization_barrier((*own[:6], *house_parts))[:6]
        siblings = [hop(part, core, 8) for part in early]
        ready, *_ = lax.optimization_barrier((query_rows, *siblings[:3]))
    qrot, krot, local, listed_cum = run_rotate(ints, wide, tall, ready, key_rows, heads, blocks)
    if by_hand:
        late = lax.optimization_barrier((*own[6:], qrot))[:2]
        siblings += [hop(part, core, 8) for part in late]
        sources, places = [], []
        for t in range(4):
            for pair in (own[2 * t : 2 * t + 2], siblings[2 * t : 2 * t + 2]):
                places.append(((len(sources), 0), (len(sources) + 1, 0)))
                sources += pair
    else:
        sources = [lax.all_gather(key_rows, "ctx"), lax.all_gather(value_rows, "ctx")]
        places = [((0, 0), (1, 0))]

    rounds = ((0, 1), (1, blocks - 1), (blocks, 1), (blocks + 1, blocks - 1))
    dq, dcum, dk_loc, dv_loc, *outs = run_attend(
        ints,
        sources,
        places,
        (query_rows, qrot, krot, value_rows, grad_out, local, listed_cum),
        heads,
        blocks,
        rounds if by_hand else (),
    )
    weights = (w_query, w_key, w_value)
    flip = jnp.where(by_hand & (lax.axis_index("head") >= 2), 1, 0).astype(jnp.int32).reshape(1)

    arrays = (dk_loc, dv_loc, dq, key_rows, dcum, local)

    def project(block, layout, afters, parts, before=()):
        return run_project(block, groups, layout, flip, afters, parts, before, arrays, weights)

    def share_sums(sums):
        sums = sums.reshape(ctx_count, blocks, 2 * width)
        return lax.all_to_all(sums, "ctx", split_axis=0, concat_axis=0, tiled=True)

    if by_hand:
        got_0 = hop(outs[2], core, 8)
        got_1 = hop(lax.optimization_barrier((outs[3], got_0))[0], core, 8)
        sent_0 = run_merge(outs[0], got_0, 0, 1, [])
        sent_1 = run_merge(outs[1], got_1, 0, 1, [sent_0[0]])
        sent_2 = run_merge(outs[1], got_1, 1, 2, [sent_1[0]])

        def give_back(own, got, first, sent):
            back = [hop(part, t, 8) for part, t in zip(sent, (across, along, across + along))]
            near = [part.reshape(-1, BLK, 2 * width) for part in (own, got)]
            parts = []
            for j in range(sent[0].shape[0]):
                mine = [(part, 4 * (first + j)) for part in near]
                parts.append(mine + [(part, j) for part in back])
            return parts, back

        parts_0, back_0 = give_back(outs[0], got_0, 0, sent_0)
        *later_1, _, _ = lax.optimization_barrier((*sent_1, back_0, sent_2))
        parts_1, back_1 = give_back(outs[1], got_1, 0, later_1)
        *later_2, _ = lax.optimization_barrier((*sent_2, back_1))
        parts_2, _ = give_back(outs[1], got_1, 1, later_2)
        rest_0, dcum_0, *grads_0 = project(0, ((1, 2, 3),), [sent_2[0]], parts_0)
        before = (dq, *grads_0)
        split_off = ((0,), (1, 2, 3))
        firsts, rest_1, dcum_1, *_ = project(1, split_off, [rest_0], parts_1, before)
        inward_0, inward_1 = slide(rest_0, INWARD), slide(rest_1, INWARD)
        far, last, dcum_2, *grads_2 = project(2, ((2,), (3,)), [rest_1], parts_2)
        swapped_0, outward_0, outer_0 = line_scatter(
            0, firsts, rest_0, inward_0, rest_0[1:] + inward_0[1:]
        )
        inward_1, *_ = lax.optimization_barrier((inward_1, swapped_0, dcum_2))
        sum_1 = rest_1[1:] + inward_1[1:]
        swapped_1, outward_1, outer_1 = line_scatter(1, firsts, rest_1, inward_1, sum_1)
        first, near = run_project_more(
            2, groups, ((0,), (1,)), flip, [sum_1], dq, *grads_2, weights
        )

        def meanwhile(after):
            dcums = [dcum_0, dcum_1, dcum_2]
            return run_adjoint(ints, (after, outer_0), dcums, unit, rows, inverse, heads, blocks)

        total_2, swapped_2, outward_2, got, outer_2 = line_scatter_apart(
            first, near, far, last, meanwhile, share_sums, outer_1
        )
        inward_0, inward_1, _ = lax.optimization_barrier((inward_0, inward_1, outer_2))
        total_0 = run_near(line_ends(), firsts, 0, rest_0, inward_0)
        total_1 = run_near(line_ends(), firsts, 1, rest_1, inward_1)
        share = run_share(None, 0, 4, total_0, swapped_0, outward_0)
        share = run_share(share, 1, 4, total_1, swapped_1, outward_1)
        share = run_share(share, 1, 2, total_2, swapped_2, outward_2)
    else:
        spots = (owners * blocks + offsets).reshape(-1)
        empty = jnp.zeros((ctx_count * blocks, BLK, 2 * width), BF16)
        filled = empty.at[spots].add(outs[0])
        back = lax.psum_scatter(filled, "ctx", scatter_dimension=0, tiled=True)
        dcums = []
        share = jnp.zeros((tok_rows, w_query.shape[0] // groups), BF16)
        for j in range(blocks):
            term, dcum_out, _, _ = project(
                j, (tuple(range(groups)),), [], [[(back, j)]]
            )
            dcums.append(dcum_out)
            done = lax.psum_scatter(term, "head", scatter_dimension=0, tiled=False)
            share = lax.dynamic_update_slice(share, done, (j * BLK, 0))

        got = share_sums(run_adjoint(ints, (), dcums, unit, rows, inverse, heads, blocks))

    house_grad = run_house(ints, got, unit, rows, house_dirs, heads, blocks)
    return (share, house_grad)


def solution(mesh):
    placed = (
        P("ctx", "head"),
        P("ctx", "head"),
        P("ctx", "head"),
        P("ctx", "head"),
        P("ctx", "head"),
        P("ctx", None),
        P("ctx", None),
        P(None, "head"),
        P(None, "head"),
        P(None, "head"),
    )
    return jax.shard_map(
        shards,
        mesh=mesh,
        in_specs=placed,
        out_specs=(P("ctx", "head"), P("ctx", "head")),
        check_vma=False,
    )
```

```python
import functools
import math

import jax
import jax.numpy as jnp
from jax import lax
from jax.experimental import pallas as pl
from jax.experimental.pallas import tpu as pltpu
from jax.sharding import PartitionSpec as P

DH = 128
BLK = 128
MAXL = 2
HIGH = lax.Precision.HIGHEST
F32 = jnp.float32
BF16 = jnp.bfloat16


def nn(a, b):
    return lax.dot_general(a, b, (((1,), (0,)), ((), ())), preferred_element_type=F32)


def nt(a, b):
    return lax.dot_general(a, b, (((1,), (1,)), ((), ())), preferred_element_type=F32)


def tn(a, b):
    return lax.dot_general(a, b, (((0,), (0,)), ((), ())), preferred_element_type=F32)


def nn_high(a, b):
    return lax.dot_general(
        a, b, (((1,), (0,)), ((), ())), precision=HIGH, preferred_element_type=F32
    )


def nt_high(a, b):
    return lax.dot_general(
        a, b, (((1,), (1,)), ((), ())), precision=HIGH, preferred_element_type=F32
    )


def split(value):
    top = value.astype(BF16)
    return top, (value - top.astype(F32)).astype(BF16)


def iota(shape, dim):
    return lax.broadcasted_iota(jnp.int32, shape, dim)


def head(h):
    return slice(h * DH, (h + 1) * DH)


def listed(ints_ref, entry, entries):
    return ints_ref[1 + entry], ints_ref[1 + entries + entry]


def grant(mebibytes):
    return pltpu.CompilerParams(vmem_limit_bytes=mebibytes * 1024 * 1024)


def cost(microseconds):
    return pl.CostEstimate(
        flops=int(microseconds * 1.15e9), bytes_accessed=1 << 20, transcendentals=0
    )


def in_smem(count):
    return [pl.BlockSpec(memory_space=pltpu.SMEM)] * count


def in_vmem(count):
    return [pl.BlockSpec(memory_space=pltpu.VMEM)] * count


def chain_kernel(heads, parts, ints_ref, *refs):
    house_refs = refs[:parts]
    unit_ref, rows_ref, inv_ref, wide_ref, tall_ref, unit_h, house_all = refs[parts:]
    count = unit_ref.shape[0]
    span = count // parts
    for t, ref in enumerate(house_refs):
        place = (ints_ref[0] // (8 // parts)) ^ t if parts > 1 else 0
        house_all[pl.ds(pl.multiple_of(place * span, span), span), :] = ref[...]
    eye = (iota((count, count), 0) == iota((count, count), 1)).astype(F32)
    for h in range(heads):
        house = house_all[:, head(h)]
        lengths = jnp.sqrt(jnp.sum(house * house, axis=1, keepdims=True) + 1e-06)
        unit_ref[:, head(h)] = house / lengths
        unit_h[h] = house / lengths
        inv_ref[h] = eye

    def eliminate(step, carry):
        below = iota((count, 1), 0) > step
        for h in range(heads):
            pivot = unit_h[h, pl.ds(step, 1), :]
            overlap = jnp.sum(unit_h[h] * pivot, axis=1, keepdims=True)
            factor = jnp.where(below, 2.0 * overlap, 0.0)
            inv_ref[h] = inv_ref[h] - factor * inv_ref[h, pl.ds(step, 1), :]
        return carry

    lax.fori_loop(0, count, eliminate, 0)
    eye_wide = (iota((DH, DH), 0) == iota((DH, DH), 1)).astype(F32)
    for h in range(heads):
        units = unit_ref[:, head(h)]
        rows = nn_high(inv_ref[h], units)
        rows_ref[:, head(h)] = rows
        unit_hi, unit_lo = split(nt_high(eye_wide, units))
        rows_hi, rows_lo = split(rows)
        wide_ref[h] = jnp.concatenate([unit_hi, unit_hi, unit_lo], axis=1)
        tall_ref[h] = jnp.concatenate([rows_hi, rows_lo, rows_hi], axis=0)


def run_chain(ints, house_parts, heads):
    span, width = house_parts[0].shape
    parts = len(house_parts)
    count = span * parts
    return pl.pallas_call(
        functools.partial(chain_kernel, heads, parts),
        out_shape=[
            jax.ShapeDtypeStruct((count, width), F32),
            jax.ShapeDtypeStruct((count, width), F32),
            jax.ShapeDtypeStruct((heads, count, count), F32),
            jax.ShapeDtypeStruct((heads, DH, 3 * count), BF16),
            jax.ShapeDtypeStruct((heads, 3 * count, DH), BF16),
        ],
        in_specs=in_smem(1) + in_vmem(parts),
        out_specs=in_vmem(5),
        scratch_shapes=[pltpu.VMEM((heads, count, DH), F32), pltpu.VMEM((count, width), F32)],
        compiler_params=grant(12),
        cost_estimate=cost(6),
        name="house_chain",
    )(ints, *house_parts)


def rotate_kernel(
    heads,
    blocks,
    ints_ref,
    wide_ref,
    tall_ref,
    query_ref,
    key_ref,
    qrot_ref,
    krot_ref,
    local_ref,
    listed_ref,
):
    count = wide_ref.shape[2] // 3
    entries = blocks * MAXL
    column = iota((DH, 3 * count), 1) % count
    eye = (iota((DH, DH), 0) == iota((DH, DH), 1)).astype(F32)

    def cumulative(h, block):
        kept = jnp.where(column <= block, wide_ref[h].astype(F32), 0.0).astype(BF16)
        return split(eye - 2.0 * nn(kept, tall_ref[h]))

    base = ints_ref[0] * blocks

    def local_block(b, carry):
        here = pl.ds(pl.multiple_of(b * BLK, BLK), BLK)
        for h in range(heads):
            hi, lo = cumulative(h, base + b)
            local_ref[b, h] = hi
            query, key = query_ref[here, head(h)], key_ref[here, head(h)]
            qrot_ref[here, head(h)] = (nn(query, hi) + nn(query, lo)).astype(BF16)
            krot_ref[here, head(h)] = (nn(key, hi) + nn(key, lo)).astype(BF16)
        return carry

    lax.fori_loop(0, blocks, local_block, 0)

    def listed_block(e, carry):
        owner, offset = listed(ints_ref, e, entries)
        for h in range(heads):
            hi, lo = cumulative(h, owner * blocks + offset)
            listed_ref[e, h, :DH] = hi
            listed_ref[e, h, DH:] = lo
        return carry

    lax.fori_loop(0, entries, listed_block, 0)


def run_rotate(ints, wide, tall, query_rows, key_rows, heads, blocks):
    rows, width = query_rows.shape
    entries = blocks * MAXL
    return pl.pallas_call(
        functools.partial(rotate_kernel, heads, blocks),
        out_shape=[
            jax.ShapeDtypeStruct((rows, width), BF16),
            jax.ShapeDtypeStruct((rows, width), BF16),
            jax.ShapeDtypeStruct((blocks, heads, DH, DH), BF16),
            jax.ShapeDtypeStruct((entries, heads, 2 * DH, DH), BF16),
        ],
        in_specs=in_smem(1) + in_vmem(4),
        out_specs=in_vmem(4),
        compiler_params=grant(16),
        cost_estimate=cost(9),
        name="rotate",
    )(ints, wide, tall, query_rows, key_rows)


def attend_kernel(heads, blocks, places, pieces, *refs):
    ints_ref = refs[0]
    source_count = 1 + max(place[0] for pair in places for place in pair)
    sources = refs[1 : 1 + source_count]
    refs = refs[1 + source_count :]
    (query_ref, qrot_ref, krot_ref, value_ref, grad_ref, local_ref, listed_ref) = refs[:7]
    dq_ref, dcum_ref, dk_ref, dv_ref = refs[7:11]
    outs = refs[11 : 11 + max(len(pieces), 1)]
    refs = refs[11 + max(len(pieces), 1) :]
    dq_all, dcum_all, dk_all, dv_all, grad_sems, far_keys, far_values, sems = refs[:8]
    entries = blocks * MAXL
    scaling = DH ** (-0.5)
    log_scale = scaling * math.log2(math.e)

    def start(e, src, kind, slot, where):
        pltpu.make_async_copy(src.at[where], slot.at[e], sems.at[kind, e]).start()

    for e in range(entries):
        owner, offset = listed(ints_ref, e, entries)
        row = pl.multiple_of(offset * BLK, BLK)
        if len(places) == 1:
            start(e, sources[0], 0, far_keys, (owner, pl.ds(row, BLK)))
            start(e, sources[1], 1, far_values, (owner, pl.ds(row, BLK)))
        else:
            distance = owner ^ ints_ref[0]
            for r, (key_place, value_place) in enumerate(places):

                @pl.when(distance == r)
                def _():
                    source, first = key_place
                    start(e, sources[source], 0, far_keys, pl.ds(first + row, BLK))
                    source, first = value_place
                    start(e, sources[source], 1, far_values, pl.ds(first + row, BLK))

    out_copies = []
    if pieces:
        payloads, out_sems = refs[8 : 8 + heads], refs[8 + heads]
        for payload in payloads:
            payload[...] = jnp.zeros_like(payload)
    for kind, slots in ((0, far_keys), (1, far_values)):
        for e in range(entries):
            pltpu.make_async_copy(slots.at[e], slots.at[e], sems.at[kind, e]).wait()

    later = iota((BLK, BLK), 0) > iota((BLK, BLK), 1)
    empty = jnp.zeros((BLK, DH), BF16)
    steps = range(blocks)
    for h in range(heads):
        lanes = head(h)
        spans = [slice(a * BLK, (a + 1) * BLK) for a in steps]
        both, keys, values = [], [], []
        for a in steps:
            qrot, grad = qrot_ref[spans[a], lanes], grad_ref[spans[a], lanes]
            upper = jnp.concatenate([qrot, empty], axis=1)
            lower = jnp.concatenate([empty, grad], axis=1)
            both.append(jnp.concatenate([upper, lower], axis=0))
            keys.append([krot_ref[spans[b], lanes] for b in range(a + 1)])
            values.append([value_ref[spans[b], lanes] for b in range(a + 1)])
            for l in range(MAXL):
                e = a * MAXL + l
                raw = far_keys[e, :, lanes]
                raw = jnp.concatenate([raw, raw], axis=1)
                keys[a].append(nn(raw, listed_ref[e, h]).astype(BF16))
                values[a].append(far_values[e, :, lanes])
        scores, dprobs, tops = [], [], []
        for a in steps:
            scores.append([])
            dprobs.append([])
            top = None
            for b in range(a + 1 + MAXL):
                pair = nt(jnp.concatenate([keys[a][b], values[a][b]], axis=1), both[a])
                part = pair[:, :BLK] * log_scale
                if b == a:
                    part = jnp.where(later, -jnp.inf, part)
                scores[a].append(part)
                dprobs[a].append(pair[:, BLK:])
                top = part if top is None else jnp.maximum(top, part)
            tops.append(jnp.max(top, axis=0, keepdims=True))
        weights, inverses, deltas = [], [], []
        for a in steps:
            weights.append([])
            total, inner = None, None
            for part, dprob in zip(scores[a], dprobs[a]):
                weight = jnp.exp2(part - tops[a])
                weights[a].append(weight)
                product = weight * dprob
                total = weight if total is None else total + weight
                inner = product if inner is None else inner + product
            inverses.append(1.0 / jnp.sum(total, axis=0, keepdims=True))
            deltas.append(jnp.sum(inner, axis=0, keepdims=True) * inverses[a])
        dscores, pairs = [], []
        for a in steps:
            dscores.append([])
            pairs.append([])
            for b in range(a + 1 + MAXL):
                probs = weights[a][b] * inverses[a]
                dscore = (probs * (dprobs[a][b] - deltas[a])).astype(BF16)
                dscores[a].append(dscore)
                wide = jnp.concatenate([dscore, probs.astype(BF16)], axis=1)
                pairs[a].append(nn(wide, both[a]))
        for b in steps:
            total = pairs[b][b]
            for a in range(b + 1, blocks):
                total = total + pairs[a][b]
            dk_all[h, spans[b]] = total[:, :DH] * scaling
            dv_all[h, spans[b]] = total[:, DH:]
        for e in range(entries):
            pair = pairs[e // MAXL][e // MAXL + 1 + e % MAXL]
            dkey, dvalue = (pair[:, :DH] * scaling).astype(BF16), pair[:, DH:].astype(BF16)
            if pieces:
                owner, offset = listed(ints_ref, e, entries)
                distance = owner ^ ints_ref[0]
                at = (distance & 1) * blocks + offset
                payloads[h][at, distance >> 1, :, :DH] += dkey
                payloads[h][at, distance >> 1, :, DH:] += dvalue
            else:
                outs[0][e, :, 2 * h * DH : (2 * h + 1) * DH] = dkey
                outs[0][e, :, (2 * h + 1) * DH : (2 * h + 2) * DH] = dvalue
        halves = []
        for a in steps:
            wide, tall = jnp.concatenate(dscores[a], axis=0), jnp.concatenate(keys[a], axis=0)
            halves.append(split(tn(wide, tall) * scaling))
        for a in steps:
            dq_top, dq_low = halves[a]
            dq_all[h, spans[a]] = nt(dq_top, local_ref[a, h]).astype(BF16)
            query = query_ref[spans[a], lanes]
            query = jnp.concatenate([query, query], axis=0)
            dcum_all[h, a] = tn(query, jnp.concatenate([dq_top, dq_low], axis=0))
        for i, (source, where) in enumerate(
            (
                (dk_all.at[h], dk_ref.at[:, lanes]),
                (dv_all.at[h], dv_ref.at[:, lanes]),
                (dq_all.at[h], dq_ref.at[:, lanes]),
                (dcum_all.at[h], dcum_ref.at[:, h]),
            )
        ):
            copy = pltpu.make_async_copy(source, where, grad_sems.at[i, h])
            copy.start()
            out_copies.append(copy)
        for i, (first, size) in enumerate(pieces):
            where = outs[i].at[:, :, :, 2 * h * DH : (2 * h + 2) * DH]
            source = payloads[h].at[pl.ds(first, size)]
            copy = pltpu.make_async_copy(source, where, out_sems.at[i, h])
            copy.start()
            out_copies.append(copy)
    for copy in out_copies:
        copy.wait()


def run_attend(ints, sources, places, arrays, heads, blocks, pieces):
    rows, width = arrays[0].shape
    entries = blocks * MAXL
    any_spec = pl.BlockSpec(memory_space=pl.ANY)
    scratch = [
        pltpu.VMEM((heads, rows, DH), BF16),
        pltpu.VMEM((heads, blocks, DH, DH), F32),
        pltpu.VMEM((heads, rows, DH), F32),
        pltpu.VMEM((heads, rows, DH), F32),
        pltpu.SemaphoreType.DMA((4, heads)),
        pltpu.VMEM((entries, BLK, width), BF16),
        pltpu.VMEM((entries, BLK, width), BF16),
        pltpu.SemaphoreType.DMA((2, entries)),
    ]
    if pieces:
        chips = len(places) // 2
        out_parts = [
            pltpu.HBM((size, chips, BLK, 2 * width), BF16) for _, size in pieces
        ]
        part_specs = [any_spec] * len(pieces)
        scratch += [pltpu.VMEM((2 * blocks, chips, BLK, 2 * DH), BF16)] * heads
        scratch += [pltpu.SemaphoreType.DMA((len(pieces), heads))]
    else:
        out_parts = [jax.ShapeDtypeStruct((entries, BLK, 2 * width), BF16)]
        part_specs = in_vmem(1)
    return pl.pallas_call(
        functools.partial(attend_kernel, heads, blocks, places, pieces),
        out_shape=[
            pltpu.HBM((rows, width), BF16),
            pltpu.HBM((blocks, heads, DH, DH), F32),
            pltpu.HBM((rows, width), F32),
            pltpu.HBM((rows, width), F32),
        ]
        + out_parts,
        in_specs=in_smem(1) + [any_spec] * len(sources) + in_vmem(7),
        out_specs=[pl.BlockSpec(memory_space=pltpu.HBM)] * 4 + part_specs,
        scratch_shapes=scratch,
        compiler_params=grant(36),
        cost_estimate=cost(15),
        name="attend",
    )(ints, *sources, *arrays)


def merge_kernel(own_ref, got_ref, *refs):
    for i, ref in enumerate(refs[-3:]):
        total = own_ref[0, i + 1].astype(F32) + got_ref[0, i + 1].astype(F32)
        ref[0] = total.astype(BF16)


def run_merge(own, got, first, size, afters):
    _, chips, rows, width = own.shape
    cut = 2
    lanes = width // cut
    whole = pl.BlockSpec((1, chips, rows, lanes), lambda j, c: (first + j, 0, 0, c))
    return pl.pallas_call(
        merge_kernel,
        grid=(size, cut),
        out_shape=[jax.ShapeDtypeStruct((size, rows, width), BF16)] * (chips - 1),
        in_specs=[whole] * 2
        + [pl.BlockSpec((1, 16, 128), lambda j, c: (0, 0, 0))] * len(afters),
        out_specs=[pl.BlockSpec((1, rows, lanes), lambda j, c: (j, 0, c))] * (chips - 1),
        compiler_params=grant(60),
        cost_estimate=cost(2),
        name="merge",
    )(own, got, *afters)


def start_tiles(chunks, groups, flip_ref, weight_refs, tiles, sems):
    count, _, tile, _ = tiles.shape
    per = count // len(chunks)
    copies = []
    for t in range(count):
        m = chunks[t // per][0]
        row = ((m + flip_ref[0] * (groups - 1 - 2 * m)) * per + t % per) * tile
        rows = pl.ds(pl.multiple_of(row, tile), tile)
        for w, ref in enumerate(weight_refs):
            copy = pltpu.make_async_copy(ref.at[rows], tiles.at[t, w], sems.at[t, w])
            copy.start()
            copies.append(copy)
    return copies


def multiply_tiles(chunks, copies, tiles, out_refs, grads_of):
    count, _, tile, _ = tiles.shape
    per = count // len(chunks)
    for t in range(count):
        term = None
        m, out, at = chunks[t // per]
        for w, grad in enumerate(grads_of(m)):
            copies[3 * t + w].wait()
            part = nt(tiles[t, w], grad)
            term = part if term is None else term + part
        spot = slice(t % per * tile, (t % per + 1) * tile)
        out_refs[out][at, :, spot] = term.T.astype(BF16)


def project_kernel(heads, parts, size, groups, before, layout, afters, flip_ref, *refs):
    refs = refs[afters:]
    outs = len(layout)
    chunks = [(m, i, at) for i, row in enumerate(layout) for at, m in enumerate(row)]
    tiles, sems = refs[-2:]
    part_refs, refs = refs[: size * parts], refs[size * parts :]
    before_refs, refs = refs[:before], refs[before:]
    dk_loc, dv_loc, dq_ref, key_ref, dcum_in, cum_ref = refs[:6]
    weight_refs, out_refs = refs[6:9], refs[9 : 9 + outs]
    dcum_out, dk_out, dv_out = refs[9 + outs : 12 + outs]
    copies = start_tiles(chunks, groups, flip_ref, weight_refs, tiles, sems)
    earlier = ()
    dk_rows, dv_rows = [], []
    for j in range(size):
        here = slice(j * BLK, (j + 1) * BLK)
        dk, dv = [], []
        for h in range(heads):
            both = slice(2 * h * DH, (2 * h + 2) * DH)
            total = part_refs[j * parts][0, :, both].astype(F32)
            for ref in part_refs[j * parts + 1 : (j + 1) * parts]:
                total = total + ref[0, :, both].astype(F32)
            dv.append((dv_loc[here, head(h)] + total[:, DH:]).astype(BF16))
            dk_top, dk_low = split(dk_loc[here, head(h)] + total[:, :DH])
            dk.append(nt(dk_top, cum_ref[j, h]).astype(BF16))
            key = key_ref[here, head(h)]
            key = jnp.concatenate([key, key], axis=0)
            dcum = tn(key, jnp.concatenate([dk_top, dk_low], axis=0))
            dcum_out[j, h] = dcum_in[j, h] + dcum
        dk_rows.append(jnp.concatenate(dk, axis=1))
        dv_rows.append(jnp.concatenate(dv, axis=1))
    dk_all, dv_all = jnp.concatenate(dk_rows, axis=0), jnp.concatenate(dv_rows, axis=0)
    dk_out[...] = dk_all
    dv_out[...] = dv_all
    grads = (dq_ref[...], dk_all, dv_all)
    if before:
        earlier = [
            jnp.concatenate([old[...], new], axis=0) for old, new in zip(before_refs, grads)
        ]

    multiply_tiles(
        chunks, copies, tiles, out_refs, lambda m: earlier if before and m == 0 else grads
    )


def project_more_kernel(groups, layout, afters, flip_ref, *refs):
    refs = refs[afters:]
    chunks = [(m, i, at) for i, row in enumerate(layout) for at, m in enumerate(row)]
    tiles, sems = refs[-2:]
    copies = start_tiles(chunks, groups, flip_ref, refs[3:6], tiles, sems)
    grads = [ref[...] for ref in refs[:3]]
    multiply_tiles(chunks, copies, tiles, refs[6:-2], lambda m: grads)


def run_project_more(block, groups, layout, flip, afters, dq, dk, dv, weights):
    rows, width = dk.shape
    model = weights[0].shape[0]
    chunk = model // groups
    tile = min(512, chunk)
    tile_count = sum(map(len, layout)) * chunk // tile

    def whole(*shape):
        return pl.BlockSpec(shape, lambda t: (0,) * len(shape))

    shapes = [(len(row), rows, chunk) for row in layout]
    return pl.pallas_call(
        functools.partial(project_more_kernel, groups, layout, len(afters)),
        grid=(1,),
        in_specs=in_smem(1)
        + [whole(1, 16, 128)] * len(afters)
        + [pl.BlockSpec((rows, width), lambda t: (block * BLK // rows, 0))]
        + [whole(rows, width)] * 2
        + [pl.BlockSpec(memory_space=pl.ANY)] * 3,
        out_specs=[whole(*shape) for shape in shapes],
        scratch_shapes=[
            pltpu.VMEM((tile_count, 3, tile, width), BF16),
            pltpu.SemaphoreType.DMA((tile_count, 3)),
        ],
        out_shape=[jax.ShapeDtypeStruct(shape, BF16) for shape in shapes],
        compiler_params=grant(60),
        cost_estimate=cost(3 * sum(map(len, layout))),
        name="project_more",
    )(flip, *afters, dq, dk, dv, *weights)


def run_project(block, groups, layout, flip, afters, parts, before, arrays, weights):
    dk_loc, dv_loc, dq, key_rows, dcum, cum = arrays
    size, width = len(parts), dq.shape[1]
    heads = width // DH
    model = weights[0].shape[0]
    chunk = model // groups
    tile = min(512, chunk)
    rows = size * BLK
    tile_count = sum(map(len, layout)) * chunk // tile

    def part_spec(index):
        return pl.BlockSpec((1, BLK, 2 * width), lambda t: (index, 0, 0))

    def whole(*shape):
        return pl.BlockSpec(shape, lambda t: (0,) * len(shape))

    rows_spec = pl.BlockSpec((rows, width), lambda t: (block // size, 0))
    head_spec = pl.BlockSpec((size, heads, DH, DH), lambda t: (block // size, 0, 0, 0))
    flat = [part for row in parts for part in row]
    heights = [2 * rows if before and row == (0,) else rows for row in layout]
    shapes = [(len(row), height, chunk) for row, height in zip(layout, heights)]
    return pl.pallas_call(
        functools.partial(
            project_kernel,
            heads,
            len(parts[0]),
            size,
            groups,
            len(before),
            layout,
            len(afters),
        ),
        grid=(1,),
        in_specs=in_smem(1)
        + [whole(1, min(16, after.shape[1]), 128) for after in afters]
        + [part_spec(index) for _, index in flat]
        + [whole(rows, width)] * len(before)
        + [rows_spec] * 4
        + [head_spec] * 2
        + [pl.BlockSpec(memory_space=pl.ANY)] * 3,
        out_specs=[whole(*shape) for shape in shapes]
        + [whole(size, heads, DH, DH)]
        + [whole(rows, width)] * 2,
        scratch_shapes=[
            pltpu.VMEM((tile_count, 3, tile, width), BF16),
            pltpu.SemaphoreType.DMA((tile_count, 3)),
        ],
        out_shape=[jax.ShapeDtypeStruct(shape, BF16) for shape in shapes]
        + [jax.ShapeDtypeStruct((size, heads, DH, DH), F32)]
        + [jax.ShapeDtypeStruct((rows, width), BF16)] * 2,
        compiler_params=grant(60),
        cost_estimate=cost(3 * sum(map(len, layout))),
        name="project",
    )(
        flip,
        *afters,
        *[part for part, _ in flat],
        *before,
        dk_loc,
        dv_loc,
        dq,
        key_rows,
        dcum,
        cum,
        *weights,
    )


def adjoint_kernel(heads, blocks, first, carried, afters, ints_ref, *refs):
    refs = refs[afters:]
    carry_refs, refs = refs[:carried], refs[carried:]
    dcums = [ref.at[j] for ref in refs[:-4] for j in range(ref.shape[0])]
    unit_ref, rows_ref, inv_ref, out_ref = refs[-4:]
    count, width = unit_ref.shape
    stacked = (len(dcums) * count, count)
    eye = (iota((count, count), 0) == iota((count, count), 1)).astype(F32)
    base = ints_ref[0] * blocks + first
    level, col = iota(stacked, 0), iota(stacked, 1)
    row = level % count
    mine = base + level // count
    alive = row[:, :1] <= mine[:, :1]
    for h in range(heads):
        units, rows, inverse = unit_ref[:, head(h)], rows_ref[:, head(h)], inv_ref[h]
        inverse_t = nt_high(eye, inverse)
        moved = jnp.concatenate([nt_high(rows, dcum[h]) for dcum in dcums], axis=0)
        overlap = jnp.where(col <= mine, nt_high(moved, units), 0.0)
        gamma = nn_high(overlap, inverse)
        gamma = jnp.where((row < col) & (col <= mine), gamma, 0.0)
        beta = jnp.concatenate([eye - inverse_t] * len(dcums), axis=0)
        beta = jnp.where(col <= mine, beta, 0.0)
        x_all = jnp.where(alive, moved - 2.0 * nn_high(gamma, units), 0.0)
        turned = jnp.concatenate([units] * len(dcums), axis=0) - nn_high(beta, units)
        turned = jnp.where(alive, turned, 0.0)
        x_total, y_total = None, None
        for j, dcum in enumerate(dcums):
            here = slice(j * count, (j + 1) * count)
            y_part = nn_high(turned[here], dcum[h])
            x_total = x_all[here] if j == 0 else x_total + x_all[here]
            y_total = y_part if j == 0 else y_total + y_part
        for total, lanes in (
            (x_total, head(h)),
            (y_total, slice(width + h * DH, width + (h + 1) * DH)),
        ):
            for c in range(count // blocks):
                part = total[c * blocks : (c + 1) * blocks]
                for ref in carry_refs:
                    part = part + ref[c, :, lanes]
                out_ref[c, :, lanes] = part


def run_adjoint(ints, first, carry, afters, dcums, unit, rows, inverse, heads, blocks):
    count, width = unit.shape
    return pl.pallas_call(
        functools.partial(adjoint_kernel, heads, blocks, first, len(carry), len(afters)),
        out_shape=jax.ShapeDtypeStruct((count // blocks, blocks, 2 * width), F32),
        in_specs=in_smem(1)
        + [pl.BlockSpec(memory_space=pl.ANY)] * len(afters)
        + in_vmem(len(carry) + len(dcums) + 3),
        out_specs=pl.BlockSpec(memory_space=pltpu.VMEM),
        compiler_params=grant(60),
        cost_estimate=cost(0.2),
        name="adjoint",
    )(ints, *afters, *carry, *dcums, unit, rows, inverse)


def house_kernel(heads, blocks, base_ref, got_ref, unit_ref, rows_ref, house_ref, out_ref):
    count, width = unit_ref.shape
    total = jnp.sum(got_ref[...], axis=0)
    for h in range(heads):
        x_part = total[:, head(h)]
        y_part = total[:, slice(width + h * DH, width + (h + 1) * DH)]
        along = nt_high(y_part, rows_ref[:, head(h)])
        spot = iota((blocks, count), 0) + base_ref[0] * blocks
        along = jnp.where(iota((blocks, count), 1) < spot, along, 0.0)
        turned = y_part - 2.0 * nn_high(along, unit_ref[:, head(h)])
        dunit = -2.0 * (x_part + turned)
        house = house_ref[:, head(h)]
        lengths = jnp.sqrt(jnp.sum(house * house, axis=1, keepdims=True) + 1e-06)
        unit = house / lengths
        inner = jnp.sum(unit * dunit, axis=1, keepdims=True)
        out_ref[:, head(h)] = (dunit - unit * inner) / lengths


def run_house(ints, got, unit, rows, house_dirs, heads, blocks):
    return pl.pallas_call(
        functools.partial(house_kernel, heads, blocks),
        out_shape=jax.ShapeDtypeStruct(house_dirs.shape, F32),
        in_specs=in_smem(1) + in_vmem(4),
        out_specs=pl.BlockSpec(memory_space=pltpu.VMEM),
        compiler_params=grant(60),
        cost_estimate=cost(2),
        name="house_grad",
    )(ints, got, unit, rows, house_dirs)


def hop(value, distance, count):
    return lax.ppermute(value, "ctx", [(i, i ^ distance) for i in range(count)])


def slide(value, pairs):
    return lax.ppermute(value, "head", pairs)


INWARD = [(0, 1), (3, 2)]
MIDDLE = [(1, 2), (2, 1)]
OUTWARD = [(1, 0), (2, 3)]


def near_kernel(ends_ref, first_ref, near_ref, inward_ref, out_ref):
    mine = jnp.where(ends_ref[0] > 0, first_ref[0], near_ref[0]).astype(F32)
    out_ref[...] = mine + inward_ref[0].astype(F32)


def run_near(ends, first, band, near, inward):
    _, rows, width = near.shape
    return pl.pallas_call(
        near_kernel,
        grid=(1,),
        out_shape=jax.ShapeDtypeStruct((rows, width), F32),
        in_specs=in_smem(1)
        + [pl.BlockSpec((1, rows, width), lambda t: (0, band, 0))]
        + [pl.BlockSpec((1, rows, width), lambda t: (0, 0, 0))] * 2,
        out_specs=pl.BlockSpec((rows, width), lambda t: (0, 0)),
        compiler_params=grant(60),
        cost_estimate=cost(5),
        name="near_sum",
    )(ends, first, near, inward)


def share_kernel(*refs):
    total_ref, far_ref, outward_ref, out_ref = refs[-4:]
    far = far_ref[0].astype(F32) + outward_ref[0].astype(F32)
    out_ref[...] = (total_ref[...] + far).astype(BF16)


def run_share(share, band, bands, total, far, outward):
    rows, width = total.shape
    tile = min(512, width)
    part = pl.BlockSpec((1, rows, tile), lambda t: (0, 0, t))
    given = [] if share is None else [share]
    return pl.pallas_call(
        share_kernel,
        grid=(width // tile,),
        out_shape=jax.ShapeDtypeStruct((bands * rows, width), BF16),
        in_specs=[pl.BlockSpec(memory_space=pl.ANY)] * len(given)
        + [pl.BlockSpec((rows, tile), lambda t: (0, t)), part, part],
        out_specs=pl.BlockSpec((rows, tile), lambda t: (band, t)),
        input_output_aliases={0: 0} if given else {},
        compiler_params=grant(60),
        cost_estimate=cost(2),
        name="share",
    )(*given, total, far, outward)


def line_ends():
    place = lax.axis_index("head")
    return ((place == 0) | (place == 3)).astype(jnp.int32).reshape(1)


def outer_kernel(first_ref, low_ref, high_ref, out_ref):
    rows = low_ref.shape[1]
    for i, ref in enumerate((low_ref, high_ref)):
        here = slice(i * rows, (i + 1) * rows)
        out_ref[0, here] = (first_ref[0, here].astype(F32) + ref[0].astype(F32)).astype(BF16)


def run_outer(firsts, low, high):
    _, rows, width = low.shape
    swapped = pl.BlockSpec((1, rows, width), lambda t: (1, 0, 0))
    both = pl.BlockSpec((1, 2 * rows, width), lambda t: (0, 0, 0))
    return pl.pallas_call(
        outer_kernel,
        grid=(1,),
        out_shape=jax.ShapeDtypeStruct(firsts.shape, BF16),
        in_specs=[both, swapped, swapped],
        out_specs=both,
        compiler_params=grant(60),
        cost_estimate=cost(2),
        name="outer",
    )(firsts, low, high)


def first_band_kernel(ends_ref, first_ref, outward_ref, *refs):
    out_ref = refs[-1]
    rows = refs[0].shape[1]
    for i in range(2):
        here = slice(i * rows, (i + 1) * rows)
        rest_ref, inward_ref, swapped_ref = refs[3 * i : 3 * i + 3]
        total = jnp.where(ends_ref[0] > 0, first_ref[0, here], rest_ref[0]).astype(F32)
        total = total + inward_ref[0].astype(F32)
        total = total + (swapped_ref[0].astype(F32) + outward_ref[0, here].astype(F32))
        out_ref[here] = total.astype(BF16)


def run_first_band(bands, firsts, outward, *parts):
    _, height, width = firsts.shape
    tile = min(512, width)
    both = pl.BlockSpec((1, height, tile), lambda t: (0, 0, t))
    part = pl.BlockSpec((1, height // 2, tile), lambda t: (0, 0, t))
    return pl.pallas_call(
        first_band_kernel,
        grid=(width // tile,),
        out_shape=jax.ShapeDtypeStruct((bands * height, width), BF16),
        in_specs=in_smem(1) + [both] * 2 + [part] * len(parts),
        out_specs=pl.BlockSpec((height, tile), lambda t: (0, t)),
        compiler_params=grant(60),
        cost_estimate=cost(2),
        name="first_band",
    )(line_ends(), firsts, outward, *parts)


def line_scatter_apart(first, near, far, last, meanwhile, exchange, earlier):
    in_last, in_far = slide(last, INWARD), slide(far, INWARD)
    near, in_far = lax.optimization_barrier((near, in_far))
    in_near = slide(near, INWARD)
    in_last, first = lax.optimization_barrier((in_last, first))
    sum_last = last + in_last
    swap_last = slide(sum_last, MIDDLE)
    other = meanwhile(sum_last)
    in_far, other = lax.optimization_barrier((in_far, other))
    sum_far = far + in_far
    swap_far = slide(sum_far, MIDDLE)
    swap_last, *_ = lax.optimization_barrier((swap_last, earlier, sum_far))
    outer = first + swap_last
    outward = slide(outer, OUTWARD)
    other, in_near, _ = lax.optimization_barrier((other, in_near, outer))
    other = exchange(other)
    total = run_near(line_ends(), first, 0, near, in_near)
    return total, swap_far, outward, other, outer


def shards(
    query_rows, key_rows, value_rows, grad_out, house_dirs, owners, offsets, w_query, w_key, w_value
):
    tok_rows, width = query_rows.shape
    heads, blocks = width // DH, tok_rows // BLK
    ctx_count, groups = lax.axis_size("ctx"), lax.axis_size("head")
    my_index = lax.axis_index("ctx").astype(jnp.int32)
    ints = jnp.concatenate([my_index.reshape(1), owners.reshape(-1), offsets.reshape(-1)])
    by_hand = ctx_count == 8 and groups == 4 and blocks == 4
    core, across, along = 1, 2, 4

    if by_hand:
        other = hop(house_dirs, core, 8)
        upper = (my_index & core) != 0
        low, high = jnp.where(upper, other, house_dirs), jnp.where(upper, house_dirs, other)
        house_pair = jnp.concatenate([low, high], axis=0)
        value_x, key_y = hop(value_rows, across, 8), hop(key_rows, along, 8)
        key_x, value_y = hop(key_rows, across, 8), hop(value_rows, along, 8)
        house_late, *_ = lax.optimization_barrier((house_pair, value_x, key_y))
        house_parts = [house_pair] + [hop(house_late, t, 8) for t in (2, 4, 6)]
        key_d, value_d = hop(key_y, across, 8), hop(value_x, along, 8)
    else:
        house_parts = [lax.all_gather(house_dirs, "ctx", axis=0, tiled=True)]

    unit, rows, inverse, wide, tall = run_chain(ints, house_parts, heads)
    ready = query_rows
    if by_hand:
        own = (key_rows, value_rows, key_x, value_x, key_y, value_y, key_d, value_d)
        early = lax.optimization_barrier((*own[:6], *house_parts))[:6]
        siblings = [hop(part, core, 8) for part in early]
        ready, *_ = lax.optimization_barrier((query_rows, *siblings[:3]))
    qrot, krot, local, listed_cum = run_rotate(ints, wide, tall, ready, key_rows, heads, blocks)
    if by_hand:
        late = lax.optimization_barrier((*own[6:], qrot))[:2]
        siblings += [hop(part, core, 8) for part in late]
        sources, places = [], []
        for t in range(4):
            for pair in (own[2 * t : 2 * t + 2], siblings[2 * t : 2 * t + 2]):
                places.append(((len(sources), 0), (len(sources) + 1, 0)))
                sources += pair
    else:
        sources = [lax.all_gather(key_rows, "ctx"), lax.all_gather(value_rows, "ctx")]
        places = [((0, 0), (1, 0))]

    rounds = ((0, 1), (1, blocks - 1), (blocks, 1), (blocks + 1, blocks - 1))
    dq, dcum, dk_loc, dv_loc, *outs = run_attend(
        ints,
        sources,
        places,
        (query_rows, qrot, krot, value_rows, grad_out, local, listed_cum),
        heads,
        blocks,
        rounds if by_hand else (),
    )
    weights = (w_query, w_key, w_value)
    flip = jnp.where(by_hand & (lax.axis_index("head") >= 2), 1, 0).astype(jnp.int32).reshape(1)

    arrays = (dk_loc, dv_loc, dq, key_rows, dcum, local)

    def project(block, layout, afters, parts, before=()):
        return run_project(block, groups, layout, flip, afters, parts, before, arrays, weights)

    def share_sums(sums):
        return lax.all_to_all(sums, "ctx", split_axis=0, concat_axis=0, tiled=True)

    if by_hand:
        got_0 = hop(outs[2], core, 8)
        got_1 = hop(lax.optimization_barrier((outs[3], got_0))[0], core, 8)
        sent_0 = run_merge(outs[0], got_0, 0, 1, [])
        sent_1 = run_merge(outs[1], got_1, 0, 1, [sent_0[0]])
        sent_2 = run_merge(outs[1], got_1, 1, 2, [sent_1[0]])

        def give_back(own, got, first, sent):
            back = [hop(part, t, 8) for part, t in zip(sent, (across, along, across + along))]
            near = [part.reshape(-1, BLK, 2 * width) for part in (own, got)]
            parts = []
            for j in range(sent[0].shape[0]):
                mine = [(part, 4 * (first + j)) for part in near]
                parts.append(mine + [(part, j) for part in back])
            return parts, back

        parts_0, back_0 = give_back(outs[0], got_0, 0, sent_0)
        *later_1, _, _ = lax.optimization_barrier((*sent_1, back_0, sent_2))
        parts_1, back_1 = give_back(outs[1], got_1, 0, later_1)
        *later_2, _ = lax.optimization_barrier((*sent_2, back_1))
        parts_2, _ = give_back(outs[1], got_1, 1, later_2)
        rest_0, dcum_0, *grads_0 = project(0, ((1, 2, 3),), [sent_2[0]], parts_0)
        before = (dq, *grads_0)
        split_off = ((0,), (1, 2, 3))
        firsts, rest_1, dcum_1, *_ = project(1, split_off, [rest_0], parts_1, before)
        inward_0, inward_1 = slide(rest_0, INWARD), slide(rest_1, INWARD)
        house = (unit, rows, inverse, heads, blocks)
        sums = run_adjoint(ints, 0, (), (), [dcum_0, dcum_1], *house)
        far, last, dcum_2, *grads_2 = project(2, ((2,), (3,)), [rest_1, sums], parts_2)
        swapped_0 = slide(rest_0[1:] + inward_0[1:], MIDDLE)
        inward_1, *_ = lax.optimization_barrier((inward_1, swapped_0, dcum_2))
        sum_1 = rest_1[1:] + inward_1[1:]
        swapped_1 = slide(sum_1, MIDDLE)
        first, near = run_project_more(
            2, groups, ((0,), (1,)), flip, [sum_1], dq, *grads_2, weights
        )
        outer = run_outer(firsts, swapped_0, swapped_1)
        outward = slide(outer, OUTWARD)

        def meanwhile(after):
            return run_adjoint(ints, 2, (sums,), (after, outer), [dcum_2], *house)

        total_2, swapped_2, outward_2, got, outer_2 = line_scatter_apart(
            first, near, far, last, meanwhile, share_sums, outer
        )
        outward, _ = lax.optimization_barrier((outward, outer_2))
        parts = (rest_0, inward_0, swapped_0, rest_1, inward_1, swapped_1)
        share = run_first_band(2, firsts, outward, *parts)
        share = run_share(share, 1, 2, total_2, swapped_2, outward_2)
    else:
        spots = (owners * blocks + offsets).reshape(-1)
        empty = jnp.zeros((ctx_count * blocks, BLK, 2 * width), BF16)
        filled = empty.at[spots].add(outs[0])
        back = lax.psum_scatter(filled, "ctx", scatter_dimension=0, tiled=True)
        dcums = []
        share = jnp.zeros((tok_rows, w_query.shape[0] // groups), BF16)
        for j in range(blocks):
            term, dcum_out, _, _ = project(
                j, (tuple(range(groups)),), [], [[(back, j)]]
            )
            dcums.append(dcum_out)
            done = lax.psum_scatter(term, "head", scatter_dimension=0, tiled=False)
            share = lax.dynamic_update_slice(share, done, (j * BLK, 0))

        sums = run_adjoint(ints, 0, (), (), dcums, unit, rows, inverse, heads, blocks)
        got = share_sums(sums)

    house_grad = run_house(ints, got, unit, rows, house_dirs, heads, blocks)
    return (share, house_grad)


def solution(mesh):
    placed = (
        P("ctx", "head"),
        P("ctx", "head"),
        P("ctx", "head"),
        P("ctx", "head"),
        P("ctx", "head"),
        P("ctx", None),
        P("ctx", None),
        P(None, "head"),
        P(None, "head"),
        P(None, "head"),
    )
    return jax.shard_map(
        shards,
        mesh=mesh,
        in_specs=placed,
        out_specs=(P("ctx", "head"), P("ctx", "head")),
        check_vma=False,
    )
```

```python
import functools
import math

import jax
import jax.numpy as jnp
from jax import lax
from jax.experimental import pallas as pl
from jax.experimental.pallas import tpu as pltpu
from jax.sharding import PartitionSpec as P

DH = 128
BLK = 128
MAXL = 2
HIGH = lax.Precision.HIGHEST
F32 = jnp.float32
BF16 = jnp.bfloat16


def nn(a, b):
    return lax.dot_general(a, b, (((1,), (0,)), ((), ())), preferred_element_type=F32)


def nt(a, b):
    return lax.dot_general(a, b, (((1,), (1,)), ((), ())), preferred_element_type=F32)


def tn(a, b):
    return lax.dot_general(a, b, (((0,), (0,)), ((), ())), preferred_element_type=F32)


def nn_high(a, b):
    return lax.dot_general(
        a, b, (((1,), (0,)), ((), ())), precision=HIGH, preferred_element_type=F32
    )


def nt_high(a, b):
    return lax.dot_general(
        a, b, (((1,), (1,)), ((), ())), precision=HIGH, preferred_element_type=F32
    )


def split(value):
    top = value.astype(BF16)
    return top, (value - top.astype(F32)).astype(BF16)


def iota(shape, dim):
    return lax.broadcasted_iota(jnp.int32, shape, dim)


def head(h):
    return slice(h * DH, (h + 1) * DH)


def listed(ints_ref, entry, entries):
    return ints_ref[1 + entry], ints_ref[1 + entries + entry]


def grant(mebibytes):
    return pltpu.CompilerParams(vmem_limit_bytes=mebibytes * 1024 * 1024)


def cost(microseconds):
    return pl.CostEstimate(
        flops=int(microseconds * 1.15e9), bytes_accessed=1 << 20, transcendentals=0
    )


def in_smem(count):
    return [pl.BlockSpec(memory_space=pltpu.SMEM)] * count


def in_vmem(count):
    return [pl.BlockSpec(memory_space=pltpu.VMEM)] * count


def chain_kernel(heads, parts, ints_ref, *refs):
    house_refs = refs[:parts]
    unit_ref, rows_ref, inv_ref, wide_ref, tall_ref, unit_h, house_all = refs[parts:]
    count = unit_ref.shape[0]
    span = count // parts
    for t, ref in enumerate(house_refs):
        place = (ints_ref[0] // (8 // parts)) ^ t if parts > 1 else 0
        house_all[pl.ds(pl.multiple_of(place * span, span), span), :] = ref[...]
    eye = (iota((count, count), 0) == iota((count, count), 1)).astype(F32)
    for h in range(heads):
        house = house_all[:, head(h)]
        lengths = jnp.sqrt(jnp.sum(house * house, axis=1, keepdims=True) + 1e-06)
        unit_ref[:, head(h)] = house / lengths
        unit_h[h] = house / lengths
        inv_ref[h] = eye

    def eliminate(step, carry):
        below = iota((count, 1), 0) > step
        for h in range(heads):
            pivot = unit_h[h, pl.ds(step, 1), :]
            overlap = jnp.sum(unit_h[h] * pivot, axis=1, keepdims=True)
            factor = jnp.where(below, 2.0 * overlap, 0.0)
            inv_ref[h] = inv_ref[h] - factor * inv_ref[h, pl.ds(step, 1), :]
        return carry

    lax.fori_loop(0, count, eliminate, 0)
    eye_wide = (iota((DH, DH), 0) == iota((DH, DH), 1)).astype(F32)
    for h in range(heads):
        units = unit_ref[:, head(h)]
        rows = nn_high(inv_ref[h], units)
        rows_ref[:, head(h)] = rows
        unit_hi, unit_lo = split(nt_high(eye_wide, units))
        rows_hi, rows_lo = split(rows)
        wide_ref[h] = jnp.concatenate([unit_hi, unit_hi, unit_lo], axis=1)
        tall_ref[h] = jnp.concatenate([rows_hi, rows_lo, rows_hi], axis=0)


def run_chain(ints, house_parts, heads):
    span, width = house_parts[0].shape
    parts = len(house_parts)
    count = span * parts
    return pl.pallas_call(
        functools.partial(chain_kernel, heads, parts),
        out_shape=[
            jax.ShapeDtypeStruct((count, width), F32),
            jax.ShapeDtypeStruct((count, width), F32),
            jax.ShapeDtypeStruct((heads, count, count), F32),
            jax.ShapeDtypeStruct((heads, DH, 3 * count), BF16),
            jax.ShapeDtypeStruct((heads, 3 * count, DH), BF16),
        ],
        in_specs=in_smem(1) + in_vmem(parts),
        out_specs=in_vmem(5),
        scratch_shapes=[pltpu.VMEM((heads, count, DH), F32), pltpu.VMEM((count, width), F32)],
        compiler_params=grant(12),
        cost_estimate=cost(6),
        name="house_chain",
    )(ints, *house_parts)


def rotate_kernel(
    heads,
    blocks,
    ints_ref,
    wide_ref,
    tall_ref,
    query_ref,
    key_ref,
    qrot_ref,
    krot_ref,
    local_ref,
    listed_ref,
):
    count = wide_ref.shape[2] // 3
    entries = blocks * MAXL
    column = iota((DH, 3 * count), 1) % count
    eye = (iota((DH, DH), 0) == iota((DH, DH), 1)).astype(F32)

    def cumulative(h, block):
        kept = jnp.where(column <= block, wide_ref[h].astype(F32), 0.0).astype(BF16)
        return split(eye - 2.0 * nn(kept, tall_ref[h]))

    base = ints_ref[0] * blocks

    def local_block(b, carry):
        here = pl.ds(pl.multiple_of(b * BLK, BLK), BLK)
        for h in range(heads):
            hi, lo = cumulative(h, base + b)
            local_ref[b, h] = hi
            query, key = query_ref[here, head(h)], key_ref[here, head(h)]
            qrot_ref[here, head(h)] = (nn(query, hi) + nn(query, lo)).astype(BF16)
            krot_ref[here, head(h)] = (nn(key, hi) + nn(key, lo)).astype(BF16)
        return carry

    lax.fori_loop(0, blocks, local_block, 0)

    def listed_block(e, carry):
        owner, offset = listed(ints_ref, e, entries)
        for h in range(heads):
            hi, lo = cumulative(h, owner * blocks + offset)
            listed_ref[e, h, :DH] = hi
            listed_ref[e, h, DH:] = lo
        return carry

    lax.fori_loop(0, entries, listed_block, 0)


def run_rotate(ints, wide, tall, query_rows, key_rows, heads, blocks):
    rows, width = query_rows.shape
    entries = blocks * MAXL
    return pl.pallas_call(
        functools.partial(rotate_kernel, heads, blocks),
        out_shape=[
            jax.ShapeDtypeStruct((rows, width), BF16),
            jax.ShapeDtypeStruct((rows, width), BF16),
            jax.ShapeDtypeStruct((blocks, heads, DH, DH), BF16),
            jax.ShapeDtypeStruct((entries, heads, 2 * DH, DH), BF16),
        ],
        in_specs=in_smem(1) + in_vmem(4),
        out_specs=in_vmem(4),
        compiler_params=grant(16),
        cost_estimate=cost(9),
        name="rotate",
    )(ints, wide, tall, query_rows, key_rows)


def attend_kernel(heads, blocks, places, pieces, *refs):
    ints_ref = refs[0]
    source_count = 1 + max(place[0] for pair in places for place in pair)
    sources = refs[1 : 1 + source_count]
    refs = refs[1 + source_count :]
    (query_ref, qrot_ref, krot_ref, value_ref, grad_ref, local_ref, listed_ref) = refs[:7]
    dq_ref, dcum_ref, dk_ref, dv_ref = refs[7:11]
    outs = refs[11 : 11 + max(len(pieces), 1)]
    refs = refs[11 + max(len(pieces), 1) :]
    dq_all, dcum_all, dk_all, dv_all, grad_sems, far_keys, far_values, sems = refs[:8]
    entries = blocks * MAXL
    scaling = DH ** (-0.5)
    log_scale = scaling * math.log2(math.e)

    def start(e, src, kind, slot, where):
        pltpu.make_async_copy(src.at[where], slot.at[e], sems.at[kind, e]).start()

    for e in range(entries):
        owner, offset = listed(ints_ref, e, entries)
        row = pl.multiple_of(offset * BLK, BLK)
        if len(places) == 1:
            start(e, sources[0], 0, far_keys, (owner, pl.ds(row, BLK)))
            start(e, sources[1], 1, far_values, (owner, pl.ds(row, BLK)))
        else:
            distance = owner ^ ints_ref[0]
            for r, (key_place, value_place) in enumerate(places):

                @pl.when(distance == r)
                def _():
                    source, first = key_place
                    start(e, sources[source], 0, far_keys, pl.ds(first + row, BLK))
                    source, first = value_place
                    start(e, sources[source], 1, far_values, pl.ds(first + row, BLK))

    out_copies = []
    if pieces:
        payloads, out_sems = refs[8 : 8 + heads], refs[8 + heads]
        for payload in payloads:
            payload[...] = jnp.zeros_like(payload)
    for kind, slots in ((0, far_keys), (1, far_values)):
        for e in range(entries):
            pltpu.make_async_copy(slots.at[e], slots.at[e], sems.at[kind, e]).wait()

    later = iota((BLK, BLK), 0) > iota((BLK, BLK), 1)
    empty = jnp.zeros((BLK, DH), BF16)
    steps = range(blocks)
    for h in range(heads):
        lanes = head(h)
        spans = [slice(a * BLK, (a + 1) * BLK) for a in steps]
        both, keys, values = [], [], []
        for a in steps:
            qrot, grad = qrot_ref[spans[a], lanes], grad_ref[spans[a], lanes]
            upper = jnp.concatenate([qrot, empty], axis=1)
            lower = jnp.concatenate([empty, grad], axis=1)
            both.append(jnp.concatenate([upper, lower], axis=0))
            keys.append([krot_ref[spans[b], lanes] for b in range(a + 1)])
            values.append([value_ref[spans[b], lanes] for b in range(a + 1)])
            for l in range(MAXL):
                e = a * MAXL + l
                raw = far_keys[e, :, lanes]
                raw = jnp.concatenate([raw, raw], axis=1)
                keys[a].append(nn(raw, listed_ref[e, h]).astype(BF16))
                values[a].append(far_values[e, :, lanes])
        scores, dprobs, tops = [], [], []
        for a in steps:
            scores.append([])
            dprobs.append([])
            top = None
            for b in range(a + 1 + MAXL):
                pair = nt(jnp.concatenate([keys[a][b], values[a][b]], axis=1), both[a])
                part = pair[:, :BLK] * log_scale
                if b == a:
                    part = jnp.where(later, -jnp.inf, part)
                scores[a].append(part)
                dprobs[a].append(pair[:, BLK:])
                top = part if top is None else jnp.maximum(top, part)
            tops.append(jnp.max(top, axis=0, keepdims=True))
        weights, inverses, deltas = [], [], []
        for a in steps:
            weights.append([])
            total, inner = None, None
            for part, dprob in zip(scores[a], dprobs[a]):
                weight = jnp.exp2(part - tops[a])
                weights[a].append(weight)
                product = weight * dprob
                total = weight if total is None else total + weight
                inner = product if inner is None else inner + product
            inverses.append(1.0 / jnp.sum(total, axis=0, keepdims=True))
            deltas.append(jnp.sum(inner, axis=0, keepdims=True) * inverses[a])
        dscores, pairs = [], []
        for a in steps:
            dscores.append([])
            pairs.append([])
            for b in range(a + 1 + MAXL):
                probs = weights[a][b] * inverses[a]
                dscore = (probs * (dprobs[a][b] - deltas[a])).astype(BF16)
                dscores[a].append(dscore)
                wide = jnp.concatenate([dscore, probs.astype(BF16)], axis=1)
                pairs[a].append(nn(wide, both[a]))
        for b in steps:
            total = pairs[b][b]
            for a in range(b + 1, blocks):
                total = total + pairs[a][b]
            dk_all[h, spans[b]] = total[:, :DH] * scaling
            dv_all[h, spans[b]] = total[:, DH:]
        for e in range(entries):
            pair = pairs[e // MAXL][e // MAXL + 1 + e % MAXL]
            dkey, dvalue = (pair[:, :DH] * scaling).astype(BF16), pair[:, DH:].astype(BF16)
            if pieces:
                owner, offset = listed(ints_ref, e, entries)
                distance = owner ^ ints_ref[0]
                at = (distance & 1) * blocks + offset
                payloads[h][at, distance >> 1, :, :DH] += dkey
                payloads[h][at, distance >> 1, :, DH:] += dvalue
            else:
                outs[0][e, :, 2 * h * DH : (2 * h + 1) * DH] = dkey
                outs[0][e, :, (2 * h + 1) * DH : (2 * h + 2) * DH] = dvalue
        halves = []
        for a in steps:
            wide, tall = jnp.concatenate(dscores[a], axis=0), jnp.concatenate(keys[a], axis=0)
            halves.append(split(tn(wide, tall) * scaling))
        for a in steps:
            dq_top, dq_low = halves[a]
            dq_all[h, spans[a]] = nt(dq_top, local_ref[a, h]).astype(BF16)
            query = query_ref[spans[a], lanes]
            query = jnp.concatenate([query, query], axis=0)
            dcum_all[h, a] = tn(query, jnp.concatenate([dq_top, dq_low], axis=0))
        for i, (source, where) in enumerate(
            (
                (dk_all.at[h], dk_ref.at[:, lanes]),
                (dv_all.at[h], dv_ref.at[:, lanes]),
                (dq_all.at[h], dq_ref.at[:, lanes]),
                (dcum_all.at[h], dcum_ref.at[:, h]),
            )
        ):
            copy = pltpu.make_async_copy(source, where, grad_sems.at[i, h])
            copy.start()
            out_copies.append(copy)
        for i, (first, size) in enumerate(pieces):
            where = outs[i].at[:, :, :, 2 * h * DH : (2 * h + 2) * DH]
            source = payloads[h].at[pl.ds(first, size)]
            copy = pltpu.make_async_copy(source, where, out_sems.at[i, h])
            copy.start()
            out_copies.append(copy)
    for copy in out_copies:
        copy.wait()


def run_attend(ints, sources, places, arrays, heads, blocks, pieces):
    rows, width = arrays[0].shape
    entries = blocks * MAXL
    any_spec = pl.BlockSpec(memory_space=pl.ANY)
    scratch = [
        pltpu.VMEM((heads, rows, DH), BF16),
        pltpu.VMEM((heads, blocks, DH, DH), F32),
        pltpu.VMEM((heads, rows, DH), F32),
        pltpu.VMEM((heads, rows, DH), F32),
        pltpu.SemaphoreType.DMA((4, heads)),
        pltpu.VMEM((entries, BLK, width), BF16),
        pltpu.VMEM((entries, BLK, width), BF16),
        pltpu.SemaphoreType.DMA((2, entries)),
    ]
    if pieces:
        chips = len(places) // 2
        out_parts = [
            pltpu.HBM((size, chips, BLK, 2 * width), BF16) for _, size in pieces
        ]
        part_specs = [any_spec] * len(pieces)
        scratch += [pltpu.VMEM((2 * blocks, chips, BLK, 2 * DH), BF16)] * heads
        scratch += [pltpu.SemaphoreType.DMA((len(pieces), heads))]
    else:
        out_parts = [jax.ShapeDtypeStruct((entries, BLK, 2 * width), BF16)]
        part_specs = in_vmem(1)
    return pl.pallas_call(
        functools.partial(attend_kernel, heads, blocks, places, pieces),
        out_shape=[
            pltpu.HBM((rows, width), BF16),
            pltpu.HBM((blocks, heads, DH, DH), F32),
            pltpu.HBM((rows, width), F32),
            pltpu.HBM((rows, width), F32),
        ]
        + out_parts,
        in_specs=in_smem(1) + [any_spec] * len(sources) + in_vmem(7),
        out_specs=[pl.BlockSpec(memory_space=pltpu.HBM)] * 4 + part_specs,
        scratch_shapes=scratch,
        compiler_params=grant(36),
        cost_estimate=cost(15),
        name="attend",
    )(ints, *sources, *arrays)


def merge_kernel(own_ref, got_ref, *refs):
    for i, ref in enumerate(refs[-3:]):
        total = own_ref[0, i + 1].astype(F32) + got_ref[0, i + 1].astype(F32)
        ref[0] = total.astype(BF16)


def run_merge(own, got, first, size, afters):
    _, chips, rows, width = own.shape
    cut = 2
    lanes = width // cut
    whole = pl.BlockSpec((1, chips, rows, lanes), lambda j, c: (first + j, 0, 0, c))
    return pl.pallas_call(
        merge_kernel,
        grid=(size, cut),
        out_shape=[jax.ShapeDtypeStruct((size, rows, width), BF16)] * (chips - 1),
        in_specs=[whole] * 2
        + [pl.BlockSpec((1, 16, 128), lambda j, c: (0, 0, 0))] * len(afters),
        out_specs=[pl.BlockSpec((1, rows, lanes), lambda j, c: (j, 0, c))] * (chips - 1),
        compiler_params=grant(60),
        cost_estimate=cost(2),
        name="merge",
    )(own, got, *afters)


def start_tiles(chunks, groups, flip_ref, weight_refs, tiles, sems):
    count, _, tile, _ = tiles.shape
    per = count // len(chunks)
    copies = []
    for t in range(count):
        m = chunks[t // per][0]
        row = ((m + flip_ref[0] * (groups - 1 - 2 * m)) * per + t % per) * tile
        rows = pl.ds(pl.multiple_of(row, tile), tile)
        for w, ref in enumerate(weight_refs):
            copy = pltpu.make_async_copy(ref.at[rows], tiles.at[t, w], sems.at[t, w])
            copy.start()
            copies.append(copy)
    return copies


def multiply_tiles(chunks, copies, tiles, out_refs, grads_of):
    count, _, tile, _ = tiles.shape
    per = count // len(chunks)
    for t in range(count):
        term = None
        m, out, at = chunks[t // per]
        for w, grad in enumerate(grads_of(m)):
            copies[3 * t + w].wait()
            part = nt(tiles[t, w], grad)
            term = part if term is None else term + part
        spot = slice(t % per * tile, (t % per + 1) * tile)
        out_refs[out][at, :, spot] = term.T.astype(BF16)


def project_kernel(heads, parts, size, groups, before, layout, afters, flip_ref, *refs):
    refs = refs[afters:]
    outs = len(layout)
    chunks = [(m, i, at) for i, row in enumerate(layout) for at, m in enumerate(row)]
    tiles, sems = refs[-2:]
    part_refs, refs = refs[: size * parts], refs[size * parts :]
    before_refs, refs = refs[:before], refs[before:]
    dk_loc, dv_loc, dq_ref, key_ref, dcum_in, cum_ref = refs[:6]
    weight_refs, out_refs = refs[6:9], refs[9 : 9 + outs]
    dcum_out, dk_out, dv_out = refs[9 + outs : 12 + outs]
    copies = start_tiles(chunks, groups, flip_ref, weight_refs, tiles, sems)
    earlier = ()
    dk_rows, dv_rows = [], []
    for j in range(size):
        here = slice(j * BLK, (j + 1) * BLK)
        dk, dv = [], []
        for h in range(heads):
            both = slice(2 * h * DH, (2 * h + 2) * DH)
            total = part_refs[j * parts][0, :, both].astype(F32)
            for ref in part_refs[j * parts + 1 : (j + 1) * parts]:
                total = total + ref[0, :, both].astype(F32)
            dv.append((dv_loc[here, head(h)] + total[:, DH:]).astype(BF16))
            dk_top, dk_low = split(dk_loc[here, head(h)] + total[:, :DH])
            dk.append(nt(dk_top, cum_ref[j, h]).astype(BF16))
            key = key_ref[here, head(h)]
            key = jnp.concatenate([key, key], axis=0)
            dcum = tn(key, jnp.concatenate([dk_top, dk_low], axis=0))
            dcum_out[j, h] = dcum_in[j, h] + dcum
        dk_rows.append(jnp.concatenate(dk, axis=1))
        dv_rows.append(jnp.concatenate(dv, axis=1))
    dk_all, dv_all = jnp.concatenate(dk_rows, axis=0), jnp.concatenate(dv_rows, axis=0)
    dk_out[...] = dk_all
    dv_out[...] = dv_all
    grads = (dq_ref[...], dk_all, dv_all)
    if before:
        earlier = [
            jnp.concatenate([old[...], new], axis=0) for old, new in zip(before_refs, grads)
        ]

    multiply_tiles(
        chunks, copies, tiles, out_refs, lambda m: earlier if before and m == 0 else grads
    )


def project_more_kernel(groups, layout, afters, flip_ref, *refs):
    refs = refs[afters:]
    chunks = [(m, i, at) for i, row in enumerate(layout) for at, m in enumerate(row)]
    tiles, sems = refs[-2:]
    copies = start_tiles(chunks, groups, flip_ref, refs[3:6], tiles, sems)
    grads = [ref[...] for ref in refs[:3]]
    multiply_tiles(chunks, copies, tiles, refs[6:-2], lambda m: grads)


def run_project_more(block, groups, layout, flip, afters, dq, dk, dv, weights):
    rows, width = dk.shape
    model = weights[0].shape[0]
    chunk = model // groups
    tile = min(512, chunk)
    tile_count = sum(map(len, layout)) * chunk // tile

    def whole(*shape):
        return pl.BlockSpec(shape, lambda t: (0,) * len(shape))

    shapes = [(len(row), rows, chunk) for row in layout]
    return pl.pallas_call(
        functools.partial(project_more_kernel, groups, layout, len(afters)),
        grid=(1,),
        in_specs=in_smem(1)
        + [whole(1, 16, 128)] * len(afters)
        + [pl.BlockSpec((rows, width), lambda t: (block * BLK // rows, 0))]
        + [whole(rows, width)] * 2
        + [pl.BlockSpec(memory_space=pl.ANY)] * 3,
        out_specs=[whole(*shape) for shape in shapes],
        scratch_shapes=[
            pltpu.VMEM((tile_count, 3, tile, width), BF16),
            pltpu.SemaphoreType.DMA((tile_count, 3)),
        ],
        out_shape=[jax.ShapeDtypeStruct(shape, BF16) for shape in shapes],
        compiler_params=grant(60),
        cost_estimate=cost(3 * sum(map(len, layout))),
        name="project_more",
    )(flip, *afters, dq, dk, dv, *weights)


def run_project(block, groups, layout, flip, afters, parts, before, arrays, weights):
    dk_loc, dv_loc, dq, key_rows, dcum, cum = arrays
    size, width = len(parts), dq.shape[1]
    heads = width // DH
    model = weights[0].shape[0]
    chunk = model // groups
    tile = min(512, chunk)
    rows = size * BLK
    tile_count = sum(map(len, layout)) * chunk // tile

    def part_spec(index):
        return pl.BlockSpec((1, BLK, 2 * width), lambda t: (index, 0, 0))

    def whole(*shape):
        return pl.BlockSpec(shape, lambda t: (0,) * len(shape))

    rows_spec = pl.BlockSpec((rows, width), lambda t: (block // size, 0))
    head_spec = pl.BlockSpec((size, heads, DH, DH), lambda t: (block // size, 0, 0, 0))
    flat = [part for row in parts for part in row]
    heights = [2 * rows if before and row == (0,) else rows for row in layout]
    shapes = [(len(row), height, chunk) for row, height in zip(layout, heights)]
    return pl.pallas_call(
        functools.partial(
            project_kernel,
            heads,
            len(parts[0]),
            size,
            groups,
            len(before),
            layout,
            len(afters),
        ),
        grid=(1,),
        in_specs=in_smem(1)
        + [whole(1, min(16, after.shape[1]), 128) for after in afters]
        + [part_spec(index) for _, index in flat]
        + [whole(rows, width)] * len(before)
        + [rows_spec] * 4
        + [head_spec] * 2
        + [pl.BlockSpec(memory_space=pl.ANY)] * 3,
        out_specs=[whole(*shape) for shape in shapes]
        + [whole(size, heads, DH, DH)]
        + [whole(rows, width)] * 2,
        scratch_shapes=[
            pltpu.VMEM((tile_count, 3, tile, width), BF16),
            pltpu.SemaphoreType.DMA((tile_count, 3)),
        ],
        out_shape=[jax.ShapeDtypeStruct(shape, BF16) for shape in shapes]
        + [jax.ShapeDtypeStruct((size, heads, DH, DH), F32)]
        + [jax.ShapeDtypeStruct((rows, width), BF16)] * 2,
        compiler_params=grant(60),
        cost_estimate=cost(3 * sum(map(len, layout))),
        name="project",
    )(
        flip,
        *afters,
        *[part for part, _ in flat],
        *before,
        dk_loc,
        dv_loc,
        dq,
        key_rows,
        dcum,
        cum,
        *weights,
    )


def adjoint_kernel(heads, blocks, afters, ints_ref, *refs):
    refs = refs[afters:]
    dcums = [ref.at[j] for ref in refs[:-4] for j in range(ref.shape[0])]
    unit_ref, rows_ref, inv_ref, out_ref = refs[-4:]
    count, width = unit_ref.shape
    stacked = (len(dcums) * count, count)
    eye = (iota((count, count), 0) == iota((count, count), 1)).astype(F32)
    base = ints_ref[0] * blocks
    level, col = iota(stacked, 0), iota(stacked, 1)
    row = level % count
    mine = base + level // count
    alive = row[:, :1] <= mine[:, :1]
    every = range(heads)
    units = [unit_ref[:, head(h)] for h in every]
    moved = [[nt_high(rows_ref[:, head(h)], dcum[h]) for dcum in dcums] for h in every]
    moved = [jnp.concatenate(parts, axis=0) for parts in moved]
    inverse_t = [nt_high(eye, inv_ref[h]) for h in every]
    overlap = [jnp.where(col <= mine, nt_high(moved[h], units[h]), 0.0) for h in every]
    beta = [jnp.concatenate([eye - inverse_t[h]] * len(dcums), axis=0) for h in every]
    beta = [jnp.where(col <= mine, beta[h], 0.0) for h in every]
    turned = [nn_high(beta[h], units[h]) for h in every]
    gamma = [nn_high(overlap[h], inv_ref[h]) for h in every]
    gamma = [jnp.where((row < col) & (col <= mine), gamma[h], 0.0) for h in every]
    lifted = [nn_high(gamma[h], units[h]) for h in every]
    for h in every:
        x_all = jnp.where(alive, moved[h] - 2.0 * lifted[h], 0.0)
        own = jnp.concatenate([units[h]] * len(dcums), axis=0)
        own = jnp.where(alive, own - turned[h], 0.0)
        x_total, y_total = None, None
        for j, dcum in enumerate(dcums):
            here = slice(j * count, (j + 1) * count)
            y_part = nn_high(own[here], dcum[h])
            x_total = x_all[here] if j == 0 else x_total + x_all[here]
            y_total = y_part if j == 0 else y_total + y_part
        for total, lanes in (
            (x_total, head(h)),
            (y_total, slice(width + h * DH, width + (h + 1) * DH)),
        ):
            for c in range(count // blocks):
                out_ref[c, :, lanes] = total[c * blocks : (c + 1) * blocks]


def run_adjoint(ints, afters, dcums, unit, rows, inverse, heads, blocks):
    count, width = unit.shape
    return pl.pallas_call(
        functools.partial(adjoint_kernel, heads, blocks, len(afters)),
        out_shape=jax.ShapeDtypeStruct((count // blocks, blocks, 2 * width), F32),
        in_specs=in_smem(1)
        + [pl.BlockSpec(memory_space=pl.ANY)] * len(afters)
        + in_vmem(len(dcums) + 3),
        out_specs=pl.BlockSpec(memory_space=pltpu.VMEM),
        compiler_params=grant(60),
        cost_estimate=cost(0.2),
        name="adjoint",
    )(ints, *afters, *dcums, unit, rows, inverse)


def house_kernel(heads, blocks, base_ref, got_ref, unit_ref, rows_ref, house_ref, out_ref):
    count, width = unit_ref.shape
    total = jnp.sum(got_ref[...], axis=0)
    for h in range(heads):
        x_part = total[:, head(h)]
        y_part = total[:, slice(width + h * DH, width + (h + 1) * DH)]
        along = nt_high(y_part, rows_ref[:, head(h)])
        spot = iota((blocks, count), 0) + base_ref[0] * blocks
        along = jnp.where(iota((blocks, count), 1) < spot, along, 0.0)
        turned = y_part - 2.0 * nn_high(along, unit_ref[:, head(h)])
        dunit = -2.0 * (x_part + turned)
        house = house_ref[:, head(h)]
        lengths = jnp.sqrt(jnp.sum(house * house, axis=1, keepdims=True) + 1e-06)
        unit = house / lengths
        inner = jnp.sum(unit * dunit, axis=1, keepdims=True)
        out_ref[:, head(h)] = (dunit - unit * inner) / lengths


def run_house(ints, got, unit, rows, house_dirs, heads, blocks):
    return pl.pallas_call(
        functools.partial(house_kernel, heads, blocks),
        out_shape=jax.ShapeDtypeStruct(house_dirs.shape, F32),
        in_specs=in_smem(1) + in_vmem(4),
        out_specs=pl.BlockSpec(memory_space=pltpu.VMEM),
        compiler_params=grant(60),
        cost_estimate=cost(2),
        name="house_grad",
    )(ints, got, unit, rows, house_dirs)


def hop(value, distance, count):
    return lax.ppermute(value, "ctx", [(i, i ^ distance) for i in range(count)])


def slide(value, pairs):
    return lax.ppermute(value, "head", pairs)


INWARD = [(0, 1), (3, 2)]
MIDDLE = [(1, 2), (2, 1)]
OUTWARD = [(1, 0), (2, 3)]


def near_kernel(ends_ref, first_ref, near_ref, inward_ref, out_ref):
    mine = jnp.where(ends_ref[0] > 0, first_ref[0], near_ref[0]).astype(F32)
    out_ref[...] = mine + inward_ref[0].astype(F32)


def run_near(ends, first, band, near, inward):
    _, rows, width = near.shape
    return pl.pallas_call(
        near_kernel,
        grid=(1,),
        out_shape=jax.ShapeDtypeStruct((rows, width), F32),
        in_specs=in_smem(1)
        + [pl.BlockSpec((1, rows, width), lambda t: (0, band, 0))]
        + [pl.BlockSpec((1, rows, width), lambda t: (0, 0, 0))] * 2,
        out_specs=pl.BlockSpec((rows, width), lambda t: (0, 0)),
        compiler_params=grant(60),
        cost_estimate=cost(5),
        name="near_sum",
    )(ends, first, near, inward)


def share_kernel(*refs):
    total_ref, far_ref, outward_ref, out_ref = refs[-4:]
    far = far_ref[0].astype(F32) + outward_ref[0].astype(F32)
    out_ref[...] = (total_ref[...] + far).astype(BF16)


def run_share(share, band, bands, total, far, outward):
    rows, width = total.shape
    tile = min(512, width)
    part = pl.BlockSpec((1, rows, tile), lambda t: (0, 0, t))
    given = [] if share is None else [share]
    return pl.pallas_call(
        share_kernel,
        grid=(width // tile,),
        out_shape=jax.ShapeDtypeStruct((bands * rows, width), BF16),
        in_specs=[pl.BlockSpec(memory_space=pl.ANY)] * len(given)
        + [pl.BlockSpec((rows, tile), lambda t: (0, t)), part, part],
        out_specs=pl.BlockSpec((rows, tile), lambda t: (band, t)),
        input_output_aliases={0: 0} if given else {},
        compiler_params=grant(60),
        cost_estimate=cost(2),
        name="share",
    )(*given, total, far, outward)


def line_ends():
    place = lax.axis_index("head")
    return ((place == 0) | (place == 3)).astype(jnp.int32).reshape(1)


def outer_kernel(first_ref, low_ref, high_ref, out_ref):
    rows = low_ref.shape[1]
    for i, ref in enumerate((low_ref, high_ref)):
        here = slice(i * rows, (i + 1) * rows)
        out_ref[0, here] = (first_ref[0, here].astype(F32) + ref[0].astype(F32)).astype(BF16)


def run_outer(firsts, low, high):
    _, rows, width = low.shape
    swapped = pl.BlockSpec((1, rows, width), lambda t: (1, 0, 0))
    both = pl.BlockSpec((1, 2 * rows, width), lambda t: (0, 0, 0))
    return pl.pallas_call(
        outer_kernel,
        grid=(1,),
        out_shape=jax.ShapeDtypeStruct(firsts.shape, BF16),
        in_specs=[both, swapped, swapped],
        out_specs=both,
        compiler_params=grant(60),
        cost_estimate=cost(2),
        name="outer",
    )(firsts, low, high)


def first_band_kernel(ends_ref, first_ref, outward_ref, *refs):
    out_ref = refs[-1]
    rows = refs[0].shape[1]
    for i in range(2):
        here = slice(i * rows, (i + 1) * rows)
        rest_ref, inward_ref, swapped_ref = refs[3 * i : 3 * i + 3]
        total = jnp.where(ends_ref[0] > 0, first_ref[0, here], rest_ref[0]).astype(F32)
        total = total + inward_ref[0].astype(F32)
        total = total + (swapped_ref[0].astype(F32) + outward_ref[0, here].astype(F32))
        out_ref[here] = total.astype(BF16)


def run_first_band(bands, firsts, outward, *parts):
    _, height, width = firsts.shape
    tile = min(512, width)
    both = pl.BlockSpec((1, height, tile), lambda t: (0, 0, t))
    part = pl.BlockSpec((1, height // 2, tile), lambda t: (0, 0, t))
    return pl.pallas_call(
        first_band_kernel,
        grid=(width // tile,),
        out_shape=jax.ShapeDtypeStruct((bands * height, width), BF16),
        in_specs=in_smem(1) + [both] * 2 + [part] * len(parts),
        out_specs=pl.BlockSpec((height, tile), lambda t: (0, t)),
        compiler_params=grant(60),
        cost_estimate=cost(2),
        name="first_band",
    )(line_ends(), firsts, outward, *parts)


def line_scatter_apart(first, near, far, last, meanwhile, exchange, earlier):
    in_last, in_far = slide(last, INWARD), slide(far, INWARD)
    in_last, first = lax.optimization_barrier((in_last, first))
    sum_last = last + in_last
    swap_last = slide(sum_last, MIDDLE)
    other = meanwhile(sum_last)
    in_far, near, other = lax.optimization_barrier((in_far, near, other))
    in_near = slide(near, INWARD)
    sum_far = far + in_far
    swap_far = slide(sum_far, MIDDLE)
    swap_last, *_ = lax.optimization_barrier((swap_last, earlier, sum_far))
    outer = first + swap_last
    outward = slide(outer, OUTWARD)
    other, in_near, _ = lax.optimization_barrier((other, in_near, outer))
    other = exchange(other)
    total = run_near(line_ends(), first, 0, near, in_near)
    return total, swap_far, outward, other, outer


def shards(
    query_rows, key_rows, value_rows, grad_out, house_dirs, owners, offsets, w_query, w_key, w_value
):
    tok_rows, width = query_rows.shape
    heads, blocks = width // DH, tok_rows // BLK
    ctx_count, groups = lax.axis_size("ctx"), lax.axis_size("head")
    my_index = lax.axis_index("ctx").astype(jnp.int32)
    ints = jnp.concatenate([my_index.reshape(1), owners.reshape(-1), offsets.reshape(-1)])
    by_hand = ctx_count == 8 and groups == 4 and blocks == 4
    core, across, along = 1, 2, 4

    if by_hand:
        other = hop(house_dirs, core, 8)
        upper = (my_index & core) != 0
        low, high = jnp.where(upper, other, house_dirs), jnp.where(upper, house_dirs, other)
        house_pair = jnp.concatenate([low, high], axis=0)
        value_x, key_y = hop(value_rows, across, 8), hop(key_rows, along, 8)
        key_x, value_y = hop(key_rows, across, 8), hop(value_rows, along, 8)
        house_late, *_ = lax.optimization_barrier((house_pair, value_x, key_y))
        house_parts = [house_pair] + [hop(house_late, t, 8) for t in (2, 4, 6)]
        key_d, value_d = hop(key_y, across, 8), hop(value_x, along, 8)
    else:
        house_parts = [lax.all_gather(house_dirs, "ctx", axis=0, tiled=True)]

    unit, rows, inverse, wide, tall = run_chain(ints, house_parts, heads)
    ready = query_rows
    if by_hand:
        own = (key_rows, value_rows, key_x, value_x, key_y, value_y, key_d, value_d)
        early = lax.optimization_barrier((*own[:6], *house_parts))[:6]
        siblings = [hop(part, core, 8) for part in early]
        ready, *_ = lax.optimization_barrier((query_rows, *siblings[:3]))
    qrot, krot, local, listed_cum = run_rotate(ints, wide, tall, ready, key_rows, heads, blocks)
    if by_hand:
        late = lax.optimization_barrier((*own[6:], qrot))[:2]
        siblings += [hop(part, core, 8) for part in late]
        sources, places = [], []
        for t in range(4):
            for pair in (own[2 * t : 2 * t + 2], siblings[2 * t : 2 * t + 2]):
                places.append(((len(sources), 0), (len(sources) + 1, 0)))
                sources += pair
    else:
        sources = [lax.all_gather(key_rows, "ctx"), lax.all_gather(value_rows, "ctx")]
        places = [((0, 0), (1, 0))]

    rounds = ((0, 1), (1, blocks - 1), (blocks, 1), (blocks + 1, blocks - 1))
    dq, dcum, dk_loc, dv_loc, *outs = run_attend(
        ints,
        sources,
        places,
        (query_rows, qrot, krot, value_rows, grad_out, local, listed_cum),
        heads,
        blocks,
        rounds if by_hand else (),
    )
    weights = (w_query, w_key, w_value)
    flip = jnp.where(by_hand & (lax.axis_index("head") >= 2), 1, 0).astype(jnp.int32).reshape(1)

    arrays = (dk_loc, dv_loc, dq, key_rows, dcum, local)

    def project(block, layout, afters, parts, before=()):
        return run_project(block, groups, layout, flip, afters, parts, before, arrays, weights)

    def share_sums(sums):
        return lax.all_to_all(sums, "ctx", split_axis=0, concat_axis=0, tiled=True)

    if by_hand:
        got_0 = hop(outs[2], core, 8)
        got_1 = hop(lax.optimization_barrier((outs[3], got_0))[0], core, 8)
        sent_0 = run_merge(outs[0], got_0, 0, 1, [])
        sent_1 = run_merge(outs[1], got_1, 0, 1, [sent_0[0]])
        sent_2 = run_merge(outs[1], got_1, 1, 2, [sent_1[0]])

        def give_back(own, got, first, sent):
            back = [hop(part, t, 8) for part, t in zip(sent, (across, along, across + along))]
            near = [part.reshape(-1, BLK, 2 * width) for part in (own, got)]
            parts = []
            for j in range(sent[0].shape[0]):
                mine = [(part, 4 * (first + j)) for part in near]
                parts.append(mine + [(part, j) for part in back])
            return parts, back

        parts_0, back_0 = give_back(outs[0], got_0, 0, sent_0)
        *later_1, _, _ = lax.optimization_barrier((*sent_1, back_0, sent_2))
        parts_1, back_1 = give_back(outs[1], got_1, 0, later_1)
        *later_2, _ = lax.optimization_barrier((*sent_2, back_1))
        parts_2, _ = give_back(outs[1], got_1, 1, later_2)
        rest_0, dcum_0, *grads_0 = project(0, ((1, 2, 3),), [sent_2[0]], parts_0)
        before = (dq, *grads_0)
        split_off = ((0,), (1, 2, 3))
        firsts, rest_1, dcum_1, *_ = project(1, split_off, [rest_0], parts_1, before)
        inward_0, inward_1 = slide(rest_0, INWARD), slide(rest_1, INWARD)
        house = (unit, rows, inverse, heads, blocks)
        far, last, dcum_2, *grads_2 = project(2, ((2,), (3,)), [rest_1], parts_2)
        swapped_0 = slide(rest_0[1:] + inward_0[1:], MIDDLE)
        inward_1, *_ = lax.optimization_barrier((inward_1, swapped_0, dcum_2))
        sum_1 = rest_1[1:] + inward_1[1:]
        swapped_1 = slide(sum_1, MIDDLE)
        first, near = run_project_more(
            2, groups, ((0,), (1,)), flip, [sum_1], dq, *grads_2, weights
        )
        outer = run_outer(firsts, swapped_0, swapped_1)
        outward = slide(outer, OUTWARD)

        def meanwhile(after):
            return run_adjoint(ints, (after, outer), [dcum_0, dcum_1, dcum_2], *house)

        total_2, swapped_2, outward_2, got, outer_2 = line_scatter_apart(
            first, near, far, last, meanwhile, share_sums, outward
        )
        outward, _ = lax.optimization_barrier((outward, outer_2))
        parts = (rest_0, inward_0, swapped_0, rest_1, inward_1, swapped_1)
        share = run_first_band(2, firsts, outward, *parts)
        share = run_share(share, 1, 2, total_2, swapped_2, outward_2)
    else:
        spots = (owners * blocks + offsets).reshape(-1)
        empty = jnp.zeros((ctx_count * blocks, BLK, 2 * width), BF16)
        filled = empty.at[spots].add(outs[0])
        back = lax.psum_scatter(filled, "ctx", scatter_dimension=0, tiled=True)
        dcums = []
        share = jnp.zeros((tok_rows, w_query.shape[0] // groups), BF16)
        for j in range(blocks):
            term, dcum_out, _, _ = project(
                j, (tuple(range(groups)),), [], [[(back, j)]]
            )
            dcums.append(dcum_out)
            done = lax.psum_scatter(term, "head", scatter_dimension=0, tiled=False)
            share = lax.dynamic_update_slice(share, done, (j * BLK, 0))

        sums = run_adjoint(ints, (), dcums, unit, rows, inverse, heads, blocks)
        got = share_sums(sums)

    house_grad = run_house(ints, got, unit, rows, house_dirs, heads, blocks)
    return (share, house_grad)


def solution(mesh):
    placed = (
        P("ctx", "head"),
        P("ctx", "head"),
        P("ctx", "head"),
        P("ctx", "head"),
        P("ctx", "head"),
        P("ctx", None),
        P("ctx", None),
        P(None, "head"),
        P(None, "head"),
        P(None, "head"),
    )
    return jax.shard_map(
        shards,
        mesh=mesh,
        in_specs=placed,
        out_specs=(P("ctx", "head"), P("ctx", "head")),
        check_vma=False,
    )
```

```python
import functools
import math

import jax
import jax.numpy as jnp
from jax import lax
from jax.experimental import pallas as pl
from jax.experimental.pallas import tpu as pltpu
from jax.sharding import PartitionSpec as P

DH = 128
BLK = 128
MAXL = 2
HIGH = lax.Precision.HIGHEST
F32 = jnp.float32
BF16 = jnp.bfloat16


def nn(a, b):
    return lax.dot_general(a, b, (((1,), (0,)), ((), ())), preferred_element_type=F32)


def nt(a, b):
    return lax.dot_general(a, b, (((1,), (1,)), ((), ())), preferred_element_type=F32)


def tn(a, b):
    return lax.dot_general(a, b, (((0,), (0,)), ((), ())), preferred_element_type=F32)


def nn_high(a, b):
    return lax.dot_general(
        a, b, (((1,), (0,)), ((), ())), precision=HIGH, preferred_element_type=F32
    )


def nt_high(a, b):
    return lax.dot_general(
        a, b, (((1,), (1,)), ((), ())), precision=HIGH, preferred_element_type=F32
    )


def split(value):
    top = value.astype(BF16)
    return top, (value - top.astype(F32)).astype(BF16)


def iota(shape, dim):
    return lax.broadcasted_iota(jnp.int32, shape, dim)


def head(h):
    return slice(h * DH, (h + 1) * DH)


def listed(ints_ref, entry, entries):
    return ints_ref[1 + entry], ints_ref[1 + entries + entry]


def grant(mebibytes):
    return pltpu.CompilerParams(vmem_limit_bytes=mebibytes * 1024 * 1024)


def cost(microseconds):
    return pl.CostEstimate(
        flops=int(microseconds * 1.15e9), bytes_accessed=1 << 20, transcendentals=0
    )


def in_smem(count):
    return [pl.BlockSpec(memory_space=pltpu.SMEM)] * count


def in_vmem(count):
    return [pl.BlockSpec(memory_space=pltpu.VMEM)] * count


def chain_kernel(heads, parts, ints_ref, *refs):
    house_refs = refs[:parts]
    unit_ref, rows_ref, inv_ref, wide_ref, tall_ref, unit_h, house_all = refs[parts:]
    count = unit_ref.shape[0]
    span = count // parts
    for t, ref in enumerate(house_refs):
        place = (ints_ref[0] // (8 // parts)) ^ t if parts > 1 else 0
        house_all[pl.ds(pl.multiple_of(place * span, span), span), :] = ref[...]
    eye = (iota((count, count), 0) == iota((count, count), 1)).astype(F32)
    for h in range(heads):
        house = house_all[:, head(h)]
        lengths = jnp.sqrt(jnp.sum(house * house, axis=1, keepdims=True) + 1e-06)
        unit_ref[:, head(h)] = house / lengths
        unit_h[h] = house / lengths
        inv_ref[h] = eye

    def eliminate(step, carry):
        below = iota((count, 1), 0) > step
        for h in range(heads):
            pivot = unit_h[h, pl.ds(step, 1), :]
            overlap = jnp.sum(unit_h[h] * pivot, axis=1, keepdims=True)
            factor = jnp.where(below, 2.0 * overlap, 0.0)
            inv_ref[h] = inv_ref[h] - factor * inv_ref[h, pl.ds(step, 1), :]
        return carry

    lax.fori_loop(0, count, eliminate, 0)
    eye_wide = (iota((DH, DH), 0) == iota((DH, DH), 1)).astype(F32)
    for h in range(heads):
        units = unit_ref[:, head(h)]
        rows = nn_high(inv_ref[h], units)
        rows_ref[:, head(h)] = rows
        unit_hi, unit_lo = split(nt_high(eye_wide, units))
        rows_hi, rows_lo = split(rows)
        wide_ref[h] = jnp.concatenate([unit_hi, unit_hi, unit_lo], axis=1)
        tall_ref[h] = jnp.concatenate([rows_hi, rows_lo, rows_hi], axis=0)


def run_chain(ints, house_parts, heads):
    span, width = house_parts[0].shape
    parts = len(house_parts)
    count = span * parts
    return pl.pallas_call(
        functools.partial(chain_kernel, heads, parts),
        out_shape=[
            jax.ShapeDtypeStruct((count, width), F32),
            jax.ShapeDtypeStruct((count, width), F32),
            jax.ShapeDtypeStruct((heads, count, count), F32),
            jax.ShapeDtypeStruct((heads, DH, 3 * count), BF16),
            jax.ShapeDtypeStruct((heads, 3 * count, DH), BF16),
        ],
        in_specs=in_smem(1) + in_vmem(parts),
        out_specs=in_vmem(5),
        scratch_shapes=[pltpu.VMEM((heads, count, DH), F32), pltpu.VMEM((count, width), F32)],
        compiler_params=grant(12),
        cost_estimate=cost(6),
        name="house_chain",
    )(ints, *house_parts)


def rotate_kernel(
    heads,
    blocks,
    ints_ref,
    wide_ref,
    tall_ref,
    query_ref,
    key_ref,
    qrot_ref,
    krot_ref,
    local_ref,
    listed_ref,
):
    count = wide_ref.shape[2] // 3
    entries = blocks * MAXL
    column = iota((DH, 3 * count), 1) % count
    eye = (iota((DH, DH), 0) == iota((DH, DH), 1)).astype(F32)

    def cumulative(h, block):
        kept = jnp.where(column <= block, wide_ref[h].astype(F32), 0.0).astype(BF16)
        return split(eye - 2.0 * nn(kept, tall_ref[h]))

    base = ints_ref[0] * blocks

    def local_block(b, carry):
        here = pl.ds(pl.multiple_of(b * BLK, BLK), BLK)
        for h in range(heads):
            hi, lo = cumulative(h, base + b)
            local_ref[b, h] = hi
            query, key = query_ref[here, head(h)], key_ref[here, head(h)]
            qrot_ref[here, head(h)] = (nn(query, hi) + nn(query, lo)).astype(BF16)
            krot_ref[here, head(h)] = (nn(key, hi) + nn(key, lo)).astype(BF16)
        return carry

    lax.fori_loop(0, blocks, local_block, 0)

    def listed_block(e, carry):
        owner, offset = listed(ints_ref, e, entries)
        for h in range(heads):
            hi, lo = cumulative(h, owner * blocks + offset)
            listed_ref[e, h, :DH] = hi
            listed_ref[e, h, DH:] = lo
        return carry

    lax.fori_loop(0, entries, listed_block, 0)


def run_rotate(ints, wide, tall, query_rows, key_rows, heads, blocks):
    rows, width = query_rows.shape
    entries = blocks * MAXL
    return pl.pallas_call(
        functools.partial(rotate_kernel, heads, blocks),
        out_shape=[
            jax.ShapeDtypeStruct((rows, width), BF16),
            jax.ShapeDtypeStruct((rows, width), BF16),
            jax.ShapeDtypeStruct((blocks, heads, DH, DH), BF16),
            jax.ShapeDtypeStruct((entries, heads, 2 * DH, DH), BF16),
        ],
        in_specs=in_smem(1) + in_vmem(4),
        out_specs=in_vmem(4),
        compiler_params=grant(16),
        cost_estimate=cost(9),
        name="rotate",
    )(ints, wide, tall, query_rows, key_rows)


def attend_kernel(heads, blocks, places, pieces, *refs):
    ints_ref = refs[0]
    source_count = 1 + max(place[0] for pair in places for place in pair)
    sources = refs[1 : 1 + source_count]
    refs = refs[1 + source_count :]
    (query_ref, qrot_ref, krot_ref, value_ref, grad_ref, local_ref, listed_ref) = refs[:7]
    dq_ref, dcum_ref, dk_ref, dv_ref = refs[7:11]
    outs = refs[11 : 11 + max(len(pieces), 1)]
    refs = refs[11 + max(len(pieces), 1) :]
    dq_all, dcum_all, dk_all, dv_all, grad_sems, far_keys, far_values, sems = refs[:8]
    entries = blocks * MAXL
    scaling = DH ** (-0.5)
    log_scale = scaling * math.log2(math.e)

    def start(e, src, kind, slot, where):
        pltpu.make_async_copy(src.at[where], slot.at[e], sems.at[kind, e]).start()

    for e in range(entries):
        owner, offset = listed(ints_ref, e, entries)
        row = pl.multiple_of(offset * BLK, BLK)
        if len(places) == 1:
            start(e, sources[0], 0, far_keys, (owner, pl.ds(row, BLK)))
            start(e, sources[1], 1, far_values, (owner, pl.ds(row, BLK)))
        else:
            distance = owner ^ ints_ref[0]
            for r, (key_place, value_place) in enumerate(places):

                @pl.when(distance == r)
                def _():
                    source, first = key_place
                    start(e, sources[source], 0, far_keys, pl.ds(first + row, BLK))
                    source, first = value_place
                    start(e, sources[source], 1, far_values, pl.ds(first + row, BLK))

    out_copies = []
    if pieces:
        payloads, out_sems = refs[8 : 8 + heads], refs[8 + heads]
        for payload in payloads:
            payload[...] = jnp.zeros_like(payload)
    for kind, slots in ((0, far_keys), (1, far_values)):
        for e in range(entries):
            pltpu.make_async_copy(slots.at[e], slots.at[e], sems.at[kind, e]).wait()

    later = iota((BLK, BLK), 0) > iota((BLK, BLK), 1)
    empty = jnp.zeros((BLK, DH), BF16)
    steps = range(blocks)
    for h in range(heads):
        lanes = head(h)
        spans = [slice(a * BLK, (a + 1) * BLK) for a in steps]
        both, keys, values = [], [], []
        for a in steps:
            qrot, grad = qrot_ref[spans[a], lanes], grad_ref[spans[a], lanes]
            upper = jnp.concatenate([qrot, empty], axis=1)
            lower = jnp.concatenate([empty, grad], axis=1)
            both.append(jnp.concatenate([upper, lower], axis=0))
            keys.append([krot_ref[spans[b], lanes] for b in range(a + 1)])
            values.append([value_ref[spans[b], lanes] for b in range(a + 1)])
            for l in range(MAXL):
                e = a * MAXL + l
                raw = far_keys[e, :, lanes]
                raw = jnp.concatenate([raw, raw], axis=1)
                keys[a].append(nn(raw, listed_ref[e, h]).astype(BF16))
                values[a].append(far_values[e, :, lanes])
        scores, dprobs, tops = [], [], []
        for a in steps:
            scores.append([])
            dprobs.append([])
            top = None
            for b in range(a + 1 + MAXL):
                pair = nt(jnp.concatenate([keys[a][b], values[a][b]], axis=1), both[a])
                part = pair[:, :BLK] * log_scale
                if b == a:
                    part = jnp.where(later, -jnp.inf, part)
                scores[a].append(part)
                dprobs[a].append(pair[:, BLK:])
                top = part if top is None else jnp.maximum(top, part)
            tops.append(jnp.max(top, axis=0, keepdims=True))
        weights, inverses, deltas = [], [], []
        for a in steps:
            weights.append([])
            total, inner = None, None
            for part, dprob in zip(scores[a], dprobs[a]):
                weight = jnp.exp2(part - tops[a])
                weights[a].append(weight)
                product = weight * dprob
                total = weight if total is None else total + weight
                inner = product if inner is None else inner + product
            inverses.append(1.0 / jnp.sum(total, axis=0, keepdims=True))
            deltas.append(jnp.sum(inner, axis=0, keepdims=True) * inverses[a])
        dscores, pairs = [], []
        for a in steps:
            dscores.append([])
            pairs.append([])
            for b in range(a + 1 + MAXL):
                probs = weights[a][b] * inverses[a]
                dscore = (probs * (dprobs[a][b] - deltas[a])).astype(BF16)
                dscores[a].append(dscore)
                wide = jnp.concatenate([dscore, probs.astype(BF16)], axis=1)
                pairs[a].append(nn(wide, both[a]))
        for b in steps:
            total = pairs[b][b]
            for a in range(b + 1, blocks):
                total = total + pairs[a][b]
            dk_all[h, spans[b]] = total[:, :DH] * scaling
            dv_all[h, spans[b]] = total[:, DH:]
        for e in range(entries):
            pair = pairs[e // MAXL][e // MAXL + 1 + e % MAXL]
            dkey, dvalue = (pair[:, :DH] * scaling).astype(BF16), pair[:, DH:].astype(BF16)
            if pieces:
                owner, offset = listed(ints_ref, e, entries)
                distance = owner ^ ints_ref[0]
                at = (distance & 1) * blocks + offset
                payloads[h][at, distance >> 1, :, :DH] += dkey
                payloads[h][at, distance >> 1, :, DH:] += dvalue
            else:
                outs[0][e, :, 2 * h * DH : (2 * h + 1) * DH] = dkey
                outs[0][e, :, (2 * h + 1) * DH : (2 * h + 2) * DH] = dvalue
        halves = []
        for a in steps:
            wide, tall = jnp.concatenate(dscores[a], axis=0), jnp.concatenate(keys[a], axis=0)
            halves.append(split(tn(wide, tall) * scaling))
        for a in steps:
            dq_top, dq_low = halves[a]
            dq_all[h, spans[a]] = nt(dq_top, local_ref[a, h]).astype(BF16)
            query = query_ref[spans[a], lanes]
            query = jnp.concatenate([query, query], axis=0)
            dcum_all[h, a] = tn(query, jnp.concatenate([dq_top, dq_low], axis=0))
        for i, (source, where) in enumerate(
            (
                (dk_all.at[h], dk_ref.at[:, lanes]),
                (dv_all.at[h], dv_ref.at[:, lanes]),
                (dq_all.at[h], dq_ref.at[:, lanes]),
                (dcum_all.at[h], dcum_ref.at[:, h]),
            )
        ):
            copy = pltpu.make_async_copy(source, where, grad_sems.at[i, h])
            copy.start()
            out_copies.append(copy)
        for i, (first, size) in enumerate(pieces):
            where = outs[i].at[:, :, :, 2 * h * DH : (2 * h + 2) * DH]
            source = payloads[h].at[pl.ds(first, size)]
            copy = pltpu.make_async_copy(source, where, out_sems.at[i, h])
            copy.start()
            out_copies.append(copy)
    for copy in out_copies:
        copy.wait()


def run_attend(ints, sources, places, arrays, heads, blocks, pieces):
    rows, width = arrays[0].shape
    entries = blocks * MAXL
    any_spec = pl.BlockSpec(memory_space=pl.ANY)
    scratch = [
        pltpu.VMEM((heads, rows, DH), BF16),
        pltpu.VMEM((heads, blocks, DH, DH), F32),
        pltpu.VMEM((heads, rows, DH), F32),
        pltpu.VMEM((heads, rows, DH), F32),
        pltpu.SemaphoreType.DMA((4, heads)),
        pltpu.VMEM((entries, BLK, width), BF16),
        pltpu.VMEM((entries, BLK, width), BF16),
        pltpu.SemaphoreType.DMA((2, entries)),
    ]
    if pieces:
        chips = len(places) // 2
        out_parts = [
            pltpu.HBM((size, chips, BLK, 2 * width), BF16) for _, size in pieces
        ]
        part_specs = [any_spec] * len(pieces)
        scratch += [pltpu.VMEM((2 * blocks, chips, BLK, 2 * DH), BF16)] * heads
        scratch += [pltpu.SemaphoreType.DMA((len(pieces), heads))]
    else:
        out_parts = [jax.ShapeDtypeStruct((entries, BLK, 2 * width), BF16)]
        part_specs = in_vmem(1)
    return pl.pallas_call(
        functools.partial(attend_kernel, heads, blocks, places, pieces),
        out_shape=[
            pltpu.HBM((rows, width), BF16),
            pltpu.HBM((blocks, heads, DH, DH), F32),
            pltpu.HBM((rows, width), F32),
            pltpu.HBM((rows, width), F32),
        ]
        + out_parts,
        in_specs=in_smem(1) + [any_spec] * len(sources) + in_vmem(7),
        out_specs=[pl.BlockSpec(memory_space=pltpu.HBM)] * 4 + part_specs,
        scratch_shapes=scratch,
        compiler_params=grant(36),
        cost_estimate=cost(15),
        name="attend",
    )(ints, *sources, *arrays)


def merge_kernel(own_ref, got_ref, *refs):
    for i, ref in enumerate(refs[-3:]):
        total = own_ref[0, i + 1].astype(F32) + got_ref[0, i + 1].astype(F32)
        ref[0] = total.astype(BF16)


def run_merge(own, got, first, size, afters):
    _, chips, rows, width = own.shape
    cut = 2
    lanes = width // cut
    whole = pl.BlockSpec((1, chips, rows, lanes), lambda j, c: (first + j, 0, 0, c))
    return pl.pallas_call(
        merge_kernel,
        grid=(size, cut),
        out_shape=[jax.ShapeDtypeStruct((size, rows, width), BF16)] * (chips - 1),
        in_specs=[whole] * 2
        + [pl.BlockSpec((1, 16, 128), lambda j, c: (0, 0, 0))] * len(afters),
        out_specs=[pl.BlockSpec((1, rows, lanes), lambda j, c: (j, 0, c))] * (chips - 1),
        compiler_params=grant(60),
        cost_estimate=cost(2),
        name="merge",
    )(own, got, *afters)


def start_tiles(chunks, groups, flip_ref, weight_refs, tiles, sems):
    count, _, tile, _ = tiles.shape
    per = count // len(chunks)
    copies = []
    for t in range(count):
        m = chunks[t // per][0]
        row = ((m + flip_ref[0] * (groups - 1 - 2 * m)) * per + t % per) * tile
        rows = pl.ds(pl.multiple_of(row, tile), tile)
        for w, ref in enumerate(weight_refs):
            copy = pltpu.make_async_copy(ref.at[rows], tiles.at[t, w], sems.at[t, w])
            copy.start()
            copies.append(copy)
    return copies


def multiply_tiles(chunks, copies, tiles, out_refs, grads_of):
    count, _, tile, _ = tiles.shape
    per = count // len(chunks)
    for t in range(count):
        term = None
        m, out, at = chunks[t // per]
        for w, grad in enumerate(grads_of(m)):
            copies[3 * t + w].wait()
            part = nt(tiles[t, w], grad)
            term = part if term is None else term + part
        spot = slice(t % per * tile, (t % per + 1) * tile)
        out_refs[out][at, :, spot] = term.T.astype(BF16)


def project_kernel(heads, parts, size, groups, before, layout, afters, flip_ref, *refs):
    refs = refs[afters:]
    outs = len(layout)
    chunks = [(m, i, at) for i, row in enumerate(layout) for at, m in enumerate(row)]
    tiles, sems = refs[-2:]
    part_refs, refs = refs[: size * parts], refs[size * parts :]
    before_refs, refs = refs[:before], refs[before:]
    dk_loc, dv_loc, dq_ref, key_ref, dcum_in, cum_ref = refs[:6]
    weight_refs, out_refs = refs[6:9], refs[9 : 9 + outs]
    dcum_out, dk_out, dv_out = refs[9 + outs : 12 + outs]
    copies = start_tiles(chunks, groups, flip_ref, weight_refs, tiles, sems)
    earlier = ()
    dk_rows, dv_rows = [], []
    for j in range(size):
        here = slice(j * BLK, (j + 1) * BLK)
        dk, dv = [], []
        for h in range(heads):
            both = slice(2 * h * DH, (2 * h + 2) * DH)
            total = part_refs[j * parts][0, :, both].astype(F32)
            for ref in part_refs[j * parts + 1 : (j + 1) * parts]:
                total = total + ref[0, :, both].astype(F32)
            dv.append((dv_loc[here, head(h)] + total[:, DH:]).astype(BF16))
            dk_top, dk_low = split(dk_loc[here, head(h)] + total[:, :DH])
            dk.append(nt(dk_top, cum_ref[j, h]).astype(BF16))
            key = key_ref[here, head(h)]
            key = jnp.concatenate([key, key], axis=0)
            dcum = tn(key, jnp.concatenate([dk_top, dk_low], axis=0))
            dcum_out[j, h] = dcum_in[j, h] + dcum
        dk_rows.append(jnp.concatenate(dk, axis=1))
        dv_rows.append(jnp.concatenate(dv, axis=1))
    dk_all, dv_all = jnp.concatenate(dk_rows, axis=0), jnp.concatenate(dv_rows, axis=0)
    dk_out[...] = dk_all
    dv_out[...] = dv_all
    grads = (dq_ref[...], dk_all, dv_all)
    if before:
        earlier = [
            jnp.concatenate([old[...], new], axis=0) for old, new in zip(before_refs, grads)
        ]

    multiply_tiles(
        chunks, copies, tiles, out_refs, lambda m: earlier if before and m == 0 else grads
    )


def project_more_kernel(groups, layout, afters, flip_ref, *refs):
    refs = refs[afters:]
    chunks = [(m, i, at) for i, row in enumerate(layout) for at, m in enumerate(row)]
    tiles, sems = refs[-2:]
    copies = start_tiles(chunks, groups, flip_ref, refs[3:6], tiles, sems)
    grads = [ref[...] for ref in refs[:3]]
    multiply_tiles(chunks, copies, tiles, refs[6:-2], lambda m: grads)


def run_project_more(block, groups, layout, flip, afters, dq, dk, dv, weights):
    rows, width = dk.shape
    model = weights[0].shape[0]
    chunk = model // groups
    tile = min(512, chunk)
    tile_count = sum(map(len, layout)) * chunk // tile

    def whole(*shape):
        return pl.BlockSpec(shape, lambda t: (0,) * len(shape))

    shapes = [(len(row), rows, chunk) for row in layout]
    return pl.pallas_call(
        functools.partial(project_more_kernel, groups, layout, len(afters)),
        grid=(1,),
        in_specs=in_smem(1)
        + [whole(1, 16, 128)] * len(afters)
        + [pl.BlockSpec((rows, width), lambda t: (block * BLK // rows, 0))]
        + [whole(rows, width)] * 2
        + [pl.BlockSpec(memory_space=pl.ANY)] * 3,
        out_specs=[whole(*shape) for shape in shapes],
        scratch_shapes=[
            pltpu.VMEM((tile_count, 3, tile, width), BF16),
            pltpu.SemaphoreType.DMA((tile_count, 3)),
        ],
        out_shape=[jax.ShapeDtypeStruct(shape, BF16) for shape in shapes],
        compiler_params=grant(60),
        cost_estimate=cost(3 * sum(map(len, layout))),
        name="project_more",
    )(flip, *afters, dq, dk, dv, *weights)


def run_project(block, groups, layout, flip, afters, parts, before, arrays, weights):
    dk_loc, dv_loc, dq, key_rows, dcum, cum = arrays
    size, width = len(parts), dq.shape[1]
    heads = width // DH
    model = weights[0].shape[0]
    chunk = model // groups
    tile = min(512, chunk)
    rows = size * BLK
    tile_count = sum(map(len, layout)) * chunk // tile

    def part_spec(index):
        return pl.BlockSpec((1, BLK, 2 * width), lambda t: (index, 0, 0))

    def whole(*shape):
        return pl.BlockSpec(shape, lambda t: (0,) * len(shape))

    rows_spec = pl.BlockSpec((rows, width), lambda t: (block // size, 0))
    head_spec = pl.BlockSpec((size, heads, DH, DH), lambda t: (block // size, 0, 0, 0))
    flat = [part for row in parts for part in row]
    heights = [2 * rows if before and row == (0,) else rows for row in layout]
    shapes = [(len(row), height, chunk) for row, height in zip(layout, heights)]
    return pl.pallas_call(
        functools.partial(
            project_kernel,
            heads,
            len(parts[0]),
            size,
            groups,
            len(before),
            layout,
            len(afters),
        ),
        grid=(1,),
        in_specs=in_smem(1)
        + [whole(1, min(16, after.shape[1]), 128) for after in afters]
        + [part_spec(index) for _, index in flat]
        + [whole(rows, width)] * len(before)
        + [rows_spec] * 4
        + [head_spec] * 2
        + [pl.BlockSpec(memory_space=pl.ANY)] * 3,
        out_specs=[whole(*shape) for shape in shapes]
        + [whole(size, heads, DH, DH)]
        + [whole(rows, width)] * 2,
        scratch_shapes=[
            pltpu.VMEM((tile_count, 3, tile, width), BF16),
            pltpu.SemaphoreType.DMA((tile_count, 3)),
        ],
        out_shape=[jax.ShapeDtypeStruct(shape, BF16) for shape in shapes]
        + [jax.ShapeDtypeStruct((size, heads, DH, DH), F32)]
        + [jax.ShapeDtypeStruct((rows, width), BF16)] * 2,
        compiler_params=grant(60),
        cost_estimate=cost(3 * sum(map(len, layout))),
        name="project",
    )(
        flip,
        *afters,
        *[part for part, _ in flat],
        *before,
        dk_loc,
        dv_loc,
        dq,
        key_rows,
        dcum,
        cum,
        *weights,
    )


def adjoint_kernel(heads, blocks, afters, ints_ref, *refs):
    refs = refs[afters:]
    dcums = [ref.at[j] for ref in refs[:-4] for j in range(ref.shape[0])]
    unit_ref, rows_ref, inv_ref, out_ref = refs[-4:]
    count, width = unit_ref.shape
    stacked = (len(dcums) * count, count)
    eye = (iota((count, count), 0) == iota((count, count), 1)).astype(F32)
    base = ints_ref[0] * blocks
    level, col = iota(stacked, 0), iota(stacked, 1)
    row = level % count
    mine = base + level // count
    alive = row[:, :1] <= mine[:, :1]
    every = range(heads)
    units = [unit_ref[:, head(h)] for h in every]
    moved = [[nt_high(rows_ref[:, head(h)], dcum[h]) for dcum in dcums] for h in every]
    moved = [jnp.concatenate(parts, axis=0) for parts in moved]
    inverse_t = [nt_high(eye, inv_ref[h]) for h in every]
    overlap = [jnp.where(col <= mine, nt_high(moved[h], units[h]), 0.0) for h in every]
    beta = [jnp.concatenate([eye - inverse_t[h]] * len(dcums), axis=0) for h in every]
    beta = [jnp.where(col <= mine, beta[h], 0.0) for h in every]
    turned = [nn_high(beta[h], units[h]) for h in every]
    gamma = [nn_high(overlap[h], inv_ref[h]) for h in every]
    gamma = [jnp.where((row < col) & (col <= mine), gamma[h], 0.0) for h in every]
    lifted = [nn_high(gamma[h], units[h]) for h in every]
    for h in every:
        x_all = jnp.where(alive, moved[h] - 2.0 * lifted[h], 0.0)
        own = jnp.concatenate([units[h]] * len(dcums), axis=0)
        own = jnp.where(alive, own - turned[h], 0.0)
        x_total, y_total = None, None
        for j, dcum in enumerate(dcums):
            here = slice(j * count, (j + 1) * count)
            y_part = nn_high(own[here], dcum[h])
            x_total = x_all[here] if j == 0 else x_total + x_all[here]
            y_total = y_part if j == 0 else y_total + y_part
        for total, lanes in (
            (x_total, head(h)),
            (y_total, slice(width + h * DH, width + (h + 1) * DH)),
        ):
            for c in range(count // blocks):
                out_ref[c, :, lanes] = total[c * blocks : (c + 1) * blocks]


def run_adjoint(ints, afters, dcums, unit, rows, inverse, heads, blocks):
    count, width = unit.shape
    return pl.pallas_call(
        functools.partial(adjoint_kernel, heads, blocks, len(afters)),
        out_shape=jax.ShapeDtypeStruct((count // blocks, blocks, 2 * width), F32),
        in_specs=in_smem(1)
        + [pl.BlockSpec(memory_space=pl.ANY)] * len(afters)
        + in_vmem(len(dcums) + 3),
        out_specs=pl.BlockSpec(memory_space=pltpu.VMEM),
        compiler_params=grant(60),
        cost_estimate=cost(0.2),
        name="adjoint",
    )(ints, *afters, *dcums, unit, rows, inverse)


def house_kernel(heads, blocks, base_ref, got_ref, unit_ref, rows_ref, house_ref, out_ref):
    count, width = unit_ref.shape
    total = jnp.sum(got_ref[...], axis=0)
    for h in range(heads):
        x_part = total[:, head(h)]
        y_part = total[:, slice(width + h * DH, width + (h + 1) * DH)]
        along = nt_high(y_part, rows_ref[:, head(h)])
        spot = iota((blocks, count), 0) + base_ref[0] * blocks
        along = jnp.where(iota((blocks, count), 1) < spot, along, 0.0)
        turned = y_part - 2.0 * nn_high(along, unit_ref[:, head(h)])
        dunit = -2.0 * (x_part + turned)
        house = house_ref[:, head(h)]
        lengths = jnp.sqrt(jnp.sum(house * house, axis=1, keepdims=True) + 1e-06)
        unit = house / lengths
        inner = jnp.sum(unit * dunit, axis=1, keepdims=True)
        out_ref[:, head(h)] = (dunit - unit * inner) / lengths


def run_house(ints, got, unit, rows, house_dirs, heads, blocks):
    return pl.pallas_call(
        functools.partial(house_kernel, heads, blocks),
        out_shape=jax.ShapeDtypeStruct(house_dirs.shape, F32),
        in_specs=in_smem(1) + in_vmem(4),
        out_specs=pl.BlockSpec(memory_space=pltpu.VMEM),
        compiler_params=grant(60),
        cost_estimate=cost(2),
        name="house_grad",
    )(ints, got, unit, rows, house_dirs)


def hop(value, distance, count):
    return lax.ppermute(value, "ctx", [(i, i ^ distance) for i in range(count)])


def slide(value, pairs):
    return lax.ppermute(value, "head", pairs)


INWARD = [(0, 1), (3, 2)]
MIDDLE = [(1, 2), (2, 1)]
OUTWARD = [(1, 0), (2, 3)]


def last_band_kernel(ends_ref, share_ref, first_ref, near_ref, inward_ref, far_ref, *refs):
    outward_ref, out_ref = refs
    total = jnp.where(ends_ref[0] > 0, first_ref[0], near_ref[0]).astype(F32)
    total = total + inward_ref[0].astype(F32)
    total = total + (far_ref[0].astype(F32) + outward_ref[0].astype(F32))
    out_ref[...] = total.astype(BF16)


def run_last_band(share, *parts):
    _, rows, width = parts[0].shape
    tile = min(512, width)
    band = share.shape[0] // rows - 1
    return pl.pallas_call(
        last_band_kernel,
        grid=(width // tile,),
        out_shape=jax.ShapeDtypeStruct(share.shape, BF16),
        in_specs=in_smem(1)
        + [pl.BlockSpec(memory_space=pl.ANY)]
        + [pl.BlockSpec((1, rows, tile), lambda t: (0, 0, t))] * len(parts),
        out_specs=pl.BlockSpec((rows, tile), lambda t: (band, t)),
        input_output_aliases={1: 0},
        compiler_params=grant(60),
        cost_estimate=cost(2),
        name="last_band",
    )(line_ends(), share, *parts)


def line_ends():
    place = lax.axis_index("head")
    return ((place == 0) | (place == 3)).astype(jnp.int32).reshape(1)


def outer_kernel(first_ref, low_ref, high_ref, out_ref):
    rows = low_ref.shape[1]
    for i, ref in enumerate((low_ref, high_ref)):
        here = slice(i * rows, (i + 1) * rows)
        out_ref[0, here] = (first_ref[0, here].astype(F32) + ref[0].astype(F32)).astype(BF16)


def run_outer(firsts, low, high):
    _, rows, width = low.shape
    swapped = pl.BlockSpec((1, rows, width), lambda t: (1, 0, 0))
    both = pl.BlockSpec((1, 2 * rows, width), lambda t: (0, 0, 0))
    return pl.pallas_call(
        outer_kernel,
        grid=(1,),
        out_shape=jax.ShapeDtypeStruct(firsts.shape, BF16),
        in_specs=[both, swapped, swapped],
        out_specs=both,
        compiler_params=grant(60),
        cost_estimate=cost(2),
        name="outer",
    )(firsts, low, high)


def first_band_kernel(ends_ref, first_ref, outward_ref, *refs):
    out_ref = refs[-1]
    rows = refs[0].shape[1]
    for i in range(2):
        here = slice(i * rows, (i + 1) * rows)
        rest_ref, inward_ref, swapped_ref = refs[3 * i : 3 * i + 3]
        total = jnp.where(ends_ref[0] > 0, first_ref[0, here], rest_ref[0]).astype(F32)
        total = total + inward_ref[0].astype(F32)
        total = total + (swapped_ref[0].astype(F32) + outward_ref[0, here].astype(F32))
        out_ref[here] = total.astype(BF16)


def run_first_band(bands, firsts, outward, *parts):
    _, height, width = firsts.shape
    tile = min(512, width)
    both = pl.BlockSpec((1, height, tile), lambda t: (0, 0, t))
    part = pl.BlockSpec((1, height // 2, tile), lambda t: (0, 0, t))
    return pl.pallas_call(
        first_band_kernel,
        grid=(width // tile,),
        out_shape=jax.ShapeDtypeStruct((bands * height, width), BF16),
        in_specs=in_smem(1) + [both] * 2 + [part] * len(parts),
        out_specs=pl.BlockSpec((height, tile), lambda t: (0, t)),
        compiler_params=grant(60),
        cost_estimate=cost(2),
        name="first_band",
    )(line_ends(), firsts, outward, *parts)


def line_scatter_apart(first, near, far, last, meanwhile, exchange, earlier):
    in_last, in_far = slide(last, INWARD), slide(far, INWARD)
    in_last, first = lax.optimization_barrier((in_last, first))
    sum_last = last + in_last
    swap_last = slide(sum_last, MIDDLE)
    other = meanwhile(sum_last)
    in_far, other = lax.optimization_barrier((in_far, other))
    sum_far = far + in_far
    swap_far = slide(sum_far, MIDDLE)
    swap_last, *_ = lax.optimization_barrier((swap_last, earlier, sum_far))
    outer = first + swap_last
    outward = slide(outer, OUTWARD)
    other, near, _ = lax.optimization_barrier((other, near, outer))
    in_near = slide(near, INWARD)
    return (first, near, in_near, swap_far, outward), exchange(other), outer


def shards(
    query_rows, key_rows, value_rows, grad_out, house_dirs, owners, offsets, w_query, w_key, w_value
):
    tok_rows, width = query_rows.shape
    heads, blocks = width // DH, tok_rows // BLK
    ctx_count, groups = lax.axis_size("ctx"), lax.axis_size("head")
    my_index = lax.axis_index("ctx").astype(jnp.int32)
    ints = jnp.concatenate([my_index.reshape(1), owners.reshape(-1), offsets.reshape(-1)])
    by_hand = ctx_count == 8 and groups == 4 and blocks == 4
    core, across, along = 1, 2, 4

    if by_hand:
        other = hop(house_dirs, core, 8)
        upper = (my_index & core) != 0
        low, high = jnp.where(upper, other, house_dirs), jnp.where(upper, house_dirs, other)
        house_pair = jnp.concatenate([low, high], axis=0)
        value_x, key_y = hop(value_rows, across, 8), hop(key_rows, along, 8)
        key_x, value_y = hop(key_rows, across, 8), hop(value_rows, along, 8)
        house_late, *_ = lax.optimization_barrier((house_pair, value_x, key_y))
        house_parts = [house_pair] + [hop(house_late, t, 8) for t in (2, 4, 6)]
        key_d, value_d = hop(key_y, across, 8), hop(value_x, along, 8)
    else:
        house_parts = [lax.all_gather(house_dirs, "ctx", axis=0, tiled=True)]

    unit, rows, inverse, wide, tall = run_chain(ints, house_parts, heads)
    ready = query_rows
    if by_hand:
        own = (key_rows, value_rows, key_x, value_x, key_y, value_y, key_d, value_d)
        early = lax.optimization_barrier((*own[:6], *house_parts))[:6]
        siblings = [hop(part, core, 8) for part in early]
        ready, *_ = lax.optimization_barrier((query_rows, *siblings[:3]))
    qrot, krot, local, listed_cum = run_rotate(ints, wide, tall, ready, key_rows, heads, blocks)
    if by_hand:
        late = lax.optimization_barrier((*own[6:], qrot))[:2]
        siblings += [hop(part, core, 8) for part in late]
        sources, places = [], []
        for t in range(4):
            for pair in (own[2 * t : 2 * t + 2], siblings[2 * t : 2 * t + 2]):
                places.append(((len(sources), 0), (len(sources) + 1, 0)))
                sources += pair
    else:
        sources = [lax.all_gather(key_rows, "ctx"), lax.all_gather(value_rows, "ctx")]
        places = [((0, 0), (1, 0))]

    rounds = ((0, 1), (1, blocks - 1), (blocks, 1), (blocks + 1, blocks - 1))
    dq, dcum, dk_loc, dv_loc, *outs = run_attend(
        ints,
        sources,
        places,
        (query_rows, qrot, krot, value_rows, grad_out, local, listed_cum),
        heads,
        blocks,
        rounds if by_hand else (),
    )
    weights = (w_query, w_key, w_value)
    flip = jnp.where(by_hand & (lax.axis_index("head") >= 2), 1, 0).astype(jnp.int32).reshape(1)

    arrays = (dk_loc, dv_loc, dq, key_rows, dcum, local)

    def project(block, layout, afters, parts, before=()):
        return run_project(block, groups, layout, flip, afters, parts, before, arrays, weights)

    def share_sums(sums):
        return lax.all_to_all(sums, "ctx", split_axis=0, concat_axis=0, tiled=True)

    if by_hand:
        got_0 = hop(outs[2], core, 8)
        got_1 = hop(lax.optimization_barrier((outs[3], got_0))[0], core, 8)
        sent_0 = run_merge(outs[0], got_0, 0, 1, [])
        sent_1 = run_merge(outs[1], got_1, 0, 1, [sent_0[0]])
        sent_2 = run_merge(outs[1], got_1, 1, 2, [sent_1[0]])

        def give_back(own, got, first, sent):
            back = [hop(part, t, 8) for part, t in zip(sent, (across, along, across + along))]
            near = [part.reshape(-1, BLK, 2 * width) for part in (own, got)]
            parts = []
            for j in range(sent[0].shape[0]):
                mine = [(part, 4 * (first + j)) for part in near]
                parts.append(mine + [(part, j) for part in back])
            return parts, back

        parts_0, back_0 = give_back(outs[0], got_0, 0, sent_0)
        *later_1, _, _ = lax.optimization_barrier((*sent_1, back_0, sent_2))
        parts_1, back_1 = give_back(outs[1], got_1, 0, later_1)
        *later_2, _ = lax.optimization_barrier((*sent_2, back_1))
        parts_2, _ = give_back(outs[1], got_1, 1, later_2)
        rest_0, dcum_0, *grads_0 = project(0, ((1, 2, 3),), [sent_2[0]], parts_0)
        before = (dq, *grads_0)
        split_off = ((0,), (1, 2, 3))
        firsts, rest_1, dcum_1, *_ = project(1, split_off, [rest_0], parts_1, before)
        inward_0, inward_1 = slide(rest_0, INWARD), slide(rest_1, INWARD)
        house = (unit, rows, inverse, heads, blocks)
        far, last, dcum_2, *grads_2 = project(2, ((2,), (3,)), [rest_1], parts_2)
        swapped_0 = slide(rest_0[1:] + inward_0[1:], MIDDLE)
        inward_1, *_ = lax.optimization_barrier((inward_1, swapped_0, dcum_2))
        sum_1 = rest_1[1:] + inward_1[1:]
        swapped_1 = slide(sum_1, MIDDLE)
        first, near = run_project_more(
            2, groups, ((0,), (1,)), flip, [sum_1], dq, *grads_2, weights
        )
        outer = run_outer(firsts, swapped_0, swapped_1)
        outward = slide(outer, OUTWARD)

        def meanwhile(after):
            return run_adjoint(ints, (after, outer), [dcum_0, dcum_1, dcum_2], *house)

        last_parts, got, outer_2 = line_scatter_apart(
            first, near, far, last, meanwhile, share_sums, outward
        )
        outward, _ = lax.optimization_barrier((outward, outer_2))
        parts = (rest_0, inward_0, swapped_0, rest_1, inward_1, swapped_1)
        share = run_first_band(2, firsts, outward, *parts)
        share = run_last_band(share, *last_parts)
    else:
        spots = (owners * blocks + offsets).reshape(-1)
        empty = jnp.zeros((ctx_count * blocks, BLK, 2 * width), BF16)
        filled = empty.at[spots].add(outs[0])
        back = lax.psum_scatter(filled, "ctx", scatter_dimension=0, tiled=True)
        dcums = []
        share = jnp.zeros((tok_rows, w_query.shape[0] // groups), BF16)
        for j in range(blocks):
            term, dcum_out, _, _ = project(
                j, (tuple(range(groups)),), [], [[(back, j)]]
            )
            dcums.append(dcum_out)
            done = lax.psum_scatter(term, "head", scatter_dimension=0, tiled=False)
            share = lax.dynamic_update_slice(share, done, (j * BLK, 0))

        sums = run_adjoint(ints, (), dcums, unit, rows, inverse, heads, blocks)
        got = share_sums(sums)

    house_grad = run_house(ints, got, unit, rows, house_dirs, heads, blocks)
    return (share, house_grad)


def solution(mesh):
    placed = (
        P("ctx", "head"),
        P("ctx", "head"),
        P("ctx", "head"),
        P("ctx", "head"),
        P("ctx", "head"),
        P("ctx", None),
        P("ctx", None),
        P(None, "head"),
        P(None, "head"),
        P(None, "head"),
    )
    return jax.shard_map(
        shards,
        mesh=mesh,
        in_specs=placed,
        out_specs=(P("ctx", "head"), P("ctx", "head")),
        check_vma=False,
    )
```

```python
import functools
import math

import jax
import jax.numpy as jnp
from jax import lax
from jax.experimental import pallas as pl
from jax.experimental.pallas import tpu as pltpu
from jax.sharding import PartitionSpec as P

DH = 128
BLK = 128
MAXL = 2
HIGH = lax.Precision.HIGHEST
F32 = jnp.float32
BF16 = jnp.bfloat16


def nn(a, b):
    return lax.dot_general(a, b, (((1,), (0,)), ((), ())), preferred_element_type=F32)


def nt(a, b):
    return lax.dot_general(a, b, (((1,), (1,)), ((), ())), preferred_element_type=F32)


def tn(a, b):
    return lax.dot_general(a, b, (((0,), (0,)), ((), ())), preferred_element_type=F32)


def nn_high(a, b):
    return lax.dot_general(
        a, b, (((1,), (0,)), ((), ())), precision=HIGH, preferred_element_type=F32
    )


def nt_high(a, b):
    return lax.dot_general(
        a, b, (((1,), (1,)), ((), ())), precision=HIGH, preferred_element_type=F32
    )


def split(value):
    top = value.astype(BF16)
    return top, (value - top.astype(F32)).astype(BF16)


def iota(shape, dim):
    return lax.broadcasted_iota(jnp.int32, shape, dim)


def head(h):
    return slice(h * DH, (h + 1) * DH)


def listed(ints_ref, entry, entries):
    return ints_ref[1 + entry], ints_ref[1 + entries + entry]


def grant(mebibytes):
    return pltpu.CompilerParams(vmem_limit_bytes=mebibytes * 1024 * 1024)


def cost(microseconds):
    return pl.CostEstimate(
        flops=int(microseconds * 1.15e9), bytes_accessed=1 << 20, transcendentals=0
    )


def in_smem(count):
    return [pl.BlockSpec(memory_space=pltpu.SMEM)] * count


def in_vmem(count):
    return [pl.BlockSpec(memory_space=pltpu.VMEM)] * count


def chain_kernel(heads, parts, ints_ref, *refs):
    house_refs = refs[:parts]
    unit_ref, rows_ref, inv_ref, wide_ref, tall_ref, unit_h, house_all = refs[parts:]
    count = unit_ref.shape[0]
    span = count // parts
    for t, ref in enumerate(house_refs):
        place = (ints_ref[0] // (8 // parts)) ^ t if parts > 1 else 0
        house_all[pl.ds(pl.multiple_of(place * span, span), span), :] = ref[...]
    eye = (iota((count, count), 0) == iota((count, count), 1)).astype(F32)
    for h in range(heads):
        house = house_all[:, head(h)]
        lengths = jnp.sqrt(jnp.sum(house * house, axis=1, keepdims=True) + 1e-06)
        unit_ref[:, head(h)] = house / lengths
        unit_h[h] = house / lengths
        inv_ref[h] = eye

    def eliminate(step, carry):
        below = iota((count, 1), 0) > step
        for h in range(heads):
            pivot = unit_h[h, pl.ds(step, 1), :]
            overlap = jnp.sum(unit_h[h] * pivot, axis=1, keepdims=True)
            factor = jnp.where(below, 2.0 * overlap, 0.0)
            inv_ref[h] = inv_ref[h] - factor * inv_ref[h, pl.ds(step, 1), :]
        return carry

    lax.fori_loop(0, count, eliminate, 0)
    eye_wide = (iota((DH, DH), 0) == iota((DH, DH), 1)).astype(F32)
    for h in range(heads):
        units = unit_ref[:, head(h)]
        rows = nn_high(inv_ref[h], units)
        rows_ref[:, head(h)] = rows
        unit_hi, unit_lo = split(nt_high(eye_wide, units))
        rows_hi, rows_lo = split(rows)
        wide_ref[h] = jnp.concatenate([unit_hi, unit_hi, unit_lo], axis=1)
        tall_ref[h] = jnp.concatenate([rows_hi, rows_lo, rows_hi], axis=0)


def run_chain(ints, house_parts, heads):
    span, width = house_parts[0].shape
    parts = len(house_parts)
    count = span * parts
    return pl.pallas_call(
        functools.partial(chain_kernel, heads, parts),
        out_shape=[
            jax.ShapeDtypeStruct((count, width), F32),
            jax.ShapeDtypeStruct((count, width), F32),
            jax.ShapeDtypeStruct((heads, count, count), F32),
            jax.ShapeDtypeStruct((heads, DH, 3 * count), BF16),
            jax.ShapeDtypeStruct((heads, 3 * count, DH), BF16),
        ],
        in_specs=in_smem(1) + in_vmem(parts),
        out_specs=in_vmem(5),
        scratch_shapes=[pltpu.VMEM((heads, count, DH), F32), pltpu.VMEM((count, width), F32)],
        compiler_params=grant(12),
        cost_estimate=cost(6),
        name="house_chain",
    )(ints, *house_parts)


def rotate_kernel(
    heads,
    blocks,
    ints_ref,
    wide_ref,
    tall_ref,
    query_ref,
    key_ref,
    qrot_ref,
    krot_ref,
    local_ref,
    listed_ref,
):
    count = wide_ref.shape[2] // 3
    entries = blocks * MAXL
    column = iota((DH, 3 * count), 1) % count
    eye = (iota((DH, DH), 0) == iota((DH, DH), 1)).astype(F32)

    def cumulative(h, block):
        kept = jnp.where(column <= block, wide_ref[h].astype(F32), 0.0).astype(BF16)
        return split(eye - 2.0 * nn(kept, tall_ref[h]))

    base = ints_ref[0] * blocks

    def local_block(b, carry):
        here = pl.ds(pl.multiple_of(b * BLK, BLK), BLK)
        for h in range(heads):
            hi, lo = cumulative(h, base + b)
            local_ref[b, h] = hi
            query, key = query_ref[here, head(h)], key_ref[here, head(h)]
            qrot_ref[here, head(h)] = (nn(query, hi) + nn(query, lo)).astype(BF16)
            krot_ref[here, head(h)] = (nn(key, hi) + nn(key, lo)).astype(BF16)
        return carry

    lax.fori_loop(0, blocks, local_block, 0)

    def listed_block(e, carry):
        owner, offset = listed(ints_ref, e, entries)
        for h in range(heads):
            hi, lo = cumulative(h, owner * blocks + offset)
            listed_ref[e, h, :DH] = hi
            listed_ref[e, h, DH:] = lo
        return carry

    lax.fori_loop(0, entries, listed_block, 0)


def run_rotate(ints, wide, tall, query_rows, key_rows, heads, blocks):
    rows, width = query_rows.shape
    entries = blocks * MAXL
    return pl.pallas_call(
        functools.partial(rotate_kernel, heads, blocks),
        out_shape=[
            jax.ShapeDtypeStruct((rows, width), BF16),
            jax.ShapeDtypeStruct((rows, width), BF16),
            jax.ShapeDtypeStruct((blocks, heads, DH, DH), BF16),
            jax.ShapeDtypeStruct((entries, heads, 2 * DH, DH), BF16),
        ],
        in_specs=in_smem(1) + in_vmem(4),
        out_specs=in_vmem(4),
        compiler_params=grant(16),
        cost_estimate=cost(9),
        name="rotate",
    )(ints, wide, tall, query_rows, key_rows)


def attend_kernel(heads, blocks, places, pieces, *refs):
    ints_ref = refs[0]
    source_count = 1 + max(place[0] for pair in places for place in pair)
    sources = refs[1 : 1 + source_count]
    refs = refs[1 + source_count :]
    (query_ref, qrot_ref, krot_ref, value_ref, grad_ref, local_ref, listed_ref) = refs[:7]
    dq_ref, dcum_ref, dk_ref, dv_ref = refs[7:11]
    outs = refs[11 : 11 + max(len(pieces), 1)]
    refs = refs[11 + max(len(pieces), 1) :]
    dq_all, dcum_all, dk_all, dv_all, grad_sems, far_keys, far_values, sems = refs[:8]
    entries = blocks * MAXL
    scaling = DH ** (-0.5)
    log_scale = scaling * math.log2(math.e)

    def start(e, src, kind, slot, where):
        pltpu.make_async_copy(src.at[where], slot.at[e], sems.at[kind, e]).start()

    for e in range(entries):
        owner, offset = listed(ints_ref, e, entries)
        row = pl.multiple_of(offset * BLK, BLK)
        if len(places) == 1:
            start(e, sources[0], 0, far_keys, (owner, pl.ds(row, BLK)))
            start(e, sources[1], 1, far_values, (owner, pl.ds(row, BLK)))
        else:
            distance = owner ^ ints_ref[0]
            for r, (key_place, value_place) in enumerate(places):

                @pl.when(distance == r)
                def _():
                    source, first = key_place
                    start(e, sources[source], 0, far_keys, pl.ds(first + row, BLK))
                    source, first = value_place
                    start(e, sources[source], 1, far_values, pl.ds(first + row, BLK))

    out_copies = []
    if pieces:
        payloads, out_sems = refs[8 : 8 + heads], refs[8 + heads]
        for payload in payloads:
            payload[...] = jnp.zeros_like(payload)
    for kind, slots in ((0, far_keys), (1, far_values)):
        for e in range(entries):
            pltpu.make_async_copy(slots.at[e], slots.at[e], sems.at[kind, e]).wait()

    later = iota((BLK, BLK), 0) > iota((BLK, BLK), 1)
    empty = jnp.zeros((BLK, DH), BF16)
    steps = range(blocks)
    for h in range(heads):
        lanes = head(h)
        spans = [slice(a * BLK, (a + 1) * BLK) for a in steps]
        both, keys, values = [], [], []
        for a in steps:
            qrot, grad = qrot_ref[spans[a], lanes], grad_ref[spans[a], lanes]
            upper = jnp.concatenate([qrot, empty], axis=1)
            lower = jnp.concatenate([empty, grad], axis=1)
            both.append(jnp.concatenate([upper, lower], axis=0))
            keys.append([krot_ref[spans[b], lanes] for b in range(a + 1)])
            values.append([value_ref[spans[b], lanes] for b in range(a + 1)])
            for l in range(MAXL):
                e = a * MAXL + l
                raw = far_keys[e, :, lanes]
                raw = jnp.concatenate([raw, raw], axis=1)
                keys[a].append(nn(raw, listed_ref[e, h]).astype(BF16))
                values[a].append(far_values[e, :, lanes])
        scores, dprobs, tops = [], [], []
        for a in steps:
            scores.append([])
            dprobs.append([])
            top = None
            for b in range(a + 1 + MAXL):
                pair = nt(jnp.concatenate([keys[a][b], values[a][b]], axis=1), both[a])
                part = pair[:, :BLK] * log_scale
                if b == a:
                    part = jnp.where(later, -jnp.inf, part)
                scores[a].append(part)
                dprobs[a].append(pair[:, BLK:])
                top = part if top is None else jnp.maximum(top, part)
            tops.append(jnp.max(top, axis=0, keepdims=True))
        weights, inverses, deltas = [], [], []
        for a in steps:
            weights.append([])
            total, inner = None, None
            for part, dprob in zip(scores[a], dprobs[a]):
                weight = jnp.exp2(part - tops[a])
                weights[a].append(weight)
                product = weight * dprob
                total = weight if total is None else total + weight
                inner = product if inner is None else inner + product
            inverses.append(1.0 / jnp.sum(total, axis=0, keepdims=True))
            deltas.append(jnp.sum(inner, axis=0, keepdims=True) * inverses[a])
        dscores, pairs = [], []
        for a in steps:
            dscores.append([])
            pairs.append([])
            for b in range(a + 1 + MAXL):
                probs = weights[a][b] * inverses[a]
                dscore = (probs * (dprobs[a][b] - deltas[a])).astype(BF16)
                dscores[a].append(dscore)
                wide = jnp.concatenate([dscore, probs.astype(BF16)], axis=1)
                pairs[a].append(nn(wide, both[a]))
        for b in steps:
            total = pairs[b][b]
            for a in range(b + 1, blocks):
                total = total + pairs[a][b]
            dk_all[h, spans[b]] = total[:, :DH] * scaling
            dv_all[h, spans[b]] = total[:, DH:]
        for e in range(entries):
            pair = pairs[e // MAXL][e // MAXL + 1 + e % MAXL]
            dkey, dvalue = (pair[:, :DH] * scaling).astype(BF16), pair[:, DH:].astype(BF16)
            if pieces:
                owner, offset = listed(ints_ref, e, entries)
                distance = owner ^ ints_ref[0]
                at = (distance & 1) * blocks + offset
                payloads[h][at, distance >> 1, :, :DH] += dkey
                payloads[h][at, distance >> 1, :, DH:] += dvalue
            else:
                outs[0][e, :, 2 * h * DH : (2 * h + 1) * DH] = dkey
                outs[0][e, :, (2 * h + 1) * DH : (2 * h + 2) * DH] = dvalue
        halves = []
        for a in steps:
            wide, tall = jnp.concatenate(dscores[a], axis=0), jnp.concatenate(keys[a], axis=0)
            halves.append(split(tn(wide, tall) * scaling))
        for a in steps:
            dq_top, dq_low = halves[a]
            dq_all[h, spans[a]] = nt(dq_top, local_ref[a, h]).astype(BF16)
            query = query_ref[spans[a], lanes]
            query = jnp.concatenate([query, query], axis=0)
            dcum_all[h, a] = tn(query, jnp.concatenate([dq_top, dq_low], axis=0))
        for i, (source, where) in enumerate(
            (
                (dk_all.at[h], dk_ref.at[:, lanes]),
                (dv_all.at[h], dv_ref.at[:, lanes]),
                (dq_all.at[h], dq_ref.at[:, lanes]),
                (dcum_all.at[h], dcum_ref.at[:, h]),
            )
        ):
            copy = pltpu.make_async_copy(source, where, grad_sems.at[i, h])
            copy.start()
            out_copies.append(copy)
        for i, (first, size) in enumerate(pieces):
            where = outs[i].at[:, :, :, 2 * h * DH : (2 * h + 2) * DH]
            source = payloads[h].at[pl.ds(first, size)]
            copy = pltpu.make_async_copy(source, where, out_sems.at[i, h])
            copy.start()
            out_copies.append(copy)
    for copy in out_copies:
        copy.wait()


def run_attend(ints, sources, places, arrays, heads, blocks, pieces):
    rows, width = arrays[0].shape
    entries = blocks * MAXL
    any_spec = pl.BlockSpec(memory_space=pl.ANY)
    scratch = [
        pltpu.VMEM((heads, rows, DH), BF16),
        pltpu.VMEM((heads, blocks, DH, DH), F32),
        pltpu.VMEM((heads, rows, DH), F32),
        pltpu.VMEM((heads, rows, DH), F32),
        pltpu.SemaphoreType.DMA((4, heads)),
        pltpu.VMEM((entries, BLK, width), BF16),
        pltpu.VMEM((entries, BLK, width), BF16),
        pltpu.SemaphoreType.DMA((2, entries)),
    ]
    if pieces:
        chips = len(places) // 2
        out_parts = [
            pltpu.HBM((size, chips, BLK, 2 * width), BF16) for _, size in pieces
        ]
        part_specs = [any_spec] * len(pieces)
        scratch += [pltpu.VMEM((2 * blocks, chips, BLK, 2 * DH), BF16)] * heads
        scratch += [pltpu.SemaphoreType.DMA((len(pieces), heads))]
    else:
        out_parts = [jax.ShapeDtypeStruct((entries, BLK, 2 * width), BF16)]
        part_specs = in_vmem(1)
    return pl.pallas_call(
        functools.partial(attend_kernel, heads, blocks, places, pieces),
        out_shape=[
            pltpu.HBM((rows, width), BF16),
            pltpu.HBM((blocks, heads, DH, DH), F32),
            pltpu.HBM((rows, width), F32),
            pltpu.HBM((rows, width), F32),
        ]
        + out_parts,
        in_specs=in_smem(1) + [any_spec] * len(sources) + in_vmem(7),
        out_specs=[pl.BlockSpec(memory_space=pltpu.HBM)] * 4 + part_specs,
        scratch_shapes=scratch,
        compiler_params=grant(36),
        cost_estimate=cost(15),
        name="attend",
    )(ints, *sources, *arrays)


def merge_kernel(own_ref, got_ref, *refs):
    for i, ref in enumerate(refs[-3:]):
        total = own_ref[0, i + 1].astype(F32) + got_ref[0, i + 1].astype(F32)
        ref[0] = total.astype(BF16)


def run_merge(own, got, first, size, afters):
    _, chips, rows, width = own.shape
    cut = 2
    lanes = width // cut
    whole = pl.BlockSpec((1, chips, rows, lanes), lambda j, c: (first + j, 0, 0, c))
    return pl.pallas_call(
        merge_kernel,
        grid=(size, cut),
        out_shape=[jax.ShapeDtypeStruct((size, rows, width), BF16)] * (chips - 1),
        in_specs=[whole] * 2
        + [pl.BlockSpec((1, 16, 128), lambda j, c: (0, 0, 0))] * len(afters),
        out_specs=[pl.BlockSpec((1, rows, lanes), lambda j, c: (j, 0, c))] * (chips - 1),
        compiler_params=grant(60),
        cost_estimate=cost(2),
        name="merge",
    )(own, got, *afters)


def start_tiles(chunks, groups, flip_ref, weight_refs, tiles, sems):
    count, _, tile, _ = tiles.shape
    per = count // len(chunks)
    copies = []
    for t in range(count):
        m = chunks[t // per][0]
        row = ((m + flip_ref[0] * (groups - 1 - 2 * m)) * per + t % per) * tile
        rows = pl.ds(pl.multiple_of(row, tile), tile)
        for w, ref in enumerate(weight_refs):
            copy = pltpu.make_async_copy(ref.at[rows], tiles.at[t, w], sems.at[t, w])
            copy.start()
            copies.append(copy)
    return copies


def multiply_tiles(chunks, copies, tiles, out_refs, grads_of):
    count, _, tile, _ = tiles.shape
    per = count // len(chunks)
    for t in range(count):
        term = None
        m, out, at = chunks[t // per]
        for w, grad in enumerate(grads_of(m)):
            copies[3 * t + w].wait()
            part = nt(tiles[t, w], grad)
            term = part if term is None else term + part
        spot = slice(t % per * tile, (t % per + 1) * tile)
        out_refs[out][at, :, spot] = term.T.astype(BF16)


def project_kernel(heads, parts, size, groups, before, layout, afters, flip_ref, *refs):
    refs = refs[afters:]
    outs = len(layout)
    chunks = [(m, i, at) for i, row in enumerate(layout) for at, m in enumerate(row)]
    tiles, sems = refs[-2:]
    part_refs, refs = refs[: size * parts], refs[size * parts :]
    before_refs, refs = refs[:before], refs[before:]
    dk_loc, dv_loc, dq_ref, key_ref, dcum_in, cum_ref = refs[:6]
    weight_refs, out_refs = refs[6:9], refs[9 : 9 + outs]
    dcum_out, dk_out, dv_out = refs[9 + outs : 12 + outs]
    copies = start_tiles(chunks, groups, flip_ref, weight_refs, tiles, sems)
    earlier = ()
    dk_rows, dv_rows = [], []
    for j in range(size):
        here = slice(j * BLK, (j + 1) * BLK)
        dk, dv = [], []
        for h in range(heads):
            both = slice(2 * h * DH, (2 * h + 2) * DH)
            total = part_refs[j * parts][0, :, both].astype(F32)
            for ref in part_refs[j * parts + 1 : (j + 1) * parts]:
                total = total + ref[0, :, both].astype(F32)
            dv.append((dv_loc[here, head(h)] + total[:, DH:]).astype(BF16))
            dk_top, dk_low = split(dk_loc[here, head(h)] + total[:, :DH])
            dk.append(nt(dk_top, cum_ref[j, h]).astype(BF16))
            key = key_ref[here, head(h)]
            key = jnp.concatenate([key, key], axis=0)
            dcum = tn(key, jnp.concatenate([dk_top, dk_low], axis=0))
            dcum_out[j, h] = dcum_in[j, h] + dcum
        dk_rows.append(jnp.concatenate(dk, axis=1))
        dv_rows.append(jnp.concatenate(dv, axis=1))
    dk_all, dv_all = jnp.concatenate(dk_rows, axis=0), jnp.concatenate(dv_rows, axis=0)
    dk_out[...] = dk_all
    dv_out[...] = dv_all
    grads = (dq_ref[...], dk_all, dv_all)
    if before:
        earlier = [
            jnp.concatenate([old[...], new], axis=0) for old, new in zip(before_refs, grads)
        ]

    multiply_tiles(
        chunks, copies, tiles, out_refs, lambda m: earlier if before and m == 0 else grads
    )


def project_more_kernel(groups, layout, afters, flip_ref, *refs):
    refs = refs[afters:]
    chunks = [(m, i, at) for i, row in enumerate(layout) for at, m in enumerate(row)]
    tiles, sems = refs[-2:]
    copies = start_tiles(chunks, groups, flip_ref, refs[3:6], tiles, sems)
    grads = [ref[...] for ref in refs[:3]]
    multiply_tiles(chunks, copies, tiles, refs[6:-2], lambda m: grads)


def run_project_more(block, groups, layout, flip, afters, dq, dk, dv, weights):
    rows, width = dk.shape
    model = weights[0].shape[0]
    chunk = model // groups
    tile = min(512, chunk)
    tile_count = sum(map(len, layout)) * chunk // tile

    def whole(*shape):
        return pl.BlockSpec(shape, lambda t: (0,) * len(shape))

    shapes = [(len(row), rows, chunk) for row in layout]
    return pl.pallas_call(
        functools.partial(project_more_kernel, groups, layout, len(afters)),
        grid=(1,),
        in_specs=in_smem(1)
        + [whole(1, 16, 128)] * len(afters)
        + [pl.BlockSpec((rows, width), lambda t: (block * BLK // rows, 0))]
        + [whole(rows, width)] * 2
        + [pl.BlockSpec(memory_space=pl.ANY)] * 3,
        out_specs=[whole(*shape) for shape in shapes],
        scratch_shapes=[
            pltpu.VMEM((tile_count, 3, tile, width), BF16),
            pltpu.SemaphoreType.DMA((tile_count, 3)),
        ],
        out_shape=[jax.ShapeDtypeStruct(shape, BF16) for shape in shapes],
        compiler_params=grant(60),
        cost_estimate=cost(3 * sum(map(len, layout))),
        name="project_more",
    )(flip, *afters, dq, dk, dv, *weights)


def run_project(block, groups, layout, flip, afters, parts, before, arrays, weights):
    dk_loc, dv_loc, dq, key_rows, dcum, cum = arrays
    size, width = len(parts), dq.shape[1]
    heads = width // DH
    model = weights[0].shape[0]
    chunk = model // groups
    tile = min(512, chunk)
    rows = size * BLK
    tile_count = sum(map(len, layout)) * chunk // tile

    def part_spec(index):
        return pl.BlockSpec((1, BLK, 2 * width), lambda t: (index, 0, 0))

    def whole(*shape):
        return pl.BlockSpec(shape, lambda t: (0,) * len(shape))

    rows_spec = pl.BlockSpec((rows, width), lambda t: (block // size, 0))
    head_spec = pl.BlockSpec((size, heads, DH, DH), lambda t: (block // size, 0, 0, 0))
    flat = [part for row in parts for part in row]
    heights = [2 * rows if before and row == (0,) else rows for row in layout]
    shapes = [(len(row), height, chunk) for row, height in zip(layout, heights)]
    return pl.pallas_call(
        functools.partial(
            project_kernel,
            heads,
            len(parts[0]),
            size,
            groups,
            len(before),
            layout,
            len(afters),
        ),
        grid=(1,),
        in_specs=in_smem(1)
        + [whole(1, min(16, after.shape[1]), 128) for after in afters]
        + [part_spec(index) for _, index in flat]
        + [whole(rows, width)] * len(before)
        + [rows_spec] * 4
        + [head_spec] * 2
        + [pl.BlockSpec(memory_space=pl.ANY)] * 3,
        out_specs=[whole(*shape) for shape in shapes]
        + [whole(size, heads, DH, DH)]
        + [whole(rows, width)] * 2,
        scratch_shapes=[
            pltpu.VMEM((tile_count, 3, tile, width), BF16),
            pltpu.SemaphoreType.DMA((tile_count, 3)),
        ],
        out_shape=[jax.ShapeDtypeStruct(shape, BF16) for shape in shapes]
        + [jax.ShapeDtypeStruct((size, heads, DH, DH), F32)]
        + [jax.ShapeDtypeStruct((rows, width), BF16)] * 2,
        compiler_params=grant(60),
        cost_estimate=cost(3 * sum(map(len, layout))),
        name="project",
    )(
        flip,
        *afters,
        *[part for part, _ in flat],
        *before,
        dk_loc,
        dv_loc,
        dq,
        key_rows,
        dcum,
        cum,
        *weights,
    )


def adjoint_kernel(heads, blocks, afters, ints_ref, *refs):
    refs = refs[afters:]
    dcums = [ref.at[j] for ref in refs[:-4] for j in range(ref.shape[0])]
    unit_ref, rows_ref, inv_ref, out_ref = refs[-4:]
    count, width = unit_ref.shape
    stacked = (len(dcums) * count, count)
    eye = (iota((count, count), 0) == iota((count, count), 1)).astype(F32)
    base = ints_ref[0] * blocks
    level, col = iota(stacked, 0), iota(stacked, 1)
    row = level % count
    mine = base + level // count
    alive = row[:, :1] <= mine[:, :1]
    every = range(heads)
    units = [unit_ref[:, head(h)] for h in every]
    moved = [[nt_high(rows_ref[:, head(h)], dcum[h]) for dcum in dcums] for h in every]
    moved = [jnp.concatenate(parts, axis=0) for parts in moved]
    inverse_t = [nt_high(eye, inv_ref[h]) for h in every]
    overlap = [jnp.where(col <= mine, nt_high(moved[h], units[h]), 0.0) for h in every]
    beta = [jnp.concatenate([eye - inverse_t[h]] * len(dcums), axis=0) for h in every]
    beta = [jnp.where(col <= mine, beta[h], 0.0) for h in every]
    turned = [nn_high(beta[h], units[h]) for h in every]
    gamma = [nn_high(overlap[h], inv_ref[h]) for h in every]
    gamma = [jnp.where((row < col) & (col <= mine), gamma[h], 0.0) for h in every]
    lifted = [nn_high(gamma[h], units[h]) for h in every]
    for h in every:
        x_all = jnp.where(alive, moved[h] - 2.0 * lifted[h], 0.0)
        own = jnp.concatenate([units[h]] * len(dcums), axis=0)
        own = jnp.where(alive, own - turned[h], 0.0)
        x_total, y_total = None, None
        for j, dcum in enumerate(dcums):
            here = slice(j * count, (j + 1) * count)
            y_part = nn_high(own[here], dcum[h])
            x_total = x_all[here] if j == 0 else x_total + x_all[here]
            y_total = y_part if j == 0 else y_total + y_part
        for total, lanes in (
            (x_total, head(h)),
            (y_total, slice(width + h * DH, width + (h + 1) * DH)),
        ):
            for c in range(count // blocks):
                out_ref[c, :, lanes] = total[c * blocks : (c + 1) * blocks]


def run_adjoint(ints, afters, dcums, unit, rows, inverse, heads, blocks):
    count, width = unit.shape
    return pl.pallas_call(
        functools.partial(adjoint_kernel, heads, blocks, len(afters)),
        out_shape=jax.ShapeDtypeStruct((count // blocks, blocks, 2 * width), F32),
        in_specs=in_smem(1)
        + [pl.BlockSpec(memory_space=pl.ANY)] * len(afters)
        + in_vmem(len(dcums) + 3),
        out_specs=pl.BlockSpec(memory_space=pltpu.VMEM),
        compiler_params=grant(16),
        cost_estimate=cost(0.2),
        name="adjoint",
    )(ints, *afters, *dcums, unit, rows, inverse)


def house_kernel(heads, blocks, base_ref, got_ref, unit_ref, rows_ref, house_ref, out_ref):
    count, width = unit_ref.shape
    total = jnp.sum(got_ref[...], axis=0)
    for h in range(heads):
        x_part = total[:, head(h)]
        y_part = total[:, slice(width + h * DH, width + (h + 1) * DH)]
        along = nt_high(y_part, rows_ref[:, head(h)])
        spot = iota((blocks, count), 0) + base_ref[0] * blocks
        along = jnp.where(iota((blocks, count), 1) < spot, along, 0.0)
        turned = y_part - 2.0 * nn_high(along, unit_ref[:, head(h)])
        dunit = -2.0 * (x_part + turned)
        house = house_ref[:, head(h)]
        lengths = jnp.sqrt(jnp.sum(house * house, axis=1, keepdims=True) + 1e-06)
        unit = house / lengths
        inner = jnp.sum(unit * dunit, axis=1, keepdims=True)
        out_ref[:, head(h)] = (dunit - unit * inner) / lengths


def run_house(ints, got, unit, rows, house_dirs, heads, blocks):
    return pl.pallas_call(
        functools.partial(house_kernel, heads, blocks),
        out_shape=jax.ShapeDtypeStruct(house_dirs.shape, F32),
        in_specs=in_smem(1) + in_vmem(4),
        out_specs=pl.BlockSpec(memory_space=pltpu.VMEM),
        compiler_params=grant(12),
        cost_estimate=cost(2),
        name="house_grad",
    )(ints, got, unit, rows, house_dirs)


def hop(value, distance, count):
    return lax.ppermute(value, "ctx", [(i, i ^ distance) for i in range(count)])


def slide(value, pairs):
    return lax.ppermute(value, "head", pairs)


INWARD = [(0, 1), (3, 2)]
MIDDLE = [(1, 2), (2, 1)]
OUTWARD = [(1, 0), (2, 3)]


def last_band_kernel(ends_ref, share_ref, first_ref, near_ref, inward_ref, far_ref, *refs):
    outward_ref, out_ref = refs
    total = jnp.where(ends_ref[0] > 0, first_ref[0], near_ref[0]).astype(F32)
    total = total + inward_ref[0].astype(F32)
    total = total + (far_ref[0].astype(F32) + outward_ref[0].astype(F32))
    out_ref[...] = total.astype(BF16)


def run_last_band(share, *parts):
    _, rows, width = parts[0].shape
    tile = min(512, width)
    band = share.shape[0] // rows - 1
    return pl.pallas_call(
        last_band_kernel,
        grid=(width // tile,),
        out_shape=jax.ShapeDtypeStruct(share.shape, BF16),
        in_specs=in_smem(1)
        + [pl.BlockSpec(memory_space=pl.ANY)]
        + [pl.BlockSpec((1, rows, tile), lambda t: (0, 0, t))] * len(parts),
        out_specs=pl.BlockSpec((rows, tile), lambda t: (band, t)),
        input_output_aliases={1: 0},
        compiler_params=grant(12),
        cost_estimate=cost(2),
        name="last_band",
    )(line_ends(), share, *parts)


def line_ends():
    place = lax.axis_index("head")
    return ((place == 0) | (place == 3)).astype(jnp.int32).reshape(1)


def outer_kernel(first_ref, low_ref, high_ref, out_ref):
    rows = low_ref.shape[1]
    for i, ref in enumerate((low_ref, high_ref)):
        here = slice(i * rows, (i + 1) * rows)
        out_ref[0, here] = (first_ref[0, here].astype(F32) + ref[0].astype(F32)).astype(BF16)


def run_outer(firsts, low, high):
    _, rows, width = low.shape
    swapped = pl.BlockSpec((1, rows, width), lambda t: (1, 0, 0))
    both = pl.BlockSpec((1, 2 * rows, width), lambda t: (0, 0, 0))
    return pl.pallas_call(
        outer_kernel,
        grid=(1,),
        out_shape=jax.ShapeDtypeStruct(firsts.shape, BF16),
        in_specs=[both, swapped, swapped],
        out_specs=both,
        compiler_params=grant(12),
        cost_estimate=cost(2),
        name="outer",
    )(firsts, low, high)


def first_band_kernel(ends_ref, first_ref, outward_ref, *refs):
    out_ref = refs[-1]
    rows = refs[0].shape[1]
    for i in range(2):
        here = slice(i * rows, (i + 1) * rows)
        rest_ref, inward_ref, swapped_ref = refs[3 * i : 3 * i + 3]
        total = jnp.where(ends_ref[0] > 0, first_ref[0, here], rest_ref[0]).astype(F32)
        total = total + inward_ref[0].astype(F32)
        total = total + (swapped_ref[0].astype(F32) + outward_ref[0, here].astype(F32))
        out_ref[here] = total.astype(BF16)


def run_first_band(bands, firsts, outward, *parts):
    _, height, width = firsts.shape
    tile = min(512, width)
    both = pl.BlockSpec((1, height, tile), lambda t: (0, 0, t))
    part = pl.BlockSpec((1, height // 2, tile), lambda t: (0, 0, t))
    return pl.pallas_call(
        first_band_kernel,
        grid=(width // tile,),
        out_shape=jax.ShapeDtypeStruct((bands * height, width), BF16),
        in_specs=in_smem(1) + [both] * 2 + [part] * len(parts),
        out_specs=pl.BlockSpec((height, tile), lambda t: (0, t)),
        compiler_params=grant(12),
        cost_estimate=cost(2),
        name="first_band",
    )(line_ends(), firsts, outward, *parts)


def line_scatter_apart(first, near, far, last, meanwhile, exchange, earlier):
    in_last, in_far = slide(last, INWARD), slide(far, INWARD)
    in_last, first = lax.optimization_barrier((in_last, first))
    sum_last = last + in_last
    swap_last = slide(sum_last, MIDDLE)
    other = meanwhile(sum_last)
    in_far, other = lax.optimization_barrier((in_far, other))
    sum_far = far + in_far
    swap_far = slide(sum_far, MIDDLE)
    other, _ = lax.optimization_barrier((other, sum_far))
    other = exchange(other)
    swap_last, *_ = lax.optimization_barrier((swap_last, earlier, sum_far))
    outer = first + swap_last
    outward = slide(outer, OUTWARD)
    near, _ = lax.optimization_barrier((near, outer))
    in_near = slide(near, INWARD)
    return (first, near, in_near, swap_far, outward), other, outer


def shards(
    query_rows, key_rows, value_rows, grad_out, house_dirs, owners, offsets, w_query, w_key, w_value
):
    tok_rows, width = query_rows.shape
    heads, blocks = width // DH, tok_rows // BLK
    ctx_count, groups = lax.axis_size("ctx"), lax.axis_size("head")
    my_index = lax.axis_index("ctx").astype(jnp.int32)
    ints = jnp.concatenate([my_index.reshape(1), owners.reshape(-1), offsets.reshape(-1)])
    by_hand = ctx_count == 8 and groups == 4 and blocks == 4
    core, across, along = 1, 2, 4

    if by_hand:
        other = hop(house_dirs, core, 8)
        upper = (my_index & core) != 0
        low, high = jnp.where(upper, other, house_dirs), jnp.where(upper, house_dirs, other)
        house_pair = jnp.concatenate([low, high], axis=0)
        value_x, key_y = hop(value_rows, across, 8), hop(key_rows, along, 8)
        key_x, value_y = hop(key_rows, across, 8), hop(value_rows, along, 8)
        house_late, *_ = lax.optimization_barrier((house_pair, value_x, key_y))
        house_parts = [house_pair] + [hop(house_late, t, 8) for t in (2, 4, 6)]
        key_d, value_d = hop(key_y, across, 8), hop(value_x, along, 8)
    else:
        house_parts = [lax.all_gather(house_dirs, "ctx", axis=0, tiled=True)]

    unit, rows, inverse, wide, tall = run_chain(ints, house_parts, heads)
    ready = query_rows
    if by_hand:
        own = (key_rows, value_rows, key_x, value_x, key_y, value_y, key_d, value_d)
        early = lax.optimization_barrier((*own[:6], *house_parts))[:6]
        siblings = [hop(part, core, 8) for part in early]
        ready, *_ = lax.optimization_barrier((query_rows, *siblings[:3]))
    qrot, krot, local, listed_cum = run_rotate(ints, wide, tall, ready, key_rows, heads, blocks)
    if by_hand:
        late = lax.optimization_barrier((*own[6:], qrot))[:2]
        siblings += [hop(part, core, 8) for part in late]
        sources, places = [], []
        for t in range(4):
            for pair in (own[2 * t : 2 * t + 2], siblings[2 * t : 2 * t + 2]):
                places.append(((len(sources), 0), (len(sources) + 1, 0)))
                sources += pair
    else:
        sources = [lax.all_gather(key_rows, "ctx"), lax.all_gather(value_rows, "ctx")]
        places = [((0, 0), (1, 0))]

    rounds = ((0, 1), (1, blocks - 1), (blocks, 1), (blocks + 1, blocks - 1))
    dq, dcum, dk_loc, dv_loc, *outs = run_attend(
        ints,
        sources,
        places,
        (query_rows, qrot, krot, value_rows, grad_out, local, listed_cum),
        heads,
        blocks,
        rounds if by_hand else (),
    )
    weights = (w_query, w_key, w_value)
    flip = jnp.where(by_hand & (lax.axis_index("head") >= 2), 1, 0).astype(jnp.int32).reshape(1)

    arrays = (dk_loc, dv_loc, dq, key_rows, dcum, local)

    def project(block, layout, afters, parts, before=()):
        return run_project(block, groups, layout, flip, afters, parts, before, arrays, weights)

    def share_sums(sums):
        return lax.all_to_all(sums, "ctx", split_axis=0, concat_axis=0, tiled=True)

    if by_hand:
        got_0 = hop(outs[2], core, 8)
        got_1 = hop(lax.optimization_barrier((outs[3], got_0))[0], core, 8)
        sent_0 = run_merge(outs[0], got_0, 0, 1, [])
        sent_1 = run_merge(outs[1], got_1, 0, 1, [sent_0[0]])
        sent_2 = run_merge(outs[1], got_1, 1, 2, [sent_1[0]])

        def give_back(own, got, first, sent):
            back = [hop(part, t, 8) for part, t in zip(sent, (across, along, across + along))]
            near = [part.reshape(-1, BLK, 2 * width) for part in (own, got)]
            parts = []
            for j in range(sent[0].shape[0]):
                mine = [(part, 4 * (first + j)) for part in near]
                parts.append(mine + [(part, j) for part in back])
            return parts, back

        parts_0, back_0 = give_back(outs[0], got_0, 0, sent_0)
        *later_1, _, _ = lax.optimization_barrier((*sent_1, back_0, sent_2))
        parts_1, back_1 = give_back(outs[1], got_1, 0, later_1)
        *later_2, _ = lax.optimization_barrier((*sent_2, back_1))
        parts_2, _ = give_back(outs[1], got_1, 1, later_2)
        rest_0, dcum_0, *grads_0 = project(0, ((1, 2, 3),), [sent_2[0]], parts_0)
        before = (dq, *grads_0)
        split_off = ((0,), (1, 2, 3))
        firsts, rest_1, dcum_1, *_ = project(1, split_off, [rest_0], parts_1, before)
        inward_0, inward_1 = slide(rest_0, INWARD), slide(rest_1, INWARD)
        house = (unit, rows, inverse, heads, blocks)
        far, last, dcum_2, *grads_2 = project(2, ((2,), (3,)), [rest_1], parts_2)
        swapped_0 = slide(rest_0[1:] + inward_0[1:], MIDDLE)
        inward_1, *_ = lax.optimization_barrier((inward_1, swapped_0, dcum_2))
        sum_1 = rest_1[1:] + inward_1[1:]
        swapped_1 = slide(sum_1, MIDDLE)
        first, near = run_project_more(
            2, groups, ((0,), (1,)), flip, [sum_1], dq, *grads_2, weights
        )
        outer = run_outer(firsts, swapped_0, swapped_1)
        outward = slide(outer, OUTWARD)

        def meanwhile(after):
            return run_adjoint(ints, (after, outer), [dcum_0, dcum_1, dcum_2], *house)

        last_parts, got, outer_2 = line_scatter_apart(
            first, near, far, last, meanwhile, share_sums, outward
        )
        outward, _ = lax.optimization_barrier((outward, outer_2))
        parts = (rest_0, inward_0, swapped_0, rest_1, inward_1, swapped_1)
        share = run_first_band(2, firsts, outward, *parts)
        share = run_last_band(share, *last_parts)
    else:
        spots = (owners * blocks + offsets).reshape(-1)
        empty = jnp.zeros((ctx_count * blocks, BLK, 2 * width), BF16)
        filled = empty.at[spots].add(outs[0])
        back = lax.psum_scatter(filled, "ctx", scatter_dimension=0, tiled=True)
        dcums = []
        share = jnp.zeros((tok_rows, w_query.shape[0] // groups), BF16)
        for j in range(blocks):
            term, dcum_out, _, _ = project(
                j, (tuple(range(groups)),), [], [[(back, j)]]
            )
            dcums.append(dcum_out)
            done = lax.psum_scatter(term, "head", scatter_dimension=0, tiled=False)
            share = lax.dynamic_update_slice(share, done, (j * BLK, 0))

        sums = run_adjoint(ints, (), dcums, unit, rows, inverse, heads, blocks)
        got = share_sums(sums)

    house_grad = run_house(ints, got, unit, rows, house_dirs, heads, blocks)
    return (share, house_grad)


def solution(mesh):
    placed = (
        P("ctx", "head"),
        P("ctx", "head"),
        P("ctx", "head"),
        P("ctx", "head"),
        P("ctx", "head"),
        P("ctx", None),
        P("ctx", None),
        P(None, "head"),
        P(None, "head"),
        P(None, "head"),
    )
    return jax.shard_map(
        shards,
        mesh=mesh,
        in_specs=placed,
        out_specs=(P("ctx", "head"), P("ctx", "head")),
        check_vma=False,
    )
```

```python
import functools
import math

import jax
import jax.numpy as jnp
from jax import lax
from jax.experimental import pallas as pl
from jax.experimental.pallas import tpu as pltpu
from jax.sharding import PartitionSpec as P

DH = 128
BLK = 128
MAXL = 2
HIGH = lax.Precision.HIGHEST
F32 = jnp.float32
BF16 = jnp.bfloat16


def nn(a, b):
    return lax.dot_general(a, b, (((1,), (0,)), ((), ())), preferred_element_type=F32)


def nt(a, b):
    return lax.dot_general(a, b, (((1,), (1,)), ((), ())), preferred_element_type=F32)


def tn(a, b):
    return lax.dot_general(a, b, (((0,), (0,)), ((), ())), preferred_element_type=F32)


def nn_high(a, b):
    return lax.dot_general(
        a, b, (((1,), (0,)), ((), ())), precision=HIGH, preferred_element_type=F32
    )


def nt_high(a, b):
    return lax.dot_general(
        a, b, (((1,), (1,)), ((), ())), precision=HIGH, preferred_element_type=F32
    )


def split(value):
    top = value.astype(BF16)
    return top, (value - top.astype(F32)).astype(BF16)


def iota(shape, dim):
    return lax.broadcasted_iota(jnp.int32, shape, dim)


def head(h):
    return slice(h * DH, (h + 1) * DH)


def listed(ints_ref, entry, entries):
    return ints_ref[1 + entry], ints_ref[1 + entries + entry]


def grant(mebibytes):
    return pltpu.CompilerParams(vmem_limit_bytes=mebibytes * 1024 * 1024)


def cost(microseconds):
    return pl.CostEstimate(
        flops=int(microseconds * 1.15e9), bytes_accessed=1 << 20, transcendentals=0
    )


def in_smem(count):
    return [pl.BlockSpec(memory_space=pltpu.SMEM)] * count


def in_vmem(count):
    return [pl.BlockSpec(memory_space=pltpu.VMEM)] * count


def chain_kernel(heads, parts, ints_ref, *refs):
    house_refs = refs[:parts]
    unit_ref, rows_ref, inv_ref, wide_ref, tall_ref, unit_h, house_all = refs[parts:]
    count = unit_ref.shape[0]
    span = count // parts
    for t, ref in enumerate(house_refs):
        place = (ints_ref[0] // (8 // parts)) ^ t if parts > 1 else 0
        house_all[pl.ds(pl.multiple_of(place * span, span), span), :] = ref[...]
    eye = (iota((count, count), 0) == iota((count, count), 1)).astype(F32)
    for h in range(heads):
        house = house_all[:, head(h)]
        lengths = jnp.sqrt(jnp.sum(house * house, axis=1, keepdims=True) + 1e-06)
        unit_ref[:, head(h)] = house / lengths
        unit_h[h] = house / lengths
        inv_ref[h] = eye

    def eliminate(step, carry):
        below = iota((count, 1), 0) > step
        for h in range(heads):
            pivot = unit_h[h, pl.ds(step, 1), :]
            overlap = jnp.sum(unit_h[h] * pivot, axis=1, keepdims=True)
            factor = jnp.where(below, 2.0 * overlap, 0.0)
            inv_ref[h] = inv_ref[h] - factor * inv_ref[h, pl.ds(step, 1), :]
        return carry

    lax.fori_loop(0, count, eliminate, 0)
    eye_wide = (iota((DH, DH), 0) == iota((DH, DH), 1)).astype(F32)
    for h in range(heads):
        units = unit_ref[:, head(h)]
        rows = nn_high(inv_ref[h], units)
        rows_ref[:, head(h)] = rows
        unit_hi, unit_lo = split(nt_high(eye_wide, units))
        rows_hi, rows_lo = split(rows)
        wide_ref[h] = jnp.concatenate([unit_hi, unit_hi, unit_lo], axis=1)
        tall_ref[h] = jnp.concatenate([rows_hi, rows_lo, rows_hi], axis=0)


def run_chain(ints, house_parts, heads):
    span, width = house_parts[0].shape
    parts = len(house_parts)
    count = span * parts
    return pl.pallas_call(
        functools.partial(chain_kernel, heads, parts),
        out_shape=[
            jax.ShapeDtypeStruct((count, width), F32),
            jax.ShapeDtypeStruct((count, width), F32),
            jax.ShapeDtypeStruct((heads, count, count), F32),
            jax.ShapeDtypeStruct((heads, DH, 3 * count), BF16),
            jax.ShapeDtypeStruct((heads, 3 * count, DH), BF16),
        ],
        in_specs=in_smem(1) + in_vmem(parts),
        out_specs=in_vmem(5),
        scratch_shapes=[pltpu.VMEM((heads, count, DH), F32), pltpu.VMEM((count, width), F32)],
        compiler_params=grant(12),
        cost_estimate=cost(6),
        name="house_chain",
    )(ints, *house_parts)


def rotate_kernel(
    heads,
    blocks,
    ints_ref,
    wide_ref,
    tall_ref,
    query_ref,
    key_ref,
    qrot_ref,
    krot_ref,
    local_ref,
    listed_ref,
):
    count = wide_ref.shape[2] // 3
    entries = blocks * MAXL
    column = iota((DH, 3 * count), 1) % count
    eye = (iota((DH, DH), 0) == iota((DH, DH), 1)).astype(F32)

    def cumulative(h, block):
        kept = jnp.where(column <= block, wide_ref[h].astype(F32), 0.0).astype(BF16)
        return split(eye - 2.0 * nn(kept, tall_ref[h]))

    base = ints_ref[0] * blocks

    def local_block(b, carry):
        here = pl.ds(pl.multiple_of(b * BLK, BLK), BLK)
        for h in range(heads):
            hi, lo = cumulative(h, base + b)
            local_ref[b, h] = hi
            query, key = query_ref[here, head(h)], key_ref[here, head(h)]
            qrot_ref[here, head(h)] = (nn(query, hi) + nn(query, lo)).astype(BF16)
            krot_ref[here, head(h)] = (nn(key, hi) + nn(key, lo)).astype(BF16)
        return carry

    lax.fori_loop(0, blocks, local_block, 0)

    def listed_block(e, carry):
        owner, offset = listed(ints_ref, e, entries)
        for h in range(heads):
            hi, lo = cumulative(h, owner * blocks + offset)
            listed_ref[e, h, :DH] = hi
            listed_ref[e, h, DH:] = lo
        return carry

    lax.fori_loop(0, entries, listed_block, 0)


def run_rotate(ints, wide, tall, query_rows, key_rows, heads, blocks):
    rows, width = query_rows.shape
    entries = blocks * MAXL
    return pl.pallas_call(
        functools.partial(rotate_kernel, heads, blocks),
        out_shape=[
            jax.ShapeDtypeStruct((rows, width), BF16),
            jax.ShapeDtypeStruct((rows, width), BF16),
            jax.ShapeDtypeStruct((blocks, heads, DH, DH), BF16),
            jax.ShapeDtypeStruct((entries, heads, 2 * DH, DH), BF16),
        ],
        in_specs=in_smem(1) + in_vmem(4),
        out_specs=in_vmem(4),
        compiler_params=grant(16),
        cost_estimate=cost(9),
        name="rotate",
    )(ints, wide, tall, query_rows, key_rows)


def attend_kernel(heads, blocks, places, pieces, *refs):
    ints_ref = refs[0]
    source_count = 1 + max(place[0] for pair in places for place in pair)
    sources = refs[1 : 1 + source_count]
    refs = refs[1 + source_count :]
    (query_ref, qrot_ref, krot_ref, value_ref, grad_ref, local_ref, listed_ref) = refs[:7]
    dq_ref, dcum_ref, dk_ref, dv_ref = refs[7:11]
    outs = refs[11 : 11 + max(len(pieces), 1)]
    refs = refs[11 + max(len(pieces), 1) :]
    dq_all, dcum_all, dk_all, dv_all, grad_sems, far_keys, far_values, sems = refs[:8]
    entries = blocks * MAXL
    scaling = DH ** (-0.5)
    log_scale = scaling * math.log2(math.e)

    def start(e, src, kind, slot, where):
        pltpu.make_async_copy(src.at[where], slot.at[e], sems.at[kind, e]).start()

    for e in range(entries):
        owner, offset = listed(ints_ref, e, entries)
        row = pl.multiple_of(offset * BLK, BLK)
        if len(places) == 1:
            start(e, sources[0], 0, far_keys, (owner, pl.ds(row, BLK)))
            start(e, sources[1], 1, far_values, (owner, pl.ds(row, BLK)))
        else:
            distance = owner ^ ints_ref[0]
            for r, (key_place, value_place) in enumerate(places):

                @pl.when(distance == r)
                def _():
                    source, first = key_place
                    start(e, sources[source], 0, far_keys, pl.ds(first + row, BLK))
                    source, first = value_place
                    start(e, sources[source], 1, far_values, pl.ds(first + row, BLK))

    out_copies = []
    if pieces:
        payloads, out_sems = refs[8 : 8 + heads], refs[8 + heads]
        for payload in payloads:
            payload[...] = jnp.zeros_like(payload)
    for kind, slots in ((0, far_keys), (1, far_values)):
        for e in range(entries):
            pltpu.make_async_copy(slots.at[e], slots.at[e], sems.at[kind, e]).wait()

    later = iota((BLK, BLK), 0) > iota((BLK, BLK), 1)
    empty = jnp.zeros((BLK, DH), BF16)
    steps = range(blocks)
    for h in range(heads):
        lanes = head(h)
        spans = [slice(a * BLK, (a + 1) * BLK) for a in steps]
        both, keys, values = [], [], []
        for a in steps:
            qrot, grad = qrot_ref[spans[a], lanes], grad_ref[spans[a], lanes]
            upper = jnp.concatenate([qrot, empty], axis=1)
            lower = jnp.concatenate([empty, grad], axis=1)
            both.append(jnp.concatenate([upper, lower], axis=0))
            keys.append([krot_ref[spans[b], lanes] for b in range(a + 1)])
            values.append([value_ref[spans[b], lanes] for b in range(a + 1)])
            for l in range(MAXL):
                e = a * MAXL + l
                raw = far_keys[e, :, lanes]
                raw = jnp.concatenate([raw, raw], axis=1)
                keys[a].append(nn(raw, listed_ref[e, h]).astype(BF16))
                values[a].append(far_values[e, :, lanes])
        scores, dprobs, tops = [], [], []
        for a in steps:
            scores.append([])
            dprobs.append([])
            top = None
            for b in range(a + 1 + MAXL):
                pair = nt(jnp.concatenate([keys[a][b], values[a][b]], axis=1), both[a])
                part = pair[:, :BLK] * log_scale
                if b == a:
                    part = jnp.where(later, -jnp.inf, part)
                scores[a].append(part)
                dprobs[a].append(pair[:, BLK:])
                top = part if top is None else jnp.maximum(top, part)
            tops.append(jnp.max(top, axis=0, keepdims=True))
        weights, inverses, deltas = [], [], []
        for a in steps:
            weights.append([])
            total, inner = None, None
            for part, dprob in zip(scores[a], dprobs[a]):
                weight = jnp.exp2(part - tops[a])
                weights[a].append(weight)
                product = weight * dprob
                total = weight if total is None else total + weight
                inner = product if inner is None else inner + product
            inverses.append(1.0 / jnp.sum(total, axis=0, keepdims=True))
            deltas.append(jnp.sum(inner, axis=0, keepdims=True) * inverses[a])
        dscores, pairs = [], []
        for a in steps:
            dscores.append([])
            pairs.append([])
            for b in range(a + 1 + MAXL):
                probs = weights[a][b] * inverses[a]
                dscore = (probs * (dprobs[a][b] - deltas[a])).astype(BF16)
                dscores[a].append(dscore)
                wide = jnp.concatenate([dscore, probs.astype(BF16)], axis=1)
                pairs[a].append(nn(wide, both[a]))
        for b in steps:
            total = pairs[b][b]
            for a in range(b + 1, blocks):
                total = total + pairs[a][b]
            dk_all[h, spans[b]] = total[:, :DH] * scaling
            dv_all[h, spans[b]] = total[:, DH:]
        for e in range(entries):
            pair = pairs[e // MAXL][e // MAXL + 1 + e % MAXL]
            dkey, dvalue = (pair[:, :DH] * scaling).astype(BF16), pair[:, DH:].astype(BF16)
            if pieces:
                owner, offset = listed(ints_ref, e, entries)
                distance = owner ^ ints_ref[0]
                at = (distance & 1) * blocks + offset
                payloads[h][at, distance >> 1, :, :DH] += dkey
                payloads[h][at, distance >> 1, :, DH:] += dvalue
            else:
                outs[0][e, :, 2 * h * DH : (2 * h + 1) * DH] = dkey
                outs[0][e, :, (2 * h + 1) * DH : (2 * h + 2) * DH] = dvalue
        halves = []
        for a in steps:
            wide, tall = jnp.concatenate(dscores[a], axis=0), jnp.concatenate(keys[a], axis=0)
            halves.append(split(tn(wide, tall) * scaling))
        for a in steps:
            dq_top, dq_low = halves[a]
            dq_all[h, spans[a]] = nt(dq_top, local_ref[a, h]).astype(BF16)
            query = query_ref[spans[a], lanes]
            query = jnp.concatenate([query, query], axis=0)
            dcum_all[h, a] = tn(query, jnp.concatenate([dq_top, dq_low], axis=0))
        for i, (source, where) in enumerate(
            (
                (dk_all.at[h], dk_ref.at[:, lanes]),
                (dv_all.at[h], dv_ref.at[:, lanes]),
                (dq_all.at[h], dq_ref.at[:, lanes]),
                (dcum_all.at[h], dcum_ref.at[:, h]),
            )
        ):
            copy = pltpu.make_async_copy(source, where, grad_sems.at[i, h])
            copy.start()
            out_copies.append(copy)
        for i, (first, size) in enumerate(pieces):
            where = outs[i].at[:, :, :, 2 * h * DH : (2 * h + 2) * DH]
            source = payloads[h].at[pl.ds(first, size)]
            copy = pltpu.make_async_copy(source, where, out_sems.at[i, h])
            copy.start()
            out_copies.append(copy)
    for copy in out_copies:
        copy.wait()


def run_attend(ints, sources, places, arrays, heads, blocks, pieces):
    rows, width = arrays[0].shape
    entries = blocks * MAXL
    any_spec = pl.BlockSpec(memory_space=pl.ANY)
    scratch = [
        pltpu.VMEM((heads, rows, DH), BF16),
        pltpu.VMEM((heads, blocks, DH, DH), F32),
        pltpu.VMEM((heads, rows, DH), F32),
        pltpu.VMEM((heads, rows, DH), F32),
        pltpu.SemaphoreType.DMA((4, heads)),
        pltpu.VMEM((entries, BLK, width), BF16),
        pltpu.VMEM((entries, BLK, width), BF16),
        pltpu.SemaphoreType.DMA((2, entries)),
    ]
    if pieces:
        chips = len(places) // 2
        out_parts = [
            pltpu.HBM((size, chips, BLK, 2 * width), BF16) for _, size in pieces
        ]
        part_specs = [any_spec] * len(pieces)
        scratch += [pltpu.VMEM((2 * blocks, chips, BLK, 2 * DH), BF16)] * heads
        scratch += [pltpu.SemaphoreType.DMA((len(pieces), heads))]
    else:
        out_parts = [jax.ShapeDtypeStruct((entries, BLK, 2 * width), BF16)]
        part_specs = in_vmem(1)
    return pl.pallas_call(
        functools.partial(attend_kernel, heads, blocks, places, pieces),
        out_shape=[
            pltpu.HBM((rows, width), BF16),
            pltpu.HBM((blocks, heads, DH, DH), F32),
            pltpu.HBM((rows, width), F32),
            pltpu.HBM((rows, width), F32),
        ]
        + out_parts,
        in_specs=in_smem(1) + [any_spec] * len(sources) + in_vmem(7),
        out_specs=[pl.BlockSpec(memory_space=pltpu.HBM)] * 4 + part_specs,
        scratch_shapes=scratch,
        compiler_params=grant(36),
        cost_estimate=cost(15),
        name="attend",
    )(ints, *sources, *arrays)


def merge_kernel(own_ref, got_ref, *refs):
    for i, ref in enumerate(refs[-3:]):
        total = own_ref[0, i + 1].astype(F32) + got_ref[0, i + 1].astype(F32)
        ref[0] = total.astype(BF16)


def run_merge(own, got, first, size, afters):
    _, chips, rows, width = own.shape
    cut = 2
    lanes = width // cut
    whole = pl.BlockSpec((1, chips, rows, lanes), lambda j, c: (first + j, 0, 0, c))
    return pl.pallas_call(
        merge_kernel,
        grid=(size, cut),
        out_shape=[jax.ShapeDtypeStruct((size, rows, width), BF16)] * (chips - 1),
        in_specs=[whole] * 2
        + [pl.BlockSpec((1, 16, 128), lambda j, c: (0, 0, 0))] * len(afters),
        out_specs=[pl.BlockSpec((1, rows, lanes), lambda j, c: (j, 0, c))] * (chips - 1),
        compiler_params=grant(60),
        cost_estimate=cost(2),
        name="merge",
    )(own, got, *afters)


def start_tiles(chunks, groups, flip_ref, weight_refs, tiles, sems):
    count, _, tile, _ = tiles.shape
    per = count // len(chunks)
    copies = []
    for t in range(count):
        m = chunks[t // per][0]
        row = ((m + flip_ref[0] * (groups - 1 - 2 * m)) * per + t % per) * tile
        rows = pl.ds(pl.multiple_of(row, tile), tile)
        for w, ref in enumerate(weight_refs):
            copy = pltpu.make_async_copy(ref.at[rows], tiles.at[t, w], sems.at[t, w])
            copy.start()
            copies.append(copy)
    return copies


def multiply_tiles(chunks, copies, tiles, out_refs, grads_of):
    count, _, tile, _ = tiles.shape
    per = count // len(chunks)
    for t in range(count):
        term = None
        m, out, at = chunks[t // per]
        for w, grad in enumerate(grads_of(m)):
            copies[3 * t + w].wait()
            part = nt(tiles[t, w], grad)
            term = part if term is None else term + part
        spot = slice(t % per * tile, (t % per + 1) * tile)
        out_refs[out][at, :, spot] = term.T.astype(BF16)


def project_kernel(heads, parts, size, groups, before, layout, afters, flip_ref, *refs):
    refs = refs[afters:]
    outs = len(layout)
    chunks = [(m, i, at) for i, row in enumerate(layout) for at, m in enumerate(row)]
    tiles, sems = refs[-2:]
    part_refs, refs = refs[: size * parts], refs[size * parts :]
    before_refs, refs = refs[:before], refs[before:]
    dk_loc, dv_loc, dq_ref, key_ref, dcum_in, cum_ref = refs[:6]
    weight_refs, out_refs = refs[6:9], refs[9 : 9 + outs]
    dcum_out, dk_out, dv_out = refs[9 + outs : 12 + outs]
    copies = start_tiles(chunks, groups, flip_ref, weight_refs, tiles, sems)
    earlier = ()
    dk_rows, dv_rows = [], []
    for j in range(size):
        here = slice(j * BLK, (j + 1) * BLK)
        dk, dv = [], []
        for h in range(heads):
            both = slice(2 * h * DH, (2 * h + 2) * DH)
            total = part_refs[j * parts][0, :, both].astype(F32)
            for ref in part_refs[j * parts + 1 : (j + 1) * parts]:
                total = total + ref[0, :, both].astype(F32)
            dv.append((dv_loc[here, head(h)] + total[:, DH:]).astype(BF16))
            dk_top, dk_low = split(dk_loc[here, head(h)] + total[:, :DH])
            dk.append(nt(dk_top, cum_ref[j, h]).astype(BF16))
            key = key_ref[here, head(h)]
            key = jnp.concatenate([key, key], axis=0)
            dcum = tn(key, jnp.concatenate([dk_top, dk_low], axis=0))
            dcum_out[j, h] = dcum_in[j, h] + dcum
        dk_rows.append(jnp.concatenate(dk, axis=1))
        dv_rows.append(jnp.concatenate(dv, axis=1))
    dk_all, dv_all = jnp.concatenate(dk_rows, axis=0), jnp.concatenate(dv_rows, axis=0)
    dk_out[...] = dk_all
    dv_out[...] = dv_all
    grads = (dq_ref[...], dk_all, dv_all)
    if before:
        earlier = [
            jnp.concatenate([old[...], new], axis=0) for old, new in zip(before_refs, grads)
        ]

    multiply_tiles(
        chunks, copies, tiles, out_refs, lambda m: earlier if before and m == 0 else grads
    )


def project_more_kernel(groups, layout, afters, flip_ref, *refs):
    refs = refs[afters:]
    chunks = [(m, i, at) for i, row in enumerate(layout) for at, m in enumerate(row)]
    tiles, sems = refs[-2:]
    copies = start_tiles(chunks, groups, flip_ref, refs[3:6], tiles, sems)
    grads = [ref[...] for ref in refs[:3]]
    multiply_tiles(chunks, copies, tiles, refs[6:-2], lambda m: grads)


def run_project_more(block, groups, layout, flip, afters, dq, dk, dv, weights):
    rows, width = dk.shape
    model = weights[0].shape[0]
    chunk = model // groups
    tile = min(512, chunk)
    tile_count = sum(map(len, layout)) * chunk // tile

    def whole(*shape):
        return pl.BlockSpec(shape, lambda t: (0,) * len(shape))

    shapes = [(len(row), rows, chunk) for row in layout]
    return pl.pallas_call(
        functools.partial(project_more_kernel, groups, layout, len(afters)),
        grid=(1,),
        in_specs=in_smem(1)
        + [whole(1, 16, 128)] * len(afters)
        + [pl.BlockSpec((rows, width), lambda t: (block * BLK // rows, 0))]
        + [whole(rows, width)] * 2
        + [pl.BlockSpec(memory_space=pl.ANY)] * 3,
        out_specs=[whole(*shape) for shape in shapes],
        scratch_shapes=[
            pltpu.VMEM((tile_count, 3, tile, width), BF16),
            pltpu.SemaphoreType.DMA((tile_count, 3)),
        ],
        out_shape=[jax.ShapeDtypeStruct(shape, BF16) for shape in shapes],
        compiler_params=grant(60),
        cost_estimate=cost(3 * sum(map(len, layout))),
        name="project_more",
    )(flip, *afters, dq, dk, dv, *weights)


def run_project(block, groups, layout, flip, afters, parts, before, arrays, weights):
    dk_loc, dv_loc, dq, key_rows, dcum, cum = arrays
    size, width = len(parts), dq.shape[1]
    heads = width // DH
    model = weights[0].shape[0]
    chunk = model // groups
    tile = min(512, chunk)
    rows = size * BLK
    tile_count = sum(map(len, layout)) * chunk // tile

    def part_spec(index):
        return pl.BlockSpec((1, BLK, 2 * width), lambda t: (index, 0, 0))

    def whole(*shape):
        return pl.BlockSpec(shape, lambda t: (0,) * len(shape))

    rows_spec = pl.BlockSpec((rows, width), lambda t: (block // size, 0))
    head_spec = pl.BlockSpec((size, heads, DH, DH), lambda t: (block // size, 0, 0, 0))
    flat = [part for row in parts for part in row]
    heights = [2 * rows if before and row == (0,) else rows for row in layout]
    shapes = [(len(row), height, chunk) for row, height in zip(layout, heights)]
    return pl.pallas_call(
        functools.partial(
            project_kernel,
            heads,
            len(parts[0]),
            size,
            groups,
            len(before),
            layout,
            len(afters),
        ),
        grid=(1,),
        in_specs=in_smem(1)
        + [whole(1, min(16, after.shape[1]), 128) for after in afters]
        + [part_spec(index) for _, index in flat]
        + [whole(rows, width)] * len(before)
        + [rows_spec] * 4
        + [head_spec] * 2
        + [pl.BlockSpec(memory_space=pl.ANY)] * 3,
        out_specs=[whole(*shape) for shape in shapes]
        + [whole(size, heads, DH, DH)]
        + [whole(rows, width)] * 2,
        scratch_shapes=[
            pltpu.VMEM((tile_count, 3, tile, width), BF16),
            pltpu.SemaphoreType.DMA((tile_count, 3)),
        ],
        out_shape=[jax.ShapeDtypeStruct(shape, BF16) for shape in shapes]
        + [jax.ShapeDtypeStruct((size, heads, DH, DH), F32)]
        + [jax.ShapeDtypeStruct((rows, width), BF16)] * 2,
        compiler_params=grant(60),
        cost_estimate=cost(3 * sum(map(len, layout))),
        name="project",
    )(
        flip,
        *afters,
        *[part for part, _ in flat],
        *before,
        dk_loc,
        dv_loc,
        dq,
        key_rows,
        dcum,
        cum,
        *weights,
    )


def adjoint_kernel(heads, blocks, afters, ints_ref, *refs):
    refs = refs[afters:]
    dcums = [ref.at[j] for ref in refs[:-4] for j in range(ref.shape[0])]
    unit_ref, rows_ref, inv_ref, out_ref = refs[-4:]
    count, width = unit_ref.shape
    stacked = (len(dcums) * count, count)
    eye = (iota((count, count), 0) == iota((count, count), 1)).astype(F32)
    base = ints_ref[0] * blocks
    level, col = iota(stacked, 0), iota(stacked, 1)
    row = level % count
    mine = base + level // count
    alive = row[:, :1] <= mine[:, :1]
    every = range(heads)
    units = [unit_ref[:, head(h)] for h in every]
    moved = [[nt_high(rows_ref[:, head(h)], dcum[h]) for dcum in dcums] for h in every]
    moved = [jnp.concatenate(parts, axis=0) for parts in moved]
    inverse_t = [nt_high(eye, inv_ref[h]) for h in every]
    overlap = [jnp.where(col <= mine, nt_high(moved[h], units[h]), 0.0) for h in every]
    beta = [jnp.concatenate([eye - inverse_t[h]] * len(dcums), axis=0) for h in every]
    beta = [jnp.where(col <= mine, beta[h], 0.0) for h in every]
    turned = [nn_high(beta[h], units[h]) for h in every]
    gamma = [nn_high(overlap[h], inv_ref[h]) for h in every]
    gamma = [jnp.where((row < col) & (col <= mine), gamma[h], 0.0) for h in every]
    lifted = [nn_high(gamma[h], units[h]) for h in every]
    for h in every:
        x_all = jnp.where(alive, moved[h] - 2.0 * lifted[h], 0.0)
        own = jnp.concatenate([units[h]] * len(dcums), axis=0)
        own = jnp.where(alive, own - turned[h], 0.0)
        x_total, y_total = None, None
        for j, dcum in enumerate(dcums):
            here = slice(j * count, (j + 1) * count)
            y_part = nn_high(own[here], dcum[h])
            x_total = x_all[here] if j == 0 else x_total + x_all[here]
            y_total = y_part if j == 0 else y_total + y_part
        for total, lanes in (
            (x_total, head(h)),
            (y_total, slice(width + h * DH, width + (h + 1) * DH)),
        ):
            for c in range(count // blocks):
                out_ref[c, :, lanes] = total[c * blocks : (c + 1) * blocks]


def run_adjoint(ints, afters, dcums, unit, rows, inverse, heads, blocks):
    count, width = unit.shape
    return pl.pallas_call(
        functools.partial(adjoint_kernel, heads, blocks, len(afters)),
        out_shape=jax.ShapeDtypeStruct((count // blocks, blocks, 2 * width), F32),
        in_specs=in_smem(1)
        + [pl.BlockSpec(memory_space=pl.ANY)] * len(afters)
        + in_vmem(len(dcums) + 3),
        out_specs=pl.BlockSpec(memory_space=pltpu.VMEM),
        compiler_params=grant(16),
        cost_estimate=cost(0.2),
        name="adjoint",
    )(ints, *afters, *dcums, unit, rows, inverse)


def house_kernel(heads, blocks, base_ref, got_ref, unit_ref, rows_ref, house_ref, out_ref):
    count, width = unit_ref.shape
    total = jnp.sum(got_ref[...], axis=0)
    for h in range(heads):
        x_part = total[:, head(h)]
        y_part = total[:, slice(width + h * DH, width + (h + 1) * DH)]
        along = nt_high(y_part, rows_ref[:, head(h)])
        spot = iota((blocks, count), 0) + base_ref[0] * blocks
        along = jnp.where(iota((blocks, count), 1) < spot, along, 0.0)
        turned = y_part - 2.0 * nn_high(along, unit_ref[:, head(h)])
        dunit = -2.0 * (x_part + turned)
        house = house_ref[:, head(h)]
        lengths = jnp.sqrt(jnp.sum(house * house, axis=1, keepdims=True) + 1e-06)
        unit = house / lengths
        inner = jnp.sum(unit * dunit, axis=1, keepdims=True)
        out_ref[:, head(h)] = (dunit - unit * inner) / lengths


def run_house(ints, got, unit, rows, house_dirs, heads, blocks):
    return pl.pallas_call(
        functools.partial(house_kernel, heads, blocks),
        out_shape=jax.ShapeDtypeStruct(house_dirs.shape, F32),
        in_specs=in_smem(1) + in_vmem(4),
        out_specs=pl.BlockSpec(memory_space=pltpu.VMEM),
        compiler_params=grant(12),
        cost_estimate=cost(2),
        name="house_grad",
    )(ints, got, unit, rows, house_dirs)


def hop(value, distance, count):
    return lax.ppermute(value, "ctx", [(i, i ^ distance) for i in range(count)])


def slide(value, pairs):
    return lax.ppermute(value, "head", pairs)


INWARD = [(0, 1), (3, 2)]
MIDDLE = [(1, 2), (2, 1)]
OUTWARD = [(1, 0), (2, 3)]


def last_band_kernel(ends_ref, share_ref, first_ref, near_ref, inward_ref, far_ref, *refs):
    outward_ref, out_ref = refs
    total = jnp.where(ends_ref[0] > 0, first_ref[0], near_ref[0]).astype(F32)
    total = total + inward_ref[0].astype(F32)
    total = total + (far_ref[0].astype(F32) + outward_ref[0].astype(F32))
    out_ref[...] = total.astype(BF16)


def run_last_band(share, *parts):
    _, rows, width = parts[0].shape
    tile = min(512, width)
    band = share.shape[0] // rows - 1
    return pl.pallas_call(
        last_band_kernel,
        grid=(width // tile,),
        out_shape=jax.ShapeDtypeStruct(share.shape, BF16),
        in_specs=in_smem(1)
        + [pl.BlockSpec(memory_space=pl.ANY)]
        + [pl.BlockSpec((1, rows, tile), lambda t: (0, 0, t))] * len(parts),
        out_specs=pl.BlockSpec((rows, tile), lambda t: (band, t)),
        input_output_aliases={1: 0},
        compiler_params=grant(12),
        cost_estimate=cost(2),
        name="last_band",
    )(line_ends(), share, *parts)


def line_ends():
    place = lax.axis_index("head")
    return ((place == 0) | (place == 3)).astype(jnp.int32).reshape(1)


def outer_kernel(first_ref, low_ref, high_ref, out_ref):
    rows = low_ref.shape[1]
    for i, ref in enumerate((low_ref, high_ref)):
        here = slice(i * rows, (i + 1) * rows)
        out_ref[0, here] = (first_ref[0, here].astype(F32) + ref[0].astype(F32)).astype(BF16)


def run_outer(firsts, low, high):
    _, rows, width = low.shape
    swapped = pl.BlockSpec((1, rows, width), lambda t: (1, 0, 0))
    both = pl.BlockSpec((1, 2 * rows, width), lambda t: (0, 0, 0))
    return pl.pallas_call(
        outer_kernel,
        grid=(1,),
        out_shape=jax.ShapeDtypeStruct(firsts.shape, BF16),
        in_specs=[both, swapped, swapped],
        out_specs=both,
        compiler_params=grant(12),
        cost_estimate=cost(2),
        name="outer",
    )(firsts, low, high)


def first_band_kernel(ends_ref, first_ref, outward_ref, *refs):
    out_ref = refs[-1]
    rows = refs[0].shape[1]
    for i in range(2):
        here = slice(i * rows, (i + 1) * rows)
        rest_ref, inward_ref, swapped_ref = refs[3 * i : 3 * i + 3]
        total = jnp.where(ends_ref[0] > 0, first_ref[0, here], rest_ref[0]).astype(F32)
        total = total + inward_ref[0].astype(F32)
        total = total + (swapped_ref[0].astype(F32) + outward_ref[0, here].astype(F32))
        out_ref[here] = total.astype(BF16)


def run_first_band(bands, firsts, outward, *parts):
    _, height, width = firsts.shape
    tile = min(512, width)
    both = pl.BlockSpec((1, height, tile), lambda t: (0, 0, t))
    part = pl.BlockSpec((1, height // 2, tile), lambda t: (0, 0, t))
    return pl.pallas_call(
        first_band_kernel,
        grid=(width // tile,),
        out_shape=jax.ShapeDtypeStruct((bands * height, width), BF16),
        in_specs=in_smem(1) + [both] * 2 + [part] * len(parts),
        out_specs=pl.BlockSpec((height, tile), lambda t: (0, t)),
        compiler_params=grant(12),
        cost_estimate=cost(2),
        name="first_band",
    )(line_ends(), firsts, outward, *parts)


def line_scatter_apart(first, near, far, last, meanwhile, exchange, earlier):
    in_last, in_far = slide(last, INWARD), slide(far, INWARD)
    in_last, first = lax.optimization_barrier((in_last, first))
    sum_last = last + in_last
    swap_last = slide(sum_last, MIDDLE)
    other = meanwhile(sum_last)
    in_far, other = lax.optimization_barrier((in_far, other))
    sum_far = far + in_far
    swap_far = slide(sum_far, MIDDLE)
    swap_last, *_ = lax.optimization_barrier((swap_last, earlier, sum_far))
    outer = first + swap_last
    outward = slide(outer, OUTWARD)
    other, near, _ = lax.optimization_barrier((other, near, outer))
    in_near = slide(near, INWARD)
    return (first, near, in_near, swap_far, outward), exchange(other), outer


def shards(
    query_rows, key_rows, value_rows, grad_out, house_dirs, owners, offsets, w_query, w_key, w_value
):
    tok_rows, width = query_rows.shape
    heads, blocks = width // DH, tok_rows // BLK
    ctx_count, groups = lax.axis_size("ctx"), lax.axis_size("head")
    my_index = lax.axis_index("ctx").astype(jnp.int32)
    ints = jnp.concatenate([my_index.reshape(1), owners.reshape(-1), offsets.reshape(-1)])
    by_hand = ctx_count == 8 and groups == 4 and blocks == 4
    core, across, along = 1, 2, 4

    if by_hand:
        other = hop(house_dirs, core, 8)
        upper = (my_index & core) != 0
        low, high = jnp.where(upper, other, house_dirs), jnp.where(upper, house_dirs, other)
        house_pair = jnp.concatenate([low, high], axis=0)
        value_x, key_y = hop(value_rows, across, 8), hop(key_rows, along, 8)
        key_x, value_y = hop(key_rows, across, 8), hop(value_rows, along, 8)
        house_late, *_ = lax.optimization_barrier((house_pair, value_x, key_y))
        house_parts = [house_pair] + [hop(house_late, t, 8) for t in (2, 4, 6)]
        key_d, value_d = hop(key_y, across, 8), hop(value_x, along, 8)
    else:
        house_parts = [lax.all_gather(house_dirs, "ctx", axis=0, tiled=True)]

    unit, rows, inverse, wide, tall = run_chain(ints, house_parts, heads)
    ready = query_rows
    if by_hand:
        own = (key_rows, value_rows, key_x, value_x, key_y, value_y, key_d, value_d)
        early = lax.optimization_barrier((*own[:6], *house_parts))[:6]
        siblings = [hop(part, core, 8) for part in early]
        ready, *_ = lax.optimization_barrier((query_rows, *siblings[:3]))
    qrot, krot, local, listed_cum = run_rotate(ints, wide, tall, ready, key_rows, heads, blocks)
    if by_hand:
        late = lax.optimization_barrier((*own[6:], qrot))[:2]
        siblings += [hop(part, core, 8) for part in late]
        sources, places = [], []
        for t in range(4):
            for pair in (own[2 * t : 2 * t + 2], siblings[2 * t : 2 * t + 2]):
                places.append(((len(sources), 0), (len(sources) + 1, 0)))
                sources += pair
    else:
        sources = [lax.all_gather(key_rows, "ctx"), lax.all_gather(value_rows, "ctx")]
        places = [((0, 0), (1, 0))]

    rounds = ((0, 1), (1, blocks - 1), (blocks, 1), (blocks + 1, blocks - 1))
    dq, dcum, dk_loc, dv_loc, *outs = run_attend(
        ints,
        sources,
        places,
        (query_rows, qrot, krot, value_rows, grad_out, local, listed_cum),
        heads,
        blocks,
        rounds if by_hand else (),
    )
    weights = (w_query, w_key, w_value)
    flip = jnp.where(by_hand & (lax.axis_index("head") >= 2), 1, 0).astype(jnp.int32).reshape(1)

    arrays = (dk_loc, dv_loc, dq, key_rows, dcum, local)

    def project(block, layout, afters, parts, before=()):
        return run_project(block, groups, layout, flip, afters, parts, before, arrays, weights)

    def share_sums(sums):
        return lax.all_to_all(sums, "ctx", split_axis=0, concat_axis=0, tiled=True)

    if by_hand:
        got_0 = hop(outs[2], core, 8)
        got_1 = hop(lax.optimization_barrier((outs[3], got_0))[0], core, 8)
        sent_0 = run_merge(outs[0], got_0, 0, 1, [])
        sent_1 = run_merge(outs[1], got_1, 0, 1, [sent_0[0]])
        sent_2 = run_merge(outs[1], got_1, 1, 2, [sent_1[0]])

        def give_back(own, got, first, sent):
            back = [hop(part, t, 8) for part, t in zip(sent, (across, along, across + along))]
            near = [part.reshape(-1, BLK, 2 * width) for part in (own, got)]
            parts = []
            for j in range(sent[0].shape[0]):
                mine = [(part, 4 * (first + j)) for part in near]
                parts.append(mine + [(part, j) for part in back])
            return parts, back

        parts_0, back_0 = give_back(outs[0], got_0, 0, sent_0)
        *later_1, _, _ = lax.optimization_barrier((*sent_1, back_0, sent_2))
        parts_1, back_1 = give_back(outs[1], got_1, 0, later_1)
        *later_2, _ = lax.optimization_barrier((*sent_2, back_1))
        parts_2, _ = give_back(outs[1], got_1, 1, later_2)
        rest_0, dcum_0, *grads_0 = project(0, ((1, 2, 3),), [sent_2[0]], parts_0)
        before = (dq, *grads_0)
        split_off = ((0,), (1, 2, 3))
        firsts, rest_1, dcum_1, *_ = project(1, split_off, [rest_0], parts_1, before)
        inward_0, inward_1 = slide(rest_0, INWARD), slide(rest_1, INWARD)
        house = (unit, rows, inverse, heads, blocks)
        far, last, dcum_2, *grads_2 = project(2, ((2,), (3,)), [rest_1], parts_2)
        swapped_0 = slide(rest_0[1:] + inward_0[1:], MIDDLE)
        inward_1, *_ = lax.optimization_barrier((inward_1, swapped_0, dcum_2))
        sum_1 = rest_1[1:] + inward_1[1:]
        swapped_1 = slide(sum_1, MIDDLE)
        first, near = run_project_more(
            2, groups, ((0,), (1,)), flip, [sum_1], dq, *grads_2, weights
        )
        outer = run_outer(firsts, swapped_0, swapped_1)
        outward = slide(outer, OUTWARD)

        def meanwhile(after):
            return run_adjoint(ints, (after, outer), [dcum_0, dcum_1, dcum_2], *house)

        last_parts, got, outer_2 = line_scatter_apart(
            first, near, far, last, meanwhile, share_sums, outward
        )
        outward, _ = lax.optimization_barrier((outward, outer_2))
        parts = (rest_0, inward_0, swapped_0, rest_1, inward_1, swapped_1)
        share = run_first_band(2, firsts, outward, *parts)
        share = run_last_band(share, *last_parts)
    else:
        spots = (owners * blocks + offsets).reshape(-1)
        empty = jnp.zeros((ctx_count * blocks, BLK, 2 * width), BF16)
        filled = empty.at[spots].add(outs[0])
        back = lax.psum_scatter(filled, "ctx", scatter_dimension=0, tiled=True)
        dcums = []
        share = jnp.zeros((tok_rows, w_query.shape[0] // groups), BF16)
        for j in range(blocks):
            term, dcum_out, _, _ = project(
                j, (tuple(range(groups)),), [], [[(back, j)]]
            )
            dcums.append(dcum_out)
            done = lax.psum_scatter(term, "head", scatter_dimension=0, tiled=False)
            share = lax.dynamic_update_slice(share, done, (j * BLK, 0))

        sums = run_adjoint(ints, (), dcums, unit, rows, inverse, heads, blocks)
        got = share_sums(sums)

    house_grad = run_house(ints, got, unit, rows, house_dirs, heads, blocks)
    return (share, house_grad)


def solution(mesh):
    placed = (
        P("ctx", "head"),
        P("ctx", "head"),
        P("ctx", "head"),
        P("ctx", "head"),
        P("ctx", "head"),
        P("ctx", None),
        P("ctx", None),
        P(None, "head"),
        P(None, "head"),
        P(None, "head"),
    )
    return jax.shard_map(
        shards,
        mesh=mesh,
        in_specs=placed,
        out_specs=(P("ctx", "head"), P("ctx", "head")),
        check_vma=False,
    )
```
